32 devices in a mesh: mod: 4 (over y, x), slab: 4 (over z), sub: 2 (over core).
Axes of the slice: x: 2, y: 2, z: 4, core: 2. Of those that a mesh axis runs over, the one named last changes fastest.
Arguments:
- design: float32 [8, 128, 128], P('slab', 'sub'), may hold values from 0.1 to 1
- fixed_mask: int32 [3, 32, 128, 128], P(None, ('mod', 'slab'), 'sub'), may hold values from 0 to 1, as said below
- load_mask: int32 [3, 32, 128, 128], P(None, ('mod', 'slab'), 'sub'), may hold values from 0 to 1, as said below
Outputs:
- displacement: float32 [3, 32, 128, 128], P(None, ('mod', 'slab'), 'sub')
- gradient: float32 [8, 128, 128], P('slab', 'sub')
The draws below stay inside these ranges and needn't reach their ends.
Inputs may be any that keep to these rules, and one draw needn't show every extreme that they name: `fixed_mask`: 1 marks a supported degree of freedom. `load_mask`: 1 marks a loaded degree of freedom, carrying a unit force.
All inputs are finite; a program needn't handle non-finite values.
Results may differ from the reference program's by a relative error of at most 0.013.
Values sent between devices are 32-bit elements; how exact they have to be, the bound alone decides.
No kernel may reach another device: no remote copies, remote signals or barrier semaphores. Data moves between devices by JAX's collectives and lax.ppermute only.
A program may use at most 64 MiB of HBM per device.

```python
import math
import jax
import jax.numpy as jnp
import numpy as np
from jax import lax

EX = 2
ITERS = 3
MX = 8
NX = 32
NY = 128
NZ = 128
N_MOD = 4


def draw_fixed_mask(key, part):
    key = jax.random.fold_in(key, 5)
    level_key, row_key, pick_key = jax.random.split(key, 3)
    level = jax.random.randint(level_key, (), 1, 5)
    row_extra = jax.random.randint(row_key, (1, NX, 1, 1), 0, 3)
    picked = jax.random.randint(pick_key, (3, NX, NY, NZ), 0, 16)
    return (picked < level + row_extra).astype(jnp.int32)


def draw_load_mask(key, part):
    key = jax.random.fold_in(key, 7)
    low_key, side_key, row_key, pick_key = jax.random.split(key, 4)
    base = 3 + jax.random.randint(low_key, (), 0, 6) + 12 * jax.random.randint(side_key, (), 0, 2)
    row_extra = jax.random.randint(row_key, (1, NX, 1, 1), 0, NX)
    picked = jax.random.randint(pick_key, (3, NX, NY, NZ), 0, 6 * NX)
    position = lax.broadcasted_iota(jnp.int32, (3, NX, NY, NZ), 1)
    bound_line = base * NX // 10 + 2 * position + row_extra
    return (picked < bound_line).astype(jnp.int32)


def steps_of(stream_key, extent, cuts, least, high):
    def one(dim, blocks):
        draws = jax.random.uniform(jax.random.fold_in(jax.random.fold_in(stream_key, 6), dim), (blocks,), jnp.float32, least / len(cuts), high / len(cuts))
        return jnp.repeat(jnp.exp(draws), extent[dim] // blocks).reshape((-1,) + (1,) * (len(extent) - dim - 1))

    factor_of = one(*cuts[0])
    for cut in cuts[1:]:
        factor_of = factor_of * one(*cut)
    return factor_of


def setup_inputs(seed: int = 0) -> dict:
    key_of = jax.random.split(jax.random.key(seed), 4)
    design = jnp.clip(0.1 + 0.9 * jax.random.uniform(key_of[0], (MX, NY, NZ), jnp.float32) ** steps_of(key_of[0], (MX, NY, NZ), ((0, 4), (1, 2)), -0.2, 0.2), 0.1, 1.0)
    fixed_mask = draw_fixed_mask(jax.random.fold_in(key_of[3], 71), 0)
    load_mask = draw_load_mask(jax.random.fold_in(key_of[3], 71), 0)
    return dict(design=design, fixed_mask=fixed_mask, load_mask=load_mask)


stiff_floor = 0.01
penalty = 3.0
sharpness = 4.0
threshold = 0.5
filter_reach = 1.8

def stiffness_table():
    poisson = 0.3
    lame_first = poisson / ((1.0 + poisson) * (1.0 - 2.0 * poisson))
    shear_modulus = 1.0 / (2.0 * (1.0 + poisson))
    elastic = np.zeros((6, 6))
    elastic[:3, :3] = lame_first
    for axis_id in range(3):
        elastic[axis_id, axis_id] += 2.0 * shear_modulus
        elastic[axis_id + 3, axis_id + 3] = shear_modulus
    offset = 0.5 / math.sqrt(3.0)
    points = [0.5 - offset, 0.5 + offset]
    stiffness = np.zeros((24, 24))
    for point_x in points:
        for point_y in points:
            for point_z in points:
                strain = np.zeros((6, 24))
                for corner in range(8):
                    bit_x, bit_y, bit_z = (corner >> 2 & 1, corner >> 1 & 1, corner & 1)
                    along_x = point_x if bit_x else 1.0 - point_x
                    along_y = point_y if bit_y else 1.0 - point_y
                    along_z = point_z if bit_z else 1.0 - point_z
                    sign_x = 1.0 if bit_x else -1.0
                    sign_y = 1.0 if bit_y else -1.0
                    sign_z = 1.0 if bit_z else -1.0
                    grad_x = sign_x * along_y * along_z
                    grad_y = along_x * sign_y * along_z
                    grad_z = along_x * along_y * sign_z
                    column = 3 * corner
                    strain[0, column] = grad_x
                    strain[1, column + 1] = grad_y
                    strain[2, column + 2] = grad_z
                    strain[3, column] = grad_y
                    strain[3, column + 1] = grad_x
                    strain[4, column + 1] = grad_z
                    strain[4, column + 2] = grad_y
                    strain[5, column] = grad_z
                    strain[5, column + 2] = grad_x
                stiffness += strain.T @ elastic @ strain / 8.0
    return jnp.asarray(stiffness, dtype=jnp.float32)

def stencil_weights():
    entries = []
    for shift_x in (-1, 0, 1):
        for shift_y in (-1, 0, 1):
            for shift_z in (-1, 0, 1):
                weight = filter_reach - math.sqrt(shift_x * shift_x + shift_y * shift_y + shift_z * shift_z)
                entries.append((shift_x, shift_y, shift_z, weight))
    return entries

def smooth_sum(padded, count_x, count_y, depth_cells):
    running = jnp.zeros((count_x, count_y, depth_cells), jnp.float32)
    for shift_x, shift_y, shift_z, weight in stencil_weights():
        running = running + weight * padded[1 + shift_x:1 + shift_x + count_x, 1 + shift_y:1 + shift_y + count_y, 1 + shift_z:1 + shift_z + depth_cells]
    return running

def project(values):
    lower_end = math.tanh(sharpness * threshold)
    upper_end = math.tanh(sharpness * (1.0 - threshold))
    return (lower_end + jnp.tanh(sharpness * (values - threshold))) / (lower_end + upper_end)

def project_slope(values):
    lower_end = math.tanh(sharpness * threshold)
    upper_end = math.tanh(sharpness * (1.0 - threshold))
    hyper = jnp.tanh(sharpness * (values - threshold))
    return sharpness * (1.0 - hyper * hyper) / (lower_end + upper_end)

def gather_corners(extended, count_x, count_y):
    depth_cells = extended.shape[3]
    shifted_z = jnp.pad(extended[..., 1:], ((0, 0), (0, 0), (0, 0), (0, 1)))
    columns = []
    for corner in range(8):
        bit_x, bit_y, bit_z = (corner >> 2 & 1, corner >> 1 & 1, corner & 1)
        source = shifted_z if bit_z else extended
        columns.append(source[:, bit_x:bit_x + count_x, bit_y:bit_y + count_y, :])
    return jnp.stack(columns).reshape(24, count_x * count_y * depth_cells)

def element_forces(extended, moduli):
    count_x, count_y, depth_cells = moduli.shape
    values = gather_corners(extended, count_x, count_y)
    forces = jnp.dot(stiffness_table(), values, precision=lax.Precision.HIGHEST) * moduli.reshape(1, -1)
    forces = forces.reshape(8, 3, count_x, count_y, depth_cells)
    result = jnp.zeros((3, count_x + 1, count_y + 1, depth_cells), forces.dtype)
    for corner in range(8):
        bit_x, bit_y, bit_z = (corner >> 2 & 1, corner >> 1 & 1, corner & 1)
        portion = forces[corner]
        if bit_z:
            portion = jnp.pad(portion[..., :-1], ((0, 0), (0, 0), (0, 0), (1, 0)))
        result = result.at[:, bit_x:bit_x + count_x, bit_y:bit_y + count_y, :].add(portion)
    return result

def element_energy(extended):
    count_x = extended.shape[1] - 1
    count_y = extended.shape[2] - 1
    depth_cells = extended.shape[3]
    values = gather_corners(extended, count_x, count_y)
    product = jnp.dot(stiffness_table(), values, precision=lax.Precision.HIGHEST)
    return lax.optimization_barrier(jnp.sum(values * product, axis=0)).reshape(count_x, count_y, depth_cells)

def operate(field, moduli_deck):
    padded = jnp.pad(field, ((0, 0), (1, 1), (1, 1), (0, 0)))
    moduli_pad = jnp.pad(moduli_deck, ((1, 0), (1, 0), (0, 0)))

    def one_block(block_id):
        first_row = (block_id * EX).astype(jnp.int32)
        slab_field = lax.dynamic_slice_in_dim(padded, first_row, EX + 2, 1)
        slab_moduli = lax.dynamic_slice_in_dim(moduli_pad, first_row, EX + 1, 0)
        forces = element_forces(slab_field, slab_moduli)
        return forces[:, 1:EX + 1, 1:NY + 1, :]
    blocks = lax.map(one_block, jnp.arange(NX // EX, dtype=jnp.int32))
    return jnp.transpose(blocks, (1, 0, 2, 3, 4)).reshape(3, NX, NY, NZ)

def deck_energy(displacement):
    upper = jnp.pad(displacement, ((0, 0), (0, 1), (0, 1), (0, 0)))

    def energy_block(block_id):
        first_row = (block_id * EX).astype(jnp.int32)
        slab_field = lax.dynamic_slice_in_dim(upper, first_row, EX + 1, 1)
        return element_energy(slab_field)
    energies = lax.map(energy_block, jnp.arange(NX // EX, dtype=jnp.int32))
    return energies.reshape(NX, NY, NZ)

def reference(design, fixed_mask, load_mask):
    padded = jnp.pad(design, ((1, 1), (0, 0), (0, 0)), mode='wrap')
    padded = jnp.pad(padded, ((0, 0), (1, 1), (1, 1)))
    ones_pad = jnp.pad(jnp.ones((MX + 2, NY, NZ), jnp.float32), ((0, 0), (1, 1), (1, 1)))
    weight_sum = smooth_sum(ones_pad, MX, NY, NZ)
    filtered = smooth_sum(padded, MX, NY, NZ) / weight_sum
    projected = project(filtered)
    moduli = stiff_floor + (1.0 - stiff_floor) * projected ** 3
    moduli_deck = jnp.tile(moduli, (N_MOD, 1, 1))
    free_dofs = (1 - fixed_mask).astype(jnp.float32)
    right_side = free_dofs * load_mask.astype(jnp.float32)

    def apply_operator(field):
        return free_dofs * operate(free_dofs * field, moduli_deck)
    displacement = jnp.zeros_like(right_side)
    residual = right_side
    direction = right_side
    norm_now = jnp.sum(residual * residual)
    for step in range(ITERS):
        image = apply_operator(direction)
        step_size = norm_now / jnp.sum(direction * image)
        displacement = displacement + step_size * direction
        residual = residual - step_size * image
        norm_next = jnp.sum(residual * residual)
        direction = residual + norm_next / norm_now * direction
        norm_now = norm_next
    energy = deck_energy(displacement)
    slope = -penalty * (1.0 - stiff_floor) * jnp.tile(projected * projected, (N_MOD, 1, 1)) * energy
    module_sens = lax.optimization_barrier(jnp.sum(slope.reshape(N_MOD, MX, NY, NZ), axis=0))
    scaled = module_sens * project_slope(filtered) / weight_sum
    scaled_pad = jnp.pad(scaled, ((1, 1), (0, 0), (0, 0)), mode='wrap')
    scaled_pad = jnp.pad(scaled_pad, ((0, 0), (1, 1), (1, 1)))
    gradient = smooth_sum(scaled_pad, MX, NY, NZ)
    return (displacement, gradient)
```

```python
import math

import jax
import jax.numpy as jnp
import numpy as np
from jax import lax
from jax.experimental import pallas as pl
from jax.experimental.pallas import tpu as pltpu
from jax.sharding import PartitionSpec as P

stiff_floor = 0.01
penalty = 3.0
sharpness = 4.0
threshold = 0.5
filter_reach = 1.8

AXES = ("mod", "slab", "sub")
ROWS = 8
FACE = filter_reach - 1.0
EDGE = filter_reach - math.sqrt(2.0)
CORNER = filter_reach - math.sqrt(3.0)
LOWER = math.tanh(sharpness * threshold)
UPPER = math.tanh(sharpness * (1.0 - threshold))


def stiffness_modes():
    poisson = 0.3
    lame = poisson / ((1.0 + poisson) * (1.0 - 2.0 * poisson))
    shear = 1.0 / (2.0 * (1.0 + poisson))
    elastic = np.zeros((6, 6))
    elastic[:3, :3] = lame
    for axis in range(3):
        elastic[axis, axis] += 2.0 * shear
        elastic[axis + 3, axis + 3] = shear
    offset = 0.5 / math.sqrt(3.0)
    points = [0.5 - offset, 0.5 + offset]
    stiffness = np.zeros((24, 24))
    for point in ((a, b, c) for a in points for b in points for c in points):
        strain = np.zeros((6, 24))
        for corner in range(8):
            bits = (corner >> 2 & 1, corner >> 1 & 1, corner & 1)
            along = [point[a] if bits[a] else 1.0 - point[a] for a in range(3)]
            sign = [1.0 if bits[a] else -1.0 for a in range(3)]
            gx = sign[0] * along[1] * along[2]
            gy = along[0] * sign[1] * along[2]
            gz = along[0] * along[1] * sign[2]
            col = 3 * corner
            strain[0, col] = gx
            strain[1, col + 1] = gy
            strain[2, col + 2] = gz
            strain[3, col], strain[3, col + 1] = gy, gx
            strain[4, col + 1], strain[4, col + 2] = gz, gy
            strain[5, col], strain[5, col + 2] = gz, gx
        stiffness += strain.T @ elastic @ strain / 8.0
    basis = np.zeros((24, 24))
    for mode in range(8):
        for corner in range(8):
            value = 1.0
            for bit in range(3):
                if mode >> bit & 1 and not corner >> bit & 1:
                    value = -value
            for k in range(3):
                basis[3 * mode + k, 3 * corner + k] = value
    table = basis @ stiffness @ basis.T / 64.0
    table[np.abs(table) < 1e-9] = 0.0
    return table


TABLE = stiffness_modes()


def lanes(shape):
    return lax.broadcasted_iota(jnp.int32, shape, 1)


def rows(shape):
    return lax.broadcasted_iota(jnp.int32, shape, 0)


def z_up(x):
    return jnp.where(lanes(x.shape) < x.shape[1] - 1, pltpu.roll(x, x.shape[1] - 1, 1), 0.0)


def z_down(x):
    return jnp.where(lanes(x.shape) > 0, pltpu.roll(x, 1, 1), 0.0)


def y_up(x):
    return jnp.where(rows(x.shape) < x.shape[0] - 1, pltpu.roll(x, x.shape[0] - 1, 0), 0.0)


def y_down(x):
    return jnp.where(rows(x.shape) > 0, pltpu.roll(x, 1, 0), 0.0)


def two_rows(read, y0, count):
    here = read(y0)
    above = y_up(here) if y0 + ROWS == count else read(y0 + 1)
    return here, above


def face_modes(here, above):
    out = []
    for part in (here + above, above - here):
        shifted = z_up(part)
        out += [part + shifted, shifted - part]
    return out


def element_modes(low, high):
    sums = [[high[k][m] + low[k][m] for m in range(4)] for k in range(3)]
    diffs = [[high[k][m] - low[k][m] for m in range(4)] for k in range(3)]
    return [sums[k] + diffs[k] for k in range(3)]


def mode_forces(q):
    made = {}

    def scaled(j, value):
        key = (j, round(value, 12))
        if key not in made:
            made[key] = q[j % 3][j // 3] * np.float32(value)
        return made[key]

    out = [[None] * 8 for _ in range(3)]
    for i in range(24):
        total = None
        for j in np.nonzero(TABLE[i])[0]:
            term = scaled(int(j), float(TABLE[i, j]))
            total = term if total is None else total + term
        out[i % 3][i // 3] = total
    return out


def element_energy(q):
    r = mode_forces(q)
    total = None
    for k in range(3):
        for m in range(1, 8):
            term = q[k][m] * r[k][m]
            total = term if total is None else total + term
    return total


def apply_rows(low, own, high, mod_low, mod_own):
    r_low = mode_forces(element_modes(low, own))
    r_own = mode_forces(element_modes(own, high))
    here, above = [], []
    for k in range(3):
        field = []
        for m in range(4):
            a, b = r_low[k][m], r_low[k][m + 4]
            c, d = r_own[k][m], r_own[k][m + 4]
            from_low = b if a is None else a + b
            from_own = -d if c is None else c - d
            field.append(mod_low * from_low + mod_own * from_own)
        part = []
        for py in range(2):
            s, d = field[2 * py], field[2 * py + 1]
            part.append((s - d) + z_down(s + d))
        here.append(part[0] - part[1])
        above.append(part[0] + part[1])
    return here, above


def operator_loop(count, read_low, read_own, read_high, read_free, mod_low_ref, mod_own_ref, out_ref):
    shape = (ROWS, out_ref.shape[2])
    square = jnp.zeros(shape, jnp.float32)
    cross = jnp.zeros(shape, jnp.float32)
    norm = jnp.zeros(shape, jnp.float32)
    carry = [jnp.zeros(shape, jnp.float32)] * 3
    first = rows(shape) == 0
    for y0 in range(0, count, ROWS):
        layers = []
        owns = []
        for read in (read_low, read_own, read_high):
            layer = []
            for k in range(3):
                here, up = two_rows(lambda y, k=k, read=read: read(k, y), y0, count)
                layer.append(face_modes(here, up))
                if read is read_own:
                    owns.append(here)
            layers.append(layer)
        here, above = apply_rows(
            *layers, mod_low_ref[pl.ds(y0, ROWS), :], mod_own_ref[pl.ds(y0, ROWS), :]
        )
        for k in range(3):
            rolled = pltpu.roll(above[k], 1, 0)
            force = here[k] + jnp.where(first, carry[k], rolled)
            carry[k] = rolled
            image = read_free(k, y0) * force
            out_ref[k, pl.ds(y0, ROWS), :] = image
            square += image * image
            cross += owns[k] * image
            norm += owns[k] * owns[k]
    return norm, cross, square


def energy_loop(count, read_own, read_high, use):
    for y0 in range(0, count, ROWS):
        layers = []
        for read in (read_own, read_high):
            layers.append(
                [
                    face_modes(*two_rows(lambda y, k=k, read=read: read(k, y), y0, count))
                    for k in range(3)
                ]
            )
        use(y0, element_energy(element_modes(*layers)))


def line(tile):
    return jnp.sum(tile, axis=0, keepdims=True)


def prepare_kernel(design, fixed, load, swap, first, second):
    sub = lax.axis_index("sub")

    def right_side(k, layer):
        return (1 - fixed[k, layer]).astype(jnp.float32) * load[k, layer].astype(jnp.float32)

    for k in range(3):
        values = [right_side(k, 0), right_side(k, 1)]
        for layer in range(2):
            swap[2 * k + layer] = values[layer]
        swap[6 + k] = (1 - fixed[k, 1 - sub]).astype(jnp.float32)

        @pl.when(sub == 0)
        def _(k=k, values=values):
            first[k] = values[1]
            second[k] = values[0]

        @pl.when(sub == 1)
        def _(k=k, values=values):
            first[k] = values[0]
            second[k] = values[1]

    swap[9] = design[0]
    swap[10] = design[1]
    first[3] = design[0]
    second[3] = design[0]
    first[4] = design[1]
    second[4] = design[1]


def filter_planes(low, mid, high):
    both = low + high

    def faces(p):
        across = y_up(p) + y_down(p)
        return across + z_up(p) + z_down(p), z_up(across) + z_down(across)

    mid_face, mid_diag = faces(mid)
    both_face, both_diag = faces(both)
    return (
        filter_reach * mid
        + FACE * (both + mid_face)
        + EDGE * (both_face + mid_diag)
        + CORNER * both_diag
    )


def weight_plane(shape, row_offset, count):
    row = rows(shape) + row_offset
    lane = lanes(shape)

    def neighbours(index, size):
        return jnp.where(index > 0, 1.0, 0.0) + jnp.where(index < size - 1, 1.0, 0.0)

    ry = neighbours(row, count)
    rz = neighbours(lane, shape[1])
    face, diag = ry + rz, ry * rz
    return (
        filter_reach
        + FACE * (2.0 + face)
        + EDGE * (2.0 * face + diag)
        + (2.0 * CORNER) * diag
    )


def start_kernel(
    mods, slabs,
    design, fixed, load, swap, first, second, third, fourth,
    v0, v0_high, v1, free, mod_low, mod_own, slope_factor, chain_factor, moments,
    v0_low, layers,
):
    mod, slab, sub = (lax.axis_index(a) for a in AXES)
    half = design.shape[1]
    count = 2 * half
    mine = pl.ds(pl.multiple_of(sub * half, half), half)
    other = pl.ds(pl.multiple_of((1 - sub) * half, half), half)
    for layer in range(2):
        layers[2 - sub + layer, mine, :] = design[layer]
        layers[2 - sub + layer, other, :] = swap[9 + layer]
    for source, part in ((first, mine), (second, other)):

        @pl.when(sub == 0)
        def _(source=source, part=part):
            layers[0, part, :] = source[3]
            layers[1, part, :] = source[4]

        @pl.when(sub == 1)
        def _(source=source, part=part):
            layers[3, part, :] = source[3]

    @pl.when(sub == 1)
    def _():
        layers[0, pl.ds(0, half), :] = third[...]
        layers[0, pl.ds(half, half), :] = fourth[...]

    weight = weight_plane((count, design.shape[2]), 0, count)
    starts = (mod == 0) & (slab == 0) & (sub == 0)
    filtered = filter_planes(layers[0], layers[1], layers[2]) / weight
    hyper = jnp.tanh(sharpness * (filtered - threshold))
    projected = (LOWER + hyper) * (1.0 / (LOWER + UPPER))
    below = stiff_floor + (1.0 - stiff_floor) * projected * projected * projected
    mod_low[...] = below * jnp.where(starts, 0.0, 1.0)
    filtered = filter_planes(layers[1], layers[2], layers[3]) / weight
    hyper = jnp.tanh(sharpness * (filtered - threshold))
    projected = (LOWER + hyper) * (1.0 / (LOWER + UPPER))
    squared = projected * projected
    mod_own[...] = stiff_floor + (1.0 - stiff_floor) * squared * projected
    slope_factor[...] = (-penalty * (1.0 - stiff_floor)) * squared
    chain_factor[...] = (sharpness / (LOWER + UPPER)) * (1.0 - hyper * hyper) / weight

    ends = (mod == mods - 1) & (slab == slabs - 1) & (sub == 1)
    inside = jnp.where(ends, 0.0, 1.0)
    for k in range(3):
        own_half = (1 - fixed[k, sub]).astype(jnp.float32)
        free[k, mine, :] = own_half
        free[k, other, :] = swap[6 + k]
        v0[k, mine, :] = own_half * load[k, sub].astype(jnp.float32)
        v0[k, other, :] = swap[2 * k + sub]
        inner = (1 - fixed[k, 1 - sub]).astype(jnp.float32) * load[k, 1 - sub].astype(jnp.float32)

        @pl.when(sub == 0)
        def _(k=k, inner=inner):
            v0_high[k, mine, :] = inner
            v0_high[k, other, :] = swap[2 * k + 1]
            v0_low[k, mine, :] = first[k]
            v0_low[k, other, :] = second[k]

        @pl.when(sub == 1)
        def _(k=k, inner=inner):
            v0_low[k, mine, :] = inner
            v0_low[k, other, :] = swap[2 * k]
            v0_high[k, mine, :] = first[k] * inside
            v0_high[k, other, :] = second[k] * inside

    norm, cross, square = operator_loop(
        count,
        lambda k, y: v0_low[k, pl.ds(y, ROWS), :],
        lambda k, y: v0[k, pl.ds(y, ROWS), :],
        lambda k, y: v0_high[k, pl.ds(y, ROWS), :],
        lambda k, y: free[k, pl.ds(y, ROWS), :],
        mod_low,
        mod_own,
        v1,
    )
    moments[...] = jnp.concatenate(
        [line(norm), line(cross), line(square), jnp.zeros((5, norm.shape[1]), jnp.float32)], axis=0
    )


def second_kernel(v1, inner, outer, free, mod_low, mod_own, before, v2, v1_high, moments):
    sub = lax.axis_index("sub")
    count = v1.shape[1]
    even = sub == 0
    for k in range(3):
        v1_high[k] = jnp.where(even, inner[k], outer[k])

    def read_low(k, y):
        return jnp.where(even, outer[k, pl.ds(y, ROWS), :], inner[k, pl.ds(y, ROWS), :])

    _, cross, square = operator_loop(
        count,
        read_low,
        lambda k, y: v1[k, pl.ds(y, ROWS), :],
        lambda k, y: v1_high[k, pl.ds(y, ROWS), :],
        lambda k, y: free[k, pl.ds(y, ROWS), :],
        mod_low,
        mod_own,
        v2,
    )
    zero = jnp.zeros((3, cross.shape[1]), jnp.float32)
    moments[...] = before[...] + jnp.concatenate(
        [zero, line(cross), line(square), zero], axis=0
    )


def third_kernel(v2, v2_high, mod_own, before, moments):
    count = v2.shape[1]
    total = [jnp.zeros((ROWS, v2.shape[2]), jnp.float32)]

    def use(y0, energy):
        total[0] += energy * mod_own[pl.ds(y0, ROWS), :]

    energy_loop(
        count,
        lambda k, y: v2[k, pl.ds(y, ROWS), :],
        lambda k, y: v2_high[k, pl.ds(y, ROWS), :],
        use,
    )
    width = v2.shape[2]
    moments[...] = before[...] + jnp.concatenate(
        [
            jnp.zeros((5, width), jnp.float32),
            line(total[0]),
            jnp.zeros((2, width), jnp.float32),
        ],
        axis=0,
    )


def coefficients(m):
    step = m[0] / m[1]
    x0 = step
    r1 = -step
    norm = m[0] + 2.0 * r1 * m[1] + r1 * r1 * m[2]
    ratio = norm / m[0]
    p0, p1 = 1.0 + ratio, r1
    step = norm / (p0 * p0 * m[1] + 2.0 * p0 * p1 * m[2] + p1 * p1 * m[3])
    x0, x1 = x0 + step * p0, step * p1
    r1, r2 = r1 - step * p0, -step * p1
    after = (
        m[0]
        + 2.0 * r1 * m[1]
        + (r1 * r1 + 2.0 * r2) * m[2]
        + 2.0 * r1 * r2 * m[3]
        + r2 * r2 * m[4]
    )
    ratio = after / norm
    p0, p1, p2 = 1.0 + ratio * p0, r1 + ratio * p1, r2
    step = after / (
        p0 * p0 * m[1]
        + 2.0 * p0 * p1 * m[2]
        + (p1 * p1 + 2.0 * p0 * p2) * m[3]
        + 2.0 * p1 * p2 * m[4]
        + p2 * p2 * m[5]
    )
    return x0 + step * p0, x1 + step * p1, step * p2


def combine_kernel(
    gathered, v0, v0_high, v1, v1_high, v2, v2_high, slope_factor,
    slope, keep, send,
    own, high,
):
    sub = lax.axis_index("sub")
    count = v0.shape[1]
    half = count // 2
    total = jnp.sum(gathered[...], axis=0)
    sums = jnp.sum(total, axis=1, keepdims=True)
    c0, c1, c2 = coefficients([sums[k : k + 1] for k in range(6)])
    for k in range(3):
        own[k] = c0 * v0[k] + c1 * v1[k] + c2 * v2[k]
        high[k] = c0 * v0_high[k] + c1 * v1_high[k] + c2 * v2_high[k]

    mine = pl.ds(pl.multiple_of(sub * half, half), half)
    other = pl.ds(pl.multiple_of((1 - sub) * half, half), half)
    for k in range(3):
        keep[k] = own[k, mine, :]
        send[k] = own[k, other, :]

    def use(y0, energy):
        slope[pl.ds(y0, ROWS), :] = slope_factor[pl.ds(y0, ROWS), :] * energy

    energy_loop(
        count,
        lambda k, y: own[k, pl.ds(y, ROWS), :],
        lambda k, y: high[k, pl.ds(y, ROWS), :],
        use,
    )


def scale_kernel(*refs):
    slopes, (chain_factor, scaled, same, cross) = refs[:-4], refs[-4:]
    sub = lax.axis_index("sub")
    total = slopes[0][...]
    for other in slopes[1:]:
        total = total + other[...]
    scaled[...] = total * chain_factor[...]
    window = same.shape[0]
    shift = scaled.shape[0] - window
    same[...] = scaled[pl.ds(pl.multiple_of(sub * shift, 8), window), :]
    cross[...] = scaled[pl.ds(pl.multiple_of((1 - sub) * shift, 8), window), :]


def gradient_kernel(scaled, partner, outer, far, gradient, planes, sums):
    sub = lax.axis_index("sub")
    window = partner.shape[0]
    shift = scaled.shape[0] - window
    mine = scaled[pl.ds(pl.multiple_of(sub * shift, 8), window), :]

    @pl.when(sub == 0)
    def _():
        planes[0] = outer[...]
        planes[1] = mine
        planes[2] = partner[...]
        planes[3] = far[...]

    @pl.when(sub == 1)
    def _():
        planes[0] = far[...]
        planes[1] = partner[...]
        planes[2] = mine
        planes[3] = outer[...]

    half = gradient.shape[1]
    part = pl.ds(pl.multiple_of(sub * (window - half), 8), half)
    for layer in range(2):
        sums[...] = filter_planes(planes[layer], planes[layer + 1], planes[layer + 2])
        gradient[layer] = sums[part, :]


def call(body, outs, scratch=(), name=None):
    return pl.pallas_call(
        body,
        out_shape=[jax.ShapeDtypeStruct(shape, jnp.float32) for shape in outs],
        scratch_shapes=[pltpu.VMEM(shape, jnp.float32) for shape in scratch],
        compiler_params=pltpu.CompilerParams(vmem_limit_bytes=16 * 2**20),
        name=name,
    )


def routes(mods, slabs):
    chips = mods * slabs

    def at(chip, sub):
        return 2 * chip + sub

    def beside(chip, steps, cyclic):
        target = chip + steps
        if cyclic:
            return target % chips
        return target if 0 <= target < chips else None

    def built(moves, cyclic):
        pairs = []
        for chip in range(chips):
            for sub, steps, to in moves:
                target = beside(chip, steps, cyclic)
                if target is not None:
                    pairs.append((at(chip, sub), at(target, to)))
        return pairs

    def in_module(moves):
        pairs = []
        for chip in range(chips):
            mod, slab = divmod(chip, slabs)
            for sub, steps, to in moves:
                pairs.append((at(chip, sub), at(mod * slabs + (slab + steps) % slabs, to)))
        return pairs

    return dict(
        swap=built([(0, 0, 1), (1, 0, 0)], True),
        first=built([(0, 1, 0), (1, -1, 1)], True),
        second=built([(1, 1, 0), (0, -1, 1)], True),
        third=built([(0, 1, 1)], True),
        fourth=built([(1, 1, 1)], True),
        outer=built([(1, 1, 0), (0, -1, 1)], False),
        down=built([(1, 0, 0), (0, -1, 1)], False),
        halo_cross=in_module([(1, 1, 0), (0, -1, 1)]),
        halo_same=in_module([(0, -1, 0), (1, 1, 1)]),
    )


def module_routes(mods):
    if mods & (mods - 1) == 0:
        return [[(m, m ^ s) for m in range(mods)] for s in range(1, mods)]
    return [[(m, (m + s) % mods) for m in range(mods)] for s in range(1, mods)]


def local(mods, slabs, design, fixed, load):
    half, width = design.shape[1:]
    count = 2 * half
    path = routes(mods, slabs)

    def move(value, name):
        return lax.ppermute(value, AXES, path[name])

    plane = (count, width)
    layer = (3, count, width)
    swap, first, second = call(
        prepare_kernel, [(11, half, width), (5, half, width), (5, half, width)], name="prepare"
    )(design, fixed, load)
    first = move(first, "first")
    second = move(second, "second")
    third = move(design[1], "third")
    fourth = move(design[1], "fourth")
    swap = move(swap, "swap")

    def start_body(*refs):
        start_kernel(mods, slabs, *refs)

    v0, v0_high, v1, free, mod_low, mod_own, slope_factor, chain_factor, moments = call(
        start_body,
        [layer, layer, layer, layer, plane, plane, plane, plane, (8, width)],
        [layer, (4,) + plane],
        name="start",
    )(design, fixed, load, swap, first, second, third, fourth)
    outer = move(v1, "outer")
    inner = move(v1, "swap")
    v2, v1_high, moments = call(second_kernel, [layer, layer, (8, width)], name="second")(
        v1, inner, outer, free, mod_low, mod_own, moments
    )
    v2_high = move(v2, "down")
    (moments,) = call(third_kernel, [(8, width)], name="third")(v2, v2_high, mod_own, moments)
    devices = 2 * mods * slabs
    gathered = lax.all_to_all(
        jnp.broadcast_to(moments, (devices, 8, width)), AXES, 0, 0, tiled=True
    )
    slope, keep, send = call(
        combine_kernel, [plane, (3, half, width), (3, half, width)], [layer, layer], name="combine"
    )(gathered, v0, v0_high, v1, v1_high, v2, v2_high, slope_factor)
    slopes = [slope] + [lax.ppermute(slope, "mod", pairs) for pairs in module_routes(mods)]
    received = move(send, "swap")
    window = half + 8
    scaled, same, cross = call(
        scale_kernel, [plane, (window, width), (window, width)], name="scale"
    )(*slopes, chain_factor)
    outer = move(cross, "halo_cross")
    far = move(same, "halo_same")
    partner = move(cross, "swap")
    even = lax.axis_index("sub") == 0
    displacement = jnp.stack(
        [jnp.where(even, keep, received), jnp.where(even, received, keep)], axis=1
    )
    (gradient,) = call(
        gradient_kernel, [(2, half, width)], [(4, window, width), (window, width)], name="gradient"
    )(scaled, partner, outer, far)
    return displacement, gradient


def solution(mesh):
    mods, slabs = mesh.shape["mod"], mesh.shape["slab"]
    assert mesh.shape["sub"] == 2
    deck = P(None, ("mod", "slab"), "sub", None)

    def body(design, fixed_mask, load_mask):
        return local(mods, slabs, design, fixed_mask, load_mask)

    return jax.shard_map(
        body,
        mesh=mesh,
        in_specs=(P("slab", "sub", None), deck, deck),
        out_specs=(deck, P("slab", "sub", None)),
        check_vma=False,
    )
```

```python
import math

import jax
import jax.numpy as jnp
import numpy as np
from jax import lax
from jax.experimental import pallas as pl
from jax.experimental.pallas import tpu as pltpu
from jax.sharding import PartitionSpec as P

stiff_floor = 0.01
penalty = 3.0
sharpness = 4.0
threshold = 0.5
filter_reach = 1.8

AXES = ("mod", "slab", "sub")
ROWS = 8
FACE = filter_reach - 1.0
EDGE = filter_reach - math.sqrt(2.0)
CORNER = filter_reach - math.sqrt(3.0)
LOWER = math.tanh(sharpness * threshold)
UPPER = math.tanh(sharpness * (1.0 - threshold))


def stiffness_modes():
    poisson = 0.3
    lame = poisson / ((1.0 + poisson) * (1.0 - 2.0 * poisson))
    shear = 1.0 / (2.0 * (1.0 + poisson))
    elastic = np.zeros((6, 6))
    elastic[:3, :3] = lame
    for axis in range(3):
        elastic[axis, axis] += 2.0 * shear
        elastic[axis + 3, axis + 3] = shear
    offset = 0.5 / math.sqrt(3.0)
    points = [0.5 - offset, 0.5 + offset]
    stiffness = np.zeros((24, 24))
    for point in ((a, b, c) for a in points for b in points for c in points):
        strain = np.zeros((6, 24))
        for corner in range(8):
            bits = (corner >> 2 & 1, corner >> 1 & 1, corner & 1)
            along = [point[a] if bits[a] else 1.0 - point[a] for a in range(3)]
            sign = [1.0 if bits[a] else -1.0 for a in range(3)]
            gx = sign[0] * along[1] * along[2]
            gy = along[0] * sign[1] * along[2]
            gz = along[0] * along[1] * sign[2]
            col = 3 * corner
            strain[0, col] = gx
            strain[1, col + 1] = gy
            strain[2, col + 2] = gz
            strain[3, col], strain[3, col + 1] = gy, gx
            strain[4, col + 1], strain[4, col + 2] = gz, gy
            strain[5, col], strain[5, col + 2] = gz, gx
        stiffness += strain.T @ elastic @ strain / 8.0
    basis = np.zeros((24, 24))
    for mode in range(8):
        for corner in range(8):
            value = 1.0
            for bit in range(3):
                if mode >> bit & 1 and not corner >> bit & 1:
                    value = -value
            for k in range(3):
                basis[3 * mode + k, 3 * corner + k] = value
    table = basis @ stiffness @ basis.T / 64.0
    table[np.abs(table) < 1e-9] = 0.0
    return table


TABLE = stiffness_modes()


def lanes(shape):
    return lax.broadcasted_iota(jnp.int32, shape, 1)


def rows(shape):
    return lax.broadcasted_iota(jnp.int32, shape, 0)


def z_up(x):
    return jnp.where(lanes(x.shape) < x.shape[1] - 1, pltpu.roll(x, x.shape[1] - 1, 1), 0.0)


def z_down(x):
    return jnp.where(lanes(x.shape) > 0, pltpu.roll(x, 1, 1), 0.0)


def y_up(x):
    return jnp.where(rows(x.shape) < x.shape[0] - 1, pltpu.roll(x, x.shape[0] - 1, 0), 0.0)


def y_down(x):
    return jnp.where(rows(x.shape) > 0, pltpu.roll(x, 1, 0), 0.0)


def two_rows(read, y0, count):
    here = read(y0)
    above = y_up(here) if y0 + ROWS == count else read(y0 + 1)
    return here, above


def face_modes(here, above):
    out = []
    for part in (here + above, above - here):
        shifted = z_up(part)
        out += [part + shifted, shifted - part]
    return out


def element_modes(low, high):
    sums = [[high[k][m] + low[k][m] for m in range(4)] for k in range(3)]
    diffs = [[high[k][m] - low[k][m] for m in range(4)] for k in range(3)]
    return [sums[k] + diffs[k] for k in range(3)]


def mode_forces(q):
    made = {}

    def scaled(j, value):
        key = (j, round(value, 12))
        if key not in made:
            made[key] = q[j % 3][j // 3] * np.float32(value)
        return made[key]

    out = [[None] * 8 for _ in range(3)]
    for i in range(24):
        total = None
        for j in np.nonzero(TABLE[i])[0]:
            term = scaled(int(j), float(TABLE[i, j]))
            total = term if total is None else total + term
        out[i % 3][i // 3] = total
    return out


def element_energy(q):
    r = mode_forces(q)
    total = None
    for k in range(3):
        for m in range(1, 8):
            term = q[k][m] * r[k][m]
            total = term if total is None else total + term
    return total


def apply_rows(low, own, high, mod_low, mod_own):
    r_low = mode_forces(element_modes(low, own))
    r_own = mode_forces(element_modes(own, high))
    here, above = [], []
    for k in range(3):
        field = []
        for m in range(4):
            a, b = r_low[k][m], r_low[k][m + 4]
            c, d = r_own[k][m], r_own[k][m + 4]
            from_low = b if a is None else a + b
            from_own = -d if c is None else c - d
            field.append(mod_low * from_low + mod_own * from_own)
        part = []
        for py in range(2):
            s, d = field[2 * py], field[2 * py + 1]
            part.append((s - d) + z_down(s + d))
        here.append(part[0] - part[1])
        above.append(part[0] + part[1])
    return here, above


def operator_loop(count, read_low, read_own, read_high, read_free, mod_low_ref, mod_own_ref, out_ref):
    shape = (ROWS, out_ref.shape[2])
    square = jnp.zeros(shape, jnp.float32)
    cross = jnp.zeros(shape, jnp.float32)
    norm = jnp.zeros(shape, jnp.float32)
    carry = [jnp.zeros(shape, jnp.float32)] * 3
    first = rows(shape) == 0
    for y0 in range(0, count, ROWS):
        layers = []
        owns = []
        for read in (read_low, read_own, read_high):
            layer = []
            for k in range(3):
                here, up = two_rows(lambda y, k=k, read=read: read(k, y), y0, count)
                layer.append(face_modes(here, up))
                if read is read_own:
                    owns.append(here)
            layers.append(layer)
        here, above = apply_rows(
            *layers, mod_low_ref[pl.ds(y0, ROWS), :], mod_own_ref[pl.ds(y0, ROWS), :]
        )
        for k in range(3):
            rolled = pltpu.roll(above[k], 1, 0)
            force = here[k] + jnp.where(first, carry[k], rolled)
            carry[k] = rolled
            image = read_free(k, y0) * force
            out_ref[k, pl.ds(y0, ROWS), :] = image
            square += image * image
            cross += owns[k] * image
            norm += owns[k] * owns[k]
    return norm, cross, square


def energy_loop(count, read_own, read_high, use):
    for y0 in range(0, count, ROWS):
        layers = []
        for read in (read_own, read_high):
            layers.append(
                [
                    face_modes(*two_rows(lambda y, k=k, read=read: read(k, y), y0, count))
                    for k in range(3)
                ]
            )
        use(y0, element_energy(element_modes(*layers)))


def line(tile):
    return jnp.sum(tile, axis=0, keepdims=True)


def prepare_kernel(design_hbm, fixed_hbm, load_hbm, swap, first, second, third, fourth, own, design, fixed, load, sems):
    sub = lax.axis_index("sub")
    copies = [
        pltpu.make_async_copy(source, target, sems.at[n])
        for n, (source, target) in enumerate(
            ((fixed_hbm, fixed), (load_hbm, load), (design_hbm, design))
        )
    ]
    for copy in copies:
        copy.start()
    for copy in copies:
        copy.wait()

    for k in range(3):
        frees = [(1 - fixed[k, layer]).astype(jnp.float32) for layer in range(2)]
        values = [frees[layer] * load[k, layer].astype(jnp.float32) for layer in range(2)]
        for layer in range(2):
            swap[2 * k + layer] = values[layer]
            own[2 * k + layer] = values[layer]
        low = sub == 0
        swap[6 + k] = jnp.where(low, frees[1], frees[0])
        own[6 + k] = jnp.where(low, frees[0], frees[1])
        first[k] = jnp.where(low, values[1], values[0])
        second[k] = jnp.where(low, values[0], values[1])
    low = sub == 0
    for layer in range(2):
        swap[9 + layer] = design[layer]
        own[9 + layer] = design[layer]
    later = jnp.where(low, design[1], design[0])
    sooner = jnp.where(low, design[0], design[1])
    first[3] = later
    third[...] = later
    second[3] = sooner
    fourth[...] = sooner


def filter_planes(low, mid, high):
    both = low + high

    def faces(p):
        across = y_up(p) + y_down(p)
        return across + z_up(p) + z_down(p), z_up(across) + z_down(across)

    mid_face, mid_diag = faces(mid)
    both_face, both_diag = faces(both)
    return (
        filter_reach * mid
        + FACE * (both + mid_face)
        + EDGE * (both_face + mid_diag)
        + CORNER * both_diag
    )


def weight_plane(shape, row_offset, count):
    row = rows(shape) + row_offset
    lane = lanes(shape)

    def neighbours(index, size):
        return jnp.where(index > 0, 1.0, 0.0) + jnp.where(index < size - 1, 1.0, 0.0)

    ry = neighbours(row, count)
    rz = neighbours(lane, shape[1])
    face, diag = ry + rz, ry * rz
    return (
        filter_reach
        + FACE * (2.0 + face)
        + EDGE * (2.0 * face + diag)
        + (2.0 * CORNER) * diag
    )


def start_kernel(
    mods, slabs,
    own, first, second, third, fourth, swap,
    v0, v0_high, v1, free, mod_low, mod_own, slope_factor, chain_factor, moments,
    v0_low, layers,
):
    mod, slab, sub = (lax.axis_index(a) for a in AXES)
    half = third.shape[0]
    count = 2 * half
    mine = pl.ds(pl.multiple_of(sub * half, half), half)
    other = pl.ds(pl.multiple_of((1 - sub) * half, half), half)
    for layer in range(2):
        layers[2 - sub + layer, mine, :] = own[9 + layer]
        layers[2 - sub + layer, other, :] = swap[9 + layer]
    for near, deep, part in ((first, fourth, mine), (second, third, other)):

        @pl.when(sub == 0)
        def _(near=near, deep=deep, part=part):
            layers[0, part, :] = deep[...]
            layers[1, part, :] = near[3]

        @pl.when(sub == 1)
        def _(near=near, deep=deep, part=part):
            layers[3, part, :] = near[3]
            layers[0, part, :] = deep[...]

    weight = weight_plane((count, third.shape[1]), 0, count)
    starts = (mod == 0) & (slab == 0) & (sub == 0)
    filtered = filter_planes(layers[0], layers[1], layers[2]) / weight
    hyper = jnp.tanh(sharpness * (filtered - threshold))
    projected = (LOWER + hyper) * (1.0 / (LOWER + UPPER))
    below = stiff_floor + (1.0 - stiff_floor) * projected * projected * projected
    mod_low[...] = below * jnp.where(starts, 0.0, 1.0)
    filtered = filter_planes(layers[1], layers[2], layers[3]) / weight
    hyper = jnp.tanh(sharpness * (filtered - threshold))
    projected = (LOWER + hyper) * (1.0 / (LOWER + UPPER))
    squared = projected * projected
    mod_own[...] = stiff_floor + (1.0 - stiff_floor) * squared * projected
    slope_factor[...] = (-penalty * (1.0 - stiff_floor)) * squared
    chain_factor[...] = (sharpness / (LOWER + UPPER)) * (1.0 - hyper * hyper) / weight

    ends = (mod == mods - 1) & (slab == slabs - 1) & (sub == 1)
    inside = jnp.where(ends, 0.0, 1.0)
    for k in range(3):
        free[k, mine, :] = own[6 + k]
        free[k, other, :] = swap[6 + k]
        v0[k, mine, :] = own[2 * k + sub]
        v0[k, other, :] = swap[2 * k + sub]

        @pl.when(sub == 0)
        def _(k=k):
            v0_high[k, mine, :] = own[2 * k + 1]
            v0_high[k, other, :] = swap[2 * k + 1]
            v0_low[k, mine, :] = first[k]
            v0_low[k, other, :] = second[k]

        @pl.when(sub == 1)
        def _(k=k):
            v0_low[k, mine, :] = own[2 * k]
            v0_low[k, other, :] = swap[2 * k]
            v0_high[k, mine, :] = first[k] * inside
            v0_high[k, other, :] = second[k] * inside

    norm, cross, square = operator_loop(
        count,
        lambda k, y: v0_low[k, pl.ds(y, ROWS), :],
        lambda k, y: v0[k, pl.ds(y, ROWS), :],
        lambda k, y: v0_high[k, pl.ds(y, ROWS), :],
        lambda k, y: free[k, pl.ds(y, ROWS), :],
        mod_low,
        mod_own,
        v1,
    )
    moments[...] = jnp.concatenate(
        [line(norm), line(cross), line(square), jnp.zeros((5, norm.shape[1]), jnp.float32)], axis=0
    )


def second_kernel(v1, outer, inner, free, mod_low, mod_own, before, v2, v1_high, moments):
    sub = lax.axis_index("sub")
    count = v1.shape[1]
    even = sub == 0
    for k in range(3):
        v1_high[k] = jnp.where(even, inner[k], outer[k])

    def read_low(k, y):
        return jnp.where(even, outer[k, pl.ds(y, ROWS), :], inner[k, pl.ds(y, ROWS), :])

    _, cross, square = operator_loop(
        count,
        read_low,
        lambda k, y: v1[k, pl.ds(y, ROWS), :],
        lambda k, y: v1_high[k, pl.ds(y, ROWS), :],
        lambda k, y: free[k, pl.ds(y, ROWS), :],
        mod_low,
        mod_own,
        v2,
    )
    zero = jnp.zeros((3, cross.shape[1]), jnp.float32)
    moments[...] = before[...] + jnp.concatenate(
        [zero, line(cross), line(square), zero], axis=0
    )


def third_kernel(v2, v2_high, mod_own, before, moments):
    count = v2.shape[1]
    total = [jnp.zeros((ROWS, v2.shape[2]), jnp.float32)]

    def use(y0, energy):
        total[0] += energy * mod_own[pl.ds(y0, ROWS), :]

    energy_loop(
        count,
        lambda k, y: v2[k, pl.ds(y, ROWS), :],
        lambda k, y: v2_high[k, pl.ds(y, ROWS), :],
        use,
    )
    width = v2.shape[2]
    moments[...] = before[...] + jnp.concatenate(
        [
            jnp.zeros((5, width), jnp.float32),
            line(total[0]),
            jnp.zeros((2, width), jnp.float32),
        ],
        axis=0,
    )


def coefficients(m):
    step = m[0] / m[1]
    x0 = step
    r1 = -step
    norm = m[0] + 2.0 * r1 * m[1] + r1 * r1 * m[2]
    ratio = norm / m[0]
    p0, p1 = 1.0 + ratio, r1
    step = norm / (p0 * p0 * m[1] + 2.0 * p0 * p1 * m[2] + p1 * p1 * m[3])
    x0, x1 = x0 + step * p0, step * p1
    r1, r2 = r1 - step * p0, -step * p1
    after = (
        m[0]
        + 2.0 * r1 * m[1]
        + (r1 * r1 + 2.0 * r2) * m[2]
        + 2.0 * r1 * r2 * m[3]
        + r2 * r2 * m[4]
    )
    ratio = after / norm
    p0, p1, p2 = 1.0 + ratio * p0, r1 + ratio * p1, r2
    step = after / (
        p0 * p0 * m[1]
        + 2.0 * p0 * p1 * m[2]
        + (p1 * p1 + 2.0 * p0 * p2) * m[3]
        + 2.0 * p1 * p2 * m[4]
        + p2 * p2 * m[5]
    )
    return x0 + step * p0, x1 + step * p1, step * p2


def combine_kernel(
    gathered, v0, v0_high, v1, v1_high, v2, v2_high, slope_factor,
    slope, keep, send,
    own, high,
):
    sub = lax.axis_index("sub")
    count = v0.shape[1]
    half = count // 2
    total = jnp.sum(gathered[...], axis=0)
    sums = jnp.sum(total, axis=1, keepdims=True)
    c0, c1, c2 = coefficients([sums[k : k + 1] for k in range(6)])
    for k in range(3):
        own[k] = c0 * v0[k] + c1 * v1[k] + c2 * v2[k]
        high[k] = c0 * v0_high[k] + c1 * v1_high[k] + c2 * v2_high[k]

    mine = pl.ds(pl.multiple_of(sub * half, half), half)
    other = pl.ds(pl.multiple_of((1 - sub) * half, half), half)
    for k in range(3):
        keep[k] = own[k, mine, :]
        send[k] = own[k, other, :]

    def use(y0, energy):
        slope[pl.ds(y0, ROWS), :] = slope_factor[pl.ds(y0, ROWS), :] * energy

    energy_loop(
        count,
        lambda k, y: own[k, pl.ds(y, ROWS), :],
        lambda k, y: high[k, pl.ds(y, ROWS), :],
        use,
    )


def scale_kernel(slopes, chain_factor, scaled, same, cross):
    sub = lax.axis_index("sub")
    scaled[...] = jnp.sum(slopes[...], axis=0) * chain_factor[...]
    window = same.shape[0]
    shift = scaled.shape[0] - window
    same[...] = scaled[pl.ds(pl.multiple_of(sub * shift, 8), window), :]
    cross[...] = scaled[pl.ds(pl.multiple_of((1 - sub) * shift, 8), window), :]


def gradient_kernel(scaled, outer, far, partner, gradient, planes, sums):
    sub = lax.axis_index("sub")
    window = partner.shape[0]
    shift = scaled.shape[0] - window
    mine = scaled[pl.ds(pl.multiple_of(sub * shift, 8), window), :]

    @pl.when(sub == 0)
    def _():
        planes[0] = outer[...]
        planes[1] = mine
        planes[2] = partner[...]
        planes[3] = far[...]

    @pl.when(sub == 1)
    def _():
        planes[0] = far[...]
        planes[1] = partner[...]
        planes[2] = mine
        planes[3] = outer[...]

    half = gradient.shape[1]
    part = pl.ds(pl.multiple_of(sub * (window - half), 8), half)
    for layer in range(2):
        sums[...] = filter_planes(planes[layer], planes[layer + 1], planes[layer + 2])
        gradient[layer] = sums[part, :]


def call(body, outs, scratch=(), name=None):
    return pl.pallas_call(
        body,
        out_shape=[jax.ShapeDtypeStruct(shape, jnp.float32) for shape in outs],
        scratch_shapes=[pltpu.VMEM(shape, jnp.float32) for shape in scratch],
        compiler_params=pltpu.CompilerParams(vmem_limit_bytes=16 * 2**20),
        name=name,
    )


def routes(mods, slabs):
    chips = mods * slabs

    def at(chip, sub):
        return 2 * chip + sub

    def beside(chip, steps, cyclic):
        target = chip + steps
        if cyclic:
            return target % chips
        return target if 0 <= target < chips else None

    def built(moves, cyclic):
        pairs = []
        for chip in range(chips):
            for sub, steps, to in moves:
                target = beside(chip, steps, cyclic)
                if target is not None:
                    pairs.append((at(chip, sub), at(target, to)))
        return pairs

    def in_module(moves):
        pairs = []
        for chip in range(chips):
            mod, slab = divmod(chip, slabs)
            for sub, steps, to in moves:
                pairs.append((at(chip, sub), at(mod * slabs + (slab + steps) % slabs, to)))
        return pairs

    return dict(
        swap=built([(0, 0, 1), (1, 0, 0)], True),
        first=built([(0, 1, 0), (1, -1, 1)], True),
        second=built([(1, 1, 0), (0, -1, 1)], True),
        third=built([(0, 1, 1), (1, 1, 0)], True),
        fourth=built([(0, 1, 0), (1, 1, 1)], True),
        outer=built([(1, 1, 0), (0, -1, 1)], False),
        down=built([(1, 0, 0), (0, -1, 1)], False),
        halo_cross=in_module([(1, 1, 0), (0, -1, 1)]),
        halo_same=in_module([(0, -1, 0), (1, 1, 1)]),
    )


def local(mods, slabs, design, fixed, load):
    half, width = design.shape[1:]
    count = 2 * half
    path = routes(mods, slabs)

    def move(value, name):
        return lax.ppermute(value, AXES, path[name])

    plane = (count, width)
    layer = (3, count, width)
    block = (half, width)
    swap, first, second, third, fourth, own = pl.pallas_call(
        prepare_kernel,
        out_shape=[
            jax.ShapeDtypeStruct(shape, jnp.float32)
            for shape in ((11,) + block, (4,) + block, (4,) + block, block, block, (11,) + block)
        ],
        in_specs=[pl.BlockSpec(memory_space=pltpu.HBM)] * 3,
        scratch_shapes=[
            pltpu.VMEM(design.shape, jnp.float32),
            pltpu.VMEM(fixed.shape, jnp.int32),
            pltpu.VMEM(load.shape, jnp.int32),
            pltpu.SemaphoreType.DMA((3,)),
        ],
        compiler_params=pltpu.CompilerParams(vmem_limit_bytes=16 * 2**20),
        name="prepare",
    )(design, fixed, load)
    first = move(first, "first")
    second = move(second, "second")
    third = move(third, "third")
    fourth = move(fourth, "fourth")
    swap = move(swap, "swap")

    def start_body(*refs):
        start_kernel(mods, slabs, *refs)

    v0, v0_high, v1, free, mod_low, mod_own, slope_factor, chain_factor, moments = call(
        start_body,
        [layer, layer, layer, layer, plane, plane, plane, plane, (8, width)],
        [layer, (4,) + plane],
        name="start",
    )(own, first, second, third, fourth, swap)
    outer = move(v1, "outer")
    inner = move(v1, "swap")
    v2, v1_high, moments = call(second_kernel, [layer, layer, (8, width)], name="second")(
        v1, outer, inner, free, mod_low, mod_own, moments
    )
    v2_high = move(v2, "down")
    (moments,) = call(third_kernel, [(8, width)], name="third")(v2, v2_high, mod_own, moments)
    def shared(value, axes, parts):
        copies = jnp.broadcast_to(value, (parts,) + value.shape)
        return lax.all_to_all(copies, axes, 0, 0, tiled=True)

    moments = jnp.sum(shared(moments, ("slab", "sub"), 2 * slabs), axis=0)
    gathered = shared(moments, "mod", mods)
    slope, keep, send = call(
        combine_kernel, [plane, (3, half, width), (3, half, width)], [layer, layer], name="combine"
    )(gathered, v0, v0_high, v1, v1_high, v2, v2_high, slope_factor)
    slopes = shared(slope, "mod", mods)
    received = move(send, "swap")
    window = half + 8
    scaled, same, cross = call(
        scale_kernel, [plane, (window, width), (window, width)], name="scale"
    )(slopes, chain_factor)
    outer = move(cross, "halo_cross")
    far = move(same, "halo_same")
    partner = move(cross, "swap")
    even = lax.axis_index("sub") == 0
    displacement = jnp.stack(
        [jnp.where(even, keep, received), jnp.where(even, received, keep)], axis=1
    )
    (gradient,) = call(
        gradient_kernel, [(2, half, width)], [(4, window, width), (window, width)], name="gradient"
    )(scaled, outer, far, partner)
    return displacement, gradient


def solution(mesh):
    mods, slabs = mesh.shape["mod"], mesh.shape["slab"]
    assert mesh.shape["sub"] == 2
    deck = P(None, ("mod", "slab"), "sub", None)

    def body(design, fixed_mask, load_mask):
        return local(mods, slabs, design, fixed_mask, load_mask)

    return jax.shard_map(
        body,
        mesh=mesh,
        in_specs=(P("slab", "sub", None), deck, deck),
        out_specs=(deck, P("slab", "sub", None)),
        check_vma=False,
    )
```

```python
import math

import jax
import jax.numpy as jnp
import numpy as np
from jax import lax
from jax.experimental import pallas as pl
from jax.experimental.pallas import tpu as pltpu
from jax.sharding import PartitionSpec as P

stiff_floor = 0.01
penalty = 3.0
sharpness = 4.0
threshold = 0.5
filter_reach = 1.8

AXES = ("mod", "slab", "sub")
ROWS = 8
FACE = filter_reach - 1.0
EDGE = filter_reach - math.sqrt(2.0)
CORNER = filter_reach - math.sqrt(3.0)
LOWER = math.tanh(sharpness * threshold)
UPPER = math.tanh(sharpness * (1.0 - threshold))


def stiffness_modes():
    poisson = 0.3
    lame = poisson / ((1.0 + poisson) * (1.0 - 2.0 * poisson))
    shear = 1.0 / (2.0 * (1.0 + poisson))
    elastic = np.zeros((6, 6))
    elastic[:3, :3] = lame
    for axis in range(3):
        elastic[axis, axis] += 2.0 * shear
        elastic[axis + 3, axis + 3] = shear
    offset = 0.5 / math.sqrt(3.0)
    points = [0.5 - offset, 0.5 + offset]
    stiffness = np.zeros((24, 24))
    for point in ((a, b, c) for a in points for b in points for c in points):
        strain = np.zeros((6, 24))
        for corner in range(8):
            bits = (corner >> 2 & 1, corner >> 1 & 1, corner & 1)
            along = [point[a] if bits[a] else 1.0 - point[a] for a in range(3)]
            sign = [1.0 if bits[a] else -1.0 for a in range(3)]
            gx = sign[0] * along[1] * along[2]
            gy = along[0] * sign[1] * along[2]
            gz = along[0] * along[1] * sign[2]
            col = 3 * corner
            strain[0, col] = gx
            strain[1, col + 1] = gy
            strain[2, col + 2] = gz
            strain[3, col], strain[3, col + 1] = gy, gx
            strain[4, col + 1], strain[4, col + 2] = gz, gy
            strain[5, col], strain[5, col + 2] = gz, gx
        stiffness += strain.T @ elastic @ strain / 8.0
    basis = np.zeros((24, 24))
    for mode in range(8):
        for corner in range(8):
            value = 1.0
            for bit in range(3):
                if mode >> bit & 1 and not corner >> bit & 1:
                    value = -value
            for k in range(3):
                basis[3 * mode + k, 3 * corner + k] = value
    table = basis @ stiffness @ basis.T / 64.0
    table[np.abs(table) < 1e-9] = 0.0
    return table


TABLE = stiffness_modes()


def lanes(shape):
    return lax.broadcasted_iota(jnp.int32, shape, 1)


def rows(shape):
    return lax.broadcasted_iota(jnp.int32, shape, 0)


def z_up(x):
    return jnp.where(lanes(x.shape) < x.shape[1] - 1, pltpu.roll(x, x.shape[1] - 1, 1), 0.0)


def z_down(x):
    return jnp.where(lanes(x.shape) > 0, pltpu.roll(x, 1, 1), 0.0)


def y_up(x):
    return jnp.where(rows(x.shape) < x.shape[0] - 1, pltpu.roll(x, x.shape[0] - 1, 0), 0.0)


def y_down(x):
    return jnp.where(rows(x.shape) > 0, pltpu.roll(x, 1, 0), 0.0)


def two_rows(read, y0, count):
    here = read(y0)
    above = y_up(here) if y0 + ROWS == count else read(y0 + 1)
    return here, above


def face_modes(here, above):
    out = []
    for part in (here + above, above - here):
        shifted = z_up(part)
        out += [part + shifted, shifted - part]
    return out


def element_modes(low, high):
    sums = [[high[k][m] + low[k][m] for m in range(4)] for k in range(3)]
    diffs = [[high[k][m] - low[k][m] for m in range(4)] for k in range(3)]
    return [sums[k] + diffs[k] for k in range(3)]


def mode_forces(q):
    made = {}

    def scaled(j, value):
        key = (j, round(value, 12))
        if key not in made:
            made[key] = q[j % 3][j // 3] * np.float32(value)
        return made[key]

    out = [[None] * 8 for _ in range(3)]
    for i in range(24):
        total = None
        for j in np.nonzero(TABLE[i])[0]:
            term = scaled(int(j), float(TABLE[i, j]))
            total = term if total is None else total + term
        out[i % 3][i // 3] = total
    return out


def element_energy(q):
    r = mode_forces(q)
    total = None
    for k in range(3):
        for m in range(1, 8):
            term = q[k][m] * r[k][m]
            total = term if total is None else total + term
    return total


def apply_rows(low, own, high, mod_low, mod_own):
    r_low = mode_forces(element_modes(low, own))
    r_own = mode_forces(element_modes(own, high))
    here, above = [], []
    for k in range(3):
        field = []
        for m in range(4):
            a, b = r_low[k][m], r_low[k][m + 4]
            c, d = r_own[k][m], r_own[k][m + 4]
            from_low = b if a is None else a + b
            from_own = -d if c is None else c - d
            field.append(mod_low * from_low + mod_own * from_own)
        part = []
        for py in range(2):
            s, d = field[2 * py], field[2 * py + 1]
            part.append((s - d) + z_down(s + d))
        here.append(part[0] - part[1])
        above.append(part[0] + part[1])
    return here, above


def operator_loop(count, read_low, read_own, read_high, read_free, mod_low_ref, mod_own_ref, out_ref):
    shape = (ROWS, out_ref.shape[2])
    square = jnp.zeros(shape, jnp.float32)
    cross = jnp.zeros(shape, jnp.float32)
    norm = jnp.zeros(shape, jnp.float32)
    carry = [jnp.zeros(shape, jnp.float32)] * 3
    first = rows(shape) == 0
    for y0 in range(0, count, ROWS):
        layers = []
        owns = []
        for read in (read_low, read_own, read_high):
            layer = []
            for k in range(3):
                here, up = two_rows(lambda y, k=k, read=read: read(k, y), y0, count)
                layer.append(face_modes(here, up))
                if read is read_own:
                    owns.append(here)
            layers.append(layer)
        here, above = apply_rows(
            *layers, mod_low_ref[pl.ds(y0, ROWS), :], mod_own_ref[pl.ds(y0, ROWS), :]
        )
        for k in range(3):
            rolled = pltpu.roll(above[k], 1, 0)
            force = here[k] + jnp.where(first, carry[k], rolled)
            carry[k] = rolled
            image = read_free(k, y0) * force
            out_ref[k, pl.ds(y0, ROWS), :] = image
            square += image * image
            cross += owns[k] * image
            norm += owns[k] * owns[k]
    return norm, cross, square


def energy_loop(count, read_own, read_high, use):
    for y0 in range(0, count, ROWS):
        layers = []
        for read in (read_own, read_high):
            layers.append(
                [
                    face_modes(*two_rows(lambda y, k=k, read=read: read(k, y), y0, count))
                    for k in range(3)
                ]
            )
        use(y0, element_energy(element_modes(*layers)))


def line(tile):
    return jnp.sum(tile, axis=0, keepdims=True)


def prepare_kernel(free, right, design, swap, first, second, third, fourth, own):
    sub = lax.axis_index("sub")
    for k in range(3):
        frees = [free[k, layer] for layer in range(2)]
        values = [right[k, layer] for layer in range(2)]
        for layer in range(2):
            swap[2 * k + layer] = values[layer]
            own[2 * k + layer] = values[layer]
        low = sub == 0
        swap[6 + k] = jnp.where(low, frees[1], frees[0])
        own[6 + k] = jnp.where(low, frees[0], frees[1])
        first[k] = jnp.where(low, values[1], values[0])
        second[k] = jnp.where(low, values[0], values[1])
    low = sub == 0
    for layer in range(2):
        swap[9 + layer] = design[layer]
        own[9 + layer] = design[layer]
    later = jnp.where(low, design[1], design[0])
    sooner = jnp.where(low, design[0], design[1])
    first[3] = later
    third[...] = later
    second[3] = sooner
    fourth[...] = sooner


def filter_planes(low, mid, high):
    both = low + high

    def faces(p):
        across = y_up(p) + y_down(p)
        return across + z_up(p) + z_down(p), z_up(across) + z_down(across)

    mid_face, mid_diag = faces(mid)
    both_face, both_diag = faces(both)
    return (
        filter_reach * mid
        + FACE * (both + mid_face)
        + EDGE * (both_face + mid_diag)
        + CORNER * both_diag
    )


def weight_plane(shape, row_offset, count):
    row = rows(shape) + row_offset
    lane = lanes(shape)

    def neighbours(index, size):
        return jnp.where(index > 0, 1.0, 0.0) + jnp.where(index < size - 1, 1.0, 0.0)

    ry = neighbours(row, count)
    rz = neighbours(lane, shape[1])
    face, diag = ry + rz, ry * rz
    return (
        filter_reach
        + FACE * (2.0 + face)
        + EDGE * (2.0 * face + diag)
        + (2.0 * CORNER) * diag
    )


def start_kernel(
    mods, slabs,
    own, first, second, third, fourth, swap,
    v0, v0_high, v1, free, mod_low, mod_own, slope_factor, chain_factor, moments,
    v0_low, layers,
):
    mod, slab, sub = (lax.axis_index(a) for a in AXES)
    half = third.shape[0]
    count = 2 * half
    mine = pl.ds(pl.multiple_of(sub * half, half), half)
    other = pl.ds(pl.multiple_of((1 - sub) * half, half), half)
    for layer in range(2):
        layers[2 - sub + layer, mine, :] = own[9 + layer]
        layers[2 - sub + layer, other, :] = swap[9 + layer]
    for near, deep, part in ((first, fourth, mine), (second, third, other)):

        @pl.when(sub == 0)
        def _(near=near, deep=deep, part=part):
            layers[0, part, :] = deep[...]
            layers[1, part, :] = near[3]

        @pl.when(sub == 1)
        def _(near=near, deep=deep, part=part):
            layers[3, part, :] = near[3]
            layers[0, part, :] = deep[...]

    weight = weight_plane((count, third.shape[1]), 0, count)
    starts = (mod == 0) & (slab == 0) & (sub == 0)
    filtered = filter_planes(layers[0], layers[1], layers[2]) / weight
    hyper = jnp.tanh(sharpness * (filtered - threshold))
    projected = (LOWER + hyper) * (1.0 / (LOWER + UPPER))
    below = stiff_floor + (1.0 - stiff_floor) * projected * projected * projected
    mod_low[...] = below * jnp.where(starts, 0.0, 1.0)
    filtered = filter_planes(layers[1], layers[2], layers[3]) / weight
    hyper = jnp.tanh(sharpness * (filtered - threshold))
    projected = (LOWER + hyper) * (1.0 / (LOWER + UPPER))
    squared = projected * projected
    mod_own[...] = stiff_floor + (1.0 - stiff_floor) * squared * projected
    slope_factor[...] = (-penalty * (1.0 - stiff_floor)) * squared
    chain_factor[...] = (sharpness / (LOWER + UPPER)) * (1.0 - hyper * hyper) / weight

    ends = (mod == mods - 1) & (slab == slabs - 1) & (sub == 1)
    inside = jnp.where(ends, 0.0, 1.0)
    for k in range(3):
        free[k, mine, :] = own[6 + k]
        free[k, other, :] = swap[6 + k]
        v0[k, mine, :] = own[2 * k + sub]
        v0[k, other, :] = swap[2 * k + sub]

        @pl.when(sub == 0)
        def _(k=k):
            v0_high[k, mine, :] = own[2 * k + 1]
            v0_high[k, other, :] = swap[2 * k + 1]
            v0_low[k, mine, :] = first[k]
            v0_low[k, other, :] = second[k]

        @pl.when(sub == 1)
        def _(k=k):
            v0_low[k, mine, :] = own[2 * k]
            v0_low[k, other, :] = swap[2 * k]
            v0_high[k, mine, :] = first[k] * inside
            v0_high[k, other, :] = second[k] * inside

    norm, cross, square = operator_loop(
        count,
        lambda k, y: v0_low[k, pl.ds(y, ROWS), :],
        lambda k, y: v0[k, pl.ds(y, ROWS), :],
        lambda k, y: v0_high[k, pl.ds(y, ROWS), :],
        lambda k, y: free[k, pl.ds(y, ROWS), :],
        mod_low,
        mod_own,
        v1,
    )
    moments[...] = jnp.concatenate(
        [line(norm), line(cross), line(square), jnp.zeros((5, norm.shape[1]), jnp.float32)], axis=0
    )


def second_kernel(v1, outer, inner, free, mod_low, mod_own, before, v2, v1_high, moments):
    sub = lax.axis_index("sub")
    count = v1.shape[1]
    even = sub == 0
    for k in range(3):
        v1_high[k] = jnp.where(even, inner[k], outer[k])

    def read_low(k, y):
        return jnp.where(even, outer[k, pl.ds(y, ROWS), :], inner[k, pl.ds(y, ROWS), :])

    _, cross, square = operator_loop(
        count,
        read_low,
        lambda k, y: v1[k, pl.ds(y, ROWS), :],
        lambda k, y: v1_high[k, pl.ds(y, ROWS), :],
        lambda k, y: free[k, pl.ds(y, ROWS), :],
        mod_low,
        mod_own,
        v2,
    )
    zero = jnp.zeros((3, cross.shape[1]), jnp.float32)
    moments[...] = before[...] + jnp.concatenate(
        [zero, line(cross), line(square), zero], axis=0
    )


def third_kernel(v2, v2_high, mod_own, before, moments):
    count = v2.shape[1]
    total = [jnp.zeros((ROWS, v2.shape[2]), jnp.float32)]

    def use(y0, energy):
        total[0] += energy * mod_own[pl.ds(y0, ROWS), :]

    energy_loop(
        count,
        lambda k, y: v2[k, pl.ds(y, ROWS), :],
        lambda k, y: v2_high[k, pl.ds(y, ROWS), :],
        use,
    )
    width = v2.shape[2]
    moments[...] = before[...] + jnp.concatenate(
        [
            jnp.zeros((5, width), jnp.float32),
            line(total[0]),
            jnp.zeros((2, width), jnp.float32),
        ],
        axis=0,
    )


def coefficients(m):
    step = m[0] / m[1]
    x0 = step
    r1 = -step
    norm = m[0] + 2.0 * r1 * m[1] + r1 * r1 * m[2]
    ratio = norm / m[0]
    p0, p1 = 1.0 + ratio, r1
    step = norm / (p0 * p0 * m[1] + 2.0 * p0 * p1 * m[2] + p1 * p1 * m[3])
    x0, x1 = x0 + step * p0, step * p1
    r1, r2 = r1 - step * p0, -step * p1
    after = (
        m[0]
        + 2.0 * r1 * m[1]
        + (r1 * r1 + 2.0 * r2) * m[2]
        + 2.0 * r1 * r2 * m[3]
        + r2 * r2 * m[4]
    )
    ratio = after / norm
    p0, p1, p2 = 1.0 + ratio * p0, r1 + ratio * p1, r2
    step = after / (
        p0 * p0 * m[1]
        + 2.0 * p0 * p1 * m[2]
        + (p1 * p1 + 2.0 * p0 * p2) * m[3]
        + 2.0 * p1 * p2 * m[4]
        + p2 * p2 * m[5]
    )
    return x0 + step * p0, x1 + step * p1, step * p2


def combine_kernel(
    moments, v0, v0_high, v1, v1_high, v2, v2_high, slope_factor,
    slope, keep, send,
    own, high,
):
    sub = lax.axis_index("sub")
    count = v0.shape[1]
    half = count // 2
    sums = jnp.sum(moments[...], axis=1, keepdims=True)
    c0, c1, c2 = coefficients([sums[k : k + 1] for k in range(6)])
    for k in range(3):
        own[k] = c0 * v0[k] + c1 * v1[k] + c2 * v2[k]
        high[k] = c0 * v0_high[k] + c1 * v1_high[k] + c2 * v2_high[k]

    mine = pl.ds(pl.multiple_of(sub * half, half), half)
    other = pl.ds(pl.multiple_of((1 - sub) * half, half), half)
    for k in range(3):
        keep[k] = own[k, mine, :]
        send[k] = own[k, other, :]

    def use(y0, energy):
        slope[pl.ds(y0, ROWS), :] = slope_factor[pl.ds(y0, ROWS), :] * energy

    energy_loop(
        count,
        lambda k, y: own[k, pl.ds(y, ROWS), :],
        lambda k, y: high[k, pl.ds(y, ROWS), :],
        use,
    )


def scale_kernel(slope, rest, chain_factor, scaled, same, cross):
    sub = lax.axis_index("sub")
    scaled[...] = (slope[...] + rest[...]) * chain_factor[...]
    window = same.shape[0]
    shift = scaled.shape[0] - window
    same[...] = scaled[pl.ds(pl.multiple_of(sub * shift, 8), window), :]
    cross[...] = scaled[pl.ds(pl.multiple_of((1 - sub) * shift, 8), window), :]


def gradient_kernel(scaled, outer, far, partner, gradient, planes, sums):
    sub = lax.axis_index("sub")
    window = partner.shape[0]
    shift = scaled.shape[0] - window
    mine = scaled[pl.ds(pl.multiple_of(sub * shift, 8), window), :]

    @pl.when(sub == 0)
    def _():
        planes[0] = outer[...]
        planes[1] = mine
        planes[2] = partner[...]
        planes[3] = far[...]

    @pl.when(sub == 1)
    def _():
        planes[0] = far[...]
        planes[1] = partner[...]
        planes[2] = mine
        planes[3] = outer[...]

    half = gradient.shape[1]
    part = pl.ds(pl.multiple_of(sub * (window - half), 8), half)
    for layer in range(2):
        sums[...] = filter_planes(planes[layer], planes[layer + 1], planes[layer + 2])
        gradient[layer] = sums[part, :]


def call(body, outs, scratch=(), name=None):
    return pl.pallas_call(
        body,
        out_shape=[jax.ShapeDtypeStruct(shape, jnp.float32) for shape in outs],
        scratch_shapes=[pltpu.VMEM(shape, jnp.float32) for shape in scratch],
        compiler_params=pltpu.CompilerParams(vmem_limit_bytes=16 * 2**20),
        name=name,
    )


def routes(mods, slabs):
    chips = mods * slabs

    def at(chip, sub):
        return 2 * chip + sub

    def beside(chip, steps, cyclic):
        target = chip + steps
        if cyclic:
            return target % chips
        return target if 0 <= target < chips else None

    def built(moves, cyclic):
        pairs = []
        for chip in range(chips):
            for sub, steps, to in moves:
                target = beside(chip, steps, cyclic)
                if target is not None:
                    pairs.append((at(chip, sub), at(target, to)))
        return pairs

    def in_module(moves):
        pairs = []
        for chip in range(chips):
            mod, slab = divmod(chip, slabs)
            for sub, steps, to in moves:
                pairs.append((at(chip, sub), at(mod * slabs + (slab + steps) % slabs, to)))
        return pairs

    return dict(
        swap=built([(0, 0, 1), (1, 0, 0)], True),
        first=built([(0, 1, 0), (1, -1, 1)], True),
        second=built([(1, 1, 0), (0, -1, 1)], True),
        third=built([(0, 1, 1), (1, 1, 0)], True),
        fourth=built([(0, 1, 0), (1, 1, 1)], True),
        outer=built([(1, 1, 0), (0, -1, 1)], False),
        down=built([(1, 0, 0), (0, -1, 1)], False),
        halo_cross=in_module([(1, 1, 0), (0, -1, 1)]),
        halo_same=in_module([(0, -1, 0), (1, 1, 1)]),
    )


def all_sum(value, axis, count):
    if count & (count - 1) == 0:
        step = 1
        while step < count:
            value = value + lax.ppermute(value, axis, [(i, i ^ step) for i in range(count)])
            step *= 2
        return value
    total = value
    for step in range(1, count):
        total = total + lax.ppermute(value, axis, [(i, (i + step) % count) for i in range(count)])
    return total


def module_sum(value, mods, slabs):
    if mods & (mods - 1):
        return all_sum(value, "mod", mods), jnp.zeros_like(value)
    steps = [1 << bit for bit in range(mods.bit_length() - 1)]
    got = jnp.zeros_like(value)
    for n, _ in enumerate(steps):
        pairs = []
        for mod in range(mods):
            for slab in range(slabs):
                for sub in range(2):
                    step = steps[n] if sub == 0 else steps[-1 - n]
                    pairs.append(
                        (2 * (mod * slabs + slab) + sub, 2 * ((mod ^ step) * slabs + slab) + sub)
                    )
        value = value + got if n else value
        got = lax.ppermute(value, AXES, pairs)
    return value, got


def local(mods, slabs, design, fixed, load):
    half, width = design.shape[1:]
    count = 2 * half
    path = routes(mods, slabs)

    def move(value, name):
        return lax.ppermute(value, AXES, path[name])

    plane = (count, width)
    layer = (3, count, width)
    block = (half, width)
    free = (1 - fixed).astype(jnp.float32)
    right = free * load.astype(jnp.float32)
    swap, first, second, third, fourth, own = call(
        prepare_kernel,
        [(11,) + block, (4,) + block, (4,) + block, block, block, (11,) + block],
        name="prepare",
    )(free, right, design)
    first = move(first, "first")
    second = move(second, "second")
    third = move(third, "third")
    fourth = move(fourth, "fourth")
    swap = move(swap, "swap")

    def start_body(*refs):
        start_kernel(mods, slabs, *refs)

    v0, v0_high, v1, free, mod_low, mod_own, slope_factor, chain_factor, moments = call(
        start_body,
        [layer, layer, layer, layer, plane, plane, plane, plane, (8, width)],
        [layer, (4,) + plane],
        name="start",
    )(own, first, second, third, fourth, swap)
    outer = move(v1, "outer")
    inner = move(v1, "swap")
    v2, v1_high, moments = call(second_kernel, [layer, layer, (8, width)], name="second")(
        v1, outer, inner, free, mod_low, mod_own, moments
    )
    v2_high = move(v2, "down")
    (moments,) = call(third_kernel, [(8, width)], name="third")(v2, v2_high, mod_own, moments)
    moments = all_sum(moments, "sub", 2)
    moments = all_sum(moments, "slab", slabs)
    moments = all_sum(moments, "mod", mods)
    slope, keep, send = call(
        combine_kernel, [plane, (3, half, width), (3, half, width)], [layer, layer], name="combine"
    )(moments, v0, v0_high, v1, v1_high, v2, v2_high, slope_factor)
    slope, rest = module_sum(slope, mods, slabs)
    received = move(send, "swap")
    window = half + 8
    scaled, same, cross = call(
        scale_kernel, [plane, (window, width), (window, width)], name="scale"
    )(slope, rest, chain_factor)
    outer = move(cross, "halo_cross")
    far = move(same, "halo_same")
    partner = move(cross, "swap")
    even = lax.axis_index("sub") == 0
    displacement = jnp.stack(
        [jnp.where(even, keep, received), jnp.where(even, received, keep)], axis=1
    )
    (gradient,) = call(
        gradient_kernel, [(2, half, width)], [(4, window, width), (window, width)], name="gradient"
    )(scaled, outer, far, partner)
    return displacement, gradient


def solution(mesh):
    mods, slabs = mesh.shape["mod"], mesh.shape["slab"]
    assert mesh.shape["sub"] == 2
    deck = P(None, ("mod", "slab"), "sub", None)

    def body(design, fixed_mask, load_mask):
        return local(mods, slabs, design, fixed_mask, load_mask)

    return jax.shard_map(
        body,
        mesh=mesh,
        in_specs=(P("slab", "sub", None), deck, deck),
        out_specs=(deck, P("slab", "sub", None)),
        check_vma=False,
    )
```

```python
import math

import jax
import jax.numpy as jnp
import numpy as np
from jax import lax
from jax.experimental import pallas as pl
from jax.experimental.pallas import tpu as pltpu
from jax.sharding import PartitionSpec as P

stiff_floor = 0.01
penalty = 3.0
sharpness = 4.0
threshold = 0.5
filter_reach = 1.8

AXES = ("mod", "slab", "sub")
ROWS = 8
FACE = filter_reach - 1.0
EDGE = filter_reach - math.sqrt(2.0)
CORNER = filter_reach - math.sqrt(3.0)
LOWER = math.tanh(sharpness * threshold)
UPPER = math.tanh(sharpness * (1.0 - threshold))


def stiffness_modes():
    poisson = 0.3
    lame = poisson / ((1.0 + poisson) * (1.0 - 2.0 * poisson))
    shear = 1.0 / (2.0 * (1.0 + poisson))
    elastic = np.zeros((6, 6))
    elastic[:3, :3] = lame
    for axis in range(3):
        elastic[axis, axis] += 2.0 * shear
        elastic[axis + 3, axis + 3] = shear
    offset = 0.5 / math.sqrt(3.0)
    points = [0.5 - offset, 0.5 + offset]
    stiffness = np.zeros((24, 24))
    for point in ((a, b, c) for a in points for b in points for c in points):
        strain = np.zeros((6, 24))
        for corner in range(8):
            bits = (corner >> 2 & 1, corner >> 1 & 1, corner & 1)
            along = [point[a] if bits[a] else 1.0 - point[a] for a in range(3)]
            sign = [1.0 if bits[a] else -1.0 for a in range(3)]
            gx = sign[0] * along[1] * along[2]
            gy = along[0] * sign[1] * along[2]
            gz = along[0] * along[1] * sign[2]
            col = 3 * corner
            strain[0, col] = gx
            strain[1, col + 1] = gy
            strain[2, col + 2] = gz
            strain[3, col], strain[3, col + 1] = gy, gx
            strain[4, col + 1], strain[4, col + 2] = gz, gy
            strain[5, col], strain[5, col + 2] = gz, gx
        stiffness += strain.T @ elastic @ strain / 8.0
    basis = np.zeros((24, 24))
    for mode in range(8):
        for corner in range(8):
            value = 1.0
            for bit in range(3):
                if mode >> bit & 1 and not corner >> bit & 1:
                    value = -value
            for k in range(3):
                basis[3 * mode + k, 3 * corner + k] = value
    table = basis @ stiffness @ basis.T / 64.0
    table[np.abs(table) < 1e-9] = 0.0
    return table


TABLE = stiffness_modes()


def lanes(shape):
    return lax.broadcasted_iota(jnp.int32, shape, 1)


def rows(shape):
    return lax.broadcasted_iota(jnp.int32, shape, 0)


def z_up(x):
    return jnp.where(lanes(x.shape) < x.shape[1] - 1, pltpu.roll(x, x.shape[1] - 1, 1), 0.0)


def z_down(x):
    return jnp.where(lanes(x.shape) > 0, pltpu.roll(x, 1, 1), 0.0)


def y_up(x):
    return jnp.where(rows(x.shape) < x.shape[0] - 1, pltpu.roll(x, x.shape[0] - 1, 0), 0.0)


def y_down(x):
    return jnp.where(rows(x.shape) > 0, pltpu.roll(x, 1, 0), 0.0)


def two_rows(read, y0, count):
    here = read(y0)
    above = y_up(here) if y0 + ROWS == count else read(y0 + 1)
    return here, above


def face_modes(here, above):
    out = []
    for part in (here + above, above - here):
        shifted = z_up(part)
        out += [part + shifted, shifted - part]
    return out


def element_modes(own, other, side):
    sums = [[other[k][m] + own[k][m] for m in range(4)] for k in range(3)]
    diffs = [[(other[k][m] - own[k][m]) * side for m in range(4)] for k in range(3)]
    return [sums[k] + diffs[k] for k in range(3)]


def mode_forces(q):
    made = {}

    def scaled(j, value):
        key = (j, round(value, 12))
        if key not in made:
            made[key] = q[j % 3][j // 3] * np.float32(value)
        return made[key]

    out = [[None] * 8 for _ in range(3)]
    for i in range(24):
        total = None
        for j in np.nonzero(TABLE[i])[0]:
            term = scaled(int(j), float(TABLE[i, j]))
            total = term if total is None else total + term
        out[i % 3][i // 3] = total
    return out


def element_energy(q):
    r = mode_forces(q)
    total = None
    for k in range(3):
        for m in range(1, 8):
            term = q[k][m] * r[k][m]
            total = term if total is None else total + term
    return total


def own_fields(own, other, side):
    r = mode_forces(element_modes(own, other, side))
    fields = []
    for k in range(3):
        for m in range(4):
            d = r[k][m + 4] * side
            fields.append(-d if r[k][m] is None else r[k][m] - d)
    return fields


def layer_modes(read, y0, count):
    heres, modes = [], []
    for k in range(3):
        here, above = two_rows(lambda y, k=k: read(k, y), y0, count)
        heres.append(here)
        modes.append(face_modes(here, above))
    return heres, modes


def fields_loop(count, read_own, read_other, side, fields):
    for y0 in range(0, count, ROWS):
        _, own = layer_modes(read_own, y0, count)
        _, other = layer_modes(read_other, y0, count)
        for n, value in enumerate(own_fields(own, other, side)):
            fields[n, pl.ds(y0, ROWS), :] = value


def operator_loop(count, read_own, read_other, side, fields, mod_inner, mod_outer, free, out_ref):
    shape = (ROWS, out_ref.shape[2])
    square = jnp.zeros(shape, jnp.float32)
    cross = jnp.zeros(shape, jnp.float32)
    norm = jnp.zeros(shape, jnp.float32)
    carry = [jnp.zeros(shape, jnp.float32)] * 3
    first = rows(shape) == 0
    for y0 in range(0, count, ROWS):
        part = pl.ds(y0, ROWS)
        owns, own = layer_modes(read_own, y0, count)
        _, other = layer_modes(read_other, y0, count)
        inner, outer = mod_inner[part, :], mod_outer[part, :]
        total = [
            outer * value + inner * fields[n, part, :]
            for n, value in enumerate(own_fields(own, other, side))
        ]
        for k in range(3):
            faces = []
            for py in range(2):
                s, d = total[4 * k + 2 * py], total[4 * k + 2 * py + 1]
                faces.append((s - d) + z_down(s + d))
            rolled = pltpu.roll(faces[0] + faces[1], 1, 0)
            force = (faces[0] - faces[1]) + jnp.where(first, carry[k], rolled)
            carry[k] = rolled
            image = free[k, part, :] * force
            out_ref[k, part, :] = image
            square += image * image
            cross += owns[k] * image
            norm += owns[k] * owns[k]
    return norm, cross, square


def energy_loop(count, read_own, read_high, use):
    for y0 in range(0, count, ROWS):
        _, own = layer_modes(read_own, y0, count)
        _, high = layer_modes(read_high, y0, count)
        use(y0, element_energy(element_modes(own, high, 1.0)))


def rows_of(ref):
    return lambda k, y: ref[k, pl.ds(y, ROWS), :]


def inner_side(sub):
    return jnp.where(sub == 0, 1.0, -1.0).astype(jnp.float32)


def line(tile):
    return jnp.sum(tile, axis=0, keepdims=True)


def prepare_kernel(free, right, design, swap, first, second, third, fourth, own):
    sub = lax.axis_index("sub")
    for k in range(3):
        frees = [free[k, layer] for layer in range(2)]
        values = [right[k, layer] for layer in range(2)]
        for layer in range(2):
            swap[2 * k + layer] = values[layer]
            own[2 * k + layer] = values[layer]
        low = sub == 0
        swap[6 + k] = jnp.where(low, frees[1], frees[0])
        own[6 + k] = jnp.where(low, frees[0], frees[1])
        first[k] = jnp.where(low, values[1], values[0])
        second[k] = jnp.where(low, values[0], values[1])
    low = sub == 0
    for layer in range(2):
        swap[9 + layer] = design[layer]
        own[9 + layer] = design[layer]
    later = jnp.where(low, design[1], design[0])
    sooner = jnp.where(low, design[0], design[1])
    first[3] = later
    third[...] = later
    second[3] = sooner
    fourth[...] = sooner


def filter_planes(low, mid, high):
    both = low + high

    def faces(p):
        across = y_up(p) + y_down(p)
        return across + z_up(p) + z_down(p), z_up(across) + z_down(across)

    mid_face, mid_diag = faces(mid)
    both_face, both_diag = faces(both)
    return (
        filter_reach * mid
        + FACE * (both + mid_face)
        + EDGE * (both_face + mid_diag)
        + CORNER * both_diag
    )


def weight_plane(shape, row_offset, count):
    row = rows(shape) + row_offset
    lane = lanes(shape)

    def neighbours(index, size):
        return jnp.where(index > 0, 1.0, 0.0) + jnp.where(index < size - 1, 1.0, 0.0)

    ry = neighbours(row, count)
    rz = neighbours(lane, shape[1])
    face, diag = ry + rz, ry * rz
    return (
        filter_reach
        + FACE * (2.0 + face)
        + EDGE * (2.0 * face + diag)
        + (2.0 * CORNER) * diag
    )


def start_inner_kernel(own, swap, v0, v0_inner, free, fields, layers):
    sub = lax.axis_index("sub")
    half = own.shape[1]
    count = 2 * half
    mine = pl.ds(pl.multiple_of(sub * half, half), half)
    other = pl.ds(pl.multiple_of((1 - sub) * half, half), half)
    for layer in range(2):
        layers[layer, mine, :] = own[9 + layer]
        layers[layer, other, :] = swap[9 + layer]
    for k in range(3):
        free[k, mine, :] = own[6 + k]
        free[k, other, :] = swap[6 + k]
        v0[k, mine, :] = own[2 * k + sub]
        v0[k, other, :] = swap[2 * k + sub]
        v0_inner[k, mine, :] = own[2 * k + 1 - sub]
        v0_inner[k, other, :] = swap[2 * k + 1 - sub]
    fields_loop(count, rows_of(v0), rows_of(v0_inner), inner_side(sub), fields)


def start_outer_kernel(
    mods, slabs,
    v0, v0_inner, free, fields, layers, first, second, third, fourth,
    v1, v0_high, mod_inner, mod_outer, mod_own, slope_factor, chain_factor, moments,
    v0_outer, near, deep,
):
    mod, slab, sub = (lax.axis_index(a) for a in AXES)
    half = third.shape[0]
    count = 2 * half
    even = sub == 0
    mine = pl.ds(pl.multiple_of(sub * half, half), half)
    other = pl.ds(pl.multiple_of((1 - sub) * half, half), half)
    near[mine, :] = first[3]
    near[other, :] = second[3]
    deep[mine, :] = fourth[...]
    deep[other, :] = third[...]
    starts = (mod == 0) & (slab == 0) & even
    ends = (mod == mods - 1) & (slab == slabs - 1) & (sub == 1)
    inside = jnp.where(ends, 0.0, 1.0)
    for k in range(3):
        v0_outer[k, mine, :] = first[k] * inside
        v0_outer[k, other, :] = second[k] * inside
        v0_high[k] = jnp.where(even, v0_inner[k], v0_outer[k])

    x1 = jnp.where(even, near[...], layers[0])
    x2 = jnp.where(even, layers[0], layers[1])
    x3 = jnp.where(even, layers[1], near[...])
    weight = weight_plane((count, third.shape[1]), 0, count)
    filtered = filter_planes(deep[...], x1, x2) / weight
    hyper = jnp.tanh(sharpness * (filtered - threshold))
    projected = (LOWER + hyper) * (1.0 / (LOWER + UPPER))
    below = stiff_floor + (1.0 - stiff_floor) * projected * projected * projected
    below = below * jnp.where(starts, 0.0, 1.0)
    filtered = filter_planes(x1, x2, x3) / weight
    hyper = jnp.tanh(sharpness * (filtered - threshold))
    projected = (LOWER + hyper) * (1.0 / (LOWER + UPPER))
    squared = projected * projected
    stiff = stiff_floor + (1.0 - stiff_floor) * squared * projected
    mod_own[...] = stiff
    mod_inner[...] = jnp.where(even, stiff, below)
    mod_outer[...] = jnp.where(even, below, stiff)
    slope_factor[...] = (-penalty * (1.0 - stiff_floor)) * squared
    chain_factor[...] = (sharpness / (LOWER + UPPER)) * (1.0 - hyper * hyper) / weight

    norm, cross, square = operator_loop(
        count, rows_of(v0), rows_of(v0_outer), -inner_side(sub), fields, mod_inner, mod_outer, free, v1
    )
    moments[...] = jnp.concatenate(
        [line(norm), line(cross), line(square), jnp.zeros((5, norm.shape[1]), jnp.float32)], axis=0
    )


def second_inner_kernel(v1, inner, fields):
    fields_loop(v1.shape[1], rows_of(v1), rows_of(inner), inner_side(lax.axis_index("sub")), fields)


def second_outer_kernel(
    v1, inner, outer, fields, free, mod_inner, mod_outer, before, v2, v1_high, moments
):
    sub = lax.axis_index("sub")
    count = v1.shape[1]
    for k in range(3):
        v1_high[k] = jnp.where(sub == 0, inner[k], outer[k])
    _, cross, square = operator_loop(
        count, rows_of(v1), rows_of(outer), -inner_side(sub), fields, mod_inner, mod_outer, free, v2
    )
    zero = jnp.zeros((3, cross.shape[1]), jnp.float32)
    moments[...] = before[...] + jnp.concatenate(
        [zero, line(cross), line(square), zero], axis=0
    )


def third_kernel(v2, v2_high, mod_own, before, moments):
    count = v2.shape[1]
    total = [jnp.zeros((ROWS, v2.shape[2]), jnp.float32)]

    def use(y0, energy):
        total[0] += energy * mod_own[pl.ds(y0, ROWS), :]

    energy_loop(
        count,
        lambda k, y: v2[k, pl.ds(y, ROWS), :],
        lambda k, y: v2_high[k, pl.ds(y, ROWS), :],
        use,
    )
    width = v2.shape[2]
    moments[...] = before[...] + jnp.concatenate(
        [
            jnp.zeros((5, width), jnp.float32),
            line(total[0]),
            jnp.zeros((2, width), jnp.float32),
        ],
        axis=0,
    )


def coefficients(m):
    step = m[0] / m[1]
    x0 = step
    r1 = -step
    norm = m[0] + 2.0 * r1 * m[1] + r1 * r1 * m[2]
    ratio = norm / m[0]
    p0, p1 = 1.0 + ratio, r1
    step = norm / (p0 * p0 * m[1] + 2.0 * p0 * p1 * m[2] + p1 * p1 * m[3])
    x0, x1 = x0 + step * p0, step * p1
    r1, r2 = r1 - step * p0, -step * p1
    after = (
        m[0]
        + 2.0 * r1 * m[1]
        + (r1 * r1 + 2.0 * r2) * m[2]
        + 2.0 * r1 * r2 * m[3]
        + r2 * r2 * m[4]
    )
    ratio = after / norm
    p0, p1, p2 = 1.0 + ratio * p0, r1 + ratio * p1, r2
    step = after / (
        p0 * p0 * m[1]
        + 2.0 * p0 * p1 * m[2]
        + (p1 * p1 + 2.0 * p0 * p2) * m[3]
        + 2.0 * p1 * p2 * m[4]
        + p2 * p2 * m[5]
    )
    return x0 + step * p0, x1 + step * p1, step * p2


def combine_kernel(
    gathered, v0, v0_high, v1, v1_high, v2, v2_high, slope_factor,
    slope, keep, send,
    own, high,
):
    sub = lax.axis_index("sub")
    count = v0.shape[1]
    half = count // 2
    sums = jnp.sum(jnp.sum(gathered[...], axis=0), axis=1, keepdims=True)
    c0, c1, c2 = coefficients([sums[k : k + 1] for k in range(6)])
    for k in range(3):
        own[k] = c0 * v0[k] + c1 * v1[k] + c2 * v2[k]
        high[k] = c0 * v0_high[k] + c1 * v1_high[k] + c2 * v2_high[k]

    mine = pl.ds(pl.multiple_of(sub * half, half), half)
    other = pl.ds(pl.multiple_of((1 - sub) * half, half), half)
    for k in range(3):
        keep[k] = own[k, mine, :]
        send[k] = own[k, other, :]

    def use(y0, energy):
        slope[pl.ds(y0, ROWS), :] = slope_factor[pl.ds(y0, ROWS), :] * energy

    energy_loop(
        count,
        lambda k, y: own[k, pl.ds(y, ROWS), :],
        lambda k, y: high[k, pl.ds(y, ROWS), :],
        use,
    )


def scale_kernel(*refs):
    slopes, (chain_factor, scaled, same, cross) = refs[:-4], refs[-4:]
    sub = lax.axis_index("sub")
    total = slopes[0][...]
    for other in slopes[1:]:
        total = total + other[...]
    scaled[...] = total * chain_factor[...]
    window = same.shape[0]
    shift = scaled.shape[0] - window
    same[...] = scaled[pl.ds(pl.multiple_of(sub * shift, 8), window), :]
    cross[...] = scaled[pl.ds(pl.multiple_of((1 - sub) * shift, 8), window), :]


def gradient_kernel(scaled, outer, far, partner, gradient, planes, sums):
    sub = lax.axis_index("sub")
    window = partner.shape[0]
    shift = scaled.shape[0] - window
    mine = scaled[pl.ds(pl.multiple_of(sub * shift, 8), window), :]

    @pl.when(sub == 0)
    def _():
        planes[0] = outer[...]
        planes[1] = mine
        planes[2] = partner[...]
        planes[3] = far[...]

    @pl.when(sub == 1)
    def _():
        planes[0] = far[...]
        planes[1] = partner[...]
        planes[2] = mine
        planes[3] = outer[...]

    half = gradient.shape[1]
    part = pl.ds(pl.multiple_of(sub * (window - half), 8), half)
    for layer in range(2):
        sums[...] = filter_planes(planes[layer], planes[layer + 1], planes[layer + 2])
        gradient[layer] = sums[part, :]


def call(body, outs, scratch=(), name=None, work=False):
    cost = pl.CostEstimate(flops=10**7, bytes_accessed=4 * 10**6, transcendentals=0)
    return pl.pallas_call(
        body,
        out_shape=[jax.ShapeDtypeStruct(shape, jnp.float32) for shape in outs],
        scratch_shapes=[pltpu.VMEM(shape, jnp.float32) for shape in scratch],
        compiler_params=pltpu.CompilerParams(vmem_limit_bytes=16 * 2**20),
        cost_estimate=cost if work else None,
        name=name,
    )


def routes(mods, slabs):
    chips = mods * slabs

    def at(chip, sub):
        return 2 * chip + sub

    def beside(chip, steps, cyclic):
        target = chip + steps
        if cyclic:
            return target % chips
        return target if 0 <= target < chips else None

    def built(moves, cyclic):
        pairs = []
        for chip in range(chips):
            for sub, steps, to in moves:
                target = beside(chip, steps, cyclic)
                if target is not None:
                    pairs.append((at(chip, sub), at(target, to)))
        return pairs

    def in_module(moves):
        pairs = []
        for chip in range(chips):
            mod, slab = divmod(chip, slabs)
            for sub, steps, to in moves:
                pairs.append((at(chip, sub), at(mod * slabs + (slab + steps) % slabs, to)))
        return pairs

    return dict(
        swap=built([(0, 0, 1), (1, 0, 0)], True),
        first=built([(0, 1, 0), (1, -1, 1)], True),
        second=built([(1, 1, 0), (0, -1, 1)], True),
        third=built([(0, 1, 1), (1, 1, 0)], True),
        fourth=built([(0, 1, 0), (1, 1, 1)], True),
        outer=built([(1, 1, 0), (0, -1, 1)], False),
        down=built([(1, 0, 0), (0, -1, 1)], False),
        halo_cross=in_module([(1, 1, 0), (0, -1, 1)]),
        halo_same=in_module([(0, -1, 0), (1, 1, 1)]),
    )


def module_routes(mods):
    if mods & (mods - 1) == 0:
        return [[(m, m ^ s) for m in range(mods)] for s in range(1, mods)]
    return [[(m, (m + s) % mods) for m in range(mods)] for s in range(1, mods)]


def local(mods, slabs, design, fixed, load):
    half, width = design.shape[1:]
    count = 2 * half
    path = routes(mods, slabs)

    def move(value, name):
        return lax.ppermute(value, AXES, path[name])

    plane = (count, width)
    layer = (3, count, width)
    block = (half, width)
    free = (1 - fixed).astype(jnp.float32)
    right = free * load.astype(jnp.float32)
    swap, first, second, third, fourth, own = call(
        prepare_kernel,
        [(11,) + block, (4,) + block, (4,) + block, block, block, (11,) + block],
        name="prepare",
    )(free, right, design)
    first = move(first, "first")
    second = move(second, "second")
    third = move(third, "third")
    fourth = move(fourth, "fourth")
    swap = move(swap, "swap")

    def start_body(*refs):
        start_outer_kernel(mods, slabs, *refs)

    v0, v0_inner, free, fields, layers = call(
        start_inner_kernel,
        [layer, layer, layer, (12,) + plane, (2,) + plane],
        name="start_inner",
        work=True,
    )(own, swap)
    v1, v0_high, mod_inner, mod_outer, mod_own, slope_factor, chain_factor, moments = call(
        start_body,
        [layer, layer, plane, plane, plane, plane, plane, (8, width)],
        [layer, plane, plane],
        name="start_outer",
    )(v0, v0_inner, free, fields, layers, first, second, third, fourth)
    outer = move(v1, "outer")
    inner = move(v1, "swap")
    (fields,) = call(second_inner_kernel, [(12,) + plane], name="second_inner", work=True)(v1, inner)
    v2, v1_high, moments = call(
        second_outer_kernel, [layer, layer, (8, width)], name="second_outer"
    )(v1, inner, outer, fields, free, mod_inner, mod_outer, moments)
    v2_high = move(v2, "down")
    (moments,) = call(third_kernel, [(8, width)], name="third")(v2, v2_high, mod_own, moments)
    devices = 2 * mods * slabs
    gathered = lax.all_to_all(
        jnp.broadcast_to(moments, (devices, 8, width)), AXES, 0, 0, tiled=True
    )
    slope, keep, send = call(
        combine_kernel, [plane, (3, half, width), (3, half, width)], [layer, layer], name="combine"
    )(gathered, v0, v0_high, v1, v1_high, v2, v2_high, slope_factor)
    slopes = [slope] + [lax.ppermute(slope, "mod", pairs) for pairs in module_routes(mods)]
    received = move(send, "swap")
    window = half + 8
    scaled, same, cross = call(
        scale_kernel, [plane, (window, width), (window, width)], name="scale"
    )(*slopes, chain_factor)
    outer = move(cross, "halo_cross")
    far = move(same, "halo_same")
    partner = move(cross, "swap")
    even = lax.axis_index("sub") == 0
    displacement = jnp.stack(
        [jnp.where(even, keep, received), jnp.where(even, received, keep)], axis=1
    )
    (gradient,) = call(
        gradient_kernel, [(2, half, width)], [(4, window, width), (window, width)], name="gradient"
    )(scaled, outer, far, partner)
    return displacement, gradient


def solution(mesh):
    mods, slabs = mesh.shape["mod"], mesh.shape["slab"]
    assert mesh.shape["sub"] == 2
    deck = P(None, ("mod", "slab"), "sub", None)

    def body(design, fixed_mask, load_mask):
        return local(mods, slabs, design, fixed_mask, load_mask)

    return jax.shard_map(
        body,
        mesh=mesh,
        in_specs=(P("slab", "sub", None), deck, deck),
        out_specs=(deck, P("slab", "sub", None)),
        check_vma=False,
    )
```

```python
import math

import jax
import jax.numpy as jnp
import numpy as np
from jax import lax
from jax.experimental import pallas as pl
from jax.experimental.pallas import tpu as pltpu
from jax.sharding import PartitionSpec as P

stiff_floor = 0.01
penalty = 3.0
sharpness = 4.0
threshold = 0.5
filter_reach = 1.8

AXES = ("mod", "slab", "sub")
ROWS = 8
FACE = filter_reach - 1.0
EDGE = filter_reach - math.sqrt(2.0)
CORNER = filter_reach - math.sqrt(3.0)
LOWER = math.tanh(sharpness * threshold)
UPPER = math.tanh(sharpness * (1.0 - threshold))


def stiffness_modes():
    poisson = 0.3
    lame = poisson / ((1.0 + poisson) * (1.0 - 2.0 * poisson))
    shear = 1.0 / (2.0 * (1.0 + poisson))
    elastic = np.zeros((6, 6))
    elastic[:3, :3] = lame
    for axis in range(3):
        elastic[axis, axis] += 2.0 * shear
        elastic[axis + 3, axis + 3] = shear
    offset = 0.5 / math.sqrt(3.0)
    points = [0.5 - offset, 0.5 + offset]
    stiffness = np.zeros((24, 24))
    for point in ((a, b, c) for a in points for b in points for c in points):
        strain = np.zeros((6, 24))
        for corner in range(8):
            bits = (corner >> 2 & 1, corner >> 1 & 1, corner & 1)
            along = [point[a] if bits[a] else 1.0 - point[a] for a in range(3)]
            sign = [1.0 if bits[a] else -1.0 for a in range(3)]
            gx = sign[0] * along[1] * along[2]
            gy = along[0] * sign[1] * along[2]
            gz = along[0] * along[1] * sign[2]
            col = 3 * corner
            strain[0, col] = gx
            strain[1, col + 1] = gy
            strain[2, col + 2] = gz
            strain[3, col], strain[3, col + 1] = gy, gx
            strain[4, col + 1], strain[4, col + 2] = gz, gy
            strain[5, col], strain[5, col + 2] = gz, gx
        stiffness += strain.T @ elastic @ strain / 8.0
    basis = np.zeros((24, 24))
    for mode in range(8):
        for corner in range(8):
            value = 1.0
            for bit in range(3):
                if mode >> bit & 1 and not corner >> bit & 1:
                    value = -value
            for k in range(3):
                basis[3 * mode + k, 3 * corner + k] = value
    table = basis @ stiffness @ basis.T / 64.0
    table[np.abs(table) < 1e-9] = 0.0
    return table


TABLE = stiffness_modes()


def lanes(shape):
    return lax.broadcasted_iota(jnp.int32, shape, 1)


def rows(shape):
    return lax.broadcasted_iota(jnp.int32, shape, 0)


def z_up(x):
    return jnp.where(lanes(x.shape) < x.shape[1] - 1, pltpu.roll(x, x.shape[1] - 1, 1), 0.0)


def z_down(x):
    return jnp.where(lanes(x.shape) > 0, pltpu.roll(x, 1, 1), 0.0)


def y_up(x):
    return jnp.where(rows(x.shape) < x.shape[0] - 1, pltpu.roll(x, x.shape[0] - 1, 0), 0.0)


def y_down(x):
    return jnp.where(rows(x.shape) > 0, pltpu.roll(x, 1, 0), 0.0)


def two_rows(read, y0, count):
    here = read(y0)
    above = y_up(here) if y0 + ROWS == count else read(y0 + 1)
    return here, above


def face_modes(here, above):
    out = []
    for part in (here + above, above - here):
        shifted = z_up(part)
        out += [part + shifted, shifted - part]
    return out


def element_modes(own, other, side):
    sums = [[other[k][m] + own[k][m] for m in range(4)] for k in range(3)]
    diffs = [[(other[k][m] - own[k][m]) * side for m in range(4)] for k in range(3)]
    return [sums[k] + diffs[k] for k in range(3)]


def mode_forces(q):
    made = {}

    def scaled(j, value):
        key = (j, round(value, 12))
        if key not in made:
            made[key] = q[j % 3][j // 3] * np.float32(value)
        return made[key]

    out = [[None] * 8 for _ in range(3)]
    for i in range(24):
        total = None
        for j in np.nonzero(TABLE[i])[0]:
            term = scaled(int(j), float(TABLE[i, j]))
            total = term if total is None else total + term
        out[i % 3][i // 3] = total
    return out


def element_energy(q):
    r = mode_forces(q)
    total = None
    for k in range(3):
        for m in range(1, 8):
            term = q[k][m] * r[k][m]
            total = term if total is None else total + term
    return total


def own_fields(own, other, side):
    r = mode_forces(element_modes(own, other, side))
    fields = []
    for k in range(3):
        for m in range(4):
            d = r[k][m + 4] * side
            fields.append(-d if r[k][m] is None else r[k][m] - d)
    return fields


def layer_modes(read, y0, count):
    heres, modes = [], []
    for k in range(3):
        here, above = two_rows(lambda y, k=k: read(k, y), y0, count)
        heres.append(here)
        modes.append(face_modes(here, above))
    return heres, modes


def fields_loop(count, read_own, read_other, side, fields):
    for y0 in range(0, count, ROWS):
        _, own = layer_modes(read_own, y0, count)
        _, other = layer_modes(read_other, y0, count)
        for n, value in enumerate(own_fields(own, other, side)):
            fields[n, pl.ds(y0, ROWS), :] = value


def operator_loop(count, read_own, read_other, side, fields, mod_inner, mod_outer, free, out_ref):
    shape = (ROWS, out_ref.shape[2])
    square = jnp.zeros(shape, jnp.float32)
    cross = jnp.zeros(shape, jnp.float32)
    norm = jnp.zeros(shape, jnp.float32)
    carry = [jnp.zeros(shape, jnp.float32)] * 3
    first = rows(shape) == 0
    for y0 in range(0, count, ROWS):
        part = pl.ds(y0, ROWS)
        owns, own = layer_modes(read_own, y0, count)
        _, other = layer_modes(read_other, y0, count)
        inner, outer = mod_inner[part, :], mod_outer[part, :]
        total = [
            outer * value + inner * fields[n, part, :]
            for n, value in enumerate(own_fields(own, other, side))
        ]
        for k in range(3):
            faces = []
            for py in range(2):
                s, d = total[4 * k + 2 * py], total[4 * k + 2 * py + 1]
                faces.append((s - d) + z_down(s + d))
            rolled = pltpu.roll(faces[0] + faces[1], 1, 0)
            force = (faces[0] - faces[1]) + jnp.where(first, carry[k], rolled)
            carry[k] = rolled
            image = free[k, part, :] * force
            out_ref[k, part, :] = image
            square += image * image
            cross += owns[k] * image
            norm += owns[k] * owns[k]
    return norm, cross, square


def energy_loop(count, read_own, read_high, use):
    for y0 in range(0, count, ROWS):
        _, own = layer_modes(read_own, y0, count)
        _, high = layer_modes(read_high, y0, count)
        use(y0, element_energy(element_modes(own, high, 1.0)))


def rows_of(ref):
    return lambda k, y: ref[k, pl.ds(y, ROWS), :]


def inner_side(sub):
    return jnp.where(sub == 0, 1.0, -1.0).astype(jnp.float32)


def line(tile):
    return jnp.sum(tile, axis=0, keepdims=True)


def prepare_kernel(free, load, design, swap, first, second, third, fourth, own):
    sub = lax.axis_index("sub")
    for k in range(3):
        frees = [free[k, layer] for layer in range(2)]
        values = [frees[layer] * load[k, layer].astype(jnp.float32) for layer in range(2)]
        for layer in range(2):
            swap[2 * k + layer] = values[layer]
            own[2 * k + layer] = values[layer]
        low = sub == 0
        swap[6 + k] = jnp.where(low, frees[1], frees[0])
        own[6 + k] = jnp.where(low, frees[0], frees[1])
        first[k] = jnp.where(low, values[1], values[0])
        second[k] = jnp.where(low, values[0], values[1])
    low = sub == 0
    for layer in range(2):
        swap[9 + layer] = design[layer]
        own[9 + layer] = design[layer]
    later = jnp.where(low, design[1], design[0])
    sooner = jnp.where(low, design[0], design[1])
    first[3] = later
    third[...] = later
    second[3] = sooner
    fourth[...] = sooner


def around(p):
    across = y_up(p) + y_down(p)
    return across + z_up(p) + z_down(p), z_up(across) + z_down(across)


def filter_mid(p):
    face, diag = around(p)
    return filter_reach * p + FACE * face + EDGE * diag


def filter_side(p):
    face, diag = around(p)
    return FACE * p + EDGE * face + CORNER * diag


def filter_planes(low, mid, high):
    return filter_side(low + high) + filter_mid(mid)


def weight_plane(shape, row_offset, count):
    row = rows(shape) + row_offset
    lane = lanes(shape)

    def neighbours(index, size):
        return jnp.where(index > 0, 1.0, 0.0) + jnp.where(index < size - 1, 1.0, 0.0)

    ry = neighbours(row, count)
    rz = neighbours(lane, shape[1])
    face, diag = ry + rz, ry * rz
    return (
        filter_reach
        + FACE * (2.0 + face)
        + EDGE * (2.0 * face + diag)
        + (2.0 * CORNER) * diag
    )


def start_inner_kernel(own, swap, v0, v0_inner, free, fields, parts, layers):
    sub = lax.axis_index("sub")
    half = own.shape[1]
    count = 2 * half
    mine = pl.ds(pl.multiple_of(sub * half, half), half)
    other = pl.ds(pl.multiple_of((1 - sub) * half, half), half)
    for layer in range(2):
        layers[layer, mine, :] = own[9 + layer]
        layers[layer, other, :] = swap[9 + layer]

    @pl.when(sub == 0)
    def _():
        parts[0] = filter_side(layers[0])
        parts[1] = filter_mid(layers[0]) + filter_side(layers[1])

    @pl.when(sub == 1)
    def _():
        parts[0] = filter_mid(layers[0]) + filter_side(layers[1])
        parts[1] = filter_side(layers[0]) + filter_mid(layers[1])

    parts[2] = 1.0 / weight_plane((count, own.shape[2]), 0, count)
    for k in range(3):
        free[k, mine, :] = own[6 + k]
        free[k, other, :] = swap[6 + k]
        v0[k, mine, :] = own[2 * k + sub]
        v0[k, other, :] = swap[2 * k + sub]
        v0_inner[k, mine, :] = own[2 * k + 1 - sub]
        v0_inner[k, other, :] = swap[2 * k + 1 - sub]
    fields_loop(count, rows_of(v0), rows_of(v0_inner), inner_side(sub), fields)


def start_outer_kernel(
    mods, slabs,
    first, second, third, fourth, v0, v0_inner, free, fields, parts,
    v1, v0_high, mod_inner, mod_outer, mod_own, slope_factor, chain_factor, moments,
    v0_outer, near, deep,
):
    mod, slab, sub = (lax.axis_index(a) for a in AXES)
    half = third.shape[0]
    count = 2 * half
    even = sub == 0
    mine = pl.ds(pl.multiple_of(sub * half, half), half)
    other = pl.ds(pl.multiple_of((1 - sub) * half, half), half)
    near[mine, :] = first[3]
    near[other, :] = second[3]
    deep[mine, :] = fourth[...]
    deep[other, :] = third[...]
    starts = (mod == 0) & (slab == 0) & even
    ends = (mod == mods - 1) & (slab == slabs - 1) & (sub == 1)
    inside = jnp.where(ends, 0.0, 1.0)
    for k in range(3):
        v0_outer[k, mine, :] = first[k] * inside
        v0_outer[k, other, :] = second[k] * inside
        v0_high[k] = jnp.where(even, v0_inner[k], v0_outer[k])

    side = filter_side(near[...])
    mid = filter_mid(near[...])
    inverse = parts[2]
    filtered = (parts[0] + filter_side(deep[...]) + jnp.where(even, mid, 0.0)) * inverse
    hyper = jnp.tanh(sharpness * (filtered - threshold))
    projected = (LOWER + hyper) * (1.0 / (LOWER + UPPER))
    below = stiff_floor + (1.0 - stiff_floor) * projected * projected * projected
    below = below * jnp.where(starts, 0.0, 1.0)
    filtered = (parts[1] + side) * inverse
    hyper = jnp.tanh(sharpness * (filtered - threshold))
    projected = (LOWER + hyper) * (1.0 / (LOWER + UPPER))
    squared = projected * projected
    stiff = stiff_floor + (1.0 - stiff_floor) * squared * projected
    mod_own[...] = stiff
    mod_inner[...] = jnp.where(even, stiff, below)
    mod_outer[...] = jnp.where(even, below, stiff)
    slope_factor[...] = (-penalty * (1.0 - stiff_floor)) * squared
    chain_factor[...] = (sharpness / (LOWER + UPPER)) * (1.0 - hyper * hyper) * inverse

    norm, cross, square = operator_loop(
        count, rows_of(v0), rows_of(v0_outer), -inner_side(sub), fields, mod_inner, mod_outer, free, v1
    )
    moments[...] = jnp.concatenate(
        [line(norm), line(cross), line(square), jnp.zeros((5, norm.shape[1]), jnp.float32)], axis=0
    )


def second_inner_kernel(v1, inner, fields):
    fields_loop(v1.shape[1], rows_of(v1), rows_of(inner), inner_side(lax.axis_index("sub")), fields)


def second_outer_kernel(
    v1, outer, inner, fields, free, mod_inner, mod_outer, before, v2, v1_high, moments
):
    sub = lax.axis_index("sub")
    count = v1.shape[1]
    for k in range(3):
        v1_high[k] = jnp.where(sub == 0, inner[k], outer[k])
    _, cross, square = operator_loop(
        count, rows_of(v1), rows_of(outer), -inner_side(sub), fields, mod_inner, mod_outer, free, v2
    )
    zero = jnp.zeros((3, cross.shape[1]), jnp.float32)
    moments[...] = before[...] + jnp.concatenate(
        [zero, line(cross), line(square), zero], axis=0
    )


def third_kernel(v2, v2_high, mod_own, before, moments):
    count = v2.shape[1]
    total = [jnp.zeros((ROWS, v2.shape[2]), jnp.float32)]

    def use(y0, energy):
        total[0] += energy * mod_own[pl.ds(y0, ROWS), :]

    energy_loop(
        count,
        lambda k, y: v2[k, pl.ds(y, ROWS), :],
        lambda k, y: v2_high[k, pl.ds(y, ROWS), :],
        use,
    )
    width = v2.shape[2]
    moments[...] = before[...] + jnp.concatenate(
        [
            jnp.zeros((5, width), jnp.float32),
            line(total[0]),
            jnp.zeros((2, width), jnp.float32),
        ],
        axis=0,
    )


def coefficients(m):
    step = m[0] / m[1]
    x0 = step
    r1 = -step
    norm = m[0] + 2.0 * r1 * m[1] + r1 * r1 * m[2]
    ratio = norm / m[0]
    p0, p1 = 1.0 + ratio, r1
    step = norm / (p0 * p0 * m[1] + 2.0 * p0 * p1 * m[2] + p1 * p1 * m[3])
    x0, x1 = x0 + step * p0, step * p1
    r1, r2 = r1 - step * p0, -step * p1
    after = (
        m[0]
        + 2.0 * r1 * m[1]
        + (r1 * r1 + 2.0 * r2) * m[2]
        + 2.0 * r1 * r2 * m[3]
        + r2 * r2 * m[4]
    )
    ratio = after / norm
    p0, p1, p2 = 1.0 + ratio * p0, r1 + ratio * p1, r2
    step = after / (
        p0 * p0 * m[1]
        + 2.0 * p0 * p1 * m[2]
        + (p1 * p1 + 2.0 * p0 * p2) * m[3]
        + 2.0 * p1 * p2 * m[4]
        + p2 * p2 * m[5]
    )
    return x0 + step * p0, x1 + step * p1, step * p2


def combine_kernel(
    gathered, v0, v0_high, v1, v1_high, v2, v2_high, slope_factor,
    slope, keep, send,
    own, high,
):
    sub = lax.axis_index("sub")
    count = v0.shape[1]
    half = count // 2
    sums = jnp.sum(jnp.sum(gathered[...], axis=0), axis=1, keepdims=True)
    c0, c1, c2 = coefficients([sums[k : k + 1] for k in range(6)])
    for k in range(3):
        own[k] = c0 * v0[k] + c1 * v1[k] + c2 * v2[k]
        high[k] = c0 * v0_high[k] + c1 * v1_high[k] + c2 * v2_high[k]

    mine = pl.ds(pl.multiple_of(sub * half, half), half)
    other = pl.ds(pl.multiple_of((1 - sub) * half, half), half)
    for k in range(3):
        keep[k] = own[k, mine, :]
        send[k] = own[k, other, :]

    def use(y0, energy):
        slope[pl.ds(y0, ROWS), :] = slope_factor[pl.ds(y0, ROWS), :] * energy

    energy_loop(
        count,
        lambda k, y: own[k, pl.ds(y, ROWS), :],
        lambda k, y: high[k, pl.ds(y, ROWS), :],
        use,
    )


def scale_kernel(*refs):
    slopes, (chain_factor, scaled, same, cross) = refs[:-4], refs[-4:]
    sub = lax.axis_index("sub")
    total = slopes[0][...]
    for other in slopes[1:]:
        total = total + other[...]
    scaled[...] = total * chain_factor[...]
    window = same.shape[0]
    shift = scaled.shape[0] - window
    same[...] = scaled[pl.ds(pl.multiple_of(sub * shift, 8), window), :]
    cross[...] = scaled[pl.ds(pl.multiple_of((1 - sub) * shift, 8), window), :]


def gradient_kernel(scaled, outer, far, partner, gradient, planes, sums):
    sub = lax.axis_index("sub")
    window = partner.shape[0]
    shift = scaled.shape[0] - window
    mine = scaled[pl.ds(pl.multiple_of(sub * shift, 8), window), :]

    @pl.when(sub == 0)
    def _():
        planes[0] = outer[...]
        planes[1] = mine
        planes[2] = partner[...]
        planes[3] = far[...]

    @pl.when(sub == 1)
    def _():
        planes[0] = far[...]
        planes[1] = partner[...]
        planes[2] = mine
        planes[3] = outer[...]

    half = gradient.shape[1]
    part = pl.ds(pl.multiple_of(sub * (window - half), 8), half)
    for layer in range(2):
        sums[...] = filter_planes(planes[layer], planes[layer + 1], planes[layer + 2])
        gradient[layer] = sums[part, :]


def call(body, outs, scratch=(), name=None, work=False):
    cost = pl.CostEstimate(flops=10**7, bytes_accessed=4 * 10**6, transcendentals=0)
    return pl.pallas_call(
        body,
        out_shape=[jax.ShapeDtypeStruct(shape, jnp.float32) for shape in outs],
        scratch_shapes=[pltpu.VMEM(shape, jnp.float32) for shape in scratch],
        compiler_params=pltpu.CompilerParams(vmem_limit_bytes=16 * 2**20),
        cost_estimate=cost if work else None,
        name=name,
    )


def routes(mods, slabs):
    chips = mods * slabs

    def at(chip, sub):
        return 2 * chip + sub

    def beside(chip, steps, cyclic):
        target = chip + steps
        if cyclic:
            return target % chips
        return target if 0 <= target < chips else None

    def built(moves, cyclic):
        pairs = []
        for chip in range(chips):
            for sub, steps, to in moves:
                target = beside(chip, steps, cyclic)
                if target is not None:
                    pairs.append((at(chip, sub), at(target, to)))
        return pairs

    def in_module(moves):
        pairs = []
        for chip in range(chips):
            mod, slab = divmod(chip, slabs)
            for sub, steps, to in moves:
                pairs.append((at(chip, sub), at(mod * slabs + (slab + steps) % slabs, to)))
        return pairs

    return dict(
        swap=built([(0, 0, 1), (1, 0, 0)], True),
        first=built([(0, 1, 0), (1, -1, 1)], True),
        second=built([(1, 1, 0), (0, -1, 1)], True),
        third=built([(0, 1, 1), (1, 1, 0)], True),
        fourth=built([(0, 1, 0), (1, 1, 1)], True),
        outer=built([(1, 1, 0), (0, -1, 1)], False),
        down=built([(1, 0, 0), (0, -1, 1)], False),
        halo_cross=in_module([(1, 1, 0), (0, -1, 1)]),
        halo_same=in_module([(0, -1, 0), (1, 1, 1)]),
    )


def module_routes(mods):
    if mods & (mods - 1) == 0:
        return [[(m, m ^ s) for m in range(mods)] for s in range(1, mods)]
    return [[(m, (m + s) % mods) for m in range(mods)] for s in range(1, mods)]


def local(mods, slabs, design, fixed, load):
    half, width = design.shape[1:]
    count = 2 * half
    path = routes(mods, slabs)

    def move(value, name):
        return lax.ppermute(value, AXES, path[name])

    plane = (count, width)
    layer = (3, count, width)
    block = (half, width)
    free = (1 - fixed).astype(jnp.float32)
    swap, first, second, third, fourth, own = call(
        prepare_kernel,
        [(11,) + block, (4,) + block, (4,) + block, block, block, (11,) + block],
        name="prepare",
    )(free, load, design)
    first = move(first, "first")
    second = move(second, "second")
    third = move(third, "third")
    fourth = move(fourth, "fourth")
    swap = move(swap, "swap")

    def start_body(*refs):
        start_outer_kernel(mods, slabs, *refs)

    v0, v0_inner, free, fields, parts = call(
        start_inner_kernel,
        [layer, layer, layer, (12,) + plane, (3,) + plane],
        [(2,) + plane],
        name="start_inner",
        work=True,
    )(own, swap)
    v1, v0_high, mod_inner, mod_outer, mod_own, slope_factor, chain_factor, moments = call(
        start_body,
        [layer, layer, plane, plane, plane, plane, plane, (8, width)],
        [layer, plane, plane],
        name="start_outer",
    )(first, second, third, fourth, v0, v0_inner, free, fields, parts)
    outer = move(v1, "outer")
    inner = move(v1, "swap")
    (fields,) = call(second_inner_kernel, [(12,) + plane], name="second_inner", work=True)(v1, inner)
    v2, v1_high, moments = call(
        second_outer_kernel, [layer, layer, (8, width)], name="second_outer"
    )(v1, outer, inner, fields, free, mod_inner, mod_outer, moments)
    v2_high = move(v2, "down")
    (moments,) = call(third_kernel, [(8, width)], name="third")(v2, v2_high, mod_own, moments)
    devices = 2 * mods * slabs
    gathered = lax.all_to_all(
        jnp.broadcast_to(moments, (devices, 8, width)), AXES, 0, 0, tiled=True
    )
    slope, keep, send = call(
        combine_kernel, [plane, (3, half, width), (3, half, width)], [layer, layer], name="combine"
    )(gathered, v0, v0_high, v1, v1_high, v2, v2_high, slope_factor)
    slopes = [slope] + [lax.ppermute(slope, "mod", pairs) for pairs in module_routes(mods)]
    received = move(send, "swap")
    window = half + 8
    scaled, same, cross = call(
        scale_kernel, [plane, (window, width), (window, width)], name="scale"
    )(*slopes, chain_factor)
    outer = move(cross, "halo_cross")
    far = move(same, "halo_same")
    partner = move(cross, "swap")
    even = lax.axis_index("sub") == 0
    displacement = jnp.stack(
        [jnp.where(even, keep, received), jnp.where(even, received, keep)], axis=1
    )
    (gradient,) = call(
        gradient_kernel, [(2, half, width)], [(4, window, width), (window, width)], name="gradient"
    )(scaled, outer, far, partner)
    return displacement, gradient


def solution(mesh):
    mods, slabs = mesh.shape["mod"], mesh.shape["slab"]
    assert mesh.shape["sub"] == 2
    deck = P(None, ("mod", "slab"), "sub", None)

    def body(design, fixed_mask, load_mask):
        return local(mods, slabs, design, fixed_mask, load_mask)

    return jax.shard_map(
        body,
        mesh=mesh,
        in_specs=(P("slab", "sub", None), deck, deck),
        out_specs=(deck, P("slab", "sub", None)),
        check_vma=False,
    )
```

```python
import math

import jax
import jax.numpy as jnp
import numpy as np
from jax import lax
from jax.experimental import pallas as pl
from jax.experimental.pallas import tpu as pltpu
from jax.sharding import PartitionSpec as P

stiff_floor = 0.01
penalty = 3.0
sharpness = 4.0
threshold = 0.5
filter_reach = 1.8

AXES = ("mod", "slab", "sub")
ROWS = 8
FACE = filter_reach - 1.0
EDGE = filter_reach - math.sqrt(2.0)
CORNER = filter_reach - math.sqrt(3.0)
LOWER = math.tanh(sharpness * threshold)
UPPER = math.tanh(sharpness * (1.0 - threshold))


def stiffness_modes():
    poisson = 0.3
    lame = poisson / ((1.0 + poisson) * (1.0 - 2.0 * poisson))
    shear = 1.0 / (2.0 * (1.0 + poisson))
    elastic = np.zeros((6, 6))
    elastic[:3, :3] = lame
    for axis in range(3):
        elastic[axis, axis] += 2.0 * shear
        elastic[axis + 3, axis + 3] = shear
    offset = 0.5 / math.sqrt(3.0)
    points = [0.5 - offset, 0.5 + offset]
    stiffness = np.zeros((24, 24))
    for point in ((a, b, c) for a in points for b in points for c in points):
        strain = np.zeros((6, 24))
        for corner in range(8):
            bits = (corner >> 2 & 1, corner >> 1 & 1, corner & 1)
            along = [point[a] if bits[a] else 1.0 - point[a] for a in range(3)]
            sign = [1.0 if bits[a] else -1.0 for a in range(3)]
            gx = sign[0] * along[1] * along[2]
            gy = along[0] * sign[1] * along[2]
            gz = along[0] * along[1] * sign[2]
            col = 3 * corner
            strain[0, col] = gx
            strain[1, col + 1] = gy
            strain[2, col + 2] = gz
            strain[3, col], strain[3, col + 1] = gy, gx
            strain[4, col + 1], strain[4, col + 2] = gz, gy
            strain[5, col], strain[5, col + 2] = gz, gx
        stiffness += strain.T @ elastic @ strain / 8.0
    basis = np.zeros((24, 24))
    for mode in range(8):
        for corner in range(8):
            value = 1.0
            for bit in range(3):
                if mode >> bit & 1 and not corner >> bit & 1:
                    value = -value
            for k in range(3):
                basis[3 * mode + k, 3 * corner + k] = value
    table = basis @ stiffness @ basis.T / 64.0
    table[np.abs(table) < 1e-9] = 0.0
    return table


TABLE = stiffness_modes()


def lanes(shape):
    return lax.broadcasted_iota(jnp.int32, shape, 1)


def rows(shape):
    return lax.broadcasted_iota(jnp.int32, shape, 0)


def z_up(x):
    return jnp.where(lanes(x.shape) < x.shape[1] - 1, pltpu.roll(x, x.shape[1] - 1, 1), 0.0)


def z_down(x):
    return jnp.where(lanes(x.shape) > 0, pltpu.roll(x, 1, 1), 0.0)


def y_up(x):
    return jnp.where(rows(x.shape) < x.shape[0] - 1, pltpu.roll(x, x.shape[0] - 1, 0), 0.0)


def y_down(x):
    return jnp.where(rows(x.shape) > 0, pltpu.roll(x, 1, 0), 0.0)


def two_rows(read, y0, count):
    here = read(y0)
    above = y_up(here) if y0 + ROWS == count else read(y0 + 1)
    return here, above


def face_modes(here, above):
    out = []
    for part in (here + above, above - here):
        shifted = z_up(part)
        out += [part + shifted, shifted - part]
    return out


def element_modes(own, other, side):
    sums = [[other[k][m] + own[k][m] for m in range(4)] for k in range(3)]
    diffs = [[(other[k][m] - own[k][m]) * side for m in range(4)] for k in range(3)]
    return [sums[k] + diffs[k] for k in range(3)]


def mode_forces(q):
    made = {}

    def scaled(j, value):
        key = (j, round(value, 12))
        if key not in made:
            made[key] = q[j % 3][j // 3] * np.float32(value)
        return made[key]

    out = [[None] * 8 for _ in range(3)]
    for i in range(24):
        total = None
        for j in np.nonzero(TABLE[i])[0]:
            term = scaled(int(j), float(TABLE[i, j]))
            total = term if total is None else total + term
        out[i % 3][i // 3] = total
    return out


def paired(q, r):
    total = None
    for k in range(3):
        for m in range(1, 8):
            term = q[k][m] * r[k][m]
            total = term if total is None else total + term
    return total


def own_fields(own, other, side):
    r = mode_forces(element_modes(own, other, side))
    fields = []
    for k in range(3):
        for m in range(4):
            d = r[k][m + 4] * side
            fields.append(-d if r[k][m] is None else r[k][m] - d)
    return fields


def layer_modes(read, y0, count):
    heres, modes = [], []
    for k in range(3):
        here, above = two_rows(lambda y, k=k: read(k, y), y0, count)
        heres.append(here)
        modes.append(face_modes(here, above))
    return heres, modes


def fields_loop(count, read_own, read_other, side, fields):
    for y0 in range(0, count, ROWS):
        _, own = layer_modes(read_own, y0, count)
        _, other = layer_modes(read_other, y0, count)
        for n, value in enumerate(own_fields(own, other, side)):
            fields[n, pl.ds(y0, ROWS), :] = value


def operator_loop(count, read_own, read_other, side, fields, mod_inner, mod_outer, free, out_ref):
    shape = (ROWS, out_ref.shape[2])
    square = jnp.zeros(shape, jnp.float32)
    cross = jnp.zeros(shape, jnp.float32)
    norm = jnp.zeros(shape, jnp.float32)
    carry = [jnp.zeros(shape, jnp.float32)] * 3
    first = rows(shape) == 0
    for y0 in range(0, count, ROWS):
        part = pl.ds(y0, ROWS)
        owns, own = layer_modes(read_own, y0, count)
        _, other = layer_modes(read_other, y0, count)
        inner, outer = mod_inner[part, :], mod_outer[part, :]
        total = [
            outer * value + inner * fields[n, part, :]
            for n, value in enumerate(own_fields(own, other, side))
        ]
        for k in range(3):
            faces = []
            for py in range(2):
                s, d = total[4 * k + 2 * py], total[4 * k + 2 * py + 1]
                faces.append((s - d) + z_down(s + d))
            rolled = pltpu.roll(faces[0] + faces[1], 1, 0)
            force = (faces[0] - faces[1]) + jnp.where(first, carry[k], rolled)
            carry[k] = rolled
            image = free[k, part, :] * force
            out_ref[k, part, :] = image
            square += image * image
            cross += owns[k] * image
            norm += owns[k] * owns[k]
    return norm, cross, square


def element_rows(own, high, y0, count):
    _, low = layer_modes(rows_of(own), y0, count)
    _, top = layer_modes(rows_of(high), y0, count)
    return element_modes(low, top, 1.0)


def rows_of(ref):
    return lambda k, y: ref[k, pl.ds(y, ROWS), :]


def inner_side(sub):
    return jnp.where(sub == 0, 1.0, -1.0).astype(jnp.float32)


def line(tile):
    return jnp.sum(tile, axis=0, keepdims=True)


def prepare_kernel(free, load, design, swap, first, second, third, fourth, own):
    sub = lax.axis_index("sub")
    for k in range(3):
        frees = [free[k, layer] for layer in range(2)]
        values = [frees[layer] * load[k, layer].astype(jnp.float32) for layer in range(2)]
        for layer in range(2):
            swap[2 * k + layer] = values[layer]
            own[2 * k + layer] = values[layer]
        low = sub == 0
        swap[6 + k] = jnp.where(low, frees[1], frees[0])
        own[6 + k] = jnp.where(low, frees[0], frees[1])
        first[k] = jnp.where(low, values[1], values[0])
        second[k] = jnp.where(low, values[0], values[1])
    low = sub == 0
    for layer in range(2):
        swap[9 + layer] = design[layer]
        own[9 + layer] = design[layer]
    later = jnp.where(low, design[1], design[0])
    sooner = jnp.where(low, design[0], design[1])
    first[3] = later
    third[...] = later
    second[3] = sooner
    fourth[...] = sooner


def around(p):
    across = y_up(p) + y_down(p)
    return across + z_up(p) + z_down(p), z_up(across) + z_down(across)


def filter_mid(p):
    face, diag = around(p)
    return filter_reach * p + FACE * face + EDGE * diag


def filter_side(p):
    face, diag = around(p)
    return FACE * p + EDGE * face + CORNER * diag


def filter_planes(low, mid, high):
    return filter_side(low + high) + filter_mid(mid)


def weight_plane(shape, row_offset, count):
    row = rows(shape) + row_offset
    lane = lanes(shape)

    def neighbours(index, size):
        return jnp.where(index > 0, 1.0, 0.0) + jnp.where(index < size - 1, 1.0, 0.0)

    ry = neighbours(row, count)
    rz = neighbours(lane, shape[1])
    face, diag = ry + rz, ry * rz
    return (
        filter_reach
        + FACE * (2.0 + face)
        + EDGE * (2.0 * face + diag)
        + (2.0 * CORNER) * diag
    )


def start_inner_kernel(own, swap, v0, v0_inner, free, fields, parts, layers):
    sub = lax.axis_index("sub")
    half = own.shape[1]
    count = 2 * half
    mine = pl.ds(pl.multiple_of(sub * half, half), half)
    other = pl.ds(pl.multiple_of((1 - sub) * half, half), half)
    for layer in range(2):
        layers[layer, mine, :] = own[9 + layer]
        layers[layer, other, :] = swap[9 + layer]

    @pl.when(sub == 0)
    def _():
        parts[0] = filter_side(layers[0])
        parts[1] = filter_mid(layers[0]) + filter_side(layers[1])

    @pl.when(sub == 1)
    def _():
        parts[0] = filter_mid(layers[0]) + filter_side(layers[1])
        parts[1] = filter_side(layers[0]) + filter_mid(layers[1])

    parts[2] = 1.0 / weight_plane((count, own.shape[2]), 0, count)
    for k in range(3):
        free[k, mine, :] = own[6 + k]
        free[k, other, :] = swap[6 + k]
        v0[k, mine, :] = own[2 * k + sub]
        v0[k, other, :] = swap[2 * k + sub]
        v0_inner[k, mine, :] = own[2 * k + 1 - sub]
        v0_inner[k, other, :] = swap[2 * k + 1 - sub]
    fields_loop(count, rows_of(v0), rows_of(v0_inner), inner_side(sub), fields)


def start_outer_kernel(
    mods, slabs,
    first, second, third, fourth, v0, v0_inner, free, fields, parts,
    v1, v0_high, mod_inner, mod_outer, mod_own, slope_factor, chain_factor, moments,
    v0_outer, near, deep,
):
    mod, slab, sub = (lax.axis_index(a) for a in AXES)
    half = third.shape[0]
    count = 2 * half
    even = sub == 0
    mine = pl.ds(pl.multiple_of(sub * half, half), half)
    other = pl.ds(pl.multiple_of((1 - sub) * half, half), half)
    near[mine, :] = first[3]
    near[other, :] = second[3]
    deep[mine, :] = fourth[...]
    deep[other, :] = third[...]
    starts = (mod == 0) & (slab == 0) & even
    ends = (mod == mods - 1) & (slab == slabs - 1) & (sub == 1)
    inside = jnp.where(ends, 0.0, 1.0)
    for k in range(3):
        v0_outer[k, mine, :] = first[k] * inside
        v0_outer[k, other, :] = second[k] * inside
        v0_high[k] = jnp.where(even, v0_inner[k], v0_outer[k])

    side = filter_side(near[...])
    mid = filter_mid(near[...])
    inverse = parts[2]
    filtered = (parts[0] + filter_side(deep[...]) + jnp.where(even, mid, 0.0)) * inverse
    hyper = jnp.tanh(sharpness * (filtered - threshold))
    projected = (LOWER + hyper) * (1.0 / (LOWER + UPPER))
    below = stiff_floor + (1.0 - stiff_floor) * projected * projected * projected
    below = below * jnp.where(starts, 0.0, 1.0)
    filtered = (parts[1] + side) * inverse
    hyper = jnp.tanh(sharpness * (filtered - threshold))
    projected = (LOWER + hyper) * (1.0 / (LOWER + UPPER))
    squared = projected * projected
    stiff = stiff_floor + (1.0 - stiff_floor) * squared * projected
    mod_own[...] = stiff
    mod_inner[...] = jnp.where(even, stiff, below)
    mod_outer[...] = jnp.where(even, below, stiff)
    slope_factor[...] = (-penalty * (1.0 - stiff_floor)) * squared
    chain_factor[...] = (sharpness / (LOWER + UPPER)) * (1.0 - hyper * hyper) * inverse

    norm, cross, square = operator_loop(
        count, rows_of(v0), rows_of(v0_outer), -inner_side(sub), fields, mod_inner, mod_outer, free, v1
    )
    moments[...] = jnp.concatenate(
        [line(norm), line(cross), line(square), jnp.zeros((5, norm.shape[1]), jnp.float32)], axis=0
    )


def second_inner_kernel(v1, inner, fields):
    fields_loop(v1.shape[1], rows_of(v1), rows_of(inner), inner_side(lax.axis_index("sub")), fields)


def second_outer_kernel(
    v1, outer, inner, fields, free, mod_inner, mod_outer, before, v2, v1_high, moments
):
    sub = lax.axis_index("sub")
    count = v1.shape[1]
    for k in range(3):
        v1_high[k] = jnp.where(sub == 0, inner[k], outer[k])
    _, cross, square = operator_loop(
        count, rows_of(v1), rows_of(outer), -inner_side(sub), fields, mod_inner, mod_outer, free, v2
    )
    zero = jnp.zeros((3, cross.shape[1]), jnp.float32)
    moments[...] = before[...] + jnp.concatenate(
        [zero, line(cross), line(square), zero], axis=0
    )


def early_kernel(v0, v0_high, v1, v1_high, pairs):
    count = v0.shape[1]
    for y0 in range(0, count, ROWS):
        part = pl.ds(y0, ROWS)
        q0 = element_rows(v0, v0_high, y0, count)
        q1 = element_rows(v1, v1_high, y0, count)
        r1 = mode_forces(q1)
        pairs[0, part, :] = paired(q0, mode_forces(q0))
        pairs[1, part, :] = paired(q0, r1)
        pairs[2, part, :] = paired(q1, r1)


def third_kernel(v2_high, v2, v0, v0_high, v1, v1_high, mod_own, before, pairs, moments):
    count, width = v2.shape[1:]
    total = jnp.zeros((ROWS, width), jnp.float32)
    for y0 in range(0, count, ROWS):
        part = pl.ds(y0, ROWS)
        q2 = element_rows(v2, v2_high, y0, count)
        r2 = mode_forces(q2)
        energy = paired(q2, r2)
        total += energy * mod_own[part, :]
        pairs[2, part, :] = energy
        pairs[0, part, :] = paired(element_rows(v0, v0_high, y0, count), r2)
        pairs[1, part, :] = paired(element_rows(v1, v1_high, y0, count), r2)
    moments[...] = before[...] + jnp.concatenate(
        [
            jnp.zeros((5, width), jnp.float32),
            line(total),
            jnp.zeros((2, width), jnp.float32),
        ],
        axis=0,
    )


def coefficients(m):
    step = m[0] / m[1]
    x0 = step
    r1 = -step
    norm = m[0] + 2.0 * r1 * m[1] + r1 * r1 * m[2]
    ratio = norm / m[0]
    p0, p1 = 1.0 + ratio, r1
    step = norm / (p0 * p0 * m[1] + 2.0 * p0 * p1 * m[2] + p1 * p1 * m[3])
    x0, x1 = x0 + step * p0, step * p1
    r1, r2 = r1 - step * p0, -step * p1
    after = (
        m[0]
        + 2.0 * r1 * m[1]
        + (r1 * r1 + 2.0 * r2) * m[2]
        + 2.0 * r1 * r2 * m[3]
        + r2 * r2 * m[4]
    )
    ratio = after / norm
    p0, p1, p2 = 1.0 + ratio * p0, r1 + ratio * p1, r2
    step = after / (
        p0 * p0 * m[1]
        + 2.0 * p0 * p1 * m[2]
        + (p1 * p1 + 2.0 * p0 * p2) * m[3]
        + 2.0 * p1 * p2 * m[4]
        + p2 * p2 * m[5]
    )
    return x0 + step * p0, x1 + step * p1, step * p2


def combine_kernel(mods, *refs):
    gathered, v0, v1, v2, slope_factor, chain_factor = refs[:6]
    early, late = refs[6 : 6 + mods], refs[6 + mods : 6 + 2 * mods]
    keep, send, scaled, same, cross, own = refs[6 + 2 * mods :]
    sub = lax.axis_index("sub")
    count = v0.shape[1]
    half = count // 2
    sums = jnp.sum(jnp.sum(gathered[...], axis=0), axis=1, keepdims=True)
    c0, c1, c2 = coefficients([sums[k : k + 1] for k in range(6)])
    weights = (
        (early, (c0 * c0, 2.0 * c0 * c1, c1 * c1)),
        (late, (2.0 * c0 * c2, 2.0 * c1 * c2, c2 * c2)),
    )
    for y0 in range(0, count, ROWS):
        part = pl.ds(y0, ROWS)
        energy = None
        for modules, factors in weights:
            for n, factor in enumerate(factors):
                plane = modules[0][n, part, :]
                for other in modules[1:]:
                    plane = plane + other[n, part, :]
                energy = factor * plane if energy is None else energy + factor * plane
        scaled[part, :] = energy * slope_factor[part, :] * chain_factor[part, :]
        for k in range(3):
            own[k, part, :] = c0 * v0[k, part, :] + c1 * v1[k, part, :] + c2 * v2[k, part, :]

    window = same.shape[0]
    shift = count - window
    same[...] = scaled[pl.ds(pl.multiple_of(sub * shift, 8), window), :]
    cross[...] = scaled[pl.ds(pl.multiple_of((1 - sub) * shift, 8), window), :]
    mine = pl.ds(pl.multiple_of(sub * half, half), half)
    other = pl.ds(pl.multiple_of((1 - sub) * half, half), half)
    for k in range(3):
        keep[k] = own[k, mine, :]
        send[k] = own[k, other, :]


def assemble_kernel(keep, received, displacement):
    sub = lax.axis_index("sub")
    for k in range(3):
        displacement[k, sub] = keep[k]
        displacement[k, 1 - sub] = received[k]


def gradient_kernel(scaled, outer, far, partner, gradient, planes, sums):
    sub = lax.axis_index("sub")
    window = partner.shape[0]
    shift = scaled.shape[0] - window
    mine = scaled[pl.ds(pl.multiple_of(sub * shift, 8), window), :]

    @pl.when(sub == 0)
    def _():
        planes[0] = outer[...]
        planes[1] = mine
        planes[2] = partner[...]
        planes[3] = far[...]

    @pl.when(sub == 1)
    def _():
        planes[0] = far[...]
        planes[1] = partner[...]
        planes[2] = mine
        planes[3] = outer[...]

    half = gradient.shape[1]
    part = pl.ds(pl.multiple_of(sub * (window - half), 8), half)
    for layer in range(2):
        sums[...] = filter_planes(planes[layer], planes[layer + 1], planes[layer + 2])
        gradient[layer] = sums[part, :]


def call(body, outs, scratch=(), name=None, work=False):
    cost = pl.CostEstimate(flops=10**7, bytes_accessed=4 * 10**6, transcendentals=0)
    return pl.pallas_call(
        body,
        out_shape=[jax.ShapeDtypeStruct(shape, jnp.float32) for shape in outs],
        scratch_shapes=[pltpu.VMEM(shape, jnp.float32) for shape in scratch],
        compiler_params=pltpu.CompilerParams(vmem_limit_bytes=16 * 2**20),
        cost_estimate=cost if work else None,
        name=name,
    )


def routes(mods, slabs):
    chips = mods * slabs

    def at(chip, sub):
        return 2 * chip + sub

    def beside(chip, steps, cyclic):
        target = chip + steps
        if cyclic:
            return target % chips
        return target if 0 <= target < chips else None

    def built(moves, cyclic):
        pairs = []
        for chip in range(chips):
            for sub, steps, to in moves:
                target = beside(chip, steps, cyclic)
                if target is not None:
                    pairs.append((at(chip, sub), at(target, to)))
        return pairs

    def in_module(moves):
        pairs = []
        for chip in range(chips):
            mod, slab = divmod(chip, slabs)
            for sub, steps, to in moves:
                pairs.append((at(chip, sub), at(mod * slabs + (slab + steps) % slabs, to)))
        return pairs

    return dict(
        swap=built([(0, 0, 1), (1, 0, 0)], True),
        first=built([(0, 1, 0), (1, -1, 1)], True),
        second=built([(1, 1, 0), (0, -1, 1)], True),
        third=built([(0, 1, 1), (1, 1, 0)], True),
        fourth=built([(0, 1, 0), (1, 1, 1)], True),
        outer=built([(1, 1, 0), (0, -1, 1)], False),
        down=built([(1, 0, 0), (0, -1, 1)], False),
        halo_cross=in_module([(1, 1, 0), (0, -1, 1)]),
        halo_same=in_module([(0, -1, 0), (1, 1, 1)]),
    )


def module_routes(mods):
    if mods & (mods - 1) == 0:
        return [[(m, m ^ s) for m in range(mods)] for s in range(1, mods)]
    return [[(m, (m + s) % mods) for m in range(mods)] for s in range(1, mods)]


def local(mods, slabs, design, fixed, load):
    half, width = design.shape[1:]
    count = 2 * half
    path = routes(mods, slabs)

    def move(value, name):
        return lax.ppermute(value, AXES, path[name])

    plane = (count, width)
    layer = (3, count, width)
    block = (half, width)
    free = (1 - fixed).astype(jnp.float32)
    swap, first, second, third, fourth, own = call(
        prepare_kernel,
        [(11,) + block, (4,) + block, (4,) + block, block, block, (11,) + block],
        name="prepare",
    )(free, load, design)
    first = move(first, "first")
    second = move(second, "second")
    third = move(third, "third")
    fourth = move(fourth, "fourth")
    swap = move(swap, "swap")

    def start_body(*refs):
        start_outer_kernel(mods, slabs, *refs)

    v0, v0_inner, free, fields, parts = call(
        start_inner_kernel,
        [layer, layer, layer, (12,) + plane, (3,) + plane],
        [(2,) + plane],
        name="start_inner",
        work=True,
    )(own, swap)
    v1, v0_high, mod_inner, mod_outer, mod_own, slope_factor, chain_factor, moments = call(
        start_body,
        [layer, layer, plane, plane, plane, plane, plane, (8, width)],
        [layer, plane, plane],
        name="start_outer",
    )(first, second, third, fourth, v0, v0_inner, free, fields, parts)
    outer = move(v1, "outer")
    inner = move(v1, "swap")
    (fields,) = call(second_inner_kernel, [(12,) + plane], name="second_inner", work=True)(v1, inner)
    v2, v1_high, moments = call(
        second_outer_kernel, [layer, layer, (8, width)], name="second_outer"
    )(v1, outer, inner, fields, free, mod_inner, mod_outer, moments)
    v2_high = move(v2, "down")

    def modules(pairs):
        return [pairs] + [lax.ppermute(pairs, "mod", route) for route in module_routes(mods)]

    (early,) = call(early_kernel, [layer], name="early", work=True)(v0, v0_high, v1, v1_high)
    early = modules(early)
    late, moments = call(third_kernel, [layer, (8, width)], name="third")(
        v2_high, v2, v0, v0_high, v1, v1_high, mod_own, moments
    )
    late = modules(late)
    devices = 2 * mods * slabs
    gathered = lax.all_to_all(
        jnp.broadcast_to(moments, (devices, 8, width)), AXES, 0, 0, tiled=True
    )

    def combine_body(*refs):
        combine_kernel(mods, *refs)

    window = half + 8
    keep, send, scaled, same, cross = call(
        combine_body,
        [(3, half, width), (3, half, width), plane, (window, width), (window, width)],
        [layer],
        name="combine",
    )(gathered, v0, v1, v2, slope_factor, chain_factor, *early, *late)
    outer = move(cross, "halo_cross")
    far = move(same, "halo_same")
    partner = move(cross, "swap")
    received = move(send, "swap")
    (displacement,) = call(assemble_kernel, [(3, 2, half, width)], name="assemble", work=True)(
        keep, received
    )
    scaled, displacement = lax.optimization_barrier((scaled, displacement))
    (gradient,) = call(
        gradient_kernel, [(2, half, width)], [(4, window, width), (window, width)], name="gradient"
    )(scaled, outer, far, partner)
    return displacement, gradient


def solution(mesh):
    mods, slabs = mesh.shape["mod"], mesh.shape["slab"]
    assert mesh.shape["sub"] == 2
    deck = P(None, ("mod", "slab"), "sub", None)

    def body(design, fixed_mask, load_mask):
        return local(mods, slabs, design, fixed_mask, load_mask)

    return jax.shard_map(
        body,
        mesh=mesh,
        in_specs=(P("slab", "sub", None), deck, deck),
        out_specs=(deck, P("slab", "sub", None)),
        check_vma=False,
    )
```

```python
import math

import jax
import jax.numpy as jnp
import numpy as np
from jax import lax
from jax.experimental import pallas as pl
from jax.experimental.pallas import tpu as pltpu
from jax.sharding import PartitionSpec as P

stiff_floor = 0.01
penalty = 3.0
sharpness = 4.0
threshold = 0.5
filter_reach = 1.8

AXES = ("mod", "slab", "sub")
ROWS = 8
FACE = filter_reach - 1.0
EDGE = filter_reach - math.sqrt(2.0)
CORNER = filter_reach - math.sqrt(3.0)
LOWER = math.tanh(sharpness * threshold)
UPPER = math.tanh(sharpness * (1.0 - threshold))


def stiffness_modes():
    poisson = 0.3
    lame = poisson / ((1.0 + poisson) * (1.0 - 2.0 * poisson))
    shear = 1.0 / (2.0 * (1.0 + poisson))
    elastic = np.zeros((6, 6))
    elastic[:3, :3] = lame
    for axis in range(3):
        elastic[axis, axis] += 2.0 * shear
        elastic[axis + 3, axis + 3] = shear
    offset = 0.5 / math.sqrt(3.0)
    points = [0.5 - offset, 0.5 + offset]
    stiffness = np.zeros((24, 24))
    for point in ((a, b, c) for a in points for b in points for c in points):
        strain = np.zeros((6, 24))
        for corner in range(8):
            bits = (corner >> 2 & 1, corner >> 1 & 1, corner & 1)
            along = [point[a] if bits[a] else 1.0 - point[a] for a in range(3)]
            sign = [1.0 if bits[a] else -1.0 for a in range(3)]
            gx = sign[0] * along[1] * along[2]
            gy = along[0] * sign[1] * along[2]
            gz = along[0] * along[1] * sign[2]
            col = 3 * corner
            strain[0, col] = gx
            strain[1, col + 1] = gy
            strain[2, col + 2] = gz
            strain[3, col], strain[3, col + 1] = gy, gx
            strain[4, col + 1], strain[4, col + 2] = gz, gy
            strain[5, col], strain[5, col + 2] = gz, gx
        stiffness += strain.T @ elastic @ strain / 8.0
    basis = np.zeros((24, 24))
    for mode in range(8):
        for corner in range(8):
            value = 1.0
            for bit in range(3):
                if mode >> bit & 1 and not corner >> bit & 1:
                    value = -value
            for k in range(3):
                basis[3 * mode + k, 3 * corner + k] = value
    table = basis @ stiffness @ basis.T / 64.0
    table[np.abs(table) < 1e-9] = 0.0
    return table


TABLE = stiffness_modes()


def lanes(shape):
    return lax.broadcasted_iota(jnp.int32, shape, 1)


def rows(shape):
    return lax.broadcasted_iota(jnp.int32, shape, 0)


def z_up(x):
    return jnp.where(lanes(x.shape) < x.shape[1] - 1, pltpu.roll(x, x.shape[1] - 1, 1), 0.0)


def z_down(x):
    return jnp.where(lanes(x.shape) > 0, pltpu.roll(x, 1, 1), 0.0)


def y_up(x):
    return jnp.where(rows(x.shape) < x.shape[0] - 1, pltpu.roll(x, x.shape[0] - 1, 0), 0.0)


def y_down(x):
    return jnp.where(rows(x.shape) > 0, pltpu.roll(x, 1, 0), 0.0)


def two_rows(read, y0, count):
    here = read(y0)
    above = y_up(here) if y0 + ROWS == count else read(y0 + 1)
    return here, above


def face_modes(here, above):
    out = []
    for part in (here + above, above - here):
        shifted = z_up(part)
        out += [part + shifted, shifted - part]
    return out


def element_modes(own, other, side):
    sums = [[other[k][m] + own[k][m] for m in range(4)] for k in range(3)]
    diffs = [[(other[k][m] - own[k][m]) * side for m in range(4)] for k in range(3)]
    return [sums[k] + diffs[k] for k in range(3)]


def mode_forces(q):
    made = {}

    def scaled(j, value):
        key = (j, round(value, 12))
        if key not in made:
            made[key] = q[j % 3][j // 3] * np.float32(value)
        return made[key]

    out = [[None] * 8 for _ in range(3)]
    for i in range(24):
        total = None
        for j in np.nonzero(TABLE[i])[0]:
            term = scaled(int(j), float(TABLE[i, j]))
            total = term if total is None else total + term
        out[i % 3][i // 3] = total
    return out


def element_energy(q):
    r = mode_forces(q)
    total = None
    for k in range(3):
        for m in range(1, 8):
            term = q[k][m] * r[k][m]
            total = term if total is None else total + term
    return total


def own_fields(own, other, side):
    r = mode_forces(element_modes(own, other, side))
    fields = []
    for k in range(3):
        for m in range(4):
            d = r[k][m + 4] * side
            fields.append(-d if r[k][m] is None else r[k][m] - d)
    return fields


def layer_modes(read, y0, count):
    heres, modes = [], []
    for k in range(3):
        here, above = two_rows(lambda y, k=k: read(k, y), y0, count)
        heres.append(here)
        modes.append(face_modes(here, above))
    return heres, modes


def fields_loop(count, read_own, read_other, side, fields):
    for y0 in range(0, count, ROWS):
        _, own = layer_modes(read_own, y0, count)
        _, other = layer_modes(read_other, y0, count)
        for n, value in enumerate(own_fields(own, other, side)):
            fields[n, pl.ds(y0, ROWS), :] = value


def operator_loop(count, read_own, read_other, side, fields, mod_inner, mod_outer, free, out_ref):
    shape = (ROWS, out_ref.shape[2])
    square = jnp.zeros(shape, jnp.float32)
    cross = jnp.zeros(shape, jnp.float32)
    norm = jnp.zeros(shape, jnp.float32)
    carry = [jnp.zeros(shape, jnp.float32)] * 3
    first = rows(shape) == 0
    for y0 in range(0, count, ROWS):
        part = pl.ds(y0, ROWS)
        owns, own = layer_modes(read_own, y0, count)
        _, other = layer_modes(read_other, y0, count)
        inner, outer = mod_inner[part, :], mod_outer[part, :]
        total = [
            outer * value + inner * fields[n, part, :]
            for n, value in enumerate(own_fields(own, other, side))
        ]
        for k in range(3):
            faces = []
            for py in range(2):
                s, d = total[4 * k + 2 * py], total[4 * k + 2 * py + 1]
                faces.append((s - d) + z_down(s + d))
            rolled = pltpu.roll(faces[0] + faces[1], 1, 0)
            force = (faces[0] - faces[1]) + jnp.where(first, carry[k], rolled)
            carry[k] = rolled
            image = free[k, part, :] * force
            out_ref[k, part, :] = image
            square += image * image
            cross += owns[k] * image
            norm += owns[k] * owns[k]
    return norm, cross, square


def energy_loop(count, read_own, read_high, use):
    for y0 in range(0, count, ROWS):
        _, own = layer_modes(read_own, y0, count)
        _, high = layer_modes(read_high, y0, count)
        use(y0, element_energy(element_modes(own, high, 1.0)))


def rows_of(ref):
    return lambda k, y: ref[k, pl.ds(y, ROWS), :]


def inner_side(sub):
    return jnp.where(sub == 0, 1.0, -1.0).astype(jnp.float32)


def line(tile):
    return jnp.sum(tile, axis=0, keepdims=True)


def prepare_kernel(free, load, design, swap, first, second, third, fourth, own):
    sub = lax.axis_index("sub")
    for k in range(3):
        frees = [free[k, layer] for layer in range(2)]
        values = [frees[layer] * load[k, layer].astype(jnp.float32) for layer in range(2)]
        for layer in range(2):
            swap[2 * k + layer] = values[layer]
            own[2 * k + layer] = values[layer]
        low = sub == 0
        swap[6 + k] = jnp.where(low, frees[1], frees[0])
        own[6 + k] = jnp.where(low, frees[0], frees[1])
        first[k] = jnp.where(low, values[1], values[0])
        second[k] = jnp.where(low, values[0], values[1])
    low = sub == 0
    for layer in range(2):
        swap[9 + layer] = design[layer]
        own[9 + layer] = design[layer]
    later = jnp.where(low, design[1], design[0])
    sooner = jnp.where(low, design[0], design[1])
    first[3] = later
    third[...] = later
    second[3] = sooner
    fourth[...] = sooner


def around(p):
    across = y_up(p) + y_down(p)
    return across + z_up(p) + z_down(p), z_up(across) + z_down(across)


def filter_mid(p):
    face, diag = around(p)
    return filter_reach * p + FACE * face + EDGE * diag


def filter_side(p):
    face, diag = around(p)
    return FACE * p + EDGE * face + CORNER * diag


def filter_planes(low, mid, high):
    return filter_side(low + high) + filter_mid(mid)


def weight_plane(shape, row_offset, count):
    row = rows(shape) + row_offset
    lane = lanes(shape)

    def neighbours(index, size):
        return jnp.where(index > 0, 1.0, 0.0) + jnp.where(index < size - 1, 1.0, 0.0)

    ry = neighbours(row, count)
    rz = neighbours(lane, shape[1])
    face, diag = ry + rz, ry * rz
    return (
        filter_reach
        + FACE * (2.0 + face)
        + EDGE * (2.0 * face + diag)
        + (2.0 * CORNER) * diag
    )


def start_inner_kernel(own, swap, v0, v0_inner, free, fields, parts, layers):
    sub = lax.axis_index("sub")
    half = own.shape[1]
    count = 2 * half
    mine = pl.ds(pl.multiple_of(sub * half, half), half)
    other = pl.ds(pl.multiple_of((1 - sub) * half, half), half)
    for layer in range(2):
        layers[layer, mine, :] = own[9 + layer]
        layers[layer, other, :] = swap[9 + layer]

    @pl.when(sub == 0)
    def _():
        parts[0] = filter_side(layers[0])
        parts[1] = filter_mid(layers[0]) + filter_side(layers[1])

    @pl.when(sub == 1)
    def _():
        parts[0] = filter_mid(layers[0]) + filter_side(layers[1])
        parts[1] = filter_side(layers[0]) + filter_mid(layers[1])

    parts[2] = 1.0 / weight_plane((count, own.shape[2]), 0, count)
    for k in range(3):
        free[k, mine, :] = own[6 + k]
        free[k, other, :] = swap[6 + k]
        v0[k, mine, :] = own[2 * k + sub]
        v0[k, other, :] = swap[2 * k + sub]
        v0_inner[k, mine, :] = own[2 * k + 1 - sub]
        v0_inner[k, other, :] = swap[2 * k + 1 - sub]
    fields_loop(count, rows_of(v0), rows_of(v0_inner), inner_side(sub), fields)


def start_outer_kernel(
    mods, slabs,
    first, second, third, fourth, v0, v0_inner, free, fields, parts,
    v1, v0_high, mod_inner, mod_outer, mod_own, slope_factor, chain_factor, moments,
    v0_outer, near, deep,
):
    mod, slab, sub = (lax.axis_index(a) for a in AXES)
    half = third.shape[0]
    count = 2 * half
    even = sub == 0
    mine = pl.ds(pl.multiple_of(sub * half, half), half)
    other = pl.ds(pl.multiple_of((1 - sub) * half, half), half)
    near[mine, :] = first[3]
    near[other, :] = second[3]
    deep[mine, :] = fourth[...]
    deep[other, :] = third[...]
    starts = (mod == 0) & (slab == 0) & even
    ends = (mod == mods - 1) & (slab == slabs - 1) & (sub == 1)
    inside = jnp.where(ends, 0.0, 1.0)
    for k in range(3):
        v0_outer[k, mine, :] = first[k] * inside
        v0_outer[k, other, :] = second[k] * inside
        v0_high[k] = jnp.where(even, v0_inner[k], v0_outer[k])

    side = filter_side(near[...])
    mid = filter_mid(near[...])
    inverse = parts[2]
    filtered = (parts[0] + filter_side(deep[...]) + jnp.where(even, mid, 0.0)) * inverse
    hyper = jnp.tanh(sharpness * (filtered - threshold))
    projected = (LOWER + hyper) * (1.0 / (LOWER + UPPER))
    below = stiff_floor + (1.0 - stiff_floor) * projected * projected * projected
    below = below * jnp.where(starts, 0.0, 1.0)
    filtered = (parts[1] + side) * inverse
    hyper = jnp.tanh(sharpness * (filtered - threshold))
    projected = (LOWER + hyper) * (1.0 / (LOWER + UPPER))
    squared = projected * projected
    stiff = stiff_floor + (1.0 - stiff_floor) * squared * projected
    mod_own[...] = stiff
    mod_inner[...] = jnp.where(even, stiff, below)
    mod_outer[...] = jnp.where(even, below, stiff)
    slope_factor[...] = (-penalty * (1.0 - stiff_floor)) * squared
    chain_factor[...] = (sharpness / (LOWER + UPPER)) * (1.0 - hyper * hyper) * inverse

    norm, cross, square = operator_loop(
        count, rows_of(v0), rows_of(v0_outer), -inner_side(sub), fields, mod_inner, mod_outer, free, v1
    )
    moments[...] = jnp.concatenate(
        [line(norm), line(cross), line(square), jnp.zeros((5, norm.shape[1]), jnp.float32)], axis=0
    )


def second_inner_kernel(v1, inner, fields):
    fields_loop(v1.shape[1], rows_of(v1), rows_of(inner), inner_side(lax.axis_index("sub")), fields)


def second_outer_kernel(
    v1, outer, inner, fields, free, mod_inner, mod_outer, before, v2, v1_high, moments
):
    sub = lax.axis_index("sub")
    count = v1.shape[1]
    for k in range(3):
        v1_high[k] = jnp.where(sub == 0, inner[k], outer[k])
    _, cross, square = operator_loop(
        count, rows_of(v1), rows_of(outer), -inner_side(sub), fields, mod_inner, mod_outer, free, v2
    )
    zero = jnp.zeros((3, cross.shape[1]), jnp.float32)
    moments[...] = before[...] + jnp.concatenate(
        [zero, line(cross), line(square), zero], axis=0
    )


def third_kernel(v2, v2_high, mod_own, before, moments):
    count = v2.shape[1]
    total = [jnp.zeros((ROWS, v2.shape[2]), jnp.float32)]

    def use(y0, energy):
        total[0] += energy * mod_own[pl.ds(y0, ROWS), :]

    energy_loop(
        count,
        lambda k, y: v2[k, pl.ds(y, ROWS), :],
        lambda k, y: v2_high[k, pl.ds(y, ROWS), :],
        use,
    )
    width = v2.shape[2]
    moments[...] = before[...] + jnp.concatenate(
        [
            jnp.zeros((5, width), jnp.float32),
            line(total[0]),
            jnp.zeros((2, width), jnp.float32),
        ],
        axis=0,
    )


def coefficients(m):
    step = m[0] / m[1]
    x0 = step
    r1 = -step
    norm = m[0] + 2.0 * r1 * m[1] + r1 * r1 * m[2]
    ratio = norm / m[0]
    p0, p1 = 1.0 + ratio, r1
    step = norm / (p0 * p0 * m[1] + 2.0 * p0 * p1 * m[2] + p1 * p1 * m[3])
    x0, x1 = x0 + step * p0, step * p1
    r1, r2 = r1 - step * p0, -step * p1
    after = (
        m[0]
        + 2.0 * r1 * m[1]
        + (r1 * r1 + 2.0 * r2) * m[2]
        + 2.0 * r1 * r2 * m[3]
        + r2 * r2 * m[4]
    )
    ratio = after / norm
    p0, p1, p2 = 1.0 + ratio * p0, r1 + ratio * p1, r2
    step = after / (
        p0 * p0 * m[1]
        + 2.0 * p0 * p1 * m[2]
        + (p1 * p1 + 2.0 * p0 * p2) * m[3]
        + 2.0 * p1 * p2 * m[4]
        + p2 * p2 * m[5]
    )
    return x0 + step * p0, x1 + step * p1, step * p2


def combine_kernel(
    gathered, v0, v0_high, v1, v1_high, v2, v2_high, slope_factor,
    slope, keep, send,
    own, high,
):
    sub = lax.axis_index("sub")
    count = v0.shape[1]
    half = count // 2
    sums = jnp.sum(jnp.sum(gathered[...], axis=0), axis=1, keepdims=True)
    c0, c1, c2 = coefficients([sums[k : k + 1] for k in range(6)])
    for k in range(3):
        own[k] = c0 * v0[k] + c1 * v1[k] + c2 * v2[k]
        high[k] = c0 * v0_high[k] + c1 * v1_high[k] + c2 * v2_high[k]

    mine = pl.ds(pl.multiple_of(sub * half, half), half)
    other = pl.ds(pl.multiple_of((1 - sub) * half, half), half)
    for k in range(3):
        keep[k] = own[k, mine, :]
        send[k] = own[k, other, :]

    def use(y0, energy):
        slope[pl.ds(y0, ROWS), :] = slope_factor[pl.ds(y0, ROWS), :] * energy

    energy_loop(
        count,
        lambda k, y: own[k, pl.ds(y, ROWS), :],
        lambda k, y: high[k, pl.ds(y, ROWS), :],
        use,
    )


def scale_kernel(*refs):
    slopes, (chain_factor, scaled, same, cross) = refs[:-4], refs[-4:]
    sub = lax.axis_index("sub")
    total = slopes[0][...]
    for other in slopes[1:]:
        total = total + other[...]
    scaled[...] = total * chain_factor[...]
    window = same.shape[0]
    shift = scaled.shape[0] - window
    same[...] = scaled[pl.ds(pl.multiple_of(sub * shift, 8), window), :]
    cross[...] = scaled[pl.ds(pl.multiple_of((1 - sub) * shift, 8), window), :]


def gradient_kernel(scaled, outer, far, partner, gradient, planes, sums):
    sub = lax.axis_index("sub")
    window = partner.shape[0]
    shift = scaled.shape[0] - window
    mine = scaled[pl.ds(pl.multiple_of(sub * shift, 8), window), :]

    @pl.when(sub == 0)
    def _():
        planes[0] = outer[...]
        planes[1] = mine
        planes[2] = partner[...]
        planes[3] = far[...]

    @pl.when(sub == 1)
    def _():
        planes[0] = far[...]
        planes[1] = partner[...]
        planes[2] = mine
        planes[3] = outer[...]

    half = gradient.shape[1]
    part = pl.ds(pl.multiple_of(sub * (window - half), 8), half)
    for layer in range(2):
        sums[...] = filter_planes(planes[layer], planes[layer + 1], planes[layer + 2])
        gradient[layer] = sums[part, :]


def call(body, outs, scratch=(), name=None, work=False):
    cost = pl.CostEstimate(flops=10**7, bytes_accessed=4 * 10**6, transcendentals=0)
    return pl.pallas_call(
        body,
        out_shape=[jax.ShapeDtypeStruct(shape, jnp.float32) for shape in outs],
        scratch_shapes=[pltpu.VMEM(shape, jnp.float32) for shape in scratch],
        compiler_params=pltpu.CompilerParams(vmem_limit_bytes=16 * 2**20),
        cost_estimate=cost if work else None,
        name=name,
    )


def routes(mods, slabs):
    chips = mods * slabs

    def at(chip, sub):
        return 2 * chip + sub

    def beside(chip, steps, cyclic):
        target = chip + steps
        if cyclic:
            return target % chips
        return target if 0 <= target < chips else None

    def built(moves, cyclic):
        pairs = []
        for chip in range(chips):
            for sub, steps, to in moves:
                target = beside(chip, steps, cyclic)
                if target is not None:
                    pairs.append((at(chip, sub), at(target, to)))
        return pairs

    def in_module(moves):
        pairs = []
        for chip in range(chips):
            mod, slab = divmod(chip, slabs)
            for sub, steps, to in moves:
                pairs.append((at(chip, sub), at(mod * slabs + (slab + steps) % slabs, to)))
        return pairs

    return dict(
        swap=built([(0, 0, 1), (1, 0, 0)], True),
        first=built([(0, 1, 0), (1, -1, 1)], True),
        second=built([(1, 1, 0), (0, -1, 1)], True),
        third=built([(0, 1, 1), (1, 1, 0)], True),
        fourth=built([(0, 1, 0), (1, 1, 1)], True),
        outer=built([(1, 1, 0), (0, -1, 1)], False),
        down=built([(1, 0, 0), (0, -1, 1)], False),
        halo_cross=in_module([(1, 1, 0), (0, -1, 1)]),
        halo_same=in_module([(0, -1, 0), (1, 1, 1)]),
    )


def module_routes(mods):
    if mods & (mods - 1) == 0:
        return [[(m, m ^ s) for m in range(mods)] for s in range(1, mods)]
    return [[(m, (m + s) % mods) for m in range(mods)] for s in range(1, mods)]


def local(mods, slabs, design, fixed, load):
    half, width = design.shape[1:]
    count = 2 * half
    path = routes(mods, slabs)

    def move(value, name):
        return lax.ppermute(value, AXES, path[name])

    plane = (count, width)
    layer = (3, count, width)
    block = (half, width)
    free = (1 - fixed).astype(jnp.float32)
    swap, first, second, third, fourth, own = call(
        prepare_kernel,
        [(11,) + block, (4,) + block, (4,) + block, block, block, (11,) + block],
        name="prepare",
    )(free, load, design)
    first = move(first, "first")
    second = move(second, "second")
    third = move(third, "third")
    fourth = move(fourth, "fourth")
    swap = move(swap, "swap")

    def start_body(*refs):
        start_outer_kernel(mods, slabs, *refs)

    v0, v0_inner, free, fields, parts = call(
        start_inner_kernel,
        [layer, layer, layer, (12,) + plane, (3,) + plane],
        [(2,) + plane],
        name="start_inner",
        work=True,
    )(own, swap)
    v1, v0_high, mod_inner, mod_outer, mod_own, slope_factor, chain_factor, moments = call(
        start_body,
        [layer, layer, plane, plane, plane, plane, plane, (8, width)],
        [layer, plane, plane],
        name="start_outer",
    )(first, second, third, fourth, v0, v0_inner, free, fields, parts)
    outer = move(v1, "outer")
    inner = move(v1, "swap")
    (fields,) = call(second_inner_kernel, [(12,) + plane], name="second_inner", work=True)(v1, inner)
    v2, v1_high, moments = call(
        second_outer_kernel, [layer, layer, (8, width)], name="second_outer"
    )(v1, outer, inner, fields, free, mod_inner, mod_outer, moments)
    v2_high = move(v2, "down")
    (moments,) = call(third_kernel, [(8, width)], name="third")(v2, v2_high, mod_own, moments)
    moments = moments + move(moments, "swap")
    chips = mods * slabs
    gathered = lax.all_to_all(
        jnp.broadcast_to(moments, (chips, 8, width)), ("mod", "slab"), 0, 0, tiled=True
    )
    slope, keep, send = call(
        combine_kernel, [plane, (3, half, width), (3, half, width)], [layer, layer], name="combine"
    )(gathered, v0, v0_high, v1, v1_high, v2, v2_high, slope_factor)
    slopes = [slope] + [lax.ppermute(slope, "mod", pairs) for pairs in module_routes(mods)]
    received = move(send, "swap")
    window = half + 8
    scaled, same, cross = call(
        scale_kernel, [plane, (window, width), (window, width)], name="scale"
    )(*slopes, chain_factor)
    outer = move(cross, "halo_cross")
    far = move(same, "halo_same")
    partner = move(cross, "swap")
    even = lax.axis_index("sub") == 0
    displacement = jnp.stack(
        [jnp.where(even, keep, received), jnp.where(even, received, keep)], axis=1
    )
    (gradient,) = call(
        gradient_kernel, [(2, half, width)], [(4, window, width), (window, width)], name="gradient"
    )(scaled, outer, far, partner)
    return displacement, gradient


def solution(mesh):
    mods, slabs = mesh.shape["mod"], mesh.shape["slab"]
    assert mesh.shape["sub"] == 2
    deck = P(None, ("mod", "slab"), "sub", None)

    def body(design, fixed_mask, load_mask):
        return local(mods, slabs, design, fixed_mask, load_mask)

    return jax.shard_map(
        body,
        mesh=mesh,
        in_specs=(P("slab", "sub", None), deck, deck),
        out_specs=(deck, P("slab", "sub", None)),
        check_vma=False,
    )
```

```python
import math

import jax
import jax.numpy as jnp
import numpy as np
from jax import lax
from jax.experimental import pallas as pl
from jax.experimental.pallas import tpu as pltpu
from jax.sharding import PartitionSpec as P

stiff_floor = 0.01
penalty = 3.0
sharpness = 4.0
threshold = 0.5
filter_reach = 1.8

AXES = ("mod", "slab", "sub")
ROWS = 8
FACE = filter_reach - 1.0
EDGE = filter_reach - math.sqrt(2.0)
CORNER = filter_reach - math.sqrt(3.0)
LOWER = math.tanh(sharpness * threshold)
UPPER = math.tanh(sharpness * (1.0 - threshold))


def stiffness_modes():
    poisson = 0.3
    lame = poisson / ((1.0 + poisson) * (1.0 - 2.0 * poisson))
    shear = 1.0 / (2.0 * (1.0 + poisson))
    elastic = np.zeros((6, 6))
    elastic[:3, :3] = lame
    for axis in range(3):
        elastic[axis, axis] += 2.0 * shear
        elastic[axis + 3, axis + 3] = shear
    offset = 0.5 / math.sqrt(3.0)
    points = [0.5 - offset, 0.5 + offset]
    stiffness = np.zeros((24, 24))
    for point in ((a, b, c) for a in points for b in points for c in points):
        strain = np.zeros((6, 24))
        for corner in range(8):
            bits = (corner >> 2 & 1, corner >> 1 & 1, corner & 1)
            along = [point[a] if bits[a] else 1.0 - point[a] for a in range(3)]
            sign = [1.0 if bits[a] else -1.0 for a in range(3)]
            gx = sign[0] * along[1] * along[2]
            gy = along[0] * sign[1] * along[2]
            gz = along[0] * along[1] * sign[2]
            col = 3 * corner
            strain[0, col] = gx
            strain[1, col + 1] = gy
            strain[2, col + 2] = gz
            strain[3, col], strain[3, col + 1] = gy, gx
            strain[4, col + 1], strain[4, col + 2] = gz, gy
            strain[5, col], strain[5, col + 2] = gz, gx
        stiffness += strain.T @ elastic @ strain / 8.0
    basis = np.zeros((24, 24))
    for mode in range(8):
        for corner in range(8):
            value = 1.0
            for bit in range(3):
                if mode >> bit & 1 and not corner >> bit & 1:
                    value = -value
            for k in range(3):
                basis[3 * mode + k, 3 * corner + k] = value
    table = basis @ stiffness @ basis.T / 64.0
    table[np.abs(table) < 1e-9] = 0.0
    return table


TABLE = stiffness_modes()


def lanes(shape):
    return lax.broadcasted_iota(jnp.int32, shape, 1)


def rows(shape):
    return lax.broadcasted_iota(jnp.int32, shape, 0)


def z_up(x):
    return jnp.where(lanes(x.shape) < x.shape[1] - 1, pltpu.roll(x, x.shape[1] - 1, 1), 0.0)


def z_down(x):
    return jnp.where(lanes(x.shape) > 0, pltpu.roll(x, 1, 1), 0.0)


def y_up(x):
    return jnp.where(rows(x.shape) < x.shape[0] - 1, pltpu.roll(x, x.shape[0] - 1, 0), 0.0)


def y_down(x):
    return jnp.where(rows(x.shape) > 0, pltpu.roll(x, 1, 0), 0.0)


def two_rows(read, y0, count):
    here = read(y0)
    above = y_up(here) if y0 + ROWS == count else read(y0 + 1)
    return here, above


def face_modes(here, above):
    out = []
    for part in (here + above, above - here):
        shifted = z_up(part)
        out += [part + shifted, shifted - part]
    return out


def element_modes(own, other, side):
    sums = [[other[k][m] + own[k][m] for m in range(4)] for k in range(3)]
    diffs = [[(other[k][m] - own[k][m]) * side for m in range(4)] for k in range(3)]
    return [sums[k] + diffs[k] for k in range(3)]


def mode_forces(q):
    made = {}

    def scaled(j, value):
        key = (j, round(value, 12))
        if key not in made:
            made[key] = q[j % 3][j // 3] * np.float32(value)
        return made[key]

    out = [[None] * 8 for _ in range(3)]
    for i in range(24):
        total = None
        for j in np.nonzero(TABLE[i])[0]:
            term = scaled(int(j), float(TABLE[i, j]))
            total = term if total is None else total + term
        out[i % 3][i // 3] = total
    return out


def element_energy(q):
    r = mode_forces(q)
    total = None
    for k in range(3):
        for m in range(1, 8):
            term = q[k][m] * r[k][m]
            total = term if total is None else total + term
    return total


def own_fields(own, other, side):
    r = mode_forces(element_modes(own, other, side))
    fields = []
    for k in range(3):
        for m in range(4):
            d = r[k][m + 4] * side
            fields.append(-d if r[k][m] is None else r[k][m] - d)
    return fields


def layer_modes(read, y0, count):
    heres, modes = [], []
    for k in range(3):
        here, above = two_rows(lambda y, k=k: read(k, y), y0, count)
        heres.append(here)
        modes.append(face_modes(here, above))
    return heres, modes


def fields_loop(count, read_own, read_other, side, fields):
    for y0 in range(0, count, ROWS):
        _, own = layer_modes(read_own, y0, count)
        _, other = layer_modes(read_other, y0, count)
        for n, value in enumerate(own_fields(own, other, side)):
            fields[n, pl.ds(y0, ROWS), :] = value


def operator_loop(count, read_own, read_other, side, fields, mod_inner, mod_outer, free, out_ref):
    shape = (ROWS, out_ref.shape[2])
    square = jnp.zeros(shape, jnp.float32)
    cross = jnp.zeros(shape, jnp.float32)
    norm = jnp.zeros(shape, jnp.float32)
    carry = [jnp.zeros(shape, jnp.float32)] * 3
    first = rows(shape) == 0
    for y0 in range(0, count, ROWS):
        part = pl.ds(y0, ROWS)
        owns, own = layer_modes(read_own, y0, count)
        _, other = layer_modes(read_other, y0, count)
        inner, outer = mod_inner[part, :], mod_outer[part, :]
        total = [
            outer * value + inner * fields[n, part, :]
            for n, value in enumerate(own_fields(own, other, side))
        ]
        for k in range(3):
            faces = []
            for py in range(2):
                s, d = total[4 * k + 2 * py], total[4 * k + 2 * py + 1]
                faces.append((s - d) + z_down(s + d))
            rolled = pltpu.roll(faces[0] + faces[1], 1, 0)
            force = (faces[0] - faces[1]) + jnp.where(first, carry[k], rolled)
            carry[k] = rolled
            image = free[k, part, :] * force
            out_ref[k, part, :] = image
            square += image * image
            cross += owns[k] * image
            norm += owns[k] * owns[k]
    return norm, cross, square


def energy_loop(count, read_own, read_high, use):
    for y0 in range(0, count, ROWS):
        _, own = layer_modes(read_own, y0, count)
        _, high = layer_modes(read_high, y0, count)
        use(y0, element_energy(element_modes(own, high, 1.0)))


def rows_of(ref):
    return lambda k, y: ref[k, pl.ds(y, ROWS), :]


def inner_side(sub):
    return jnp.where(sub == 0, 1.0, -1.0).astype(jnp.float32)


def line(tile):
    return jnp.sum(tile, axis=0, keepdims=True)


def prepare_kernel(free, load, design, swap, first, second, third, fourth, own):
    sub = lax.axis_index("sub")
    for k in range(3):
        frees = [free[k, layer] for layer in range(2)]
        values = [frees[layer] * load[k, layer].astype(jnp.float32) for layer in range(2)]
        for layer in range(2):
            swap[2 * k + layer] = values[layer]
            own[2 * k + layer] = values[layer]
        low = sub == 0
        swap[6 + k] = jnp.where(low, frees[1], frees[0])
        own[6 + k] = jnp.where(low, frees[0], frees[1])
        first[k] = jnp.where(low, values[1], values[0])
        second[k] = jnp.where(low, values[0], values[1])
    low = sub == 0
    for layer in range(2):
        swap[9 + layer] = design[layer]
        own[9 + layer] = design[layer]
    later = jnp.where(low, design[1], design[0])
    sooner = jnp.where(low, design[0], design[1])
    first[3] = later
    third[...] = later
    second[3] = sooner
    fourth[...] = sooner


def around(p):
    across = y_up(p) + y_down(p)
    return across + z_up(p) + z_down(p), z_up(across) + z_down(across)


def filter_mid(p):
    face, diag = around(p)
    return filter_reach * p + FACE * face + EDGE * diag


def filter_side(p):
    face, diag = around(p)
    return FACE * p + EDGE * face + CORNER * diag


def filter_planes(low, mid, high):
    return filter_side(low + high) + filter_mid(mid)


def weight_plane(shape, row_offset, count):
    row = rows(shape) + row_offset
    lane = lanes(shape)

    def neighbours(index, size):
        return jnp.where(index > 0, 1.0, 0.0) + jnp.where(index < size - 1, 1.0, 0.0)

    ry = neighbours(row, count)
    rz = neighbours(lane, shape[1])
    face, diag = ry + rz, ry * rz
    return (
        filter_reach
        + FACE * (2.0 + face)
        + EDGE * (2.0 * face + diag)
        + (2.0 * CORNER) * diag
    )


def start_inner_kernel(own, swap, v0, v0_inner, free, fields, parts, layers):
    sub = lax.axis_index("sub")
    half = own.shape[1]
    count = 2 * half
    mine = pl.ds(pl.multiple_of(sub * half, half), half)
    other = pl.ds(pl.multiple_of((1 - sub) * half, half), half)
    for layer in range(2):
        layers[layer, mine, :] = own[9 + layer]
        layers[layer, other, :] = swap[9 + layer]

    @pl.when(sub == 0)
    def _():
        parts[0] = filter_side(layers[0])
        parts[1] = filter_mid(layers[0]) + filter_side(layers[1])

    @pl.when(sub == 1)
    def _():
        parts[0] = filter_mid(layers[0]) + filter_side(layers[1])
        parts[1] = filter_side(layers[0]) + filter_mid(layers[1])

    parts[2] = 1.0 / weight_plane((count, own.shape[2]), 0, count)
    for k in range(3):
        free[k, mine, :] = own[6 + k]
        free[k, other, :] = swap[6 + k]
        v0[k, mine, :] = own[2 * k + sub]
        v0[k, other, :] = swap[2 * k + sub]
        v0_inner[k, mine, :] = own[2 * k + 1 - sub]
        v0_inner[k, other, :] = swap[2 * k + 1 - sub]
    fields_loop(count, rows_of(v0), rows_of(v0_inner), inner_side(sub), fields)


def start_outer_kernel(
    mods, slabs,
    first, second, third, fourth, v0, v0_inner, free, fields, parts,
    v1, v0_high, mod_inner, mod_outer, mod_own, slope_factor, chain_factor, moments,
    v0_outer, near, deep,
):
    mod, slab, sub = (lax.axis_index(a) for a in AXES)
    half = third.shape[0]
    count = 2 * half
    even = sub == 0
    mine = pl.ds(pl.multiple_of(sub * half, half), half)
    other = pl.ds(pl.multiple_of((1 - sub) * half, half), half)
    near[mine, :] = first[3]
    near[other, :] = second[3]
    deep[mine, :] = fourth[...]
    deep[other, :] = third[...]
    starts = (mod == 0) & (slab == 0) & even
    ends = (mod == mods - 1) & (slab == slabs - 1) & (sub == 1)
    inside = jnp.where(ends, 0.0, 1.0)
    for k in range(3):
        v0_outer[k, mine, :] = first[k] * inside
        v0_outer[k, other, :] = second[k] * inside
        v0_high[k] = jnp.where(even, v0_inner[k], v0_outer[k])

    side = filter_side(near[...])
    mid = filter_mid(near[...])
    inverse = parts[2]
    filtered = (parts[0] + filter_side(deep[...]) + jnp.where(even, mid, 0.0)) * inverse
    hyper = jnp.tanh(sharpness * (filtered - threshold))
    projected = (LOWER + hyper) * (1.0 / (LOWER + UPPER))
    below = stiff_floor + (1.0 - stiff_floor) * projected * projected * projected
    below = below * jnp.where(starts, 0.0, 1.0)
    filtered = (parts[1] + side) * inverse
    hyper = jnp.tanh(sharpness * (filtered - threshold))
    projected = (LOWER + hyper) * (1.0 / (LOWER + UPPER))
    squared = projected * projected
    stiff = stiff_floor + (1.0 - stiff_floor) * squared * projected
    mod_own[...] = stiff
    mod_inner[...] = jnp.where(even, stiff, below)
    mod_outer[...] = jnp.where(even, below, stiff)
    slope_factor[...] = (-penalty * (1.0 - stiff_floor)) * squared
    chain_factor[...] = (sharpness / (LOWER + UPPER)) * (1.0 - hyper * hyper) * inverse

    norm, cross, square = operator_loop(
        count, rows_of(v0), rows_of(v0_outer), -inner_side(sub), fields, mod_inner, mod_outer, free, v1
    )
    moments[...] = jnp.concatenate(
        [line(norm), line(cross), line(square), jnp.zeros((5, norm.shape[1]), jnp.float32)], axis=0
    )


def second_inner_kernel(v1, inner, fields):
    fields_loop(v1.shape[1], rows_of(v1), rows_of(inner), inner_side(lax.axis_index("sub")), fields)


def second_outer_kernel(
    v1, outer, inner, fields, free, mod_inner, mod_outer, before, v2, v1_high, moments
):
    sub = lax.axis_index("sub")
    count = v1.shape[1]
    for k in range(3):
        v1_high[k] = jnp.where(sub == 0, inner[k], outer[k])
    _, cross, square = operator_loop(
        count, rows_of(v1), rows_of(outer), -inner_side(sub), fields, mod_inner, mod_outer, free, v2
    )
    zero = jnp.zeros((3, cross.shape[1]), jnp.float32)
    moments[...] = before[...] + jnp.concatenate(
        [zero, line(cross), line(square), zero], axis=0
    )


def third_kernel(v2_outer, v2_inner, v2, mod_own, before, moments, v2_high):
    even = lax.axis_index("sub") == 0
    for k in range(3):
        v2_high[k] = jnp.where(even, v2_inner[k], v2_outer[k])
    count = v2.shape[1]
    total = [jnp.zeros((ROWS, v2.shape[2]), jnp.float32)]

    def use(y0, energy):
        total[0] += energy * mod_own[pl.ds(y0, ROWS), :]

    energy_loop(
        count,
        lambda k, y: v2[k, pl.ds(y, ROWS), :],
        lambda k, y: v2_high[k, pl.ds(y, ROWS), :],
        use,
    )
    width = v2.shape[2]
    moments[...] = before[...] + jnp.concatenate(
        [
            jnp.zeros((5, width), jnp.float32),
            line(total[0]),
            jnp.zeros((2, width), jnp.float32),
        ],
        axis=0,
    )


def coefficients(m):
    step = m[0] / m[1]
    x0 = step
    r1 = -step
    norm = m[0] + 2.0 * r1 * m[1] + r1 * r1 * m[2]
    ratio = norm / m[0]
    p0, p1 = 1.0 + ratio, r1
    step = norm / (p0 * p0 * m[1] + 2.0 * p0 * p1 * m[2] + p1 * p1 * m[3])
    x0, x1 = x0 + step * p0, step * p1
    r1, r2 = r1 - step * p0, -step * p1
    after = (
        m[0]
        + 2.0 * r1 * m[1]
        + (r1 * r1 + 2.0 * r2) * m[2]
        + 2.0 * r1 * r2 * m[3]
        + r2 * r2 * m[4]
    )
    ratio = after / norm
    p0, p1, p2 = 1.0 + ratio * p0, r1 + ratio * p1, r2
    step = after / (
        p0 * p0 * m[1]
        + 2.0 * p0 * p1 * m[2]
        + (p1 * p1 + 2.0 * p0 * p2) * m[3]
        + 2.0 * p1 * p2 * m[4]
        + p2 * p2 * m[5]
    )
    return x0 + step * p0, x1 + step * p1, step * p2


def combine_kernel(
    gathered, v0, v0_high, v1, v1_high, v2, v2_high, slope_factor,
    slope, keep, send,
    own, high,
):
    sub = lax.axis_index("sub")
    count = v0.shape[1]
    half = count // 2
    sums = jnp.sum(jnp.sum(gathered[...], axis=0), axis=1, keepdims=True)
    c0, c1, c2 = coefficients([sums[k : k + 1] for k in range(6)])
    for k in range(3):
        own[k] = c0 * v0[k] + c1 * v1[k] + c2 * v2[k]
        high[k] = c0 * v0_high[k] + c1 * v1_high[k] + c2 * v2_high[k]

    mine = pl.ds(pl.multiple_of(sub * half, half), half)
    other = pl.ds(pl.multiple_of((1 - sub) * half, half), half)
    for k in range(3):
        keep[k] = own[k, mine, :]
        send[k] = own[k, other, :]

    def use(y0, energy):
        slope[pl.ds(y0, ROWS), :] = slope_factor[pl.ds(y0, ROWS), :] * energy

    energy_loop(
        count,
        lambda k, y: own[k, pl.ds(y, ROWS), :],
        lambda k, y: high[k, pl.ds(y, ROWS), :],
        use,
    )


def scale_kernel(*refs):
    slopes, (chain_factor, scaled, same, cross) = refs[:-4], refs[-4:]
    sub = lax.axis_index("sub")
    total = slopes[0][...]
    for other in slopes[1:]:
        total = total + other[...]
    scaled[...] = total * chain_factor[...]
    window = same.shape[0]
    shift = scaled.shape[0] - window
    same[...] = scaled[pl.ds(pl.multiple_of(sub * shift, 8), window), :]
    cross[...] = scaled[pl.ds(pl.multiple_of((1 - sub) * shift, 8), window), :]


def gradient_kernel(scaled, outer, far, partner, gradient, planes, sums):
    sub = lax.axis_index("sub")
    window = partner.shape[0]
    shift = scaled.shape[0] - window
    mine = scaled[pl.ds(pl.multiple_of(sub * shift, 8), window), :]

    @pl.when(sub == 0)
    def _():
        planes[0] = outer[...]
        planes[1] = mine
        planes[2] = partner[...]
        planes[3] = far[...]

    @pl.when(sub == 1)
    def _():
        planes[0] = far[...]
        planes[1] = partner[...]
        planes[2] = mine
        planes[3] = outer[...]

    half = gradient.shape[1]
    part = pl.ds(pl.multiple_of(sub * (window - half), 8), half)
    for layer in range(2):
        sums[...] = filter_planes(planes[layer], planes[layer + 1], planes[layer + 2])
        gradient[layer] = sums[part, :]


def call(body, outs, scratch=(), name=None, work=False):
    cost = pl.CostEstimate(flops=10**7, bytes_accessed=4 * 10**6, transcendentals=0)
    return pl.pallas_call(
        body,
        out_shape=[jax.ShapeDtypeStruct(shape, jnp.float32) for shape in outs],
        scratch_shapes=[pltpu.VMEM(shape, jnp.float32) for shape in scratch],
        compiler_params=pltpu.CompilerParams(vmem_limit_bytes=16 * 2**20),
        cost_estimate=cost if work else None,
        name=name,
    )


def routes(mods, slabs):
    chips = mods * slabs

    def at(chip, sub):
        return 2 * chip + sub

    def beside(chip, steps, cyclic):
        target = chip + steps
        if cyclic:
            return target % chips
        return target if 0 <= target < chips else None

    def built(moves, cyclic):
        pairs = []
        for chip in range(chips):
            for sub, steps, to in moves:
                target = beside(chip, steps, cyclic)
                if target is not None:
                    pairs.append((at(chip, sub), at(target, to)))
        return pairs

    def in_module(moves):
        pairs = []
        for chip in range(chips):
            mod, slab = divmod(chip, slabs)
            for sub, steps, to in moves:
                pairs.append((at(chip, sub), at(mod * slabs + (slab + steps) % slabs, to)))
        return pairs

    return dict(
        swap=built([(0, 0, 1), (1, 0, 0)], True),
        first=built([(0, 1, 0), (1, -1, 1)], True),
        second=built([(1, 1, 0), (0, -1, 1)], True),
        third=built([(0, 1, 1), (1, 1, 0)], True),
        fourth=built([(0, 1, 0), (1, 1, 1)], True),
        outer=built([(1, 1, 0), (0, -1, 1)], False),
        down=built([(0, -1, 1)], False),
        across=built([(1, 0, 0)], False),
        halo_cross=in_module([(1, 1, 0), (0, -1, 1)]),
        halo_same=in_module([(0, -1, 0), (1, 1, 1)]),
    )


def module_routes(mods):
    if mods & (mods - 1) == 0:
        return [[(m, m ^ s) for m in range(mods)] for s in range(1, mods)]
    return [[(m, (m + s) % mods) for m in range(mods)] for s in range(1, mods)]


def local(mods, slabs, design, fixed, load):
    half, width = design.shape[1:]
    count = 2 * half
    path = routes(mods, slabs)

    def move(value, name):
        return lax.ppermute(value, AXES, path[name])

    plane = (count, width)
    layer = (3, count, width)
    block = (half, width)
    free = (1 - fixed).astype(jnp.float32)
    swap, first, second, third, fourth, own = call(
        prepare_kernel,
        [(11,) + block, (4,) + block, (4,) + block, block, block, (11,) + block],
        name="prepare",
    )(free, load, design)
    first = move(first, "first")
    second = move(second, "second")
    third = move(third, "third")
    fourth = move(fourth, "fourth")
    swap = move(swap, "swap")

    def start_body(*refs):
        start_outer_kernel(mods, slabs, *refs)

    v0, v0_inner, free, fields, parts = call(
        start_inner_kernel,
        [layer, layer, layer, (12,) + plane, (3,) + plane],
        [(2,) + plane],
        name="start_inner",
        work=True,
    )(own, swap)
    v1, v0_high, mod_inner, mod_outer, mod_own, slope_factor, chain_factor, moments = call(
        start_body,
        [layer, layer, plane, plane, plane, plane, plane, (8, width)],
        [layer, plane, plane],
        name="start_outer",
    )(first, second, third, fourth, v0, v0_inner, free, fields, parts)
    outer = move(v1, "outer")
    inner = move(v1, "swap")
    (fields,) = call(second_inner_kernel, [(12,) + plane], name="second_inner", work=True)(v1, inner)
    v2, v1_high, moments = call(
        second_outer_kernel, [layer, layer, (8, width)], name="second_outer"
    )(v1, outer, inner, fields, free, mod_inner, mod_outer, moments)
    v2_outer = move(v2, "down")
    v2_inner = move(v2, "across")
    moments, v2_high = call(third_kernel, [(8, width), layer], name="third")(
        v2_outer, v2_inner, v2, mod_own, moments
    )
    devices = 2 * mods * slabs
    gathered = lax.all_to_all(
        jnp.broadcast_to(moments, (devices, 8, width)), AXES, 0, 0, tiled=True
    )
    slope, keep, send = call(
        combine_kernel, [plane, (3, half, width), (3, half, width)], [layer, layer], name="combine"
    )(gathered, v0, v0_high, v1, v1_high, v2, v2_high, slope_factor)
    slopes = [slope] + [lax.ppermute(slope, "mod", pairs) for pairs in module_routes(mods)]
    received = move(send, "swap")
    window = half + 8
    scaled, same, cross = call(
        scale_kernel, [plane, (window, width), (window, width)], name="scale"
    )(*slopes, chain_factor)
    outer = move(cross, "halo_cross")
    far = move(same, "halo_same")
    partner = move(cross, "swap")
    even = lax.axis_index("sub") == 0
    displacement = jnp.stack(
        [jnp.where(even, keep, received), jnp.where(even, received, keep)], axis=1
    )
    (gradient,) = call(
        gradient_kernel, [(2, half, width)], [(4, window, width), (window, width)], name="gradient"
    )(scaled, outer, far, partner)
    return displacement, gradient


def solution(mesh):
    mods, slabs = mesh.shape["mod"], mesh.shape["slab"]
    assert mesh.shape["sub"] == 2
    deck = P(None, ("mod", "slab"), "sub", None)

    def body(design, fixed_mask, load_mask):
        return local(mods, slabs, design, fixed_mask, load_mask)

    return jax.shard_map(
        body,
        mesh=mesh,
        in_specs=(P("slab", "sub", None), deck, deck),
        out_specs=(deck, P("slab", "sub", None)),
        check_vma=False,
    )
```

```python
import math

import jax
import jax.numpy as jnp
import numpy as np
from jax import lax
from jax.experimental import pallas as pl
from jax.experimental.pallas import tpu as pltpu
from jax.sharding import PartitionSpec as P

stiff_floor = 0.01
penalty = 3.0
sharpness = 4.0
threshold = 0.5
filter_reach = 1.8

AXES = ("mod", "slab", "sub")
ROWS = 8
FACE = filter_reach - 1.0
EDGE = filter_reach - math.sqrt(2.0)
CORNER = filter_reach - math.sqrt(3.0)
LOWER = math.tanh(sharpness * threshold)
UPPER = math.tanh(sharpness * (1.0 - threshold))


def stiffness_modes():
    poisson = 0.3
    lame = poisson / ((1.0 + poisson) * (1.0 - 2.0 * poisson))
    shear = 1.0 / (2.0 * (1.0 + poisson))
    elastic = np.zeros((6, 6))
    elastic[:3, :3] = lame
    for axis in range(3):
        elastic[axis, axis] += 2.0 * shear
        elastic[axis + 3, axis + 3] = shear
    offset = 0.5 / math.sqrt(3.0)
    points = [0.5 - offset, 0.5 + offset]
    stiffness = np.zeros((24, 24))
    for point in ((a, b, c) for a in points for b in points for c in points):
        strain = np.zeros((6, 24))
        for corner in range(8):
            bits = (corner >> 2 & 1, corner >> 1 & 1, corner & 1)
            along = [point[a] if bits[a] else 1.0 - point[a] for a in range(3)]
            sign = [1.0 if bits[a] else -1.0 for a in range(3)]
            gx = sign[0] * along[1] * along[2]
            gy = along[0] * sign[1] * along[2]
            gz = along[0] * along[1] * sign[2]
            col = 3 * corner
            strain[0, col] = gx
            strain[1, col + 1] = gy
            strain[2, col + 2] = gz
            strain[3, col], strain[3, col + 1] = gy, gx
            strain[4, col + 1], strain[4, col + 2] = gz, gy
            strain[5, col], strain[5, col + 2] = gz, gx
        stiffness += strain.T @ elastic @ strain / 8.0
    basis = np.zeros((24, 24))
    for mode in range(8):
        for corner in range(8):
            value = 1.0
            for bit in range(3):
                if mode >> bit & 1 and not corner >> bit & 1:
                    value = -value
            for k in range(3):
                basis[3 * mode + k, 3 * corner + k] = value
    table = basis @ stiffness @ basis.T / 64.0
    table[np.abs(table) < 1e-9] = 0.0
    return table


TABLE = stiffness_modes()


def lanes(shape):
    return lax.broadcasted_iota(jnp.int32, shape, 1)


def rows(shape):
    return lax.broadcasted_iota(jnp.int32, shape, 0)


def z_up(x):
    return jnp.where(lanes(x.shape) < x.shape[1] - 1, pltpu.roll(x, x.shape[1] - 1, 1), 0.0)


def z_down(x):
    return jnp.where(lanes(x.shape) > 0, pltpu.roll(x, 1, 1), 0.0)


def y_up(x):
    return jnp.where(rows(x.shape) < x.shape[0] - 1, pltpu.roll(x, x.shape[0] - 1, 0), 0.0)


def y_down(x):
    return jnp.where(rows(x.shape) > 0, pltpu.roll(x, 1, 0), 0.0)


def two_rows(read, y0, count):
    here = read(y0)
    above = y_up(here) if y0 + ROWS == count else read(y0 + 1)
    return here, above


def face_modes(here, above):
    out = []
    for part in (here + above, above - here):
        shifted = z_up(part)
        out += [part + shifted, shifted - part]
    return out


def element_modes(own, other, side):
    sums = [[other[k][m] + own[k][m] for m in range(4)] for k in range(3)]
    diffs = [[(other[k][m] - own[k][m]) * side for m in range(4)] for k in range(3)]
    return [sums[k] + diffs[k] for k in range(3)]


def mode_forces(q):
    made = {}

    def scaled(j, value):
        key = (j, round(value, 12))
        if key not in made:
            made[key] = q[j % 3][j // 3] * np.float32(value)
        return made[key]

    out = [[None] * 8 for _ in range(3)]
    for i in range(24):
        total = None
        for j in np.nonzero(TABLE[i])[0]:
            term = scaled(int(j), float(TABLE[i, j]))
            total = term if total is None else total + term
        out[i % 3][i // 3] = total
    return out


def element_energy(q):
    r = mode_forces(q)
    total = None
    for k in range(3):
        for m in range(1, 8):
            term = q[k][m] * r[k][m]
            total = term if total is None else total + term
    return total


def own_fields(own, other, side):
    r = mode_forces(element_modes(own, other, side))
    fields = []
    for k in range(3):
        for m in range(4):
            d = r[k][m + 4] * side
            fields.append(-d if r[k][m] is None else r[k][m] - d)
    return fields


def layer_modes(read, y0, count):
    heres, modes = [], []
    for k in range(3):
        here, above = two_rows(lambda y, k=k: read(k, y), y0, count)
        heres.append(here)
        modes.append(face_modes(here, above))
    return heres, modes


def fields_loop(count, read_own, read_other, side, fields):
    for y0 in range(0, count, ROWS):
        _, own = layer_modes(read_own, y0, count)
        _, other = layer_modes(read_other, y0, count)
        for n, value in enumerate(own_fields(own, other, side)):
            fields[n, pl.ds(y0, ROWS), :] = value


def operator_loop(count, read_own, read_other, side, fields, mod_inner, mod_outer, free, out_ref):
    shape = (ROWS, out_ref.shape[2])
    square = jnp.zeros(shape, jnp.float32)
    cross = jnp.zeros(shape, jnp.float32)
    norm = jnp.zeros(shape, jnp.float32)
    carry = [jnp.zeros(shape, jnp.float32)] * 3
    first = rows(shape) == 0
    for y0 in range(0, count, ROWS):
        part = pl.ds(y0, ROWS)
        owns, own = layer_modes(read_own, y0, count)
        _, other = layer_modes(read_other, y0, count)
        inner, outer = mod_inner[part, :], mod_outer[part, :]
        total = [
            outer * value + inner * fields[n, part, :]
            for n, value in enumerate(own_fields(own, other, side))
        ]
        for k in range(3):
            faces = []
            for py in range(2):
                s, d = total[4 * k + 2 * py], total[4 * k + 2 * py + 1]
                faces.append((s - d) + z_down(s + d))
            rolled = pltpu.roll(faces[0] + faces[1], 1, 0)
            force = (faces[0] - faces[1]) + jnp.where(first, carry[k], rolled)
            carry[k] = rolled
            image = free[k, part, :] * force
            out_ref[k, part, :] = image
            square += image * image
            cross += owns[k] * image
            norm += owns[k] * owns[k]
    return norm, cross, square


def energy_loop(count, read_own, read_high, use):
    for y0 in range(0, count, ROWS):
        _, own = layer_modes(read_own, y0, count)
        _, high = layer_modes(read_high, y0, count)
        use(y0, element_energy(element_modes(own, high, 1.0)))


def rows_of(ref):
    return lambda k, y: ref[k, pl.ds(y, ROWS), :]


def inner_side(sub):
    return jnp.where(sub == 0, 1.0, -1.0).astype(jnp.float32)


def line(tile):
    return jnp.sum(tile, axis=0, keepdims=True)


def prepare_kernel(free, load, design, swap, first, second, third, fourth, own):
    sub = lax.axis_index("sub")
    for k in range(3):
        frees = [free[k, layer] for layer in range(2)]
        values = [frees[layer] * load[k, layer].astype(jnp.float32) for layer in range(2)]
        for layer in range(2):
            swap[2 * k + layer] = values[layer]
            own[2 * k + layer] = values[layer]
        low = sub == 0
        swap[6 + k] = jnp.where(low, frees[1], frees[0])
        own[6 + k] = jnp.where(low, frees[0], frees[1])
        first[k] = jnp.where(low, values[1], values[0])
        second[k] = jnp.where(low, values[0], values[1])
    low = sub == 0
    for layer in range(2):
        swap[9 + layer] = design[layer]
        own[9 + layer] = design[layer]
    later = jnp.where(low, design[1], design[0])
    sooner = jnp.where(low, design[0], design[1])
    first[3] = later
    third[...] = later
    second[3] = sooner
    fourth[...] = sooner


def around(p):
    across = y_up(p) + y_down(p)
    return across + z_up(p) + z_down(p), z_up(across) + z_down(across)


def filter_mid(p):
    face, diag = around(p)
    return filter_reach * p + FACE * face + EDGE * diag


def filter_side(p):
    face, diag = around(p)
    return FACE * p + EDGE * face + CORNER * diag


def filter_planes(low, mid, high):
    return filter_side(low + high) + filter_mid(mid)


def weight_plane(shape, row_offset, count):
    row = rows(shape) + row_offset
    lane = lanes(shape)

    def neighbours(index, size):
        return jnp.where(index > 0, 1.0, 0.0) + jnp.where(index < size - 1, 1.0, 0.0)

    ry = neighbours(row, count)
    rz = neighbours(lane, shape[1])
    face, diag = ry + rz, ry * rz
    return (
        filter_reach
        + FACE * (2.0 + face)
        + EDGE * (2.0 * face + diag)
        + (2.0 * CORNER) * diag
    )


def start_inner_kernel(own, swap, v0, v0_inner, free, fields, parts, layers):
    sub = lax.axis_index("sub")
    half = own.shape[1]
    count = 2 * half
    mine = pl.ds(pl.multiple_of(sub * half, half), half)
    other = pl.ds(pl.multiple_of((1 - sub) * half, half), half)
    for layer in range(2):
        layers[layer, mine, :] = own[9 + layer]
        layers[layer, other, :] = swap[9 + layer]

    @pl.when(sub == 0)
    def _():
        parts[0] = filter_side(layers[0])
        parts[1] = filter_mid(layers[0]) + filter_side(layers[1])

    @pl.when(sub == 1)
    def _():
        parts[0] = filter_mid(layers[0]) + filter_side(layers[1])
        parts[1] = filter_side(layers[0]) + filter_mid(layers[1])

    parts[2] = 1.0 / weight_plane((count, own.shape[2]), 0, count)
    for k in range(3):
        free[k, mine, :] = own[6 + k]
        free[k, other, :] = swap[6 + k]
        v0[k, mine, :] = own[2 * k + sub]
        v0[k, other, :] = swap[2 * k + sub]
        v0_inner[k, mine, :] = own[2 * k + 1 - sub]
        v0_inner[k, other, :] = swap[2 * k + 1 - sub]
    fields_loop(count, rows_of(v0), rows_of(v0_inner), inner_side(sub), fields)


def start_outer_kernel(
    mods, slabs,
    first, second, third, fourth, v0, v0_inner, free, fields, parts,
    v1, v0_high, mod_inner, mod_outer, mod_own, slope_factor, chain_factor, moments,
    v0_outer, near, deep,
):
    mod, slab, sub = (lax.axis_index(a) for a in AXES)
    half = third.shape[0]
    count = 2 * half
    even = sub == 0
    mine = pl.ds(pl.multiple_of(sub * half, half), half)
    other = pl.ds(pl.multiple_of((1 - sub) * half, half), half)
    near[mine, :] = first[3]
    near[other, :] = second[3]
    deep[mine, :] = fourth[...]
    deep[other, :] = third[...]
    starts = (mod == 0) & (slab == 0) & even
    ends = (mod == mods - 1) & (slab == slabs - 1) & (sub == 1)
    inside = jnp.where(ends, 0.0, 1.0)
    for k in range(3):
        v0_outer[k, mine, :] = first[k] * inside
        v0_outer[k, other, :] = second[k] * inside
        v0_high[k] = jnp.where(even, v0_inner[k], v0_outer[k])

    side = filter_side(near[...])
    mid = filter_mid(near[...])
    inverse = parts[2]
    filtered = (parts[0] + filter_side(deep[...]) + jnp.where(even, mid, 0.0)) * inverse
    hyper = jnp.tanh(sharpness * (filtered - threshold))
    projected = (LOWER + hyper) * (1.0 / (LOWER + UPPER))
    below = stiff_floor + (1.0 - stiff_floor) * projected * projected * projected
    below = below * jnp.where(starts, 0.0, 1.0)
    filtered = (parts[1] + side) * inverse
    hyper = jnp.tanh(sharpness * (filtered - threshold))
    projected = (LOWER + hyper) * (1.0 / (LOWER + UPPER))
    squared = projected * projected
    stiff = stiff_floor + (1.0 - stiff_floor) * squared * projected
    mod_own[...] = stiff
    mod_inner[...] = jnp.where(even, stiff, below)
    mod_outer[...] = jnp.where(even, below, stiff)
    slope_factor[...] = (-penalty * (1.0 - stiff_floor)) * squared
    chain_factor[...] = (sharpness / (LOWER + UPPER)) * (1.0 - hyper * hyper) * inverse

    norm, cross, square = operator_loop(
        count, rows_of(v0), rows_of(v0_outer), -inner_side(sub), fields, mod_inner, mod_outer, free, v1
    )
    moments[...] = jnp.concatenate(
        [line(norm), line(cross), line(square), jnp.zeros((5, norm.shape[1]), jnp.float32)], axis=0
    )


def second_inner_kernel(v1, inner, fields):
    fields_loop(v1.shape[1], rows_of(v1), rows_of(inner), inner_side(lax.axis_index("sub")), fields)


def second_outer_kernel(
    v1, outer, inner, fields, free, mod_inner, mod_outer, before, v2, v1_high, moments
):
    sub = lax.axis_index("sub")
    count = v1.shape[1]
    for k in range(3):
        v1_high[k] = jnp.where(sub == 0, inner[k], outer[k])
    _, cross, square = operator_loop(
        count, rows_of(v1), rows_of(outer), -inner_side(sub), fields, mod_inner, mod_outer, free, v2
    )
    zero = jnp.zeros((3, cross.shape[1]), jnp.float32)
    moments[...] = before[...] + jnp.concatenate(
        [zero, line(cross), line(square), zero], axis=0
    )


def third_kernel(v2_outer, v2_inner, v2, mod_own, before, moments, v2_high):
    even = lax.axis_index("sub") == 0
    for k in range(3):
        v2_high[k] = jnp.where(even, v2_inner[k], v2_outer[k])
    count = v2.shape[1]
    total = [jnp.zeros((ROWS, v2.shape[2]), jnp.float32)]

    def use(y0, energy):
        total[0] += energy * mod_own[pl.ds(y0, ROWS), :]

    energy_loop(
        count,
        lambda k, y: v2[k, pl.ds(y, ROWS), :],
        lambda k, y: v2_high[k, pl.ds(y, ROWS), :],
        use,
    )
    width = v2.shape[2]
    moments[...] = before[...] + jnp.concatenate(
        [
            jnp.zeros((5, width), jnp.float32),
            line(total[0]),
            jnp.zeros((2, width), jnp.float32),
        ],
        axis=0,
    )


def coefficients(m):
    step = m[0] / m[1]
    x0 = step
    r1 = -step
    norm = m[0] + 2.0 * r1 * m[1] + r1 * r1 * m[2]
    ratio = norm / m[0]
    p0, p1 = 1.0 + ratio, r1
    step = norm / (p0 * p0 * m[1] + 2.0 * p0 * p1 * m[2] + p1 * p1 * m[3])
    x0, x1 = x0 + step * p0, step * p1
    r1, r2 = r1 - step * p0, -step * p1
    after = (
        m[0]
        + 2.0 * r1 * m[1]
        + (r1 * r1 + 2.0 * r2) * m[2]
        + 2.0 * r1 * r2 * m[3]
        + r2 * r2 * m[4]
    )
    ratio = after / norm
    p0, p1, p2 = 1.0 + ratio * p0, r1 + ratio * p1, r2
    step = after / (
        p0 * p0 * m[1]
        + 2.0 * p0 * p1 * m[2]
        + (p1 * p1 + 2.0 * p0 * p2) * m[3]
        + 2.0 * p1 * p2 * m[4]
        + p2 * p2 * m[5]
    )
    return x0 + step * p0, x1 + step * p1, step * p2


def combine_kernel(
    gathered, v0, v0_high, v1, v1_high, v2, v2_high, slope_factor, slope, factors, own, high
):
    count = v0.shape[1]
    sums = jnp.sum(jnp.sum(gathered[...], axis=0), axis=1, keepdims=True)
    c0, c1, c2 = coefficients([sums[k : k + 1] for k in range(6)])
    for n, c in enumerate((c0, c1, c2)):
        factors[n] = jnp.broadcast_to(c, factors.shape[1:])
    for k in range(3):
        own[k] = c0 * v0[k] + c1 * v1[k] + c2 * v2[k]
        high[k] = c0 * v0_high[k] + c1 * v1_high[k] + c2 * v2_high[k]

    def use(y0, energy):
        slope[pl.ds(y0, ROWS), :] = slope_factor[pl.ds(y0, ROWS), :] * energy

    energy_loop(count, rows_of(own), rows_of(high), use)


def displace_kernel(factors, v0, v0_inner, v1, v1_inner, v2, v2_inner, displacement):
    sub = lax.axis_index("sub")
    half = displacement.shape[2]
    mine = pl.ds(pl.multiple_of(sub * half, half), half)
    c0, c1, c2 = (factors[n][:1, :1] for n in range(3))
    for k in range(3):
        displacement[k, sub] = c0 * v0[k, mine, :] + c1 * v1[k, mine, :] + c2 * v2[k, mine, :]
        displacement[k, 1 - sub] = (
            c0 * v0_inner[k, mine, :] + c1 * v1_inner[k, mine, :] + c2 * v2_inner[k, mine, :]
        )


def scale_kernel(*refs):
    slopes, (chain_factor, scaled, same, cross, across) = refs[:-5], refs[-5:]
    sub = lax.axis_index("sub")
    total = slopes[0][...]
    for other in slopes[1:]:
        total = total + other[...]
    scaled[...] = total * chain_factor[...]
    window = same.shape[0]
    shift = scaled.shape[0] - window
    same[...] = scaled[pl.ds(pl.multiple_of(sub * shift, 8), window), :]
    cross[...] = scaled[pl.ds(pl.multiple_of((1 - sub) * shift, 8), window), :]
    across[...] = cross[...]


def gradient_kernel(scaled, outer, far, partner, gradient, planes, sums):
    sub = lax.axis_index("sub")
    window = partner.shape[0]
    shift = scaled.shape[0] - window
    mine = scaled[pl.ds(pl.multiple_of(sub * shift, 8), window), :]

    @pl.when(sub == 0)
    def _():
        planes[0] = outer[...]
        planes[1] = mine
        planes[2] = partner[...]
        planes[3] = far[...]

    @pl.when(sub == 1)
    def _():
        planes[0] = far[...]
        planes[1] = partner[...]
        planes[2] = mine
        planes[3] = outer[...]

    half = gradient.shape[1]
    part = pl.ds(pl.multiple_of(sub * (window - half), 8), half)
    for layer in range(2):
        sums[...] = filter_planes(planes[layer], planes[layer + 1], planes[layer + 2])
        gradient[layer] = sums[part, :]


def call(body, outs, scratch=(), name=None, work=False):
    cost = pl.CostEstimate(flops=10**7, bytes_accessed=4 * 10**6, transcendentals=0)
    return pl.pallas_call(
        body,
        out_shape=[jax.ShapeDtypeStruct(shape, jnp.float32) for shape in outs],
        scratch_shapes=[pltpu.VMEM(shape, jnp.float32) for shape in scratch],
        compiler_params=pltpu.CompilerParams(vmem_limit_bytes=16 * 2**20),
        cost_estimate=cost if work else None,
        name=name,
    )


def routes(mods, slabs):
    chips = mods * slabs

    def at(chip, sub):
        return 2 * chip + sub

    def beside(chip, steps, cyclic):
        target = chip + steps
        if cyclic:
            return target % chips
        return target if 0 <= target < chips else None

    def built(moves, cyclic):
        pairs = []
        for chip in range(chips):
            for sub, steps, to in moves:
                target = beside(chip, steps, cyclic)
                if target is not None:
                    pairs.append((at(chip, sub), at(target, to)))
        return pairs

    def in_module(moves):
        pairs = []
        for chip in range(chips):
            mod, slab = divmod(chip, slabs)
            for sub, steps, to in moves:
                pairs.append((at(chip, sub), at(mod * slabs + (slab + steps) % slabs, to)))
        return pairs

    return dict(
        swap=built([(0, 0, 1), (1, 0, 0)], True),
        first=built([(0, 1, 0), (1, -1, 1)], True),
        second=built([(1, 1, 0), (0, -1, 1)], True),
        third=built([(0, 1, 1), (1, 1, 0)], True),
        fourth=built([(0, 1, 0), (1, 1, 1)], True),
        outer=built([(1, 1, 0), (0, -1, 1)], False),
        down=built([(0, -1, 1)], False),
        halo_cross=in_module([(1, 1, 0), (0, -1, 1)]),
        halo_same=in_module([(0, -1, 0), (1, 1, 1)]),
    )


def module_routes(mods):
    if mods & (mods - 1) == 0:
        return [[(m, m ^ s) for m in range(mods)] for s in range(1, mods)]
    return [[(m, (m + s) % mods) for m in range(mods)] for s in range(1, mods)]


def local(mods, slabs, design, fixed, load):
    half, width = design.shape[1:]
    count = 2 * half
    path = routes(mods, slabs)

    def move(value, name):
        return lax.ppermute(value, AXES, path[name])

    plane = (count, width)
    layer = (3, count, width)
    block = (half, width)
    free = (1 - fixed).astype(jnp.float32)
    swap, first, second, third, fourth, own = call(
        prepare_kernel,
        [(11,) + block, (4,) + block, (4,) + block, block, block, (11,) + block],
        name="prepare",
    )(free, load, design)
    first = move(first, "first")
    second = move(second, "second")
    third = move(third, "third")
    fourth = move(fourth, "fourth")
    swap = move(swap, "swap")

    def start_body(*refs):
        start_outer_kernel(mods, slabs, *refs)

    v0, v0_inner, free, fields, parts = call(
        start_inner_kernel,
        [layer, layer, layer, (12,) + plane, (3,) + plane],
        [(2,) + plane],
        name="start_inner",
        work=True,
    )(own, swap)
    v1, v0_high, mod_inner, mod_outer, mod_own, slope_factor, chain_factor, moments = call(
        start_body,
        [layer, layer, plane, plane, plane, plane, plane, (8, width)],
        [layer, plane, plane],
        name="start_outer",
    )(first, second, third, fourth, v0, v0_inner, free, fields, parts)
    outer = move(v1, "outer")
    inner = move(v1, "swap")
    (fields,) = call(second_inner_kernel, [(12,) + plane], name="second_inner", work=True)(v1, inner)
    v2, v1_high, moments = call(
        second_outer_kernel, [layer, layer, (8, width)], name="second_outer"
    )(v1, outer, inner, fields, free, mod_inner, mod_outer, moments)
    v2_outer = move(v2, "down")
    v2_inner = move(v2, "swap")
    moments, v2_high = call(third_kernel, [(8, width), layer], name="third")(
        v2_outer, v2_inner, v2, mod_own, moments
    )
    devices = 2 * mods * slabs
    gathered = lax.all_to_all(
        jnp.broadcast_to(moments, (devices, 8, width)), AXES, 0, 0, tiled=True
    )
    slope, factors = call(
        combine_kernel, [plane, (3, 8, width)], [layer, layer], name="combine"
    )(gathered, v0, v0_high, v1, v1_high, v2, v2_high, slope_factor)
    slopes = [slope] + [lax.ppermute(slope, "mod", pairs) for pairs in module_routes(mods)]
    (displacement,) = call(displace_kernel, [(3, 2, half, width)], name="displace", work=True)(
        factors, v0, v0_inner, v1, inner, v2, v2_inner
    )
    window = half + 8
    scaled, same, cross, across = call(
        scale_kernel, [plane, (window, width), (window, width), (window, width)], name="scale"
    )(*slopes, chain_factor)
    scaled, displacement = lax.optimization_barrier((scaled, displacement))
    outer = move(cross, "halo_cross")
    far = move(same, "halo_same")
    partner = move(across, "swap")
    (gradient,) = call(
        gradient_kernel, [(2, half, width)], [(4, window, width), (window, width)], name="gradient"
    )(scaled, outer, far, partner)
    return displacement, gradient


def solution(mesh):
    mods, slabs = mesh.shape["mod"], mesh.shape["slab"]
    assert mesh.shape["sub"] == 2
    deck = P(None, ("mod", "slab"), "sub", None)

    def body(design, fixed_mask, load_mask):
        return local(mods, slabs, design, fixed_mask, load_mask)

    return jax.shard_map(
        body,
        mesh=mesh,
        in_specs=(P("slab", "sub", None), deck, deck),
        out_specs=(deck, P("slab", "sub", None)),
        check_vma=False,
    )
```

```python
import math

import jax
import jax.numpy as jnp
import numpy as np
from jax import lax
from jax.experimental import pallas as pl
from jax.experimental.pallas import tpu as pltpu
from jax.sharding import PartitionSpec as P

stiff_floor = 0.01
penalty = 3.0
sharpness = 4.0
threshold = 0.5
filter_reach = 1.8

AXES = ("mod", "slab", "sub")
ROWS = 8
FACE = filter_reach - 1.0
EDGE = filter_reach - math.sqrt(2.0)
CORNER = filter_reach - math.sqrt(3.0)
LOWER = math.tanh(sharpness * threshold)
UPPER = math.tanh(sharpness * (1.0 - threshold))


def stiffness_modes():
    poisson = 0.3
    lame = poisson / ((1.0 + poisson) * (1.0 - 2.0 * poisson))
    shear = 1.0 / (2.0 * (1.0 + poisson))
    elastic = np.zeros((6, 6))
    elastic[:3, :3] = lame
    for axis in range(3):
        elastic[axis, axis] += 2.0 * shear
        elastic[axis + 3, axis + 3] = shear
    offset = 0.5 / math.sqrt(3.0)
    points = [0.5 - offset, 0.5 + offset]
    stiffness = np.zeros((24, 24))
    for point in ((a, b, c) for a in points for b in points for c in points):
        strain = np.zeros((6, 24))
        for corner in range(8):
            bits = (corner >> 2 & 1, corner >> 1 & 1, corner & 1)
            along = [point[a] if bits[a] else 1.0 - point[a] for a in range(3)]
            sign = [1.0 if bits[a] else -1.0 for a in range(3)]
            gx = sign[0] * along[1] * along[2]
            gy = along[0] * sign[1] * along[2]
            gz = along[0] * along[1] * sign[2]
            col = 3 * corner
            strain[0, col] = gx
            strain[1, col + 1] = gy
            strain[2, col + 2] = gz
            strain[3, col], strain[3, col + 1] = gy, gx
            strain[4, col + 1], strain[4, col + 2] = gz, gy
            strain[5, col], strain[5, col + 2] = gz, gx
        stiffness += strain.T @ elastic @ strain / 8.0
    basis = np.zeros((24, 24))
    for mode in range(8):
        for corner in range(8):
            value = 1.0
            for bit in range(3):
                if mode >> bit & 1 and not corner >> bit & 1:
                    value = -value
            for k in range(3):
                basis[3 * mode + k, 3 * corner + k] = value
    table = basis @ stiffness @ basis.T / 64.0
    table[np.abs(table) < 1e-9] = 0.0
    return table


TABLE = stiffness_modes()


def lanes(shape):
    return lax.broadcasted_iota(jnp.int32, shape, 1)


def rows(shape):
    return lax.broadcasted_iota(jnp.int32, shape, 0)


def z_up(x):
    return jnp.where(lanes(x.shape) < x.shape[1] - 1, pltpu.roll(x, x.shape[1] - 1, 1), 0.0)


def z_down(x):
    return jnp.where(lanes(x.shape) > 0, pltpu.roll(x, 1, 1), 0.0)


def y_up(x):
    return jnp.where(rows(x.shape) < x.shape[0] - 1, pltpu.roll(x, x.shape[0] - 1, 0), 0.0)


def y_down(x):
    return jnp.where(rows(x.shape) > 0, pltpu.roll(x, 1, 0), 0.0)


def two_rows(read, y0, count):
    here = read(y0)
    above = y_up(here) if y0 + ROWS == count else read(y0 + 1)
    return here, above


def face_modes(here, above):
    out = []
    for part in (here + above, above - here):
        shifted = z_up(part)
        out += [part + shifted, shifted - part]
    return out


def element_modes(own, other, side):
    sums = [[other[k][m] + own[k][m] for m in range(4)] for k in range(3)]
    diffs = [[(other[k][m] - own[k][m]) * side for m in range(4)] for k in range(3)]
    return [sums[k] + diffs[k] for k in range(3)]


def mode_forces(q):
    made = {}

    def scaled(j, value):
        key = (j, round(value, 12))
        if key not in made:
            made[key] = q[j % 3][j // 3] * np.float32(value)
        return made[key]

    out = [[None] * 8 for _ in range(3)]
    for i in range(24):
        total = None
        for j in np.nonzero(TABLE[i])[0]:
            term = scaled(int(j), float(TABLE[i, j]))
            total = term if total is None else total + term
        out[i % 3][i // 3] = total
    return out


def element_energy(q):
    r = mode_forces(q)
    total = None
    for k in range(3):
        for m in range(1, 8):
            term = q[k][m] * r[k][m]
            total = term if total is None else total + term
    return total


def own_fields(own, other, side):
    r = mode_forces(element_modes(own, other, side))
    fields = []
    for k in range(3):
        for m in range(4):
            d = r[k][m + 4] * side
            fields.append(-d if r[k][m] is None else r[k][m] - d)
    return fields


def layer_modes(read, y0, count):
    heres, modes = [], []
    for k in range(3):
        here, above = two_rows(lambda y, k=k: read(k, y), y0, count)
        heres.append(here)
        modes.append(face_modes(here, above))
    return heres, modes


def fields_loop(count, read_own, read_other, side, fields):
    for y0 in range(0, count, ROWS):
        _, own = layer_modes(read_own, y0, count)
        _, other = layer_modes(read_other, y0, count)
        for n, value in enumerate(own_fields(own, other, side)):
            fields[n, pl.ds(y0, ROWS), :] = value


def operator_loop(count, read_own, read_other, side, fields, mod_inner, mod_outer, free, out_ref):
    shape = (ROWS, out_ref.shape[2])
    square = jnp.zeros(shape, jnp.float32)
    cross = jnp.zeros(shape, jnp.float32)
    norm = jnp.zeros(shape, jnp.float32)
    carry = [jnp.zeros(shape, jnp.float32)] * 3
    first = rows(shape) == 0
    for y0 in range(0, count, ROWS):
        part = pl.ds(y0, ROWS)
        owns, own = layer_modes(read_own, y0, count)
        _, other = layer_modes(read_other, y0, count)
        inner, outer = mod_inner[part, :], mod_outer[part, :]
        total = [
            outer * value + inner * fields[n, part, :]
            for n, value in enumerate(own_fields(own, other, side))
        ]
        for k in range(3):
            faces = []
            for py in range(2):
                s, d = total[4 * k + 2 * py], total[4 * k + 2 * py + 1]
                faces.append((s - d) + z_down(s + d))
            rolled = pltpu.roll(faces[0] + faces[1], 1, 0)
            force = (faces[0] - faces[1]) + jnp.where(first, carry[k], rolled)
            carry[k] = rolled
            image = free[k, part, :] * force
            out_ref[k, part, :] = image
            square += image * image
            cross += owns[k] * image
            norm += owns[k] * owns[k]
    return norm, cross, square


def energy_loop(count, read_own, read_high, use):
    for y0 in range(0, count, ROWS):
        _, own = layer_modes(read_own, y0, count)
        _, high = layer_modes(read_high, y0, count)
        use(y0, element_energy(element_modes(own, high, 1.0)))


def rows_of(ref):
    return lambda k, y: ref[k, pl.ds(y, ROWS), :]


def inner_side(sub):
    return jnp.where(sub == 0, 1.0, -1.0).astype(jnp.float32)


def line(tile):
    return jnp.sum(tile, axis=0, keepdims=True)


def prepare_kernel(free, load, design, swap, first, second, third, fourth, own):
    sub = lax.axis_index("sub")
    for k in range(3):
        frees = [free[k, layer] for layer in range(2)]
        values = [frees[layer] * load[k, layer].astype(jnp.float32) for layer in range(2)]
        for layer in range(2):
            swap[2 * k + layer] = values[layer]
            own[2 * k + layer] = values[layer]
        low = sub == 0
        swap[6 + k] = jnp.where(low, frees[1], frees[0])
        own[6 + k] = jnp.where(low, frees[0], frees[1])
        first[k] = jnp.where(low, values[1], values[0])
        second[k] = jnp.where(low, values[0], values[1])
    low = sub == 0
    for layer in range(2):
        swap[9 + layer] = design[layer]
        own[9 + layer] = design[layer]
    later = jnp.where(low, design[1], design[0])
    sooner = jnp.where(low, design[0], design[1])
    first[3] = later
    third[...] = later
    second[3] = sooner
    fourth[...] = sooner


def around(p):
    across = y_up(p) + y_down(p)
    return across + z_up(p) + z_down(p), z_up(across) + z_down(across)


def filter_mid(p):
    face, diag = around(p)
    return filter_reach * p + FACE * face + EDGE * diag


def filter_side(p):
    face, diag = around(p)
    return FACE * p + EDGE * face + CORNER * diag


def filter_planes(low, mid, high):
    return filter_side(low + high) + filter_mid(mid)


def weight_plane(shape, row_offset, count):
    row = rows(shape) + row_offset
    lane = lanes(shape)

    def neighbours(index, size):
        return jnp.where(index > 0, 1.0, 0.0) + jnp.where(index < size - 1, 1.0, 0.0)

    ry = neighbours(row, count)
    rz = neighbours(lane, shape[1])
    face, diag = ry + rz, ry * rz
    return (
        filter_reach
        + FACE * (2.0 + face)
        + EDGE * (2.0 * face + diag)
        + (2.0 * CORNER) * diag
    )


def start_inner_kernel(own, swap, v0, v0_inner, free, fields, parts, layers):
    sub = lax.axis_index("sub")
    half = own.shape[1]
    count = 2 * half
    mine = pl.ds(pl.multiple_of(sub * half, half), half)
    other = pl.ds(pl.multiple_of((1 - sub) * half, half), half)
    for layer in range(2):
        layers[layer, mine, :] = own[9 + layer]
        layers[layer, other, :] = swap[9 + layer]

    @pl.when(sub == 0)
    def _():
        parts[0] = filter_side(layers[0])
        parts[1] = filter_mid(layers[0]) + filter_side(layers[1])

    @pl.when(sub == 1)
    def _():
        parts[0] = filter_mid(layers[0]) + filter_side(layers[1])
        parts[1] = filter_side(layers[0]) + filter_mid(layers[1])

    parts[2] = 1.0 / weight_plane((count, own.shape[2]), 0, count)
    for k in range(3):
        free[k, mine, :] = own[6 + k]
        free[k, other, :] = swap[6 + k]
        v0[k, mine, :] = own[2 * k + sub]
        v0[k, other, :] = swap[2 * k + sub]
        v0_inner[k, mine, :] = own[2 * k + 1 - sub]
        v0_inner[k, other, :] = swap[2 * k + 1 - sub]
    fields_loop(count, rows_of(v0), rows_of(v0_inner), inner_side(sub), fields)


def start_outer_kernel(
    first, second, third, fourth, ends_first, ends_second, v0, v0_inner, free, fields, parts,
    v1, v0_high, mod_inner, mod_outer, mod_own, slope_factor, chain_factor, moments,
    v0_outer, near, deep,
):
    mod, slab, sub = (lax.axis_index(a) for a in AXES)
    half = third.shape[0]
    count = 2 * half
    even = sub == 0
    mine = pl.ds(pl.multiple_of(sub * half, half), half)
    other = pl.ds(pl.multiple_of((1 - sub) * half, half), half)
    near[mine, :] = first[3] + ends_first[...]
    near[other, :] = second[3] + ends_second[...]
    deep[mine, :] = fourth[...]
    deep[other, :] = third[...]
    starts = (mod == 0) & (slab == 0) & even
    for k in range(3):
        v0_outer[k, mine, :] = first[k]
        v0_outer[k, other, :] = second[k]
        v0_high[k] = jnp.where(even, v0_inner[k], v0_outer[k])

    side = filter_side(near[...])
    mid = filter_mid(near[...])
    inverse = parts[2]
    filtered = (parts[0] + filter_side(deep[...]) + jnp.where(even, mid, 0.0)) * inverse
    hyper = jnp.tanh(sharpness * (filtered - threshold))
    projected = (LOWER + hyper) * (1.0 / (LOWER + UPPER))
    below = stiff_floor + (1.0 - stiff_floor) * projected * projected * projected
    below = below * jnp.where(starts, 0.0, 1.0)
    filtered = (parts[1] + side) * inverse
    hyper = jnp.tanh(sharpness * (filtered - threshold))
    projected = (LOWER + hyper) * (1.0 / (LOWER + UPPER))
    squared = projected * projected
    stiff = stiff_floor + (1.0 - stiff_floor) * squared * projected
    mod_own[...] = stiff
    mod_inner[...] = jnp.where(even, stiff, below)
    mod_outer[...] = jnp.where(even, below, stiff)
    slope_factor[...] = (-penalty * (1.0 - stiff_floor)) * squared
    chain_factor[...] = (sharpness / (LOWER + UPPER)) * (1.0 - hyper * hyper) * inverse

    norm, cross, square = operator_loop(
        count, rows_of(v0), rows_of(v0_outer), -inner_side(sub), fields, mod_inner, mod_outer, free, v1
    )
    moments[...] = jnp.concatenate(
        [line(norm), line(cross), line(square), jnp.zeros((5, norm.shape[1]), jnp.float32)], axis=0
    )


def second_inner_kernel(v1, inner, fields):
    fields_loop(v1.shape[1], rows_of(v1), rows_of(inner), inner_side(lax.axis_index("sub")), fields)


def second_outer_kernel(
    v1, outer, inner, fields, free, mod_inner, mod_outer, before, v2, v1_high, moments
):
    sub = lax.axis_index("sub")
    count = v1.shape[1]
    for k in range(3):
        v1_high[k] = jnp.where(sub == 0, inner[k], outer[k])
    _, cross, square = operator_loop(
        count, rows_of(v1), rows_of(outer), -inner_side(sub), fields, mod_inner, mod_outer, free, v2
    )
    zero = jnp.zeros((3, cross.shape[1]), jnp.float32)
    moments[...] = before[...] + jnp.concatenate(
        [zero, line(cross), line(square), zero], axis=0
    )


def third_kernel(v2_outer, v2_inner, v2, mod_own, before, moments, v2_high):
    even = lax.axis_index("sub") == 0
    for k in range(3):
        v2_high[k] = jnp.where(even, v2_inner[k], v2_outer[k])
    count = v2.shape[1]
    total = [jnp.zeros((ROWS, v2.shape[2]), jnp.float32)]

    def use(y0, energy):
        total[0] += energy * mod_own[pl.ds(y0, ROWS), :]

    energy_loop(
        count,
        lambda k, y: v2[k, pl.ds(y, ROWS), :],
        lambda k, y: v2_high[k, pl.ds(y, ROWS), :],
        use,
    )
    width = v2.shape[2]
    moments[...] = before[...] + jnp.concatenate(
        [
            jnp.zeros((5, width), jnp.float32),
            line(total[0]),
            jnp.zeros((2, width), jnp.float32),
        ],
        axis=0,
    )


def coefficients(m):
    step = m[0] / m[1]
    x0 = step
    r1 = -step
    norm = m[0] + 2.0 * r1 * m[1] + r1 * r1 * m[2]
    ratio = norm / m[0]
    p0, p1 = 1.0 + ratio, r1
    step = norm / (p0 * p0 * m[1] + 2.0 * p0 * p1 * m[2] + p1 * p1 * m[3])
    x0, x1 = x0 + step * p0, step * p1
    r1, r2 = r1 - step * p0, -step * p1
    after = (
        m[0]
        + 2.0 * r1 * m[1]
        + (r1 * r1 + 2.0 * r2) * m[2]
        + 2.0 * r1 * r2 * m[3]
        + r2 * r2 * m[4]
    )
    ratio = after / norm
    p0, p1, p2 = 1.0 + ratio * p0, r1 + ratio * p1, r2
    step = after / (
        p0 * p0 * m[1]
        + 2.0 * p0 * p1 * m[2]
        + (p1 * p1 + 2.0 * p0 * p2) * m[3]
        + 2.0 * p1 * p2 * m[4]
        + p2 * p2 * m[5]
    )
    return x0 + step * p0, x1 + step * p1, step * p2


def combine_kernel(
    gathered, v0, v0_high, v1, v1_high, v2, v2_high, slope_factor, slope, factors, own, high
):
    count = v0.shape[1]
    sums = jnp.sum(jnp.sum(gathered[...], axis=0), axis=1, keepdims=True)
    c0, c1, c2 = coefficients([sums[k : k + 1] for k in range(6)])
    for n, c in enumerate((c0, c1, c2)):
        factors[n] = jnp.broadcast_to(c, factors.shape[1:])
    for k in range(3):
        own[k] = c0 * v0[k] + c1 * v1[k] + c2 * v2[k]
        high[k] = c0 * v0_high[k] + c1 * v1_high[k] + c2 * v2_high[k]

    def use(y0, energy):
        slope[pl.ds(y0, ROWS), :] = slope_factor[pl.ds(y0, ROWS), :] * energy

    energy_loop(count, rows_of(own), rows_of(high), use)


def displace_kernel(factors, v0, v0_inner, v1, v1_inner, v2, v2_inner, displacement):
    sub = lax.axis_index("sub")
    half = displacement.shape[2]
    mine = pl.ds(pl.multiple_of(sub * half, half), half)
    c0, c1, c2 = (factors[n][:1, :1] for n in range(3))
    for k in range(3):
        displacement[k, sub] = c0 * v0[k, mine, :] + c1 * v1[k, mine, :] + c2 * v2[k, mine, :]
        displacement[k, 1 - sub] = (
            c0 * v0_inner[k, mine, :] + c1 * v1_inner[k, mine, :] + c2 * v2_inner[k, mine, :]
        )


def scale_kernel(*refs):
    slopes, (chain_factor, scaled, same, cross, across) = refs[:-5], refs[-5:]
    sub = lax.axis_index("sub")
    total = slopes[0][...]
    for other in slopes[1:]:
        total = total + other[...]
    scaled[...] = total * chain_factor[...]
    window = same.shape[0]
    shift = scaled.shape[0] - window
    same[...] = scaled[pl.ds(pl.multiple_of(sub * shift, 8), window), :]
    cross[...] = scaled[pl.ds(pl.multiple_of((1 - sub) * shift, 8), window), :]
    across[...] = cross[...]


def gradient_kernel(scaled, outer, far, partner, gradient, planes, sums):
    sub = lax.axis_index("sub")
    window = partner.shape[0]
    shift = scaled.shape[0] - window
    mine = scaled[pl.ds(pl.multiple_of(sub * shift, 8), window), :]

    @pl.when(sub == 0)
    def _():
        planes[0] = outer[...]
        planes[1] = mine
        planes[2] = partner[...]
        planes[3] = far[...]

    @pl.when(sub == 1)
    def _():
        planes[0] = far[...]
        planes[1] = partner[...]
        planes[2] = mine
        planes[3] = outer[...]

    half = gradient.shape[1]
    part = pl.ds(pl.multiple_of(sub * (window - half), 8), half)
    for layer in range(2):
        sums[...] = filter_planes(planes[layer], planes[layer + 1], planes[layer + 2])
        gradient[layer] = sums[part, :]


def call(body, outs, scratch=(), name=None, work=False):
    cost = pl.CostEstimate(flops=10**7, bytes_accessed=4 * 10**6, transcendentals=0)
    return pl.pallas_call(
        body,
        out_shape=[jax.ShapeDtypeStruct(shape, jnp.float32) for shape in outs],
        scratch_shapes=[pltpu.VMEM(shape, jnp.float32) for shape in scratch],
        compiler_params=pltpu.CompilerParams(vmem_limit_bytes=16 * 2**20),
        cost_estimate=cost if work else None,
        name=name,
    )


def routes(mods, slabs):
    chips = mods * slabs

    def at(chip, sub):
        return 2 * chip + sub

    last = (mods - 1) * slabs

    def beside(chip, steps, cyclic):
        target = chip + steps
        if cyclic:
            return target % chips
        return target if 0 <= target < chips else None

    def built(moves, cyclic):
        pairs = []
        for chip in range(chips):
            for sub, steps, to in moves:
                target = beside(chip, steps, cyclic)
                if target is not None:
                    pairs.append((at(chip, sub), at(target, to)))
        return pairs

    def in_module(moves):
        pairs = []
        for chip in range(chips):
            mod, slab = divmod(chip, slabs)
            for sub, steps, to in moves:
                pairs.append((at(chip, sub), at(mod * slabs + (slab + steps) % slabs, to)))
        return pairs

    return dict(
        swap=built([(0, 0, 1), (1, 0, 0)], True),
        first=built([(0, 1, 0), (1, -1, 1)], False),
        second=built([(1, 1, 0), (0, -1, 1)], False),
        third=in_module([(0, 1, 1), (1, 1, 0)]),
        fourth=in_module([(0, 1, 0), (1, 1, 1)]),
        ends_first=[(at(slabs - 1, 0), at(0, 0)), (at(last, 1), at(chips - 1, 1))],
        ends_second=[(at(slabs - 1, 1), at(0, 0)), (at(last, 0), at(chips - 1, 1))],
        outer=built([(1, 1, 0), (0, -1, 1)], False),
        down=built([(0, -1, 1)], False),
        halo_cross=in_module([(1, 1, 0), (0, -1, 1)]),
        halo_same=in_module([(0, -1, 0), (1, 1, 1)]),
    )


def module_routes(mods):
    if mods & (mods - 1) == 0:
        return [[(m, m ^ s) for m in range(mods)] for s in range(1, mods)]
    return [[(m, (m + s) % mods) for m in range(mods)] for s in range(1, mods)]


def local(mods, slabs, design, fixed, load):
    half, width = design.shape[1:]
    count = 2 * half
    path = routes(mods, slabs)

    def move(value, name):
        return lax.ppermute(value, AXES, path[name])

    plane = (count, width)
    layer = (3, count, width)
    block = (half, width)
    free = (1 - fixed).astype(jnp.float32)
    swap, first, second, third, fourth, own = call(
        prepare_kernel,
        [(11,) + block, (4,) + block, (4,) + block, block, block, (11,) + block],
        name="prepare",
    )(free, load, design)
    first = move(first, "first")
    second = move(second, "second")
    ends_first = move(third, "ends_first")
    ends_second = move(fourth, "ends_second")
    third = move(third, "third")
    fourth = move(fourth, "fourth")
    swap = move(swap, "swap")

    v0, v0_inner, free, fields, parts = call(
        start_inner_kernel,
        [layer, layer, layer, (12,) + plane, (3,) + plane],
        [(2,) + plane],
        name="start_inner",
        work=True,
    )(own, swap)
    v1, v0_high, mod_inner, mod_outer, mod_own, slope_factor, chain_factor, moments = call(
        start_outer_kernel,
        [layer, layer, plane, plane, plane, plane, plane, (8, width)],
        [layer, plane, plane],
        name="start_outer",
    )(first, second, third, fourth, ends_first, ends_second, v0, v0_inner, free, fields, parts)
    outer = move(v1, "outer")
    inner = move(v1, "swap")
    (fields,) = call(second_inner_kernel, [(12,) + plane], name="second_inner", work=True)(v1, inner)
    v2, v1_high, moments = call(
        second_outer_kernel, [layer, layer, (8, width)], name="second_outer"
    )(v1, outer, inner, fields, free, mod_inner, mod_outer, moments)
    v2_outer = move(v2, "down")
    v2_inner = move(v2, "swap")
    moments, v2_high = call(third_kernel, [(8, width), layer], name="third")(
        v2_outer, v2_inner, v2, mod_own, moments
    )
    devices = 2 * mods * slabs
    gathered = lax.all_to_all(
        jnp.broadcast_to(moments, (devices, 8, width)), AXES, 0, 0, tiled=True
    )
    slope, factors = call(
        combine_kernel, [plane, (3, 8, width)], [layer, layer], name="combine"
    )(gathered, v0, v0_high, v1, v1_high, v2, v2_high, slope_factor)
    slopes = [slope] + [lax.ppermute(slope, "mod", pairs) for pairs in module_routes(mods)]
    (displacement,) = call(displace_kernel, [(3, 2, half, width)], name="displace", work=True)(
        factors, v0, v0_inner, v1, inner, v2, v2_inner
    )
    window = half + 8
    scaled, same, cross, across = call(
        scale_kernel, [plane, (window, width), (window, width), (window, width)], name="scale"
    )(*slopes, chain_factor)
    scaled, displacement = lax.optimization_barrier((scaled, displacement))
    outer = move(cross, "halo_cross")
    far = move(same, "halo_same")
    partner = move(across, "swap")
    (gradient,) = call(
        gradient_kernel, [(2, half, width)], [(4, window, width), (window, width)], name="gradient"
    )(scaled, outer, far, partner)
    return displacement, gradient


def solution(mesh):
    mods, slabs = mesh.shape["mod"], mesh.shape["slab"]
    assert mesh.shape["sub"] == 2
    deck = P(None, ("mod", "slab"), "sub", None)

    def body(design, fixed_mask, load_mask):
        return local(mods, slabs, design, fixed_mask, load_mask)

    return jax.shard_map(
        body,
        mesh=mesh,
        in_specs=(P("slab", "sub", None), deck, deck),
        out_specs=(deck, P("slab", "sub", None)),
        check_vma=False,
    )
```

```python
import math

import jax
import jax.numpy as jnp
import numpy as np
from jax import lax
from jax.experimental import pallas as pl
from jax.experimental.pallas import tpu as pltpu
from jax.sharding import PartitionSpec as P

stiff_floor = 0.01
penalty = 3.0
sharpness = 4.0
threshold = 0.5
filter_reach = 1.8

AXES = ("mod", "slab", "sub")
ROWS = 8
FACE = filter_reach - 1.0
EDGE = filter_reach - math.sqrt(2.0)
CORNER = filter_reach - math.sqrt(3.0)
LOWER = math.tanh(sharpness * threshold)
UPPER = math.tanh(sharpness * (1.0 - threshold))


def stiffness_modes():
    poisson = 0.3
    lame = poisson / ((1.0 + poisson) * (1.0 - 2.0 * poisson))
    shear = 1.0 / (2.0 * (1.0 + poisson))
    elastic = np.zeros((6, 6))
    elastic[:3, :3] = lame
    for axis in range(3):
        elastic[axis, axis] += 2.0 * shear
        elastic[axis + 3, axis + 3] = shear
    offset = 0.5 / math.sqrt(3.0)
    points = [0.5 - offset, 0.5 + offset]
    stiffness = np.zeros((24, 24))
    for point in ((a, b, c) for a in points for b in points for c in points):
        strain = np.zeros((6, 24))
        for corner in range(8):
            bits = (corner >> 2 & 1, corner >> 1 & 1, corner & 1)
            along = [point[a] if bits[a] else 1.0 - point[a] for a in range(3)]
            sign = [1.0 if bits[a] else -1.0 for a in range(3)]
            gx = sign[0] * along[1] * along[2]
            gy = along[0] * sign[1] * along[2]
            gz = along[0] * along[1] * sign[2]
            col = 3 * corner
            strain[0, col] = gx
            strain[1, col + 1] = gy
            strain[2, col + 2] = gz
            strain[3, col], strain[3, col + 1] = gy, gx
            strain[4, col + 1], strain[4, col + 2] = gz, gy
            strain[5, col], strain[5, col + 2] = gz, gx
        stiffness += strain.T @ elastic @ strain / 8.0
    basis = np.zeros((24, 24))
    for mode in range(8):
        for corner in range(8):
            value = 1.0
            for bit in range(3):
                if mode >> bit & 1 and not corner >> bit & 1:
                    value = -value
            for k in range(3):
                basis[3 * mode + k, 3 * corner + k] = value
    table = basis @ stiffness @ basis.T / 64.0
    table[np.abs(table) < 1e-9] = 0.0
    return table


TABLE = stiffness_modes()


def lanes(shape):
    return lax.broadcasted_iota(jnp.int32, shape, 1)


def rows(shape):
    return lax.broadcasted_iota(jnp.int32, shape, 0)


def z_up(x):
    return jnp.where(lanes(x.shape) < x.shape[1] - 1, pltpu.roll(x, x.shape[1] - 1, 1), 0.0)


def z_down(x):
    return jnp.where(lanes(x.shape) > 0, pltpu.roll(x, 1, 1), 0.0)


def y_up(x):
    return jnp.where(rows(x.shape) < x.shape[0] - 1, pltpu.roll(x, x.shape[0] - 1, 0), 0.0)


def y_down(x):
    return jnp.where(rows(x.shape) > 0, pltpu.roll(x, 1, 0), 0.0)


def two_rows(read, y0, count):
    here = read(y0)
    above = y_up(here) if y0 + ROWS == count else read(y0 + 1)
    return here, above


def face_modes(here, above):
    out = []
    for part in (here + above, above - here):
        shifted = z_up(part)
        out += [part + shifted, shifted - part]
    return out


def element_modes(own, other, side):
    sums = [[other[k][m] + own[k][m] for m in range(4)] for k in range(3)]
    diffs = [[(other[k][m] - own[k][m]) * side for m in range(4)] for k in range(3)]
    return [sums[k] + diffs[k] for k in range(3)]


def mode_forces(q):
    made = {}

    def scaled(j, value):
        key = (j, round(value, 12))
        if key not in made:
            made[key] = q[j % 3][j // 3] * np.float32(value)
        return made[key]

    out = [[None] * 8 for _ in range(3)]
    for i in range(24):
        total = None
        for j in np.nonzero(TABLE[i])[0]:
            term = scaled(int(j), float(TABLE[i, j]))
            total = term if total is None else total + term
        out[i % 3][i // 3] = total
    return out


def element_energy(q):
    r = mode_forces(q)
    total = None
    for k in range(3):
        for m in range(1, 8):
            term = q[k][m] * r[k][m]
            total = term if total is None else total + term
    return total


def own_fields(own, other, side):
    r = mode_forces(element_modes(own, other, side))
    fields = []
    for k in range(3):
        for m in range(4):
            d = r[k][m + 4] * side
            fields.append(-d if r[k][m] is None else r[k][m] - d)
    return fields


def layer_modes(read, y0, count):
    heres, modes = [], []
    for k in range(3):
        here, above = two_rows(lambda y, k=k: read(k, y), y0, count)
        heres.append(here)
        modes.append(face_modes(here, above))
    return heres, modes


def fields_loop(count, read_own, read_other, side, fields):
    for y0 in range(0, count, ROWS):
        _, own = layer_modes(read_own, y0, count)
        _, other = layer_modes(read_other, y0, count)
        for n, value in enumerate(own_fields(own, other, side)):
            fields[n, pl.ds(y0, ROWS), :] = value


def operator_loop(count, read_own, read_other, side, fields, mod_inner, mod_outer, free, out_ref):
    shape = (ROWS, out_ref.shape[2])
    square = jnp.zeros(shape, jnp.float32)
    cross = jnp.zeros(shape, jnp.float32)
    norm = jnp.zeros(shape, jnp.float32)
    carry = [jnp.zeros(shape, jnp.float32)] * 3
    first = rows(shape) == 0
    for y0 in range(0, count, ROWS):
        part = pl.ds(y0, ROWS)
        owns, own = layer_modes(read_own, y0, count)
        _, other = layer_modes(read_other, y0, count)
        inner, outer = mod_inner[part, :], mod_outer[part, :]
        total = [
            outer * value + inner * fields[n, part, :]
            for n, value in enumerate(own_fields(own, other, side))
        ]
        for k in range(3):
            faces = []
            for py in range(2):
                s, d = total[4 * k + 2 * py], total[4 * k + 2 * py + 1]
                faces.append((s - d) + z_down(s + d))
            rolled = pltpu.roll(faces[0] + faces[1], 1, 0)
            force = (faces[0] - faces[1]) + jnp.where(first, carry[k], rolled)
            carry[k] = rolled
            image = free[k, part, :] * force
            out_ref[k, part, :] = image
            square += image * image
            cross += owns[k] * image
            norm += owns[k] * owns[k]
    return norm, cross, square


def energy_loop(count, read_own, read_high, use):
    for y0 in range(0, count, ROWS):
        _, own = layer_modes(read_own, y0, count)
        _, high = layer_modes(read_high, y0, count)
        use(y0, element_energy(element_modes(own, high, 1.0)))


def rows_of(ref):
    return lambda k, y: ref[k, pl.ds(y, ROWS), :]


def inner_side(sub):
    return jnp.where(sub == 0, 1.0, -1.0).astype(jnp.float32)


def line(tile):
    return jnp.sum(tile, axis=0, keepdims=True)


def prepare_kernel(free, load, design, swap, first, second, third, fourth, own):
    sub = lax.axis_index("sub")
    for k in range(3):
        frees = [free[k, layer] for layer in range(2)]
        values = [frees[layer] * load[k, layer].astype(jnp.float32) for layer in range(2)]
        for layer in range(2):
            swap[2 * k + layer] = values[layer]
            own[2 * k + layer] = values[layer]
        low = sub == 0
        swap[6 + k] = jnp.where(low, frees[1], frees[0])
        own[6 + k] = jnp.where(low, frees[0], frees[1])
        first[k] = jnp.where(low, values[1], values[0])
        second[k] = jnp.where(low, values[0], values[1])
    low = sub == 0
    for layer in range(2):
        swap[9 + layer] = design[layer]
        own[9 + layer] = design[layer]
    later = jnp.where(low, design[1], design[0])
    sooner = jnp.where(low, design[0], design[1])
    first[3] = later
    third[...] = later
    second[3] = sooner
    fourth[...] = sooner


def around(p):
    across = y_up(p) + y_down(p)
    return across + z_up(p) + z_down(p), z_up(across) + z_down(across)


def filter_mid(p):
    face, diag = around(p)
    return filter_reach * p + FACE * face + EDGE * diag


def filter_side(p):
    face, diag = around(p)
    return FACE * p + EDGE * face + CORNER * diag


def filter_planes(low, mid, high):
    return filter_side(low + high) + filter_mid(mid)


def weight_plane(shape, row_offset, count):
    row = rows(shape) + row_offset
    lane = lanes(shape)

    def neighbours(index, size):
        return jnp.where(index > 0, 1.0, 0.0) + jnp.where(index < size - 1, 1.0, 0.0)

    ry = neighbours(row, count)
    rz = neighbours(lane, shape[1])
    face, diag = ry + rz, ry * rz
    return (
        filter_reach
        + FACE * (2.0 + face)
        + EDGE * (2.0 * face + diag)
        + (2.0 * CORNER) * diag
    )


def start_inner_kernel(own, swap, v0, v0_inner, free, fields, parts, layers):
    sub = lax.axis_index("sub")
    half = own.shape[1]
    count = 2 * half
    mine = pl.ds(pl.multiple_of(sub * half, half), half)
    other = pl.ds(pl.multiple_of((1 - sub) * half, half), half)
    for layer in range(2):
        layers[layer, mine, :] = own[9 + layer]
        layers[layer, other, :] = swap[9 + layer]

    @pl.when(sub == 0)
    def _():
        parts[0] = filter_side(layers[0])
        parts[1] = filter_mid(layers[0]) + filter_side(layers[1])

    @pl.when(sub == 1)
    def _():
        parts[0] = filter_mid(layers[0]) + filter_side(layers[1])
        parts[1] = filter_side(layers[0]) + filter_mid(layers[1])

    parts[2] = 1.0 / weight_plane((count, own.shape[2]), 0, count)
    for k in range(3):
        free[k, mine, :] = own[6 + k]
        free[k, other, :] = swap[6 + k]
        v0[k, mine, :] = own[2 * k + sub]
        v0[k, other, :] = swap[2 * k + sub]
        v0_inner[k, mine, :] = own[2 * k + 1 - sub]
        v0_inner[k, other, :] = swap[2 * k + 1 - sub]
    fields_loop(count, rows_of(v0), rows_of(v0_inner), inner_side(sub), fields)


def start_outer_kernel(
    mods, slabs,
    first, second, third, fourth, v0, v0_inner, free, fields, parts,
    v1, v0_high, mod_inner, mod_outer, mod_own, slope_factor, chain_factor, moments,
    v0_outer, near, deep,
):
    mod, slab, sub = (lax.axis_index(a) for a in AXES)
    half = third.shape[0]
    count = 2 * half
    even = sub == 0
    mine = pl.ds(pl.multiple_of(sub * half, half), half)
    other = pl.ds(pl.multiple_of((1 - sub) * half, half), half)
    near[mine, :] = first[3]
    near[other, :] = second[3]
    deep[mine, :] = fourth[...]
    deep[other, :] = third[...]
    starts = (mod == 0) & (slab == 0) & even
    ends = (mod == mods - 1) & (slab == slabs - 1) & (sub == 1)
    inside = jnp.where(ends, 0.0, 1.0)
    for k in range(3):
        v0_outer[k, mine, :] = first[k] * inside
        v0_outer[k, other, :] = second[k] * inside
        v0_high[k] = jnp.where(even, v0_inner[k], v0_outer[k])

    side = filter_side(near[...])
    mid = filter_mid(near[...])
    inverse = parts[2]
    filtered = (parts[0] + filter_side(deep[...]) + jnp.where(even, mid, 0.0)) * inverse
    hyper = jnp.tanh(sharpness * (filtered - threshold))
    projected = (LOWER + hyper) * (1.0 / (LOWER + UPPER))
    below = stiff_floor + (1.0 - stiff_floor) * projected * projected * projected
    below = below * jnp.where(starts, 0.0, 1.0)
    filtered = (parts[1] + side) * inverse
    hyper = jnp.tanh(sharpness * (filtered - threshold))
    projected = (LOWER + hyper) * (1.0 / (LOWER + UPPER))
    squared = projected * projected
    stiff = stiff_floor + (1.0 - stiff_floor) * squared * projected
    mod_own[...] = stiff
    mod_inner[...] = jnp.where(even, stiff, below)
    mod_outer[...] = jnp.where(even, below, stiff)
    slope_factor[...] = (-penalty * (1.0 - stiff_floor)) * squared
    chain_factor[...] = (sharpness / (LOWER + UPPER)) * (1.0 - hyper * hyper) * inverse

    norm, cross, square = operator_loop(
        count, rows_of(v0), rows_of(v0_outer), -inner_side(sub), fields, mod_inner, mod_outer, free, v1
    )
    moments[...] = jnp.concatenate(
        [line(norm), line(cross), line(square), jnp.zeros((5, norm.shape[1]), jnp.float32)], axis=0
    )


def second_inner_kernel(v1, inner, fields):
    fields_loop(v1.shape[1], rows_of(v1), rows_of(inner), inner_side(lax.axis_index("sub")), fields)


def second_outer_kernel(
    v1, outer, inner, fields, free, mod_inner, mod_outer, before, v2, v1_high, moments
):
    sub = lax.axis_index("sub")
    count = v1.shape[1]
    for k in range(3):
        v1_high[k] = jnp.where(sub == 0, inner[k], outer[k])
    _, cross, square = operator_loop(
        count, rows_of(v1), rows_of(outer), -inner_side(sub), fields, mod_inner, mod_outer, free, v2
    )
    zero = jnp.zeros((3, cross.shape[1]), jnp.float32)
    moments[...] = before[...] + jnp.concatenate(
        [zero, line(cross), line(square), zero], axis=0
    )


def third_kernel(v2_outer, v2_inner, v2, mod_own, before, moments, v2_high):
    even = lax.axis_index("sub") == 0
    for k in range(3):
        v2_high[k] = jnp.where(even, v2_inner[k], v2_outer[k])
    count = v2.shape[1]
    total = [jnp.zeros((ROWS, v2.shape[2]), jnp.float32)]

    def use(y0, energy):
        total[0] += energy * mod_own[pl.ds(y0, ROWS), :]

    energy_loop(
        count,
        lambda k, y: v2[k, pl.ds(y, ROWS), :],
        lambda k, y: v2_high[k, pl.ds(y, ROWS), :],
        use,
    )
    width = v2.shape[2]
    moments[...] = before[...] + jnp.concatenate(
        [
            jnp.zeros((5, width), jnp.float32),
            line(total[0]),
            jnp.zeros((2, width), jnp.float32),
        ],
        axis=0,
    )


def coefficients(m):
    step = m[0] / m[1]
    x0 = step
    r1 = -step
    norm = m[0] + 2.0 * r1 * m[1] + r1 * r1 * m[2]
    ratio = norm / m[0]
    p0, p1 = 1.0 + ratio, r1
    step = norm / (p0 * p0 * m[1] + 2.0 * p0 * p1 * m[2] + p1 * p1 * m[3])
    x0, x1 = x0 + step * p0, step * p1
    r1, r2 = r1 - step * p0, -step * p1
    after = (
        m[0]
        + 2.0 * r1 * m[1]
        + (r1 * r1 + 2.0 * r2) * m[2]
        + 2.0 * r1 * r2 * m[3]
        + r2 * r2 * m[4]
    )
    ratio = after / norm
    p0, p1, p2 = 1.0 + ratio * p0, r1 + ratio * p1, r2
    step = after / (
        p0 * p0 * m[1]
        + 2.0 * p0 * p1 * m[2]
        + (p1 * p1 + 2.0 * p0 * p2) * m[3]
        + 2.0 * p1 * p2 * m[4]
        + p2 * p2 * m[5]
    )
    return x0 + step * p0, x1 + step * p1, step * p2


def combine_kernel(
    gathered, v0, v0_high, v1, v1_high, v2, v2_high, slope_factor, slope, factors, own, high
):
    count = v0.shape[1]
    sums = jnp.sum(jnp.sum(gathered[...], axis=0), axis=1, keepdims=True)
    c0, c1, c2 = coefficients([sums[k : k + 1] for k in range(6)])
    for n, c in enumerate((c0, c1, c2)):
        factors[n] = jnp.broadcast_to(c, factors.shape[1:])
    for k in range(3):
        own[k] = c0 * v0[k] + c1 * v1[k] + c2 * v2[k]
        high[k] = c0 * v0_high[k] + c1 * v1_high[k] + c2 * v2_high[k]

    def use(y0, energy):
        slope[pl.ds(y0, ROWS), :] = slope_factor[pl.ds(y0, ROWS), :] * energy

    energy_loop(count, rows_of(own), rows_of(high), use)


def displace_kernel(factors, v0, v0_inner, v1, v1_inner, v2, v2_inner, displacement):
    sub = lax.axis_index("sub")
    half = displacement.shape[2]
    mine = pl.ds(pl.multiple_of(sub * half, half), half)
    c0, c1, c2 = (factors[n][:1, :1] for n in range(3))
    for k in range(3):
        displacement[k, sub] = c0 * v0[k, mine, :] + c1 * v1[k, mine, :] + c2 * v2[k, mine, :]
        displacement[k, 1 - sub] = (
            c0 * v0_inner[k, mine, :] + c1 * v1_inner[k, mine, :] + c2 * v2_inner[k, mine, :]
        )


def scale_kernel(*refs):
    slopes, (chain_factor, scaled, same, cross, across) = refs[:-5], refs[-5:]
    sub = lax.axis_index("sub")
    total = slopes[0][...]
    for other in slopes[1:]:
        total = total + other[...]
    scaled[...] = total * chain_factor[...]
    window = same.shape[0]
    shift = scaled.shape[0] - window
    same[...] = scaled[pl.ds(pl.multiple_of(sub * shift, 8), window), :]
    cross[...] = scaled[pl.ds(pl.multiple_of((1 - sub) * shift, 8), window), :]
    across[...] = cross[...]


def gradient_kernel(scaled, outer, far, partner, gradient, planes, sums):
    sub = lax.axis_index("sub")
    window = partner.shape[0]
    shift = scaled.shape[0] - window
    mine = scaled[pl.ds(pl.multiple_of(sub * shift, 8), window), :]

    @pl.when(sub == 0)
    def _():
        planes[0] = outer[...]
        planes[1] = mine
        planes[2] = partner[...]
        planes[3] = far[...]

    @pl.when(sub == 1)
    def _():
        planes[0] = far[...]
        planes[1] = partner[...]
        planes[2] = mine
        planes[3] = outer[...]

    half = gradient.shape[1]
    part = pl.ds(pl.multiple_of(sub * (window - half), 8), half)
    for layer in range(2):
        sums[...] = filter_planes(planes[layer], planes[layer + 1], planes[layer + 2])
        gradient[layer] = sums[part, :]


def call(body, outs, scratch=(), name=None, work=False):
    cost = pl.CostEstimate(flops=10**7, bytes_accessed=4 * 10**6, transcendentals=0)
    return pl.pallas_call(
        body,
        out_shape=[jax.ShapeDtypeStruct(shape, jnp.float32) for shape in outs],
        scratch_shapes=[pltpu.VMEM(shape, jnp.float32) for shape in scratch],
        compiler_params=pltpu.CompilerParams(vmem_limit_bytes=16 * 2**20),
        cost_estimate=cost if work else None,
        name=name,
    )


def routes(mods, slabs):
    chips = mods * slabs

    def at(chip, sub):
        return 2 * chip + sub

    def beside(chip, steps, cyclic):
        target = chip + steps
        if cyclic:
            return target % chips
        return target if 0 <= target < chips else None

    def built(moves, cyclic):
        pairs = []
        for chip in range(chips):
            for sub, steps, to in moves:
                target = beside(chip, steps, cyclic)
                if target is not None:
                    pairs.append((at(chip, sub), at(target, to)))
        return pairs

    def in_module(moves):
        pairs = []
        for chip in range(chips):
            mod, slab = divmod(chip, slabs)
            for sub, steps, to in moves:
                pairs.append((at(chip, sub), at(mod * slabs + (slab + steps) % slabs, to)))
        return pairs

    return dict(
        swap=built([(0, 0, 1), (1, 0, 0)], True),
        first=built([(0, 1, 0), (1, -1, 1)], True),
        second=built([(1, 1, 0), (0, -1, 1)], True),
        third=in_module([(0, 1, 1), (1, 1, 0)]),
        fourth=in_module([(0, 1, 0), (1, 1, 1)]),
        outer=built([(1, 1, 0), (0, -1, 1)], False),
        down=built([(0, -1, 1)], False),
        halo_cross=in_module([(1, 1, 0), (0, -1, 1)]),
        halo_same=in_module([(0, -1, 0), (1, 1, 1)]),
    )


def module_routes(mods):
    if mods & (mods - 1) == 0:
        return [[(m, m ^ s) for m in range(mods)] for s in range(1, mods)]
    return [[(m, (m + s) % mods) for m in range(mods)] for s in range(1, mods)]


def local(mods, slabs, design, fixed, load):
    half, width = design.shape[1:]
    count = 2 * half
    path = routes(mods, slabs)

    def move(value, name):
        return lax.ppermute(value, AXES, path[name])

    plane = (count, width)
    layer = (3, count, width)
    block = (half, width)
    free = (1 - fixed).astype(jnp.float32)
    swap, first, second, third, fourth, own = call(
        prepare_kernel,
        [(11,) + block, (4,) + block, (4,) + block, block, block, (11,) + block],
        name="prepare",
    )(free, load, design)
    first = move(first, "first")
    second = move(second, "second")
    third = move(third, "third")
    fourth = move(fourth, "fourth")
    swap = move(swap, "swap")

    def start_body(*refs):
        start_outer_kernel(mods, slabs, *refs)

    v0, v0_inner, free, fields, parts = call(
        start_inner_kernel,
        [layer, layer, layer, (12,) + plane, (3,) + plane],
        [(2,) + plane],
        name="start_inner",
        work=True,
    )(own, swap)
    v1, v0_high, mod_inner, mod_outer, mod_own, slope_factor, chain_factor, moments = call(
        start_body,
        [layer, layer, plane, plane, plane, plane, plane, (8, width)],
        [layer, plane, plane],
        name="start_outer",
    )(first, second, third, fourth, v0, v0_inner, free, fields, parts)
    outer = move(v1, "outer")
    inner = move(v1, "swap")
    (fields,) = call(second_inner_kernel, [(12,) + plane], name="second_inner", work=True)(v1, inner)
    v2, v1_high, moments = call(
        second_outer_kernel, [layer, layer, (8, width)], name="second_outer"
    )(v1, outer, inner, fields, free, mod_inner, mod_outer, moments)
    v2_outer = move(v2, "down")
    v2_inner = move(v2, "swap")
    moments, v2_high = call(third_kernel, [(8, width), layer], name="third")(
        v2_outer, v2_inner, v2, mod_own, moments
    )
    devices = 2 * mods * slabs
    gathered = lax.all_to_all(
        jnp.broadcast_to(moments, (devices, 8, width)), AXES, 0, 0, tiled=True
    )
    slope, factors = call(
        combine_kernel, [plane, (3, 8, width)], [layer, layer], name="combine"
    )(gathered, v0, v0_high, v1, v1_high, v2, v2_high, slope_factor)
    slopes = [slope] + [lax.ppermute(slope, "mod", pairs) for pairs in module_routes(mods)]
    (displacement,) = call(displace_kernel, [(3, 2, half, width)], name="displace", work=True)(
        factors, v0, v0_inner, v1, inner, v2, v2_inner
    )
    window = half + 8
    scaled, same, cross, across = call(
        scale_kernel, [plane, (window, width), (window, width), (window, width)], name="scale"
    )(*slopes, chain_factor)
    scaled, displacement = lax.optimization_barrier((scaled, displacement))
    outer = move(cross, "halo_cross")
    far = move(same, "halo_same")
    partner = move(across, "swap")
    (gradient,) = call(
        gradient_kernel, [(2, half, width)], [(4, window, width), (window, width)], name="gradient"
    )(scaled, outer, far, partner)
    return displacement, gradient


def solution(mesh):
    mods, slabs = mesh.shape["mod"], mesh.shape["slab"]
    assert mesh.shape["sub"] == 2
    deck = P(None, ("mod", "slab"), "sub", None)

    def body(design, fixed_mask, load_mask):
        return local(mods, slabs, design, fixed_mask, load_mask)

    return jax.shard_map(
        body,
        mesh=mesh,
        in_specs=(P("slab", "sub", None), deck, deck),
        out_specs=(deck, P("slab", "sub", None)),
        check_vma=False,
    )
```

```python
import math

import jax
import jax.numpy as jnp
import numpy as np
from jax import lax
from jax.experimental import pallas as pl
from jax.experimental.pallas import tpu as pltpu
from jax.sharding import PartitionSpec as P

stiff_floor = 0.01
penalty = 3.0
sharpness = 4.0
threshold = 0.5
filter_reach = 1.8

AXES = ("mod", "slab", "sub")
ROWS = 8
FACE = filter_reach - 1.0
EDGE = filter_reach - math.sqrt(2.0)
CORNER = filter_reach - math.sqrt(3.0)
LOWER = math.tanh(sharpness * threshold)
UPPER = math.tanh(sharpness * (1.0 - threshold))


def stiffness_modes():
    poisson = 0.3
    lame = poisson / ((1.0 + poisson) * (1.0 - 2.0 * poisson))
    shear = 1.0 / (2.0 * (1.0 + poisson))
    elastic = np.zeros((6, 6))
    elastic[:3, :3] = lame
    for axis in range(3):
        elastic[axis, axis] += 2.0 * shear
        elastic[axis + 3, axis + 3] = shear
    offset = 0.5 / math.sqrt(3.0)
    points = [0.5 - offset, 0.5 + offset]
    stiffness = np.zeros((24, 24))
    for point in ((a, b, c) for a in points for b in points for c in points):
        strain = np.zeros((6, 24))
        for corner in range(8):
            bits = (corner >> 2 & 1, corner >> 1 & 1, corner & 1)
            along = [point[a] if bits[a] else 1.0 - point[a] for a in range(3)]
            sign = [1.0 if bits[a] else -1.0 for a in range(3)]
            gx = sign[0] * along[1] * along[2]
            gy = along[0] * sign[1] * along[2]
            gz = along[0] * along[1] * sign[2]
            col = 3 * corner
            strain[0, col] = gx
            strain[1, col + 1] = gy
            strain[2, col + 2] = gz
            strain[3, col], strain[3, col + 1] = gy, gx
            strain[4, col + 1], strain[4, col + 2] = gz, gy
            strain[5, col], strain[5, col + 2] = gz, gx
        stiffness += strain.T @ elastic @ strain / 8.0
    basis = np.zeros((24, 24))
    for mode in range(8):
        for corner in range(8):
            value = 1.0
            for bit in range(3):
                if mode >> bit & 1 and not corner >> bit & 1:
                    value = -value
            for k in range(3):
                basis[3 * mode + k, 3 * corner + k] = value
    table = basis @ stiffness @ basis.T / 64.0
    table[np.abs(table) < 1e-9] = 0.0
    return table


TABLE = stiffness_modes()


def lanes(shape):
    return lax.broadcasted_iota(jnp.int32, shape, 1)


def rows(shape):
    return lax.broadcasted_iota(jnp.int32, shape, 0)


def z_up(x):
    return jnp.where(lanes(x.shape) < x.shape[1] - 1, pltpu.roll(x, x.shape[1] - 1, 1), 0.0)


def z_down(x):
    return jnp.where(lanes(x.shape) > 0, pltpu.roll(x, 1, 1), 0.0)


def y_up(x):
    return jnp.where(rows(x.shape) < x.shape[0] - 1, pltpu.roll(x, x.shape[0] - 1, 0), 0.0)


def y_down(x):
    return jnp.where(rows(x.shape) > 0, pltpu.roll(x, 1, 0), 0.0)


def two_rows(read, y0, count):
    here = read(y0)
    above = y_up(here) if y0 + ROWS == count else read(y0 + 1)
    return here, above


def face_modes(here, above):
    out = []
    for part in (here + above, above - here):
        shifted = z_up(part)
        out += [part + shifted, shifted - part]
    return out


def element_modes(own, other, side):
    sums = [[other[k][m] + own[k][m] for m in range(4)] for k in range(3)]
    diffs = [[(other[k][m] - own[k][m]) * side for m in range(4)] for k in range(3)]
    return [sums[k] + diffs[k] for k in range(3)]


def mode_forces(q):
    made = {}

    def scaled(j, value):
        key = (j, round(value, 12))
        if key not in made:
            made[key] = q[j % 3][j // 3] * np.float32(value)
        return made[key]

    out = [[None] * 8 for _ in range(3)]
    for i in range(24):
        total = None
        for j in np.nonzero(TABLE[i])[0]:
            term = scaled(int(j), float(TABLE[i, j]))
            total = term if total is None else total + term
        out[i % 3][i // 3] = total
    return out


def element_energy(q):
    r = mode_forces(q)
    total = None
    for k in range(3):
        for m in range(1, 8):
            term = q[k][m] * r[k][m]
            total = term if total is None else total + term
    return total


def own_fields(own, other, side):
    r = mode_forces(element_modes(own, other, side))
    fields = []
    for k in range(3):
        for m in range(4):
            d = r[k][m + 4] * side
            fields.append(-d if r[k][m] is None else r[k][m] - d)
    return fields


def layer_modes(read, y0, count):
    heres, modes = [], []
    for k in range(3):
        here, above = two_rows(lambda y, k=k: read(k, y), y0, count)
        heres.append(here)
        modes.append(face_modes(here, above))
    return heres, modes


def fields_loop(count, read_own, read_other, side, fields):
    for y0 in range(0, count, ROWS):
        _, own = layer_modes(read_own, y0, count)
        _, other = layer_modes(read_other, y0, count)
        for n, value in enumerate(own_fields(own, other, side)):
            fields[n, pl.ds(y0, ROWS), :] = value


def operator_loop(count, read_own, read_other, side, fields, mod_inner, mod_outer, free, out_ref):
    shape = (ROWS, out_ref.shape[2])
    square = jnp.zeros(shape, jnp.float32)
    cross = jnp.zeros(shape, jnp.float32)
    norm = jnp.zeros(shape, jnp.float32)
    carry = [jnp.zeros(shape, jnp.float32)] * 3
    first = rows(shape) == 0
    for y0 in range(0, count, ROWS):
        part = pl.ds(y0, ROWS)
        owns, own = layer_modes(read_own, y0, count)
        _, other = layer_modes(read_other, y0, count)
        inner, outer = mod_inner[part, :], mod_outer[part, :]
        total = [
            outer * value + inner * fields[n, part, :]
            for n, value in enumerate(own_fields(own, other, side))
        ]
        for k in range(3):
            faces = []
            for py in range(2):
                s, d = total[4 * k + 2 * py], total[4 * k + 2 * py + 1]
                faces.append((s - d) + z_down(s + d))
            rolled = pltpu.roll(faces[0] + faces[1], 1, 0)
            force = (faces[0] - faces[1]) + jnp.where(first, carry[k], rolled)
            carry[k] = rolled
            image = free[k, part, :] * force
            out_ref[k, part, :] = image
            square += image * image
            cross += owns[k] * image
            norm += owns[k] * owns[k]
    return norm, cross, square


def energy_loop(count, read_own, read_high, use):
    for y0 in range(0, count, ROWS):
        _, own = layer_modes(read_own, y0, count)
        _, high = layer_modes(read_high, y0, count)
        use(y0, element_energy(element_modes(own, high, 1.0)))


def rows_of(ref):
    return lambda k, y: ref[k, pl.ds(y, ROWS), :]


def inner_side(sub):
    return jnp.where(sub == 0, 1.0, -1.0).astype(jnp.float32)


def line(tile):
    return jnp.sum(tile, axis=0, keepdims=True)


def prepare_kernel(free, load, design, swap, first, second, third, fourth, own):
    sub = lax.axis_index("sub")
    for k in range(3):
        frees = [free[k, layer] for layer in range(2)]
        values = [frees[layer] * load[k, layer].astype(jnp.float32) for layer in range(2)]
        for layer in range(2):
            swap[2 * k + layer] = values[layer]
            own[2 * k + layer] = values[layer]
        low = sub == 0
        swap[6 + k] = jnp.where(low, frees[1], frees[0])
        own[6 + k] = jnp.where(low, frees[0], frees[1])
        first[k] = jnp.where(low, values[1], values[0])
        second[k] = jnp.where(low, values[0], values[1])
    low = sub == 0
    for layer in range(2):
        swap[9 + layer] = design[layer]
        own[9 + layer] = design[layer]
    later = jnp.where(low, design[1], design[0])
    sooner = jnp.where(low, design[0], design[1])
    first[3] = later
    third[...] = later
    second[3] = sooner
    fourth[...] = sooner


def around(p):
    across = y_up(p) + y_down(p)
    return across + z_up(p) + z_down(p), z_up(across) + z_down(across)


def filter_mid(p):
    face, diag = around(p)
    return filter_reach * p + FACE * face + EDGE * diag


def filter_side(p):
    face, diag = around(p)
    return FACE * p + EDGE * face + CORNER * diag


def filter_planes(low, mid, high):
    return filter_side(low + high) + filter_mid(mid)


def weight_plane(shape, row_offset, count):
    row = rows(shape) + row_offset
    lane = lanes(shape)

    def neighbours(index, size):
        return jnp.where(index > 0, 1.0, 0.0) + jnp.where(index < size - 1, 1.0, 0.0)

    ry = neighbours(row, count)
    rz = neighbours(lane, shape[1])
    face, diag = ry + rz, ry * rz
    return (
        filter_reach
        + FACE * (2.0 + face)
        + EDGE * (2.0 * face + diag)
        + (2.0 * CORNER) * diag
    )


def start_inner_kernel(own, swap, v0, v0_inner, free, fields, parts, layers):
    sub = lax.axis_index("sub")
    half = own.shape[1]
    count = 2 * half
    mine = pl.ds(pl.multiple_of(sub * half, half), half)
    other = pl.ds(pl.multiple_of((1 - sub) * half, half), half)
    for layer in range(2):
        layers[layer, mine, :] = own[9 + layer]
        layers[layer, other, :] = swap[9 + layer]

    @pl.when(sub == 0)
    def _():
        parts[0] = filter_side(layers[0])
        parts[1] = filter_mid(layers[0]) + filter_side(layers[1])

    @pl.when(sub == 1)
    def _():
        parts[0] = filter_mid(layers[0]) + filter_side(layers[1])
        parts[1] = filter_side(layers[0]) + filter_mid(layers[1])

    parts[2] = 1.0 / weight_plane((count, own.shape[2]), 0, count)
    for k in range(3):
        free[k, mine, :] = own[6 + k]
        free[k, other, :] = swap[6 + k]
        v0[k, mine, :] = own[2 * k + sub]
        v0[k, other, :] = swap[2 * k + sub]
        v0_inner[k, mine, :] = own[2 * k + 1 - sub]
        v0_inner[k, other, :] = swap[2 * k + 1 - sub]
    fields_loop(count, rows_of(v0), rows_of(v0_inner), inner_side(sub), fields)


def start_outer_kernel(
    mods, slabs,
    first, second, third, fourth, v0, v0_inner, free, fields, parts,
    v1, v0_high, mod_inner, mod_outer, mod_own, slope_factor, chain_factor, moments,
    v0_outer, near, deep,
):
    mod, slab, sub = (lax.axis_index(a) for a in AXES)
    half = third.shape[0]
    count = 2 * half
    even = sub == 0
    mine = pl.ds(pl.multiple_of(sub * half, half), half)
    other = pl.ds(pl.multiple_of((1 - sub) * half, half), half)
    near[mine, :] = first[3]
    near[other, :] = second[3]
    deep[mine, :] = fourth[...]
    deep[other, :] = third[...]
    starts = (mod == 0) & (slab == 0) & even
    ends = (mod == mods - 1) & (slab == slabs - 1) & (sub == 1)
    inside = jnp.where(ends, 0.0, 1.0)
    for k in range(3):
        v0_outer[k, mine, :] = first[k] * inside
        v0_outer[k, other, :] = second[k] * inside
        v0_high[k] = jnp.where(even, v0_inner[k], v0_outer[k])

    side = filter_side(near[...])
    mid = filter_mid(near[...])
    inverse = parts[2]
    filtered = (parts[0] + filter_side(deep[...]) + jnp.where(even, mid, 0.0)) * inverse
    hyper = jnp.tanh(sharpness * (filtered - threshold))
    projected = (LOWER + hyper) * (1.0 / (LOWER + UPPER))
    below = stiff_floor + (1.0 - stiff_floor) * projected * projected * projected
    below = below * jnp.where(starts, 0.0, 1.0)
    filtered = (parts[1] + side) * inverse
    hyper = jnp.tanh(sharpness * (filtered - threshold))
    projected = (LOWER + hyper) * (1.0 / (LOWER + UPPER))
    squared = projected * projected
    stiff = stiff_floor + (1.0 - stiff_floor) * squared * projected
    mod_own[...] = stiff
    mod_inner[...] = jnp.where(even, stiff, below)
    mod_outer[...] = jnp.where(even, below, stiff)
    slope_factor[...] = (-penalty * (1.0 - stiff_floor)) * squared
    chain_factor[...] = (sharpness / (LOWER + UPPER)) * (1.0 - hyper * hyper) * inverse

    norm, cross, square = operator_loop(
        count, rows_of(v0), rows_of(v0_outer), -inner_side(sub), fields, mod_inner, mod_outer, free, v1
    )
    moments[...] = jnp.concatenate(
        [line(norm), line(cross), line(square), jnp.zeros((5, norm.shape[1]), jnp.float32)], axis=0
    )


def second_inner_kernel(v1, inner, fields):
    fields_loop(v1.shape[1], rows_of(v1), rows_of(inner), inner_side(lax.axis_index("sub")), fields)


def second_outer_kernel(
    v1, outer, inner, fields, free, mod_inner, mod_outer, before,
    v2, v1_high, moments, window, upper,
):
    sub = lax.axis_index("sub")
    count = v1.shape[1]
    for k in range(3):
        v1_high[k] = jnp.where(sub == 0, inner[k], outer[k])
    _, cross, square = operator_loop(
        count, rows_of(v1), rows_of(outer), -inner_side(sub), fields, mod_inner, mod_outer, free, v2
    )
    zero = jnp.zeros((3, cross.shape[1]), jnp.float32)
    moments[...] = before[...] + jnp.concatenate(
        [zero, line(cross), line(square), zero], axis=0
    )
    size, half = window.shape[1], upper.shape[1]
    for k in range(3):
        window[k] = v2[k, pl.ds(pl.multiple_of(sub * (count - size), 8), size), :]
        upper[k] = v2[k, pl.ds(count - half, half), :]


def third_kernel(mods, slabs, outer, inner, v2, mod_own, mod_outer, before, moments):
    mod, slab, sub = (lax.axis_index(a) for a in AXES)
    even = sub == 0
    ends = (mod == mods - 1) & (slab == slabs - 1) & (sub == 1)
    count, width = v2.shape[1:]
    half = count // 2
    shift = count - outer.shape[1]
    upper_part = jnp.where(even | ends, 1.0, 0.0)
    outer_part = jnp.where(even, 1.0, 0.0)

    def above(k, y):
        beyond = outer[k, pl.ds(y, ROWS), :] if y < half + ROWS - 1 else jnp.zeros((ROWS, width))
        return jnp.where(even, inner[k, pl.ds(y, ROWS), :], beyond)

    def above_upper(k, y):
        return jnp.where(even, inner[k, pl.ds(y, ROWS), :], 0.0)

    def below(k, y):
        return outer[k, pl.ds(y - shift, ROWS), :]

    total = jnp.zeros((ROWS, width), jnp.float32)
    for y0 in range(0, count, ROWS):
        part = pl.ds(y0, ROWS)
        lower_half = y0 < half
        _, own = layer_modes(rows_of(v2), y0, count)
        _, high = layer_modes(above if lower_half else above_upper, y0, count)
        energy = element_energy(element_modes(own, high, 1.0)) * mod_own[part, :]
        total += energy if lower_half else energy * upper_part
        if not lower_half:
            _, low = layer_modes(below, y0, count)
            energy = element_energy(element_modes(low, own, 1.0)) * mod_outer[part, :]
            total += energy * outer_part
    moments[...] = before[...] + jnp.concatenate(
        [
            jnp.zeros((5, width), jnp.float32),
            line(total),
            jnp.zeros((2, width), jnp.float32),
        ],
        axis=0,
    )


def coefficients(m):
    step = m[0] / m[1]
    x0 = step
    r1 = -step
    norm = m[0] + 2.0 * r1 * m[1] + r1 * r1 * m[2]
    ratio = norm / m[0]
    p0, p1 = 1.0 + ratio, r1
    step = norm / (p0 * p0 * m[1] + 2.0 * p0 * p1 * m[2] + p1 * p1 * m[3])
    x0, x1 = x0 + step * p0, step * p1
    r1, r2 = r1 - step * p0, -step * p1
    after = (
        m[0]
        + 2.0 * r1 * m[1]
        + (r1 * r1 + 2.0 * r2) * m[2]
        + 2.0 * r1 * r2 * m[3]
        + r2 * r2 * m[4]
    )
    ratio = after / norm
    p0, p1, p2 = 1.0 + ratio * p0, r1 + ratio * p1, r2
    step = after / (
        p0 * p0 * m[1]
        + 2.0 * p0 * p1 * m[2]
        + (p1 * p1 + 2.0 * p0 * p2) * m[3]
        + 2.0 * p1 * p2 * m[4]
        + p2 * p2 * m[5]
    )
    return x0 + step * p0, x1 + step * p1, step * p2


def combine_kernel(
    gathered, v0, v0_high, v1, v1_high, v2, v2_outer, v2_inner, v2_upper, slope_factor,
    slope, factors,
    own, high,
):
    even = lax.axis_index("sub") == 0
    count = v0.shape[1]
    half = count // 2
    sums = jnp.sum(jnp.sum(gathered[...], axis=0), axis=1, keepdims=True)
    c0, c1, c2 = coefficients([sums[k : k + 1] for k in range(6)])
    for n, c in enumerate((c0, c1, c2)):
        factors[n] = jnp.broadcast_to(c, factors.shape[1:])
    for k in range(3):
        own[k] = c0 * v0[k] + c1 * v1[k] + c2 * v2[k]
        for part, beyond in (
            (pl.ds(0, half), v2_outer[k, pl.ds(0, half), :]),
            (pl.ds(half, half), v2_upper[k]),
        ):
            third = jnp.where(even, v2_inner[k, part, :], beyond)
            high[k, part, :] = c0 * v0_high[k, part, :] + c1 * v1_high[k, part, :] + c2 * third

    def use(y0, energy):
        slope[pl.ds(y0, ROWS), :] = slope_factor[pl.ds(y0, ROWS), :] * energy

    energy_loop(count, rows_of(own), rows_of(high), use)


def displace_kernel(factors, v0, v0_inner, v1, v1_inner, v2, v2_inner, displacement):
    sub = lax.axis_index("sub")
    half = displacement.shape[2]
    mine = pl.ds(pl.multiple_of(sub * half, half), half)
    c0, c1, c2 = (factors[n][:1, :1] for n in range(3))
    for k in range(3):
        displacement[k, sub] = c0 * v0[k, mine, :] + c1 * v1[k, mine, :] + c2 * v2[k, mine, :]
        displacement[k, 1 - sub] = (
            c0 * v0_inner[k, mine, :] + c1 * v1_inner[k, mine, :] + c2 * v2_inner[k, mine, :]
        )


def scale_kernel(*refs):
    slopes, (chain_factor, scaled, same, cross, across) = refs[:-5], refs[-5:]
    sub = lax.axis_index("sub")
    total = slopes[0][...]
    for other in slopes[1:]:
        total = total + other[...]
    scaled[...] = total * chain_factor[...]
    window = same.shape[0]
    shift = scaled.shape[0] - window
    same[...] = scaled[pl.ds(pl.multiple_of(sub * shift, 8), window), :]
    cross[...] = scaled[pl.ds(pl.multiple_of((1 - sub) * shift, 8), window), :]
    across[...] = cross[...]


def gradient_kernel(scaled, outer, far, partner, gradient, planes, sums):
    sub = lax.axis_index("sub")
    window = partner.shape[0]
    shift = scaled.shape[0] - window
    mine = scaled[pl.ds(pl.multiple_of(sub * shift, 8), window), :]

    @pl.when(sub == 0)
    def _():
        planes[0] = outer[...]
        planes[1] = mine
        planes[2] = partner[...]
        planes[3] = far[...]

    @pl.when(sub == 1)
    def _():
        planes[0] = far[...]
        planes[1] = partner[...]
        planes[2] = mine
        planes[3] = outer[...]

    half = gradient.shape[1]
    part = pl.ds(pl.multiple_of(sub * (window - half), 8), half)
    for layer in range(2):
        sums[...] = filter_planes(planes[layer], planes[layer + 1], planes[layer + 2])
        gradient[layer] = sums[part, :]


def call(body, outs, scratch=(), name=None, work=False):
    cost = pl.CostEstimate(flops=10**7, bytes_accessed=4 * 10**6, transcendentals=0)
    return pl.pallas_call(
        body,
        out_shape=[jax.ShapeDtypeStruct(shape, jnp.float32) for shape in outs],
        scratch_shapes=[pltpu.VMEM(shape, jnp.float32) for shape in scratch],
        compiler_params=pltpu.CompilerParams(vmem_limit_bytes=16 * 2**20),
        cost_estimate=cost if work else None,
        name=name,
    )


def routes(mods, slabs):
    chips = mods * slabs

    def at(chip, sub):
        return 2 * chip + sub

    def beside(chip, steps, cyclic):
        target = chip + steps
        if cyclic:
            return target % chips
        return target if 0 <= target < chips else None

    def built(moves, cyclic):
        pairs = []
        for chip in range(chips):
            for sub, steps, to in moves:
                target = beside(chip, steps, cyclic)
                if target is not None:
                    pairs.append((at(chip, sub), at(target, to)))
        return pairs

    def in_module(moves):
        pairs = []
        for chip in range(chips):
            mod, slab = divmod(chip, slabs)
            for sub, steps, to in moves:
                pairs.append((at(chip, sub), at(mod * slabs + (slab + steps) % slabs, to)))
        return pairs

    return dict(
        swap=built([(0, 0, 1), (1, 0, 0)], True),
        first=built([(0, 1, 0), (1, -1, 1)], True),
        second=built([(1, 1, 0), (0, -1, 1)], True),
        third=in_module([(0, 1, 1), (1, 1, 0)]),
        fourth=in_module([(0, 1, 0), (1, 1, 1)]),
        outer=built([(1, 1, 0), (0, -1, 1)], False),
        down=built([(0, -1, 1)], False),
        halo_cross=in_module([(1, 1, 0), (0, -1, 1)]),
        halo_same=in_module([(0, -1, 0), (1, 1, 1)]),
    )


def module_routes(mods):
    if mods & (mods - 1) == 0:
        return [[(m, m ^ s) for m in range(mods)] for s in range(1, mods)]
    return [[(m, (m + s) % mods) for m in range(mods)] for s in range(1, mods)]


def local(mods, slabs, design, fixed, load):
    half, width = design.shape[1:]
    count = 2 * half
    path = routes(mods, slabs)

    def move(value, name):
        return lax.ppermute(value, AXES, path[name])

    plane = (count, width)
    layer = (3, count, width)
    block = (half, width)
    free = (1 - fixed).astype(jnp.float32)
    swap, first, second, third, fourth, own = call(
        prepare_kernel,
        [(11,) + block, (4,) + block, (4,) + block, block, block, (11,) + block],
        name="prepare",
    )(free, load, design)
    first = move(first, "first")
    second = move(second, "second")
    third = move(third, "third")
    fourth = move(fourth, "fourth")
    swap = move(swap, "swap")

    def start_body(*refs):
        start_outer_kernel(mods, slabs, *refs)

    v0, v0_inner, free, fields, parts = call(
        start_inner_kernel,
        [layer, layer, layer, (12,) + plane, (3,) + plane],
        [(2,) + plane],
        name="start_inner",
        work=True,
    )(own, swap)
    v1, v0_high, mod_inner, mod_outer, mod_own, slope_factor, chain_factor, moments = call(
        start_body,
        [layer, layer, plane, plane, plane, plane, plane, (8, width)],
        [layer, plane, plane],
        name="start_outer",
    )(first, second, third, fourth, v0, v0_inner, free, fields, parts)
    outer = move(v1, "outer")
    inner = move(v1, "swap")
    (fields,) = call(second_inner_kernel, [(12,) + plane], name="second_inner", work=True)(v1, inner)
    window = half + 8
    v2, v1_high, moments, v2_window, v2_upper = call(
        second_outer_kernel,
        [layer, layer, (8, width), (3, window, width), (3, half, width)],
        name="second_outer",
    )(v1, outer, inner, fields, free, mod_inner, mod_outer, moments)
    v2_outer = move(v2_window, "outer")
    v2_inner = move(v2, "swap")
    v2_upper = move(v2_upper, "down")

    def third_body(*refs):
        third_kernel(mods, slabs, *refs)

    (moments,) = call(third_body, [(8, width)], name="third")(
        v2_outer, v2_inner, v2, mod_own, mod_outer, moments
    )
    devices = 2 * mods * slabs
    gathered = lax.all_to_all(
        jnp.broadcast_to(moments, (devices, 8, width)), AXES, 0, 0, tiled=True
    )
    slope, factors = call(
        combine_kernel, [plane, (3, 8, width)], [layer, layer], name="combine"
    )(gathered, v0, v0_high, v1, v1_high, v2, v2_outer, v2_inner, v2_upper, slope_factor)
    slopes = [slope] + [lax.ppermute(slope, "mod", pairs) for pairs in module_routes(mods)]
    (displacement,) = call(displace_kernel, [(3, 2, half, width)], name="displace", work=True)(
        factors, v0, v0_inner, v1, inner, v2, v2_inner
    )
    window = half + 8
    scaled, same, cross, across = call(
        scale_kernel, [plane, (window, width), (window, width), (window, width)], name="scale"
    )(*slopes, chain_factor)
    scaled, displacement = lax.optimization_barrier((scaled, displacement))
    outer = move(cross, "halo_cross")
    far = move(same, "halo_same")
    partner = move(across, "swap")
    (gradient,) = call(
        gradient_kernel, [(2, half, width)], [(4, window, width), (window, width)], name="gradient"
    )(scaled, outer, far, partner)
    return displacement, gradient


def solution(mesh):
    mods, slabs = mesh.shape["mod"], mesh.shape["slab"]
    assert mesh.shape["sub"] == 2
    deck = P(None, ("mod", "slab"), "sub", None)

    def body(design, fixed_mask, load_mask):
        return local(mods, slabs, design, fixed_mask, load_mask)

    return jax.shard_map(
        body,
        mesh=mesh,
        in_specs=(P("slab", "sub", None), deck, deck),
        out_specs=(deck, P("slab", "sub", None)),
        check_vma=False,
    )
```

```python
import math

import jax
import jax.numpy as jnp
import numpy as np
from jax import lax
from jax.experimental import pallas as pl
from jax.experimental.pallas import tpu as pltpu
from jax.sharding import PartitionSpec as P

stiff_floor = 0.01
penalty = 3.0
sharpness = 4.0
threshold = 0.5
filter_reach = 1.8

AXES = ("mod", "slab", "sub")
ROWS = 16
FACE = filter_reach - 1.0
EDGE = filter_reach - math.sqrt(2.0)
CORNER = filter_reach - math.sqrt(3.0)
LOWER = math.tanh(sharpness * threshold)
UPPER = math.tanh(sharpness * (1.0 - threshold))


def stiffness_modes():
    poisson = 0.3
    lame = poisson / ((1.0 + poisson) * (1.0 - 2.0 * poisson))
    shear = 1.0 / (2.0 * (1.0 + poisson))
    elastic = np.zeros((6, 6))
    elastic[:3, :3] = lame
    for axis in range(3):
        elastic[axis, axis] += 2.0 * shear
        elastic[axis + 3, axis + 3] = shear
    offset = 0.5 / math.sqrt(3.0)
    points = [0.5 - offset, 0.5 + offset]
    stiffness = np.zeros((24, 24))
    for point in ((a, b, c) for a in points for b in points for c in points):
        strain = np.zeros((6, 24))
        for corner in range(8):
            bits = (corner >> 2 & 1, corner >> 1 & 1, corner & 1)
            along = [point[a] if bits[a] else 1.0 - point[a] for a in range(3)]
            sign = [1.0 if bits[a] else -1.0 for a in range(3)]
            gx = sign[0] * along[1] * along[2]
            gy = along[0] * sign[1] * along[2]
            gz = along[0] * along[1] * sign[2]
            col = 3 * corner
            strain[0, col] = gx
            strain[1, col + 1] = gy
            strain[2, col + 2] = gz
            strain[3, col], strain[3, col + 1] = gy, gx
            strain[4, col + 1], strain[4, col + 2] = gz, gy
            strain[5, col], strain[5, col + 2] = gz, gx
        stiffness += strain.T @ elastic @ strain / 8.0
    basis = np.zeros((24, 24))
    for mode in range(8):
        for corner in range(8):
            value = 1.0
            for bit in range(3):
                if mode >> bit & 1 and not corner >> bit & 1:
                    value = -value
            for k in range(3):
                basis[3 * mode + k, 3 * corner + k] = value
    table = basis @ stiffness @ basis.T / 64.0
    table[np.abs(table) < 1e-9] = 0.0
    return table


TABLE = stiffness_modes()


def lanes(shape):
    return lax.broadcasted_iota(jnp.int32, shape, 1)


def rows(shape):
    return lax.broadcasted_iota(jnp.int32, shape, 0)


def z_up(x):
    return jnp.where(lanes(x.shape) < x.shape[1] - 1, pltpu.roll(x, x.shape[1] - 1, 1), 0.0)


def z_down(x):
    return jnp.where(lanes(x.shape) > 0, pltpu.roll(x, 1, 1), 0.0)


def y_up(x):
    return jnp.where(rows(x.shape) < x.shape[0] - 1, pltpu.roll(x, x.shape[0] - 1, 0), 0.0)


def y_down(x):
    return jnp.where(rows(x.shape) > 0, pltpu.roll(x, 1, 0), 0.0)


def two_rows(read, y0, count):
    here = read(y0)
    above = y_up(here) if y0 + ROWS == count else read(y0 + 1)
    return here, above


def face_modes(here, above):
    out = []
    for part in (here + above, above - here):
        shifted = z_up(part)
        out += [part + shifted, shifted - part]
    return out


def element_modes(own, other, side):
    sums = [[other[k][m] + own[k][m] for m in range(4)] for k in range(3)]
    diffs = [[(other[k][m] - own[k][m]) * side for m in range(4)] for k in range(3)]
    return [sums[k] + diffs[k] for k in range(3)]


def mode_forces(q):
    made = {}

    def scaled(j, value):
        key = (j, round(value, 12))
        if key not in made:
            made[key] = q[j % 3][j // 3] * np.float32(value)
        return made[key]

    out = [[None] * 8 for _ in range(3)]
    for i in range(24):
        total = None
        for j in np.nonzero(TABLE[i])[0]:
            term = scaled(int(j), float(TABLE[i, j]))
            total = term if total is None else total + term
        out[i % 3][i // 3] = total
    return out


def element_energy(q):
    r = mode_forces(q)
    total = None
    for k in range(3):
        for m in range(1, 8):
            term = q[k][m] * r[k][m]
            total = term if total is None else total + term
    return total


def own_fields(own, other, side):
    r = mode_forces(element_modes(own, other, side))
    fields = []
    for k in range(3):
        for m in range(4):
            d = r[k][m + 4] * side
            fields.append(-d if r[k][m] is None else r[k][m] - d)
    return fields


def layer_modes(read, y0, count):
    heres, modes = [], []
    for k in range(3):
        here, above = two_rows(lambda y, k=k: read(k, y), y0, count)
        heres.append(here)
        modes.append(face_modes(here, above))
    return heres, modes


def fields_loop(count, read_own, read_other, side, fields):
    for y0 in range(0, count, ROWS):
        _, own = layer_modes(read_own, y0, count)
        _, other = layer_modes(read_other, y0, count)
        for n, value in enumerate(own_fields(own, other, side)):
            fields[n, pl.ds(y0, ROWS), :] = value


def operator_loop(count, read_own, read_other, side, fields, mod_inner, mod_outer, free, out_ref):
    shape = (ROWS, out_ref.shape[2])
    square = jnp.zeros(shape, jnp.float32)
    cross = jnp.zeros(shape, jnp.float32)
    norm = jnp.zeros(shape, jnp.float32)
    carry = [jnp.zeros(shape, jnp.float32)] * 3
    first = rows(shape) == 0
    for y0 in range(0, count, ROWS):
        part = pl.ds(y0, ROWS)
        owns, own = layer_modes(read_own, y0, count)
        _, other = layer_modes(read_other, y0, count)
        inner, outer = mod_inner[part, :], mod_outer[part, :]
        total = [
            outer * value + inner * fields[n, part, :]
            for n, value in enumerate(own_fields(own, other, side))
        ]
        for k in range(3):
            faces = []
            for py in range(2):
                s, d = total[4 * k + 2 * py], total[4 * k + 2 * py + 1]
                faces.append((s - d) + z_down(s + d))
            rolled = pltpu.roll(faces[0] + faces[1], 1, 0)
            force = (faces[0] - faces[1]) + jnp.where(first, carry[k], rolled)
            carry[k] = rolled
            image = free[k, part, :] * force
            out_ref[k, part, :] = image
            square += image * image
            cross += owns[k] * image
            norm += owns[k] * owns[k]
    return norm, cross, square


def energy_loop(count, read_own, read_high, use):
    for y0 in range(0, count, ROWS):
        _, own = layer_modes(read_own, y0, count)
        _, high = layer_modes(read_high, y0, count)
        use(y0, element_energy(element_modes(own, high, 1.0)))


def rows_of(ref):
    return lambda k, y: ref[k, pl.ds(y, ROWS), :]


def inner_side(sub):
    return jnp.where(sub == 0, 1.0, -1.0).astype(jnp.float32)


def line(tile):
    return jnp.sum(tile, axis=0, keepdims=True)


def prepare_kernel(free, load, design, swap, first, second, third, fourth, own):
    sub = lax.axis_index("sub")
    for k in range(3):
        frees = [free[k, layer] for layer in range(2)]
        values = [frees[layer] * load[k, layer].astype(jnp.float32) for layer in range(2)]
        for layer in range(2):
            swap[2 * k + layer] = values[layer]
            own[2 * k + layer] = values[layer]
        low = sub == 0
        swap[6 + k] = jnp.where(low, frees[1], frees[0])
        own[6 + k] = jnp.where(low, frees[0], frees[1])
        first[k] = jnp.where(low, values[1], values[0])
        second[k] = jnp.where(low, values[0], values[1])
    low = sub == 0
    for layer in range(2):
        swap[9 + layer] = design[layer]
        own[9 + layer] = design[layer]
    later = jnp.where(low, design[1], design[0])
    sooner = jnp.where(low, design[0], design[1])
    first[3] = later
    third[...] = later
    second[3] = sooner
    fourth[...] = sooner


def around(p):
    across = y_up(p) + y_down(p)
    return across + z_up(p) + z_down(p), z_up(across) + z_down(across)


def filter_mid(p):
    face, diag = around(p)
    return filter_reach * p + FACE * face + EDGE * diag


def filter_side(p):
    face, diag = around(p)
    return FACE * p + EDGE * face + CORNER * diag


def filter_planes(low, mid, high):
    return filter_side(low + high) + filter_mid(mid)


def weight_plane(shape, row_offset, count):
    row = rows(shape) + row_offset
    lane = lanes(shape)

    def neighbours(index, size):
        return jnp.where(index > 0, 1.0, 0.0) + jnp.where(index < size - 1, 1.0, 0.0)

    ry = neighbours(row, count)
    rz = neighbours(lane, shape[1])
    face, diag = ry + rz, ry * rz
    return (
        filter_reach
        + FACE * (2.0 + face)
        + EDGE * (2.0 * face + diag)
        + (2.0 * CORNER) * diag
    )


def start_inner_kernel(own, swap, v0, v0_inner, free, fields, parts, layers):
    sub = lax.axis_index("sub")
    half = own.shape[1]
    count = 2 * half
    mine = pl.ds(pl.multiple_of(sub * half, half), half)
    other = pl.ds(pl.multiple_of((1 - sub) * half, half), half)
    for layer in range(2):
        layers[layer, mine, :] = own[9 + layer]
        layers[layer, other, :] = swap[9 + layer]

    @pl.when(sub == 0)
    def _():
        parts[0] = filter_side(layers[0])
        parts[1] = filter_mid(layers[0]) + filter_side(layers[1])

    @pl.when(sub == 1)
    def _():
        parts[0] = filter_mid(layers[0]) + filter_side(layers[1])
        parts[1] = filter_side(layers[0]) + filter_mid(layers[1])

    parts[2] = 1.0 / weight_plane((count, own.shape[2]), 0, count)
    for k in range(3):
        free[k, mine, :] = own[6 + k]
        free[k, other, :] = swap[6 + k]
        v0[k, mine, :] = own[2 * k + sub]
        v0[k, other, :] = swap[2 * k + sub]
        v0_inner[k, mine, :] = own[2 * k + 1 - sub]
        v0_inner[k, other, :] = swap[2 * k + 1 - sub]
    fields_loop(count, rows_of(v0), rows_of(v0_inner), inner_side(sub), fields)


def start_outer_kernel(
    mods, slabs,
    first, second, third, fourth, v0, v0_inner, free, fields, parts,
    v1, v0_high, mod_inner, mod_outer, mod_own, slope_factor, chain_factor, moments,
    v0_outer, near, deep,
):
    mod, slab, sub = (lax.axis_index(a) for a in AXES)
    half = third.shape[0]
    count = 2 * half
    even = sub == 0
    mine = pl.ds(pl.multiple_of(sub * half, half), half)
    other = pl.ds(pl.multiple_of((1 - sub) * half, half), half)
    near[mine, :] = first[3]
    near[other, :] = second[3]
    deep[mine, :] = fourth[...]
    deep[other, :] = third[...]
    starts = (mod == 0) & (slab == 0) & even
    ends = (mod == mods - 1) & (slab == slabs - 1) & (sub == 1)
    inside = jnp.where(ends, 0.0, 1.0)
    for k in range(3):
        v0_outer[k, mine, :] = first[k] * inside
        v0_outer[k, other, :] = second[k] * inside
        v0_high[k] = jnp.where(even, v0_inner[k], v0_outer[k])

    side = filter_side(near[...])
    mid = filter_mid(near[...])
    inverse = parts[2]
    filtered = (parts[0] + filter_side(deep[...]) + jnp.where(even, mid, 0.0)) * inverse
    hyper = jnp.tanh(sharpness * (filtered - threshold))
    projected = (LOWER + hyper) * (1.0 / (LOWER + UPPER))
    below = stiff_floor + (1.0 - stiff_floor) * projected * projected * projected
    below = below * jnp.where(starts, 0.0, 1.0)
    filtered = (parts[1] + side) * inverse
    hyper = jnp.tanh(sharpness * (filtered - threshold))
    projected = (LOWER + hyper) * (1.0 / (LOWER + UPPER))
    squared = projected * projected
    stiff = stiff_floor + (1.0 - stiff_floor) * squared * projected
    mod_own[...] = stiff
    mod_inner[...] = jnp.where(even, stiff, below)
    mod_outer[...] = jnp.where(even, below, stiff)
    slope_factor[...] = (-penalty * (1.0 - stiff_floor)) * squared
    chain_factor[...] = (sharpness / (LOWER + UPPER)) * (1.0 - hyper * hyper) * inverse

    norm, cross, square = operator_loop(
        count, rows_of(v0), rows_of(v0_outer), -inner_side(sub), fields, mod_inner, mod_outer, free, v1
    )
    moments[...] = jnp.concatenate(
        [line(norm), line(cross), line(square), jnp.zeros((5, norm.shape[1]), jnp.float32)], axis=0
    )


def second_inner_kernel(v1, inner, fields):
    fields_loop(v1.shape[1], rows_of(v1), rows_of(inner), inner_side(lax.axis_index("sub")), fields)


def second_outer_kernel(
    v1, outer, inner, fields, free, mod_inner, mod_outer, before, v2, v1_high, moments
):
    sub = lax.axis_index("sub")
    count = v1.shape[1]
    for k in range(3):
        v1_high[k] = jnp.where(sub == 0, inner[k], outer[k])
    _, cross, square = operator_loop(
        count, rows_of(v1), rows_of(outer), -inner_side(sub), fields, mod_inner, mod_outer, free, v2
    )
    zero = jnp.zeros((3, cross.shape[1]), jnp.float32)
    moments[...] = before[...] + jnp.concatenate(
        [zero, line(cross), line(square), zero], axis=0
    )


def third_kernel(v2_outer, v2_inner, v2, mod_own, before, moments, v2_high):
    even = lax.axis_index("sub") == 0
    for k in range(3):
        v2_high[k] = jnp.where(even, v2_inner[k], v2_outer[k])
    count = v2.shape[1]
    total = [jnp.zeros((ROWS, v2.shape[2]), jnp.float32)]

    def use(y0, energy):
        total[0] += energy * mod_own[pl.ds(y0, ROWS), :]

    energy_loop(
        count,
        lambda k, y: v2[k, pl.ds(y, ROWS), :],
        lambda k, y: v2_high[k, pl.ds(y, ROWS), :],
        use,
    )
    width = v2.shape[2]
    moments[...] = before[...] + jnp.concatenate(
        [
            jnp.zeros((5, width), jnp.float32),
            line(total[0]),
            jnp.zeros((2, width), jnp.float32),
        ],
        axis=0,
    )


def coefficients(m):
    step = m[0] / m[1]
    x0 = step
    r1 = -step
    norm = m[0] + 2.0 * r1 * m[1] + r1 * r1 * m[2]
    ratio = norm / m[0]
    p0, p1 = 1.0 + ratio, r1
    step = norm / (p0 * p0 * m[1] + 2.0 * p0 * p1 * m[2] + p1 * p1 * m[3])
    x0, x1 = x0 + step * p0, step * p1
    r1, r2 = r1 - step * p0, -step * p1
    after = (
        m[0]
        + 2.0 * r1 * m[1]
        + (r1 * r1 + 2.0 * r2) * m[2]
        + 2.0 * r1 * r2 * m[3]
        + r2 * r2 * m[4]
    )
    ratio = after / norm
    p0, p1, p2 = 1.0 + ratio * p0, r1 + ratio * p1, r2
    step = after / (
        p0 * p0 * m[1]
        + 2.0 * p0 * p1 * m[2]
        + (p1 * p1 + 2.0 * p0 * p2) * m[3]
        + 2.0 * p1 * p2 * m[4]
        + p2 * p2 * m[5]
    )
    return x0 + step * p0, x1 + step * p1, step * p2


def combine_kernel(
    gathered, v0, v0_high, v1, v1_high, v2, v2_high, slope_factor, slope, factors, own, high
):
    count = v0.shape[1]
    sums = jnp.sum(jnp.sum(gathered[...], axis=0), axis=1, keepdims=True)
    c0, c1, c2 = coefficients([sums[k : k + 1] for k in range(6)])
    for n, c in enumerate((c0, c1, c2)):
        factors[n] = jnp.broadcast_to(c, factors.shape[1:])
    for k in range(3):
        own[k] = c0 * v0[k] + c1 * v1[k] + c2 * v2[k]
        high[k] = c0 * v0_high[k] + c1 * v1_high[k] + c2 * v2_high[k]

    def use(y0, energy):
        slope[pl.ds(y0, ROWS), :] = slope_factor[pl.ds(y0, ROWS), :] * energy

    energy_loop(count, rows_of(own), rows_of(high), use)


def displace_kernel(factors, v0, v0_inner, v1, v1_inner, v2, v2_inner, displacement):
    sub = lax.axis_index("sub")
    half = displacement.shape[2]
    mine = pl.ds(pl.multiple_of(sub * half, half), half)
    c0, c1, c2 = (factors[n][:1, :1] for n in range(3))
    for k in range(3):
        displacement[k, sub] = c0 * v0[k, mine, :] + c1 * v1[k, mine, :] + c2 * v2[k, mine, :]
        displacement[k, 1 - sub] = (
            c0 * v0_inner[k, mine, :] + c1 * v1_inner[k, mine, :] + c2 * v2_inner[k, mine, :]
        )


def scale_kernel(*refs):
    slopes, (chain_factor, scaled, same, cross, across) = refs[:-5], refs[-5:]
    sub = lax.axis_index("sub")
    total = slopes[0][...]
    for other in slopes[1:]:
        total = total + other[...]
    scaled[...] = total * chain_factor[...]
    window = same.shape[0]
    shift = scaled.shape[0] - window
    same[...] = scaled[pl.ds(pl.multiple_of(sub * shift, 8), window), :]
    cross[...] = scaled[pl.ds(pl.multiple_of((1 - sub) * shift, 8), window), :]
    across[...] = cross[...]


def gradient_kernel(scaled, outer, far, partner, gradient, planes, sums):
    sub = lax.axis_index("sub")
    window = partner.shape[0]
    shift = scaled.shape[0] - window
    mine = scaled[pl.ds(pl.multiple_of(sub * shift, 8), window), :]

    @pl.when(sub == 0)
    def _():
        planes[0] = outer[...]
        planes[1] = mine
        planes[2] = partner[...]
        planes[3] = far[...]

    @pl.when(sub == 1)
    def _():
        planes[0] = far[...]
        planes[1] = partner[...]
        planes[2] = mine
        planes[3] = outer[...]

    half = gradient.shape[1]
    part = pl.ds(pl.multiple_of(sub * (window - half), 8), half)
    for layer in range(2):
        sums[...] = filter_planes(planes[layer], planes[layer + 1], planes[layer + 2])
        gradient[layer] = sums[part, :]


def call(body, outs, scratch=(), name=None, work=False):
    cost = pl.CostEstimate(flops=10**7, bytes_accessed=4 * 10**6, transcendentals=0)
    return pl.pallas_call(
        body,
        out_shape=[jax.ShapeDtypeStruct(shape, jnp.float32) for shape in outs],
        scratch_shapes=[pltpu.VMEM(shape, jnp.float32) for shape in scratch],
        compiler_params=pltpu.CompilerParams(vmem_limit_bytes=16 * 2**20),
        cost_estimate=cost if work else None,
        name=name,
    )


def routes(mods, slabs):
    chips = mods * slabs

    def at(chip, sub):
        return 2 * chip + sub

    def beside(chip, steps, cyclic):
        target = chip + steps
        if cyclic:
            return target % chips
        return target if 0 <= target < chips else None

    def built(moves, cyclic):
        pairs = []
        for chip in range(chips):
            for sub, steps, to in moves:
                target = beside(chip, steps, cyclic)
                if target is not None:
                    pairs.append((at(chip, sub), at(target, to)))
        return pairs

    def in_module(moves):
        pairs = []
        for chip in range(chips):
            mod, slab = divmod(chip, slabs)
            for sub, steps, to in moves:
                pairs.append((at(chip, sub), at(mod * slabs + (slab + steps) % slabs, to)))
        return pairs

    return dict(
        swap=built([(0, 0, 1), (1, 0, 0)], True),
        first=built([(0, 1, 0), (1, -1, 1)], True),
        second=built([(1, 1, 0), (0, -1, 1)], True),
        third=in_module([(0, 1, 1), (1, 1, 0)]),
        fourth=in_module([(0, 1, 0), (1, 1, 1)]),
        outer=built([(1, 1, 0), (0, -1, 1)], False),
        down=built([(0, -1, 1)], False),
        halo_cross=in_module([(1, 1, 0), (0, -1, 1)]),
        halo_same=in_module([(0, -1, 0), (1, 1, 1)]),
    )


def module_routes(mods):
    if mods & (mods - 1) == 0:
        return [[(m, m ^ s) for m in range(mods)] for s in range(1, mods)]
    return [[(m, (m + s) % mods) for m in range(mods)] for s in range(1, mods)]


def local(mods, slabs, design, fixed, load):
    half, width = design.shape[1:]
    count = 2 * half
    path = routes(mods, slabs)

    def move(value, name):
        return lax.ppermute(value, AXES, path[name])

    plane = (count, width)
    layer = (3, count, width)
    block = (half, width)
    free = (1 - fixed).astype(jnp.float32)
    swap, first, second, third, fourth, own = call(
        prepare_kernel,
        [(11,) + block, (4,) + block, (4,) + block, block, block, (11,) + block],
        name="prepare",
    )(free, load, design)
    first = move(first, "first")
    second = move(second, "second")
    third = move(third, "third")
    fourth = move(fourth, "fourth")
    swap = move(swap, "swap")

    def start_body(*refs):
        start_outer_kernel(mods, slabs, *refs)

    v0, v0_inner, free, fields, parts = call(
        start_inner_kernel,
        [layer, layer, layer, (12,) + plane, (3,) + plane],
        [(2,) + plane],
        name="start_inner",
        work=True,
    )(own, swap)
    v1, v0_high, mod_inner, mod_outer, mod_own, slope_factor, chain_factor, moments = call(
        start_body,
        [layer, layer, plane, plane, plane, plane, plane, (8, width)],
        [layer, plane, plane],
        name="start_outer",
    )(first, second, third, fourth, v0, v0_inner, free, fields, parts)
    outer = move(v1, "outer")
    inner = move(v1, "swap")
    (fields,) = call(second_inner_kernel, [(12,) + plane], name="second_inner", work=True)(v1, inner)
    v2, v1_high, moments = call(
        second_outer_kernel, [layer, layer, (8, width)], name="second_outer"
    )(v1, outer, inner, fields, free, mod_inner, mod_outer, moments)
    v2_outer = move(v2, "down")
    v2_inner = move(v2, "swap")
    moments, v2_high = call(third_kernel, [(8, width), layer], name="third")(
        v2_outer, v2_inner, v2, mod_own, moments
    )
    devices = 2 * mods * slabs
    gathered = lax.all_to_all(
        jnp.broadcast_to(moments, (devices, 8, width)), AXES, 0, 0, tiled=True
    )
    slope, factors = call(
        combine_kernel, [plane, (3, 8, width)], [layer, layer], name="combine"
    )(gathered, v0, v0_high, v1, v1_high, v2, v2_high, slope_factor)
    slopes = [slope] + [lax.ppermute(slope, "mod", pairs) for pairs in module_routes(mods)]
    (displacement,) = call(displace_kernel, [(3, 2, half, width)], name="displace", work=True)(
        factors, v0, v0_inner, v1, inner, v2, v2_inner
    )
    window = half + 8
    scaled, same, cross, across = call(
        scale_kernel, [plane, (window, width), (window, width), (window, width)], name="scale"
    )(*slopes, chain_factor)
    scaled, displacement = lax.optimization_barrier((scaled, displacement))
    outer = move(cross, "halo_cross")
    far = move(same, "halo_same")
    partner = move(across, "swap")
    (gradient,) = call(
        gradient_kernel, [(2, half, width)], [(4, window, width), (window, width)], name="gradient"
    )(scaled, outer, far, partner)
    return displacement, gradient


def solution(mesh):
    mods, slabs = mesh.shape["mod"], mesh.shape["slab"]
    assert mesh.shape["sub"] == 2
    deck = P(None, ("mod", "slab"), "sub", None)

    def body(design, fixed_mask, load_mask):
        return local(mods, slabs, design, fixed_mask, load_mask)

    return jax.shard_map(
        body,
        mesh=mesh,
        in_specs=(P("slab", "sub", None), deck, deck),
        out_specs=(deck, P("slab", "sub", None)),
        check_vma=False,
    )
```

```python
import math

import jax
import jax.numpy as jnp
import numpy as np
from jax import lax
from jax.experimental import pallas as pl
from jax.experimental.pallas import tpu as pltpu
from jax.sharding import PartitionSpec as P

stiff_floor = 0.01
penalty = 3.0
sharpness = 4.0
threshold = 0.5
filter_reach = 1.8

AXES = ("mod", "slab", "sub")
ROWS = 32
FACE = filter_reach - 1.0
EDGE = filter_reach - math.sqrt(2.0)
CORNER = filter_reach - math.sqrt(3.0)
LOWER = math.tanh(sharpness * threshold)
UPPER = math.tanh(sharpness * (1.0 - threshold))


def stiffness_modes():
    poisson = 0.3
    lame = poisson / ((1.0 + poisson) * (1.0 - 2.0 * poisson))
    shear = 1.0 / (2.0 * (1.0 + poisson))
    elastic = np.zeros((6, 6))
    elastic[:3, :3] = lame
    for axis in range(3):
        elastic[axis, axis] += 2.0 * shear
        elastic[axis + 3, axis + 3] = shear
    offset = 0.5 / math.sqrt(3.0)
    points = [0.5 - offset, 0.5 + offset]
    stiffness = np.zeros((24, 24))
    for point in ((a, b, c) for a in points for b in points for c in points):
        strain = np.zeros((6, 24))
        for corner in range(8):
            bits = (corner >> 2 & 1, corner >> 1 & 1, corner & 1)
            along = [point[a] if bits[a] else 1.0 - point[a] for a in range(3)]
            sign = [1.0 if bits[a] else -1.0 for a in range(3)]
            gx = sign[0] * along[1] * along[2]
            gy = along[0] * sign[1] * along[2]
            gz = along[0] * along[1] * sign[2]
            col = 3 * corner
            strain[0, col] = gx
            strain[1, col + 1] = gy
            strain[2, col + 2] = gz
            strain[3, col], strain[3, col + 1] = gy, gx
            strain[4, col + 1], strain[4, col + 2] = gz, gy
            strain[5, col], strain[5, col + 2] = gz, gx
        stiffness += strain.T @ elastic @ strain / 8.0
    basis = np.zeros((24, 24))
    for mode in range(8):
        for corner in range(8):
            value = 1.0
            for bit in range(3):
                if mode >> bit & 1 and not corner >> bit & 1:
                    value = -value
            for k in range(3):
                basis[3 * mode + k, 3 * corner + k] = value
    table = basis @ stiffness @ basis.T / 64.0
    table[np.abs(table) < 1e-9] = 0.0
    return table


TABLE = stiffness_modes()


def lanes(shape):
    return lax.broadcasted_iota(jnp.int32, shape, 1)


def rows(shape):
    return lax.broadcasted_iota(jnp.int32, shape, 0)


def z_up(x):
    return jnp.where(lanes(x.shape) < x.shape[1] - 1, pltpu.roll(x, x.shape[1] - 1, 1), 0.0)


def z_down(x):
    return jnp.where(lanes(x.shape) > 0, pltpu.roll(x, 1, 1), 0.0)


def y_up(x):
    return jnp.where(rows(x.shape) < x.shape[0] - 1, pltpu.roll(x, x.shape[0] - 1, 0), 0.0)


def y_down(x):
    return jnp.where(rows(x.shape) > 0, pltpu.roll(x, 1, 0), 0.0)


def two_rows(read, y0, count):
    here = read(y0)
    above = y_up(here) if y0 + ROWS == count else read(y0 + 1)
    return here, above


def face_modes(here, above):
    out = []
    for part in (here + above, above - here):
        shifted = z_up(part)
        out += [part + shifted, shifted - part]
    return out


def element_modes(own, other, side):
    sums = [[other[k][m] + own[k][m] for m in range(4)] for k in range(3)]
    diffs = [[(other[k][m] - own[k][m]) * side for m in range(4)] for k in range(3)]
    return [sums[k] + diffs[k] for k in range(3)]


def mode_forces(q):
    made = {}

    def scaled(j, value):
        key = (j, round(value, 12))
        if key not in made:
            made[key] = q[j % 3][j // 3] * np.float32(value)
        return made[key]

    out = [[None] * 8 for _ in range(3)]
    for i in range(24):
        total = None
        for j in np.nonzero(TABLE[i])[0]:
            term = scaled(int(j), float(TABLE[i, j]))
            total = term if total is None else total + term
        out[i % 3][i // 3] = total
    return out


def element_energy(q):
    r = mode_forces(q)
    total = None
    for k in range(3):
        for m in range(1, 8):
            term = q[k][m] * r[k][m]
            total = term if total is None else total + term
    return total


def own_fields(own, other, side):
    r = mode_forces(element_modes(own, other, side))
    fields = []
    for k in range(3):
        for m in range(4):
            d = r[k][m + 4] * side
            fields.append(-d if r[k][m] is None else r[k][m] - d)
    return fields


def layer_modes(read, y0, count):
    heres, modes = [], []
    for k in range(3):
        here, above = two_rows(lambda y, k=k: read(k, y), y0, count)
        heres.append(here)
        modes.append(face_modes(here, above))
    return heres, modes


def fields_loop(count, read_own, read_other, side, fields):
    for y0 in range(0, count, ROWS):
        _, own = layer_modes(read_own, y0, count)
        _, other = layer_modes(read_other, y0, count)
        for n, value in enumerate(own_fields(own, other, side)):
            fields[n, pl.ds(y0, ROWS), :] = value


def operator_loop(count, read_own, read_other, side, fields, mod_inner, mod_outer, free, out_ref):
    shape = (ROWS, out_ref.shape[2])
    square = jnp.zeros(shape, jnp.float32)
    cross = jnp.zeros(shape, jnp.float32)
    norm = jnp.zeros(shape, jnp.float32)
    carry = [jnp.zeros(shape, jnp.float32)] * 3
    first = rows(shape) == 0
    for y0 in range(0, count, ROWS):
        part = pl.ds(y0, ROWS)
        owns, own = layer_modes(read_own, y0, count)
        _, other = layer_modes(read_other, y0, count)
        inner, outer = mod_inner[part, :], mod_outer[part, :]
        total = [
            outer * value + inner * fields[n, part, :]
            for n, value in enumerate(own_fields(own, other, side))
        ]
        for k in range(3):
            faces = []
            for py in range(2):
                s, d = total[4 * k + 2 * py], total[4 * k + 2 * py + 1]
                faces.append((s - d) + z_down(s + d))
            rolled = pltpu.roll(faces[0] + faces[1], 1, 0)
            force = (faces[0] - faces[1]) + jnp.where(first, carry[k], rolled)
            carry[k] = rolled
            image = free[k, part, :] * force
            out_ref[k, part, :] = image
            square += image * image
            cross += owns[k] * image
            norm += owns[k] * owns[k]
    return norm, cross, square


def energy_loop(count, read_own, read_high, use):
    for y0 in range(0, count, ROWS):
        _, own = layer_modes(read_own, y0, count)
        _, high = layer_modes(read_high, y0, count)
        use(y0, element_energy(element_modes(own, high, 1.0)))


def rows_of(ref):
    return lambda k, y: ref[k, pl.ds(y, ROWS), :]


def inner_side(sub):
    return jnp.where(sub == 0, 1.0, -1.0).astype(jnp.float32)


def line(tile):
    return jnp.sum(tile, axis=0, keepdims=True)


def prepare_kernel(free, load, design, swap, first, second, third, fourth, own):
    sub = lax.axis_index("sub")
    for k in range(3):
        frees = [free[k, layer] for layer in range(2)]
        values = [frees[layer] * load[k, layer].astype(jnp.float32) for layer in range(2)]
        for layer in range(2):
            swap[2 * k + layer] = values[layer]
            own[2 * k + layer] = values[layer]
        low = sub == 0
        swap[6 + k] = jnp.where(low, frees[1], frees[0])
        own[6 + k] = jnp.where(low, frees[0], frees[1])
        first[k] = jnp.where(low, values[1], values[0])
        second[k] = jnp.where(low, values[0], values[1])
    low = sub == 0
    for layer in range(2):
        swap[9 + layer] = design[layer]
        own[9 + layer] = design[layer]
    later = jnp.where(low, design[1], design[0])
    sooner = jnp.where(low, design[0], design[1])
    first[3] = later
    third[...] = later
    second[3] = sooner
    fourth[...] = sooner


def around(p):
    across = y_up(p) + y_down(p)
    return across + z_up(p) + z_down(p), z_up(across) + z_down(across)


def filter_mid(p):
    face, diag = around(p)
    return filter_reach * p + FACE * face + EDGE * diag


def filter_side(p):
    face, diag = around(p)
    return FACE * p + EDGE * face + CORNER * diag


def filter_planes(low, mid, high):
    return filter_side(low + high) + filter_mid(mid)


def weight_plane(shape, row_offset, count):
    row = rows(shape) + row_offset
    lane = lanes(shape)

    def neighbours(index, size):
        return jnp.where(index > 0, 1.0, 0.0) + jnp.where(index < size - 1, 1.0, 0.0)

    ry = neighbours(row, count)
    rz = neighbours(lane, shape[1])
    face, diag = ry + rz, ry * rz
    return (
        filter_reach
        + FACE * (2.0 + face)
        + EDGE * (2.0 * face + diag)
        + (2.0 * CORNER) * diag
    )


def start_inner_kernel(own, swap, v0, v0_inner, free, fields, parts, layers):
    sub = lax.axis_index("sub")
    half = own.shape[1]
    count = 2 * half
    mine = pl.ds(pl.multiple_of(sub * half, half), half)
    other = pl.ds(pl.multiple_of((1 - sub) * half, half), half)
    for layer in range(2):
        layers[layer, mine, :] = own[9 + layer]
        layers[layer, other, :] = swap[9 + layer]

    @pl.when(sub == 0)
    def _():
        parts[0] = filter_side(layers[0])
        parts[1] = filter_mid(layers[0]) + filter_side(layers[1])

    @pl.when(sub == 1)
    def _():
        parts[0] = filter_mid(layers[0]) + filter_side(layers[1])
        parts[1] = filter_side(layers[0]) + filter_mid(layers[1])

    parts[2] = 1.0 / weight_plane((count, own.shape[2]), 0, count)
    for k in range(3):
        free[k, mine, :] = own[6 + k]
        free[k, other, :] = swap[6 + k]
        v0[k, mine, :] = own[2 * k + sub]
        v0[k, other, :] = swap[2 * k + sub]
        v0_inner[k, mine, :] = own[2 * k + 1 - sub]
        v0_inner[k, other, :] = swap[2 * k + 1 - sub]
    fields_loop(count, rows_of(v0), rows_of(v0_inner), inner_side(sub), fields)


def start_outer_kernel(
    mods, slabs,
    first, second, third, fourth, v0, v0_inner, free, fields, parts,
    v1, v0_high, mod_inner, mod_outer, mod_own, slope_factor, chain_factor, moments,
    v0_outer, near, deep,
):
    mod, slab, sub = (lax.axis_index(a) for a in AXES)
    half = third.shape[0]
    count = 2 * half
    even = sub == 0
    mine = pl.ds(pl.multiple_of(sub * half, half), half)
    other = pl.ds(pl.multiple_of((1 - sub) * half, half), half)
    near[mine, :] = first[3]
    near[other, :] = second[3]
    deep[mine, :] = fourth[...]
    deep[other, :] = third[...]
    starts = (mod == 0) & (slab == 0) & even
    ends = (mod == mods - 1) & (slab == slabs - 1) & (sub == 1)
    inside = jnp.where(ends, 0.0, 1.0)
    for k in range(3):
        v0_outer[k, mine, :] = first[k] * inside
        v0_outer[k, other, :] = second[k] * inside
        v0_high[k] = jnp.where(even, v0_inner[k], v0_outer[k])

    side = filter_side(near[...])
    mid = filter_mid(near[...])
    inverse = parts[2]
    filtered = (parts[0] + filter_side(deep[...]) + jnp.where(even, mid, 0.0)) * inverse
    hyper = jnp.tanh(sharpness * (filtered - threshold))
    projected = (LOWER + hyper) * (1.0 / (LOWER + UPPER))
    below = stiff_floor + (1.0 - stiff_floor) * projected * projected * projected
    below = below * jnp.where(starts, 0.0, 1.0)
    filtered = (parts[1] + side) * inverse
    hyper = jnp.tanh(sharpness * (filtered - threshold))
    projected = (LOWER + hyper) * (1.0 / (LOWER + UPPER))
    squared = projected * projected
    stiff = stiff_floor + (1.0 - stiff_floor) * squared * projected
    mod_own[...] = stiff
    mod_inner[...] = jnp.where(even, stiff, below)
    mod_outer[...] = jnp.where(even, below, stiff)
    slope_factor[...] = (-penalty * (1.0 - stiff_floor)) * squared
    chain_factor[...] = (sharpness / (LOWER + UPPER)) * (1.0 - hyper * hyper) * inverse

    norm, cross, square = operator_loop(
        count, rows_of(v0), rows_of(v0_outer), -inner_side(sub), fields, mod_inner, mod_outer, free, v1
    )
    moments[...] = jnp.concatenate(
        [line(norm), line(cross), line(square), jnp.zeros((5, norm.shape[1]), jnp.float32)], axis=0
    )


def second_inner_kernel(v1, inner, fields):
    fields_loop(v1.shape[1], rows_of(v1), rows_of(inner), inner_side(lax.axis_index("sub")), fields)


def second_outer_kernel(
    v1, outer, inner, fields, free, mod_inner, mod_outer, before, v2, v1_high, moments
):
    sub = lax.axis_index("sub")
    count = v1.shape[1]
    for k in range(3):
        v1_high[k] = jnp.where(sub == 0, inner[k], outer[k])
    _, cross, square = operator_loop(
        count, rows_of(v1), rows_of(outer), -inner_side(sub), fields, mod_inner, mod_outer, free, v2
    )
    zero = jnp.zeros((3, cross.shape[1]), jnp.float32)
    moments[...] = before[...] + jnp.concatenate(
        [zero, line(cross), line(square), zero], axis=0
    )


def third_kernel(v2_outer, v2_inner, v2, mod_own, before, moments, v2_high):
    even = lax.axis_index("sub") == 0
    for k in range(3):
        v2_high[k] = jnp.where(even, v2_inner[k], v2_outer[k])
    count = v2.shape[1]
    total = [jnp.zeros((ROWS, v2.shape[2]), jnp.float32)]

    def use(y0, energy):
        total[0] += energy * mod_own[pl.ds(y0, ROWS), :]

    energy_loop(
        count,
        lambda k, y: v2[k, pl.ds(y, ROWS), :],
        lambda k, y: v2_high[k, pl.ds(y, ROWS), :],
        use,
    )
    width = v2.shape[2]
    moments[...] = before[...] + jnp.concatenate(
        [
            jnp.zeros((5, width), jnp.float32),
            line(total[0]),
            jnp.zeros((2, width), jnp.float32),
        ],
        axis=0,
    )


def coefficients(m):
    step = m[0] / m[1]
    x0 = step
    r1 = -step
    norm = m[0] + 2.0 * r1 * m[1] + r1 * r1 * m[2]
    ratio = norm / m[0]
    p0, p1 = 1.0 + ratio, r1
    step = norm / (p0 * p0 * m[1] + 2.0 * p0 * p1 * m[2] + p1 * p1 * m[3])
    x0, x1 = x0 + step * p0, step * p1
    r1, r2 = r1 - step * p0, -step * p1
    after = (
        m[0]
        + 2.0 * r1 * m[1]
        + (r1 * r1 + 2.0 * r2) * m[2]
        + 2.0 * r1 * r2 * m[3]
        + r2 * r2 * m[4]
    )
    ratio = after / norm
    p0, p1, p2 = 1.0 + ratio * p0, r1 + ratio * p1, r2
    step = after / (
        p0 * p0 * m[1]
        + 2.0 * p0 * p1 * m[2]
        + (p1 * p1 + 2.0 * p0 * p2) * m[3]
        + 2.0 * p1 * p2 * m[4]
        + p2 * p2 * m[5]
    )
    return x0 + step * p0, x1 + step * p1, step * p2


def combine_kernel(
    gathered, v0, v0_high, v1, v1_high, v2, v2_high, slope_factor, slope, factors, own, high
):
    count = v0.shape[1]
    sums = jnp.sum(jnp.sum(gathered[...], axis=0), axis=1, keepdims=True)
    c0, c1, c2 = coefficients([sums[k : k + 1] for k in range(6)])
    for n, c in enumerate((c0, c1, c2)):
        factors[n] = jnp.broadcast_to(c, factors.shape[1:])
    for k in range(3):
        own[k] = c0 * v0[k] + c1 * v1[k] + c2 * v2[k]
        high[k] = c0 * v0_high[k] + c1 * v1_high[k] + c2 * v2_high[k]

    def use(y0, energy):
        slope[pl.ds(y0, ROWS), :] = slope_factor[pl.ds(y0, ROWS), :] * energy

    energy_loop(count, rows_of(own), rows_of(high), use)


def displace_kernel(factors, v0, v0_inner, v1, v1_inner, v2, v2_inner, displacement):
    sub = lax.axis_index("sub")
    half = displacement.shape[2]
    mine = pl.ds(pl.multiple_of(sub * half, half), half)
    c0, c1, c2 = (factors[n][:1, :1] for n in range(3))
    for k in range(3):
        displacement[k, sub] = c0 * v0[k, mine, :] + c1 * v1[k, mine, :] + c2 * v2[k, mine, :]
        displacement[k, 1 - sub] = (
            c0 * v0_inner[k, mine, :] + c1 * v1_inner[k, mine, :] + c2 * v2_inner[k, mine, :]
        )


def scale_kernel(*refs):
    slopes, (chain_factor, scaled, same, cross, across) = refs[:-5], refs[-5:]
    sub = lax.axis_index("sub")
    total = slopes[0][...]
    for other in slopes[1:]:
        total = total + other[...]
    scaled[...] = total * chain_factor[...]
    window = same.shape[0]
    shift = scaled.shape[0] - window
    same[...] = scaled[pl.ds(pl.multiple_of(sub * shift, 8), window), :]
    cross[...] = scaled[pl.ds(pl.multiple_of((1 - sub) * shift, 8), window), :]
    across[...] = cross[...]


def gradient_kernel(scaled, outer, far, partner, gradient, planes, sums):
    sub = lax.axis_index("sub")
    window = partner.shape[0]
    shift = scaled.shape[0] - window
    mine = scaled[pl.ds(pl.multiple_of(sub * shift, 8), window), :]

    @pl.when(sub == 0)
    def _():
        planes[0] = outer[...]
        planes[1] = mine
        planes[2] = partner[...]
        planes[3] = far[...]

    @pl.when(sub == 1)
    def _():
        planes[0] = far[...]
        planes[1] = partner[...]
        planes[2] = mine
        planes[3] = outer[...]

    half = gradient.shape[1]
    part = pl.ds(pl.multiple_of(sub * (window - half), 8), half)
    for layer in range(2):
        sums[...] = filter_planes(planes[layer], planes[layer + 1], planes[layer + 2])
        gradient[layer] = sums[part, :]


def call(body, outs, scratch=(), name=None, work=False):
    cost = pl.CostEstimate(flops=10**7, bytes_accessed=4 * 10**6, transcendentals=0)
    return pl.pallas_call(
        body,
        out_shape=[jax.ShapeDtypeStruct(shape, jnp.float32) for shape in outs],
        scratch_shapes=[pltpu.VMEM(shape, jnp.float32) for shape in scratch],
        compiler_params=pltpu.CompilerParams(vmem_limit_bytes=16 * 2**20),
        cost_estimate=cost if work else None,
        name=name,
    )


def routes(mods, slabs):
    chips = mods * slabs

    def at(chip, sub):
        return 2 * chip + sub

    def beside(chip, steps, cyclic):
        target = chip + steps
        if cyclic:
            return target % chips
        return target if 0 <= target < chips else None

    def built(moves, cyclic):
        pairs = []
        for chip in range(chips):
            for sub, steps, to in moves:
                target = beside(chip, steps, cyclic)
                if target is not None:
                    pairs.append((at(chip, sub), at(target, to)))
        return pairs

    def in_module(moves):
        pairs = []
        for chip in range(chips):
            mod, slab = divmod(chip, slabs)
            for sub, steps, to in moves:
                pairs.append((at(chip, sub), at(mod * slabs + (slab + steps) % slabs, to)))
        return pairs

    return dict(
        swap=built([(0, 0, 1), (1, 0, 0)], True),
        first=built([(0, 1, 0), (1, -1, 1)], True),
        second=built([(1, 1, 0), (0, -1, 1)], True),
        third=in_module([(0, 1, 1), (1, 1, 0)]),
        fourth=in_module([(0, 1, 0), (1, 1, 1)]),
        outer=built([(1, 1, 0), (0, -1, 1)], False),
        down=built([(0, -1, 1)], False),
        halo_cross=in_module([(1, 1, 0), (0, -1, 1)]),
        halo_same=in_module([(0, -1, 0), (1, 1, 1)]),
    )


def module_routes(mods):
    if mods & (mods - 1) == 0:
        return [[(m, m ^ s) for m in range(mods)] for s in range(1, mods)]
    return [[(m, (m + s) % mods) for m in range(mods)] for s in range(1, mods)]


def local(mods, slabs, design, fixed, load):
    half, width = design.shape[1:]
    count = 2 * half
    path = routes(mods, slabs)

    def move(value, name):
        return lax.ppermute(value, AXES, path[name])

    plane = (count, width)
    layer = (3, count, width)
    block = (half, width)
    free = (1 - fixed).astype(jnp.float32)
    swap, first, second, third, fourth, own = call(
        prepare_kernel,
        [(11,) + block, (4,) + block, (4,) + block, block, block, (11,) + block],
        name="prepare",
    )(free, load, design)
    first = move(first, "first")
    second = move(second, "second")
    third = move(third, "third")
    fourth = move(fourth, "fourth")
    swap = move(swap, "swap")

    def start_body(*refs):
        start_outer_kernel(mods, slabs, *refs)

    v0, v0_inner, free, fields, parts = call(
        start_inner_kernel,
        [layer, layer, layer, (12,) + plane, (3,) + plane],
        [(2,) + plane],
        name="start_inner",
        work=True,
    )(own, swap)
    v1, v0_high, mod_inner, mod_outer, mod_own, slope_factor, chain_factor, moments = call(
        start_body,
        [layer, layer, plane, plane, plane, plane, plane, (8, width)],
        [layer, plane, plane],
        name="start_outer",
    )(first, second, third, fourth, v0, v0_inner, free, fields, parts)
    outer = move(v1, "outer")
    inner = move(v1, "swap")
    (fields,) = call(second_inner_kernel, [(12,) + plane], name="second_inner", work=True)(v1, inner)
    v2, v1_high, moments = call(
        second_outer_kernel, [layer, layer, (8, width)], name="second_outer"
    )(v1, outer, inner, fields, free, mod_inner, mod_outer, moments)
    v2_outer = move(v2, "down")
    v2_inner = move(v2, "swap")
    moments, v2_high = call(third_kernel, [(8, width), layer], name="third")(
        v2_outer, v2_inner, v2, mod_own, moments
    )
    devices = 2 * mods * slabs
    gathered = lax.all_to_all(
        jnp.broadcast_to(moments, (devices, 8, width)), AXES, 0, 0, tiled=True
    )
    slope, factors = call(
        combine_kernel, [plane, (3, 8, width)], [layer, layer], name="combine"
    )(gathered, v0, v0_high, v1, v1_high, v2, v2_high, slope_factor)
    slopes = [slope] + [lax.ppermute(slope, "mod", pairs) for pairs in module_routes(mods)]
    (displacement,) = call(displace_kernel, [(3, 2, half, width)], name="displace", work=True)(
        factors, v0, v0_inner, v1, inner, v2, v2_inner
    )
    window = half + 8
    scaled, same, cross, across = call(
        scale_kernel, [plane, (window, width), (window, width), (window, width)], name="scale"
    )(*slopes, chain_factor)
    scaled, displacement = lax.optimization_barrier((scaled, displacement))
    outer = move(cross, "halo_cross")
    far = move(same, "halo_same")
    partner = move(across, "swap")
    (gradient,) = call(
        gradient_kernel, [(2, half, width)], [(4, window, width), (window, width)], name="gradient"
    )(scaled, outer, far, partner)
    return displacement, gradient


def solution(mesh):
    mods, slabs = mesh.shape["mod"], mesh.shape["slab"]
    assert mesh.shape["sub"] == 2
    deck = P(None, ("mod", "slab"), "sub", None)

    def body(design, fixed_mask, load_mask):
        return local(mods, slabs, design, fixed_mask, load_mask)

    return jax.shard_map(
        body,
        mesh=mesh,
        in_specs=(P("slab", "sub", None), deck, deck),
        out_specs=(deck, P("slab", "sub", None)),
        check_vma=False,
    )
```

```python
import math

import jax
import jax.numpy as jnp
import numpy as np
from jax import lax
from jax.experimental import pallas as pl
from jax.experimental.pallas import tpu as pltpu
from jax.sharding import PartitionSpec as P

stiff_floor = 0.01
penalty = 3.0
sharpness = 4.0
threshold = 0.5
filter_reach = 1.8

AXES = ("mod", "slab", "sub")
ROWS = 64
FACE = filter_reach - 1.0
EDGE = filter_reach - math.sqrt(2.0)
CORNER = filter_reach - math.sqrt(3.0)
LOWER = math.tanh(sharpness * threshold)
UPPER = math.tanh(sharpness * (1.0 - threshold))


def stiffness_modes():
    poisson = 0.3
    lame = poisson / ((1.0 + poisson) * (1.0 - 2.0 * poisson))
    shear = 1.0 / (2.0 * (1.0 + poisson))
    elastic = np.zeros((6, 6))
    elastic[:3, :3] = lame
    for axis in range(3):
        elastic[axis, axis] += 2.0 * shear
        elastic[axis + 3, axis + 3] = shear
    offset = 0.5 / math.sqrt(3.0)
    points = [0.5 - offset, 0.5 + offset]
    stiffness = np.zeros((24, 24))
    for point in ((a, b, c) for a in points for b in points for c in points):
        strain = np.zeros((6, 24))
        for corner in range(8):
            bits = (corner >> 2 & 1, corner >> 1 & 1, corner & 1)
            along = [point[a] if bits[a] else 1.0 - point[a] for a in range(3)]
            sign = [1.0 if bits[a] else -1.0 for a in range(3)]
            gx = sign[0] * along[1] * along[2]
            gy = along[0] * sign[1] * along[2]
            gz = along[0] * along[1] * sign[2]
            col = 3 * corner
            strain[0, col] = gx
            strain[1, col + 1] = gy
            strain[2, col + 2] = gz
            strain[3, col], strain[3, col + 1] = gy, gx
            strain[4, col + 1], strain[4, col + 2] = gz, gy
            strain[5, col], strain[5, col + 2] = gz, gx
        stiffness += strain.T @ elastic @ strain / 8.0
    basis = np.zeros((24, 24))
    for mode in range(8):
        for corner in range(8):
            value = 1.0
            for bit in range(3):
                if mode >> bit & 1 and not corner >> bit & 1:
                    value = -value
            for k in range(3):
                basis[3 * mode + k, 3 * corner + k] = value
    table = basis @ stiffness @ basis.T / 64.0
    table[np.abs(table) < 1e-9] = 0.0
    return table


TABLE = stiffness_modes()


def lanes(shape):
    return lax.broadcasted_iota(jnp.int32, shape, 1)


def rows(shape):
    return lax.broadcasted_iota(jnp.int32, shape, 0)


def z_up(x):
    return jnp.where(lanes(x.shape) < x.shape[1] - 1, pltpu.roll(x, x.shape[1] - 1, 1), 0.0)


def z_down(x):
    return jnp.where(lanes(x.shape) > 0, pltpu.roll(x, 1, 1), 0.0)


def y_up(x):
    return jnp.where(rows(x.shape) < x.shape[0] - 1, pltpu.roll(x, x.shape[0] - 1, 0), 0.0)


def y_down(x):
    return jnp.where(rows(x.shape) > 0, pltpu.roll(x, 1, 0), 0.0)


def two_rows(read, y0, count):
    here = read(y0)
    above = y_up(here) if y0 + ROWS == count else read(y0 + 1)
    return here, above


def face_modes(here, above):
    out = []
    for part in (here + above, above - here):
        shifted = z_up(part)
        out += [part + shifted, shifted - part]
    return out


def element_modes(own, other, side):
    sums = [[other[k][m] + own[k][m] for m in range(4)] for k in range(3)]
    diffs = [[(other[k][m] - own[k][m]) * side for m in range(4)] for k in range(3)]
    return [sums[k] + diffs[k] for k in range(3)]


def mode_forces(q):
    made = {}

    def scaled(j, value):
        key = (j, round(value, 12))
        if key not in made:
            made[key] = q[j % 3][j // 3] * np.float32(value)
        return made[key]

    out = [[None] * 8 for _ in range(3)]
    for i in range(24):
        total = None
        for j in np.nonzero(TABLE[i])[0]:
            term = scaled(int(j), float(TABLE[i, j]))
            total = term if total is None else total + term
        out[i % 3][i // 3] = total
    return out


def element_energy(q):
    r = mode_forces(q)
    total = None
    for k in range(3):
        for m in range(1, 8):
            term = q[k][m] * r[k][m]
            total = term if total is None else total + term
    return total


def own_fields(own, other, side):
    r = mode_forces(element_modes(own, other, side))
    fields = []
    for k in range(3):
        for m in range(4):
            d = r[k][m + 4] * side
            fields.append(-d if r[k][m] is None else r[k][m] - d)
    return fields


def layer_modes(read, y0, count):
    heres, modes = [], []
    for k in range(3):
        here, above = two_rows(lambda y, k=k: read(k, y), y0, count)
        heres.append(here)
        modes.append(face_modes(here, above))
    return heres, modes


def fields_loop(count, read_own, read_other, side, fields):
    for y0 in range(0, count, ROWS):
        _, own = layer_modes(read_own, y0, count)
        _, other = layer_modes(read_other, y0, count)
        for n, value in enumerate(own_fields(own, other, side)):
            fields[n, pl.ds(y0, ROWS), :] = value


def operator_loop(count, read_own, read_other, side, fields, mod_inner, mod_outer, free, out_ref):
    shape = (ROWS, out_ref.shape[2])
    square = jnp.zeros(shape, jnp.float32)
    cross = jnp.zeros(shape, jnp.float32)
    norm = jnp.zeros(shape, jnp.float32)
    carry = [jnp.zeros(shape, jnp.float32)] * 3
    first = rows(shape) == 0
    for y0 in range(0, count, ROWS):
        part = pl.ds(y0, ROWS)
        owns, own = layer_modes(read_own, y0, count)
        _, other = layer_modes(read_other, y0, count)
        inner, outer = mod_inner[part, :], mod_outer[part, :]
        total = [
            outer * value + inner * fields[n, part, :]
            for n, value in enumerate(own_fields(own, other, side))
        ]
        for k in range(3):
            faces = []
            for py in range(2):
                s, d = total[4 * k + 2 * py], total[4 * k + 2 * py + 1]
                faces.append((s - d) + z_down(s + d))
            rolled = pltpu.roll(faces[0] + faces[1], 1, 0)
            force = (faces[0] - faces[1]) + jnp.where(first, carry[k], rolled)
            carry[k] = rolled
            image = free[k, part, :] * force
            out_ref[k, part, :] = image
            square += image * image
            cross += owns[k] * image
            norm += owns[k] * owns[k]
    return norm, cross, square


def energy_loop(count, read_own, read_high, use):
    for y0 in range(0, count, ROWS):
        _, own = layer_modes(read_own, y0, count)
        _, high = layer_modes(read_high, y0, count)
        use(y0, element_energy(element_modes(own, high, 1.0)))


def rows_of(ref):
    return lambda k, y: ref[k, pl.ds(y, ROWS), :]


def inner_side(sub):
    return jnp.where(sub == 0, 1.0, -1.0).astype(jnp.float32)


def line(tile):
    return jnp.sum(tile, axis=0, keepdims=True)


def prepare_kernel(free, load, design, swap, first, second, third, fourth, own):
    sub = lax.axis_index("sub")
    for k in range(3):
        frees = [free[k, layer] for layer in range(2)]
        values = [frees[layer] * load[k, layer].astype(jnp.float32) for layer in range(2)]
        for layer in range(2):
            swap[2 * k + layer] = values[layer]
            own[2 * k + layer] = values[layer]
        low = sub == 0
        swap[6 + k] = jnp.where(low, frees[1], frees[0])
        own[6 + k] = jnp.where(low, frees[0], frees[1])
        first[k] = jnp.where(low, values[1], values[0])
        second[k] = jnp.where(low, values[0], values[1])
    low = sub == 0
    for layer in range(2):
        swap[9 + layer] = design[layer]
        own[9 + layer] = design[layer]
    later = jnp.where(low, design[1], design[0])
    sooner = jnp.where(low, design[0], design[1])
    first[3] = later
    third[...] = later
    second[3] = sooner
    fourth[...] = sooner


def around(p):
    across = y_up(p) + y_down(p)
    return across + z_up(p) + z_down(p), z_up(across) + z_down(across)


def filter_mid(p):
    face, diag = around(p)
    return filter_reach * p + FACE * face + EDGE * diag


def filter_side(p):
    face, diag = around(p)
    return FACE * p + EDGE * face + CORNER * diag


def filter_planes(low, mid, high):
    return filter_side(low + high) + filter_mid(mid)


def weight_plane(shape, row_offset, count):
    row = rows(shape) + row_offset
    lane = lanes(shape)

    def neighbours(index, size):
        return jnp.where(index > 0, 1.0, 0.0) + jnp.where(index < size - 1, 1.0, 0.0)

    ry = neighbours(row, count)
    rz = neighbours(lane, shape[1])
    face, diag = ry + rz, ry * rz
    return (
        filter_reach
        + FACE * (2.0 + face)
        + EDGE * (2.0 * face + diag)
        + (2.0 * CORNER) * diag
    )


def start_inner_kernel(own, swap, v0, v0_inner, free, fields, parts, layers):
    sub = lax.axis_index("sub")
    half = own.shape[1]
    count = 2 * half
    mine = pl.ds(pl.multiple_of(sub * half, half), half)
    other = pl.ds(pl.multiple_of((1 - sub) * half, half), half)
    for layer in range(2):
        layers[layer, mine, :] = own[9 + layer]
        layers[layer, other, :] = swap[9 + layer]

    @pl.when(sub == 0)
    def _():
        parts[0] = filter_side(layers[0])
        parts[1] = filter_mid(layers[0]) + filter_side(layers[1])

    @pl.when(sub == 1)
    def _():
        parts[0] = filter_mid(layers[0]) + filter_side(layers[1])
        parts[1] = filter_side(layers[0]) + filter_mid(layers[1])

    parts[2] = 1.0 / weight_plane((count, own.shape[2]), 0, count)
    for k in range(3):
        free[k, mine, :] = own[6 + k]
        free[k, other, :] = swap[6 + k]
        v0[k, mine, :] = own[2 * k + sub]
        v0[k, other, :] = swap[2 * k + sub]
        v0_inner[k, mine, :] = own[2 * k + 1 - sub]
        v0_inner[k, other, :] = swap[2 * k + 1 - sub]
    fields_loop(count, rows_of(v0), rows_of(v0_inner), inner_side(sub), fields)


def start_outer_kernel(
    mods, slabs,
    first, second, third, fourth, v0, v0_inner, free, fields, parts,
    v1, v0_high, mod_inner, mod_outer, mod_own, slope_factor, chain_factor, moments,
    v0_outer, near, deep,
):
    mod, slab, sub = (lax.axis_index(a) for a in AXES)
    half = third.shape[0]
    count = 2 * half
    even = sub == 0
    mine = pl.ds(pl.multiple_of(sub * half, half), half)
    other = pl.ds(pl.multiple_of((1 - sub) * half, half), half)
    near[mine, :] = first[3]
    near[other, :] = second[3]
    deep[mine, :] = fourth[...]
    deep[other, :] = third[...]
    starts = (mod == 0) & (slab == 0) & even
    ends = (mod == mods - 1) & (slab == slabs - 1) & (sub == 1)
    inside = jnp.where(ends, 0.0, 1.0)
    for k in range(3):
        v0_outer[k, mine, :] = first[k] * inside
        v0_outer[k, other, :] = second[k] * inside
        v0_high[k] = jnp.where(even, v0_inner[k], v0_outer[k])

    side = filter_side(near[...])
    mid = filter_mid(near[...])
    inverse = parts[2]
    filtered = (parts[0] + filter_side(deep[...]) + jnp.where(even, mid, 0.0)) * inverse
    hyper = jnp.tanh(sharpness * (filtered - threshold))
    projected = (LOWER + hyper) * (1.0 / (LOWER + UPPER))
    below = stiff_floor + (1.0 - stiff_floor) * projected * projected * projected
    below = below * jnp.where(starts, 0.0, 1.0)
    filtered = (parts[1] + side) * inverse
    hyper = jnp.tanh(sharpness * (filtered - threshold))
    projected = (LOWER + hyper) * (1.0 / (LOWER + UPPER))
    squared = projected * projected
    stiff = stiff_floor + (1.0 - stiff_floor) * squared * projected
    mod_own[...] = stiff
    mod_inner[...] = jnp.where(even, stiff, below)
    mod_outer[...] = jnp.where(even, below, stiff)
    slope_factor[...] = (-penalty * (1.0 - stiff_floor)) * squared
    chain_factor[...] = (sharpness / (LOWER + UPPER)) * (1.0 - hyper * hyper) * inverse

    norm, cross, square = operator_loop(
        count, rows_of(v0), rows_of(v0_outer), -inner_side(sub), fields, mod_inner, mod_outer, free, v1
    )
    moments[...] = jnp.concatenate(
        [line(norm), line(cross), line(square), jnp.zeros((5, norm.shape[1]), jnp.float32)], axis=0
    )


def second_inner_kernel(v1, inner, fields):
    fields_loop(v1.shape[1], rows_of(v1), rows_of(inner), inner_side(lax.axis_index("sub")), fields)


def second_outer_kernel(
    v1, outer, inner, fields, free, mod_inner, mod_outer, before, v2, v1_high, moments
):
    sub = lax.axis_index("sub")
    count = v1.shape[1]
    for k in range(3):
        v1_high[k] = jnp.where(sub == 0, inner[k], outer[k])
    _, cross, square = operator_loop(
        count, rows_of(v1), rows_of(outer), -inner_side(sub), fields, mod_inner, mod_outer, free, v2
    )
    zero = jnp.zeros((3, cross.shape[1]), jnp.float32)
    moments[...] = before[...] + jnp.concatenate(
        [zero, line(cross), line(square), zero], axis=0
    )


def third_kernel(v2_outer, v2_inner, v2, mod_own, before, moments, v2_high):
    even = lax.axis_index("sub") == 0
    for k in range(3):
        v2_high[k] = jnp.where(even, v2_inner[k], v2_outer[k])
    count = v2.shape[1]
    total = [jnp.zeros((ROWS, v2.shape[2]), jnp.float32)]

    def use(y0, energy):
        total[0] += energy * mod_own[pl.ds(y0, ROWS), :]

    energy_loop(
        count,
        lambda k, y: v2[k, pl.ds(y, ROWS), :],
        lambda k, y: v2_high[k, pl.ds(y, ROWS), :],
        use,
    )
    width = v2.shape[2]
    moments[...] = before[...] + jnp.concatenate(
        [
            jnp.zeros((5, width), jnp.float32),
            line(total[0]),
            jnp.zeros((2, width), jnp.float32),
        ],
        axis=0,
    )


def coefficients(m):
    step = m[0] / m[1]
    x0 = step
    r1 = -step
    norm = m[0] + 2.0 * r1 * m[1] + r1 * r1 * m[2]
    ratio = norm / m[0]
    p0, p1 = 1.0 + ratio, r1
    step = norm / (p0 * p0 * m[1] + 2.0 * p0 * p1 * m[2] + p1 * p1 * m[3])
    x0, x1 = x0 + step * p0, step * p1
    r1, r2 = r1 - step * p0, -step * p1
    after = (
        m[0]
        + 2.0 * r1 * m[1]
        + (r1 * r1 + 2.0 * r2) * m[2]
        + 2.0 * r1 * r2 * m[3]
        + r2 * r2 * m[4]
    )
    ratio = after / norm
    p0, p1, p2 = 1.0 + ratio * p0, r1 + ratio * p1, r2
    step = after / (
        p0 * p0 * m[1]
        + 2.0 * p0 * p1 * m[2]
        + (p1 * p1 + 2.0 * p0 * p2) * m[3]
        + 2.0 * p1 * p2 * m[4]
        + p2 * p2 * m[5]
    )
    return x0 + step * p0, x1 + step * p1, step * p2


def combine_kernel(
    gathered, v0, v0_high, v1, v1_high, v2, v2_high, slope_factor, slope, factors, own, high
):
    count = v0.shape[1]
    sums = jnp.sum(jnp.sum(gathered[...], axis=0), axis=1, keepdims=True)
    c0, c1, c2 = coefficients([sums[k : k + 1] for k in range(6)])
    for n, c in enumerate((c0, c1, c2)):
        factors[n] = jnp.broadcast_to(c, factors.shape[1:])
    for k in range(3):
        own[k] = c0 * v0[k] + c1 * v1[k] + c2 * v2[k]
        high[k] = c0 * v0_high[k] + c1 * v1_high[k] + c2 * v2_high[k]

    def use(y0, energy):
        slope[pl.ds(y0, ROWS), :] = slope_factor[pl.ds(y0, ROWS), :] * energy

    energy_loop(count, rows_of(own), rows_of(high), use)


def displace_kernel(factors, v0, v0_inner, v1, v1_inner, v2, v2_inner, displacement):
    sub = lax.axis_index("sub")
    half = displacement.shape[2]
    mine = pl.ds(pl.multiple_of(sub * half, half), half)
    c0, c1, c2 = (factors[n][:1, :1] for n in range(3))
    for k in range(3):
        displacement[k, sub] = c0 * v0[k, mine, :] + c1 * v1[k, mine, :] + c2 * v2[k, mine, :]
        displacement[k, 1 - sub] = (
            c0 * v0_inner[k, mine, :] + c1 * v1_inner[k, mine, :] + c2 * v2_inner[k, mine, :]
        )


def scale_kernel(*refs):
    slopes, (chain_factor, scaled, same, cross, across) = refs[:-5], refs[-5:]
    sub = lax.axis_index("sub")
    total = slopes[0][...]
    for other in slopes[1:]:
        total = total + other[...]
    scaled[...] = total * chain_factor[...]
    window = same.shape[0]
    shift = scaled.shape[0] - window
    same[...] = scaled[pl.ds(pl.multiple_of(sub * shift, 8), window), :]
    cross[...] = scaled[pl.ds(pl.multiple_of((1 - sub) * shift, 8), window), :]
    across[...] = cross[...]


def gradient_kernel(scaled, outer, far, partner, gradient, planes, sums):
    sub = lax.axis_index("sub")
    window = partner.shape[0]
    shift = scaled.shape[0] - window
    mine = scaled[pl.ds(pl.multiple_of(sub * shift, 8), window), :]

    @pl.when(sub == 0)
    def _():
        planes[0] = outer[...]
        planes[1] = mine
        planes[2] = partner[...]
        planes[3] = far[...]

    @pl.when(sub == 1)
    def _():
        planes[0] = far[...]
        planes[1] = partner[...]
        planes[2] = mine
        planes[3] = outer[...]

    half = gradient.shape[1]
    part = pl.ds(pl.multiple_of(sub * (window - half), 8), half)
    for layer in range(2):
        sums[...] = filter_planes(planes[layer], planes[layer + 1], planes[layer + 2])
        gradient[layer] = sums[part, :]


def call(body, outs, scratch=(), name=None, work=False):
    cost = pl.CostEstimate(flops=10**7, bytes_accessed=4 * 10**6, transcendentals=0)
    return pl.pallas_call(
        body,
        out_shape=[jax.ShapeDtypeStruct(shape, jnp.float32) for shape in outs],
        scratch_shapes=[pltpu.VMEM(shape, jnp.float32) for shape in scratch],
        compiler_params=pltpu.CompilerParams(vmem_limit_bytes=16 * 2**20),
        cost_estimate=cost if work else None,
        name=name,
    )


def routes(mods, slabs):
    chips = mods * slabs

    def at(chip, sub):
        return 2 * chip + sub

    def beside(chip, steps, cyclic):
        target = chip + steps
        if cyclic:
            return target % chips
        return target if 0 <= target < chips else None

    def built(moves, cyclic):
        pairs = []
        for chip in range(chips):
            for sub, steps, to in moves:
                target = beside(chip, steps, cyclic)
                if target is not None:
                    pairs.append((at(chip, sub), at(target, to)))
        return pairs

    def in_module(moves):
        pairs = []
        for chip in range(chips):
            mod, slab = divmod(chip, slabs)
            for sub, steps, to in moves:
                pairs.append((at(chip, sub), at(mod * slabs + (slab + steps) % slabs, to)))
        return pairs

    return dict(
        swap=built([(0, 0, 1), (1, 0, 0)], True),
        first=built([(0, 1, 0), (1, -1, 1)], True),
        second=built([(1, 1, 0), (0, -1, 1)], True),
        third=in_module([(0, 1, 1), (1, 1, 0)]),
        fourth=in_module([(0, 1, 0), (1, 1, 1)]),
        outer=built([(1, 1, 0), (0, -1, 1)], False),
        down=built([(0, -1, 1)], False),
        halo_cross=in_module([(1, 1, 0), (0, -1, 1)]),
        halo_same=in_module([(0, -1, 0), (1, 1, 1)]),
    )


def module_routes(mods):
    if mods & (mods - 1) == 0:
        return [[(m, m ^ s) for m in range(mods)] for s in range(1, mods)]
    return [[(m, (m + s) % mods) for m in range(mods)] for s in range(1, mods)]


def local(mods, slabs, design, fixed, load):
    half, width = design.shape[1:]
    count = 2 * half
    path = routes(mods, slabs)

    def move(value, name):
        return lax.ppermute(value, AXES, path[name])

    plane = (count, width)
    layer = (3, count, width)
    block = (half, width)
    free = (1 - fixed).astype(jnp.float32)
    swap, first, second, third, fourth, own = call(
        prepare_kernel,
        [(11,) + block, (4,) + block, (4,) + block, block, block, (11,) + block],
        name="prepare",
    )(free, load, design)
    first = move(first, "first")
    second = move(second, "second")
    third = move(third, "third")
    fourth = move(fourth, "fourth")
    swap = move(swap, "swap")

    def start_body(*refs):
        start_outer_kernel(mods, slabs, *refs)

    v0, v0_inner, free, fields, parts = call(
        start_inner_kernel,
        [layer, layer, layer, (12,) + plane, (3,) + plane],
        [(2,) + plane],
        name="start_inner",
        work=True,
    )(own, swap)
    v1, v0_high, mod_inner, mod_outer, mod_own, slope_factor, chain_factor, moments = call(
        start_body,
        [layer, layer, plane, plane, plane, plane, plane, (8, width)],
        [layer, plane, plane],
        name="start_outer",
    )(first, second, third, fourth, v0, v0_inner, free, fields, parts)
    outer = move(v1, "outer")
    inner = move(v1, "swap")
    (fields,) = call(second_inner_kernel, [(12,) + plane], name="second_inner", work=True)(v1, inner)
    v2, v1_high, moments = call(
        second_outer_kernel, [layer, layer, (8, width)], name="second_outer"
    )(v1, outer, inner, fields, free, mod_inner, mod_outer, moments)
    v2_outer = move(v2, "down")
    v2_inner = move(v2, "swap")
    moments, v2_high = call(third_kernel, [(8, width), layer], name="third")(
        v2_outer, v2_inner, v2, mod_own, moments
    )
    devices = 2 * mods * slabs
    gathered = lax.all_to_all(
        jnp.broadcast_to(moments, (devices, 8, width)), AXES, 0, 0, tiled=True
    )
    slope, factors = call(
        combine_kernel, [plane, (3, 8, width)], [layer, layer], name="combine"
    )(gathered, v0, v0_high, v1, v1_high, v2, v2_high, slope_factor)
    slopes = [slope] + [lax.ppermute(slope, "mod", pairs) for pairs in module_routes(mods)]
    (displacement,) = call(displace_kernel, [(3, 2, half, width)], name="displace", work=True)(
        factors, v0, v0_inner, v1, inner, v2, v2_inner
    )
    window = half + 8
    scaled, same, cross, across = call(
        scale_kernel, [plane, (window, width), (window, width), (window, width)], name="scale"
    )(*slopes, chain_factor)
    scaled, displacement = lax.optimization_barrier((scaled, displacement))
    outer = move(cross, "halo_cross")
    far = move(same, "halo_same")
    partner = move(across, "swap")
    (gradient,) = call(
        gradient_kernel, [(2, half, width)], [(4, window, width), (window, width)], name="gradient"
    )(scaled, outer, far, partner)
    return displacement, gradient


def solution(mesh):
    mods, slabs = mesh.shape["mod"], mesh.shape["slab"]
    assert mesh.shape["sub"] == 2
    deck = P(None, ("mod", "slab"), "sub", None)

    def body(design, fixed_mask, load_mask):
        return local(mods, slabs, design, fixed_mask, load_mask)

    return jax.shard_map(
        body,
        mesh=mesh,
        in_specs=(P("slab", "sub", None), deck, deck),
        out_specs=(deck, P("slab", "sub", None)),
        check_vma=False,
    )
```

```python
import math

import jax
import jax.numpy as jnp
import numpy as np
from jax import lax
from jax.experimental import pallas as pl
from jax.experimental.pallas import tpu as pltpu
from jax.sharding import PartitionSpec as P

stiff_floor = 0.01
penalty = 3.0
sharpness = 4.0
threshold = 0.5
filter_reach = 1.8

AXES = ("mod", "slab", "sub")
ROWS = 128
FACE = filter_reach - 1.0
EDGE = filter_reach - math.sqrt(2.0)
CORNER = filter_reach - math.sqrt(3.0)
LOWER = math.tanh(sharpness * threshold)
UPPER = math.tanh(sharpness * (1.0 - threshold))


def stiffness_modes():
    poisson = 0.3
    lame = poisson / ((1.0 + poisson) * (1.0 - 2.0 * poisson))
    shear = 1.0 / (2.0 * (1.0 + poisson))
    elastic = np.zeros((6, 6))
    elastic[:3, :3] = lame
    for axis in range(3):
        elastic[axis, axis] += 2.0 * shear
        elastic[axis + 3, axis + 3] = shear
    offset = 0.5 / math.sqrt(3.0)
    points = [0.5 - offset, 0.5 + offset]
    stiffness = np.zeros((24, 24))
    for point in ((a, b, c) for a in points for b in points for c in points):
        strain = np.zeros((6, 24))
        for corner in range(8):
            bits = (corner >> 2 & 1, corner >> 1 & 1, corner & 1)
            along = [point[a] if bits[a] else 1.0 - point[a] for a in range(3)]
            sign = [1.0 if bits[a] else -1.0 for a in range(3)]
            gx = sign[0] * along[1] * along[2]
            gy = along[0] * sign[1] * along[2]
            gz = along[0] * along[1] * sign[2]
            col = 3 * corner
            strain[0, col] = gx
            strain[1, col + 1] = gy
            strain[2, col + 2] = gz
            strain[3, col], strain[3, col + 1] = gy, gx
            strain[4, col + 1], strain[4, col + 2] = gz, gy
            strain[5, col], strain[5, col + 2] = gz, gx
        stiffness += strain.T @ elastic @ strain / 8.0
    basis = np.zeros((24, 24))
    for mode in range(8):
        for corner in range(8):
            value = 1.0
            for bit in range(3):
                if mode >> bit & 1 and not corner >> bit & 1:
                    value = -value
            for k in range(3):
                basis[3 * mode + k, 3 * corner + k] = value
    table = basis @ stiffness @ basis.T / 64.0
    table[np.abs(table) < 1e-9] = 0.0
    return table


TABLE = stiffness_modes()


def lanes(shape):
    return lax.broadcasted_iota(jnp.int32, shape, 1)


def rows(shape):
    return lax.broadcasted_iota(jnp.int32, shape, 0)


def z_up(x):
    return jnp.where(lanes(x.shape) < x.shape[1] - 1, pltpu.roll(x, x.shape[1] - 1, 1), 0.0)


def z_down(x):
    return jnp.where(lanes(x.shape) > 0, pltpu.roll(x, 1, 1), 0.0)


def y_up(x):
    return jnp.where(rows(x.shape) < x.shape[0] - 1, pltpu.roll(x, x.shape[0] - 1, 0), 0.0)


def y_down(x):
    return jnp.where(rows(x.shape) > 0, pltpu.roll(x, 1, 0), 0.0)


def two_rows(read, y0, count):
    here = read(y0)
    above = y_up(here) if y0 + ROWS == count else read(y0 + 1)
    return here, above


def face_modes(here, above):
    out = []
    for part in (here + above, above - here):
        shifted = z_up(part)
        out += [part + shifted, shifted - part]
    return out


def element_modes(own, other, side):
    sums = [[other[k][m] + own[k][m] for m in range(4)] for k in range(3)]
    diffs = [[(other[k][m] - own[k][m]) * side for m in range(4)] for k in range(3)]
    return [sums[k] + diffs[k] for k in range(3)]


def mode_forces(q):
    made = {}

    def scaled(j, value):
        key = (j, round(value, 12))
        if key not in made:
            made[key] = q[j % 3][j // 3] * np.float32(value)
        return made[key]

    out = [[None] * 8 for _ in range(3)]
    for i in range(24):
        total = None
        for j in np.nonzero(TABLE[i])[0]:
            term = scaled(int(j), float(TABLE[i, j]))
            total = term if total is None else total + term
        out[i % 3][i // 3] = total
    return out


def element_energy(q):
    r = mode_forces(q)
    total = None
    for k in range(3):
        for m in range(1, 8):
            term = q[k][m] * r[k][m]
            total = term if total is None else total + term
    return total


def own_fields(own, other, side):
    r = mode_forces(element_modes(own, other, side))
    fields = []
    for k in range(3):
        for m in range(4):
            d = r[k][m + 4] * side
            fields.append(-d if r[k][m] is None else r[k][m] - d)
    return fields


def layer_modes(read, y0, count):
    heres, modes = [], []
    for k in range(3):
        here, above = two_rows(lambda y, k=k: read(k, y), y0, count)
        heres.append(here)
        modes.append(face_modes(here, above))
    return heres, modes


def fields_loop(count, read_own, read_other, side, fields):
    for y0 in range(0, count, ROWS):
        _, own = layer_modes(read_own, y0, count)
        _, other = layer_modes(read_other, y0, count)
        for n, value in enumerate(own_fields(own, other, side)):
            fields[n, pl.ds(y0, ROWS), :] = value


def operator_loop(count, read_own, read_other, side, fields, mod_inner, mod_outer, free, out_ref):
    shape = (ROWS, out_ref.shape[2])
    square = jnp.zeros(shape, jnp.float32)
    cross = jnp.zeros(shape, jnp.float32)
    norm = jnp.zeros(shape, jnp.float32)
    carry = [jnp.zeros(shape, jnp.float32)] * 3
    first = rows(shape) == 0
    for y0 in range(0, count, ROWS):
        part = pl.ds(y0, ROWS)
        owns, own = layer_modes(read_own, y0, count)
        _, other = layer_modes(read_other, y0, count)
        inner, outer = mod_inner[part, :], mod_outer[part, :]
        total = [
            outer * value + inner * fields[n, part, :]
            for n, value in enumerate(own_fields(own, other, side))
        ]
        for k in range(3):
            faces = []
            for py in range(2):
                s, d = total[4 * k + 2 * py], total[4 * k + 2 * py + 1]
                faces.append((s - d) + z_down(s + d))
            rolled = pltpu.roll(faces[0] + faces[1], 1, 0)
            force = (faces[0] - faces[1]) + jnp.where(first, carry[k], rolled)
            carry[k] = rolled
            image = free[k, part, :] * force
            out_ref[k, part, :] = image
            square += image * image
            cross += owns[k] * image
            norm += owns[k] * owns[k]
    return norm, cross, square


def energy_loop(count, read_own, read_high, use):
    for y0 in range(0, count, ROWS):
        _, own = layer_modes(read_own, y0, count)
        _, high = layer_modes(read_high, y0, count)
        use(y0, element_energy(element_modes(own, high, 1.0)))


def rows_of(ref):
    return lambda k, y: ref[k, pl.ds(y, ROWS), :]


def inner_side(sub):
    return jnp.where(sub == 0, 1.0, -1.0).astype(jnp.float32)


def line(tile):
    return jnp.sum(tile, axis=0, keepdims=True)


def prepare_kernel(free, load, design, swap, first, second, third, fourth, own):
    sub = lax.axis_index("sub")
    for k in range(3):
        frees = [free[k, layer] for layer in range(2)]
        values = [frees[layer] * load[k, layer].astype(jnp.float32) for layer in range(2)]
        for layer in range(2):
            swap[2 * k + layer] = values[layer]
            own[2 * k + layer] = values[layer]
        low = sub == 0
        swap[6 + k] = jnp.where(low, frees[1], frees[0])
        own[6 + k] = jnp.where(low, frees[0], frees[1])
        first[k] = jnp.where(low, values[1], values[0])
        second[k] = jnp.where(low, values[0], values[1])
    low = sub == 0
    for layer in range(2):
        swap[9 + layer] = design[layer]
        own[9 + layer] = design[layer]
    later = jnp.where(low, design[1], design[0])
    sooner = jnp.where(low, design[0], design[1])
    first[3] = later
    third[...] = later
    second[3] = sooner
    fourth[...] = sooner


def around(p):
    across = y_up(p) + y_down(p)
    return across + z_up(p) + z_down(p), z_up(across) + z_down(across)


def filter_mid(p):
    face, diag = around(p)
    return filter_reach * p + FACE * face + EDGE * diag


def filter_side(p):
    face, diag = around(p)
    return FACE * p + EDGE * face + CORNER * diag


def filter_planes(low, mid, high):
    return filter_side(low + high) + filter_mid(mid)


def weight_plane(shape, row_offset, count):
    row = rows(shape) + row_offset
    lane = lanes(shape)

    def neighbours(index, size):
        return jnp.where(index > 0, 1.0, 0.0) + jnp.where(index < size - 1, 1.0, 0.0)

    ry = neighbours(row, count)
    rz = neighbours(lane, shape[1])
    face, diag = ry + rz, ry * rz
    return (
        filter_reach
        + FACE * (2.0 + face)
        + EDGE * (2.0 * face + diag)
        + (2.0 * CORNER) * diag
    )


def start_inner_kernel(own, swap, v0, v0_inner, free, fields, parts, layers):
    sub = lax.axis_index("sub")
    half = own.shape[1]
    count = 2 * half
    mine = pl.ds(pl.multiple_of(sub * half, half), half)
    other = pl.ds(pl.multiple_of((1 - sub) * half, half), half)
    for layer in range(2):
        layers[layer, mine, :] = own[9 + layer]
        layers[layer, other, :] = swap[9 + layer]

    @pl.when(sub == 0)
    def _():
        parts[0] = filter_side(layers[0])
        parts[1] = filter_mid(layers[0]) + filter_side(layers[1])

    @pl.when(sub == 1)
    def _():
        parts[0] = filter_mid(layers[0]) + filter_side(layers[1])
        parts[1] = filter_side(layers[0]) + filter_mid(layers[1])

    parts[2] = 1.0 / weight_plane((count, own.shape[2]), 0, count)
    for k in range(3):
        free[k, mine, :] = own[6 + k]
        free[k, other, :] = swap[6 + k]
        v0[k, mine, :] = own[2 * k + sub]
        v0[k, other, :] = swap[2 * k + sub]
        v0_inner[k, mine, :] = own[2 * k + 1 - sub]
        v0_inner[k, other, :] = swap[2 * k + 1 - sub]
    fields_loop(count, rows_of(v0), rows_of(v0_inner), inner_side(sub), fields)


def start_outer_kernel(
    mods, slabs,
    first, second, third, fourth, v0, v0_inner, free, fields, parts,
    v1, v0_high, mod_inner, mod_outer, mod_own, slope_factor, chain_factor, moments,
    v0_outer, near, deep,
):
    mod, slab, sub = (lax.axis_index(a) for a in AXES)
    half = third.shape[0]
    count = 2 * half
    even = sub == 0
    mine = pl.ds(pl.multiple_of(sub * half, half), half)
    other = pl.ds(pl.multiple_of((1 - sub) * half, half), half)
    near[mine, :] = first[3]
    near[other, :] = second[3]
    deep[mine, :] = fourth[...]
    deep[other, :] = third[...]
    starts = (mod == 0) & (slab == 0) & even
    ends = (mod == mods - 1) & (slab == slabs - 1) & (sub == 1)
    inside = jnp.where(ends, 0.0, 1.0)
    for k in range(3):
        v0_outer[k, mine, :] = first[k] * inside
        v0_outer[k, other, :] = second[k] * inside
        v0_high[k] = jnp.where(even, v0_inner[k], v0_outer[k])

    side = filter_side(near[...])
    mid = filter_mid(near[...])
    inverse = parts[2]
    filtered = (parts[0] + filter_side(deep[...]) + jnp.where(even, mid, 0.0)) * inverse
    hyper = jnp.tanh(sharpness * (filtered - threshold))
    projected = (LOWER + hyper) * (1.0 / (LOWER + UPPER))
    below = stiff_floor + (1.0 - stiff_floor) * projected * projected * projected
    below = below * jnp.where(starts, 0.0, 1.0)
    filtered = (parts[1] + side) * inverse
    hyper = jnp.tanh(sharpness * (filtered - threshold))
    projected = (LOWER + hyper) * (1.0 / (LOWER + UPPER))
    squared = projected * projected
    stiff = stiff_floor + (1.0 - stiff_floor) * squared * projected
    mod_own[...] = stiff
    mod_inner[...] = jnp.where(even, stiff, below)
    mod_outer[...] = jnp.where(even, below, stiff)
    slope_factor[...] = (-penalty * (1.0 - stiff_floor)) * squared
    chain_factor[...] = (sharpness / (LOWER + UPPER)) * (1.0 - hyper * hyper) * inverse

    norm, cross, square = operator_loop(
        count, rows_of(v0), rows_of(v0_outer), -inner_side(sub), fields, mod_inner, mod_outer, free, v1
    )
    moments[...] = jnp.concatenate(
        [line(norm), line(cross), line(square), jnp.zeros((5, norm.shape[1]), jnp.float32)], axis=0
    )


def second_inner_kernel(v1, inner, fields):
    fields_loop(v1.shape[1], rows_of(v1), rows_of(inner), inner_side(lax.axis_index("sub")), fields)


def second_outer_kernel(
    v1, outer, inner, fields, free, mod_inner, mod_outer, before, v2, v1_high, moments
):
    sub = lax.axis_index("sub")
    count = v1.shape[1]
    for k in range(3):
        v1_high[k] = jnp.where(sub == 0, inner[k], outer[k])
    _, cross, square = operator_loop(
        count, rows_of(v1), rows_of(outer), -inner_side(sub), fields, mod_inner, mod_outer, free, v2
    )
    zero = jnp.zeros((3, cross.shape[1]), jnp.float32)
    moments[...] = before[...] + jnp.concatenate(
        [zero, line(cross), line(square), zero], axis=0
    )


def third_kernel(v2_outer, v2_inner, v2, mod_own, before, moments, v2_high):
    even = lax.axis_index("sub") == 0
    for k in range(3):
        v2_high[k] = jnp.where(even, v2_inner[k], v2_outer[k])
    count = v2.shape[1]
    total = [jnp.zeros((ROWS, v2.shape[2]), jnp.float32)]

    def use(y0, energy):
        total[0] += energy * mod_own[pl.ds(y0, ROWS), :]

    energy_loop(
        count,
        lambda k, y: v2[k, pl.ds(y, ROWS), :],
        lambda k, y: v2_high[k, pl.ds(y, ROWS), :],
        use,
    )
    width = v2.shape[2]
    moments[...] = before[...] + jnp.concatenate(
        [
            jnp.zeros((5, width), jnp.float32),
            line(total[0]),
            jnp.zeros((2, width), jnp.float32),
        ],
        axis=0,
    )


def coefficients(m):
    step = m[0] / m[1]
    x0 = step
    r1 = -step
    norm = m[0] + 2.0 * r1 * m[1] + r1 * r1 * m[2]
    ratio = norm / m[0]
    p0, p1 = 1.0 + ratio, r1
    step = norm / (p0 * p0 * m[1] + 2.0 * p0 * p1 * m[2] + p1 * p1 * m[3])
    x0, x1 = x0 + step * p0, step * p1
    r1, r2 = r1 - step * p0, -step * p1
    after = (
        m[0]
        + 2.0 * r1 * m[1]
        + (r1 * r1 + 2.0 * r2) * m[2]
        + 2.0 * r1 * r2 * m[3]
        + r2 * r2 * m[4]
    )
    ratio = after / norm
    p0, p1, p2 = 1.0 + ratio * p0, r1 + ratio * p1, r2
    step = after / (
        p0 * p0 * m[1]
        + 2.0 * p0 * p1 * m[2]
        + (p1 * p1 + 2.0 * p0 * p2) * m[3]
        + 2.0 * p1 * p2 * m[4]
        + p2 * p2 * m[5]
    )
    return x0 + step * p0, x1 + step * p1, step * p2


def combine_kernel(
    gathered, v0, v0_high, v1, v1_high, v2, v2_high, slope_factor, slope, factors, own, high
):
    count = v0.shape[1]
    sums = jnp.sum(jnp.sum(gathered[...], axis=0), axis=1, keepdims=True)
    c0, c1, c2 = coefficients([sums[k : k + 1] for k in range(6)])
    for n, c in enumerate((c0, c1, c2)):
        factors[n] = jnp.broadcast_to(c, factors.shape[1:])
    for k in range(3):
        own[k] = c0 * v0[k] + c1 * v1[k] + c2 * v2[k]
        high[k] = c0 * v0_high[k] + c1 * v1_high[k] + c2 * v2_high[k]

    def use(y0, energy):
        slope[pl.ds(y0, ROWS), :] = slope_factor[pl.ds(y0, ROWS), :] * energy

    energy_loop(count, rows_of(own), rows_of(high), use)


def displace_kernel(factors, v0, v0_inner, v1, v1_inner, v2, v2_inner, displacement):
    sub = lax.axis_index("sub")
    half = displacement.shape[2]
    mine = pl.ds(pl.multiple_of(sub * half, half), half)
    c0, c1, c2 = (factors[n][:1, :1] for n in range(3))
    for k in range(3):
        displacement[k, sub] = c0 * v0[k, mine, :] + c1 * v1[k, mine, :] + c2 * v2[k, mine, :]
        displacement[k, 1 - sub] = (
            c0 * v0_inner[k, mine, :] + c1 * v1_inner[k, mine, :] + c2 * v2_inner[k, mine, :]
        )


def scale_kernel(*refs):
    slopes, (chain_factor, scaled, same, cross, across) = refs[:-5], refs[-5:]
    sub = lax.axis_index("sub")
    total = slopes[0][...]
    for other in slopes[1:]:
        total = total + other[...]
    scaled[...] = total * chain_factor[...]
    window = same.shape[0]
    shift = scaled.shape[0] - window
    same[...] = scaled[pl.ds(pl.multiple_of(sub * shift, 8), window), :]
    cross[...] = scaled[pl.ds(pl.multiple_of((1 - sub) * shift, 8), window), :]
    across[...] = cross[...]


def gradient_kernel(scaled, outer, far, partner, gradient, planes, sums):
    sub = lax.axis_index("sub")
    window = partner.shape[0]
    shift = scaled.shape[0] - window
    mine = scaled[pl.ds(pl.multiple_of(sub * shift, 8), window), :]

    @pl.when(sub == 0)
    def _():
        planes[0] = outer[...]
        planes[1] = mine
        planes[2] = partner[...]
        planes[3] = far[...]

    @pl.when(sub == 1)
    def _():
        planes[0] = far[...]
        planes[1] = partner[...]
        planes[2] = mine
        planes[3] = outer[...]

    half = gradient.shape[1]
    part = pl.ds(pl.multiple_of(sub * (window - half), 8), half)
    for layer in range(2):
        sums[...] = filter_planes(planes[layer], planes[layer + 1], planes[layer + 2])
        gradient[layer] = sums[part, :]


def call(body, outs, scratch=(), name=None, work=False):
    cost = pl.CostEstimate(flops=10**7, bytes_accessed=4 * 10**6, transcendentals=0)
    return pl.pallas_call(
        body,
        out_shape=[jax.ShapeDtypeStruct(shape, jnp.float32) for shape in outs],
        scratch_shapes=[pltpu.VMEM(shape, jnp.float32) for shape in scratch],
        compiler_params=pltpu.CompilerParams(vmem_limit_bytes=16 * 2**20),
        cost_estimate=cost if work else None,
        name=name,
    )


def routes(mods, slabs):
    chips = mods * slabs

    def at(chip, sub):
        return 2 * chip + sub

    def beside(chip, steps, cyclic):
        target = chip + steps
        if cyclic:
            return target % chips
        return target if 0 <= target < chips else None

    def built(moves, cyclic):
        pairs = []
        for chip in range(chips):
            for sub, steps, to in moves:
                target = beside(chip, steps, cyclic)
                if target is not None:
                    pairs.append((at(chip, sub), at(target, to)))
        return pairs

    def in_module(moves):
        pairs = []
        for chip in range(chips):
            mod, slab = divmod(chip, slabs)
            for sub, steps, to in moves:
                pairs.append((at(chip, sub), at(mod * slabs + (slab + steps) % slabs, to)))
        return pairs

    return dict(
        swap=built([(0, 0, 1), (1, 0, 0)], True),
        first=built([(0, 1, 0), (1, -1, 1)], True),
        second=built([(1, 1, 0), (0, -1, 1)], True),
        third=in_module([(0, 1, 1), (1, 1, 0)]),
        fourth=in_module([(0, 1, 0), (1, 1, 1)]),
        outer=built([(1, 1, 0), (0, -1, 1)], False),
        down=built([(0, -1, 1)], False),
        halo_cross=in_module([(1, 1, 0), (0, -1, 1)]),
        halo_same=in_module([(0, -1, 0), (1, 1, 1)]),
    )


def module_routes(mods):
    if mods & (mods - 1) == 0:
        return [[(m, m ^ s) for m in range(mods)] for s in range(1, mods)]
    return [[(m, (m + s) % mods) for m in range(mods)] for s in range(1, mods)]


def local(mods, slabs, design, fixed, load):
    half, width = design.shape[1:]
    count = 2 * half
    path = routes(mods, slabs)

    def move(value, name):
        return lax.ppermute(value, AXES, path[name])

    plane = (count, width)
    layer = (3, count, width)
    block = (half, width)
    free = (1 - fixed).astype(jnp.float32)
    swap, first, second, third, fourth, own = call(
        prepare_kernel,
        [(11,) + block, (4,) + block, (4,) + block, block, block, (11,) + block],
        name="prepare",
    )(free, load, design)
    first = move(first, "first")
    second = move(second, "second")
    third = move(third, "third")
    fourth = move(fourth, "fourth")
    swap = move(swap, "swap")

    def start_body(*refs):
        start_outer_kernel(mods, slabs, *refs)

    v0, v0_inner, free, fields, parts = call(
        start_inner_kernel,
        [layer, layer, layer, (12,) + plane, (3,) + plane],
        [(2,) + plane],
        name="start_inner",
        work=True,
    )(own, swap)
    v1, v0_high, mod_inner, mod_outer, mod_own, slope_factor, chain_factor, moments = call(
        start_body,
        [layer, layer, plane, plane, plane, plane, plane, (8, width)],
        [layer, plane, plane],
        name="start_outer",
    )(first, second, third, fourth, v0, v0_inner, free, fields, parts)
    outer = move(v1, "outer")
    inner = move(v1, "swap")
    (fields,) = call(second_inner_kernel, [(12,) + plane], name="second_inner", work=True)(v1, inner)
    v2, v1_high, moments = call(
        second_outer_kernel, [layer, layer, (8, width)], name="second_outer"
    )(v1, outer, inner, fields, free, mod_inner, mod_outer, moments)
    v2_outer = move(v2, "down")
    v2_inner = move(v2, "swap")
    moments, v2_high = call(third_kernel, [(8, width), layer], name="third")(
        v2_outer, v2_inner, v2, mod_own, moments
    )
    devices = 2 * mods * slabs
    gathered = lax.all_to_all(
        jnp.broadcast_to(moments, (devices, 8, width)), AXES, 0, 0, tiled=True
    )
    slope, factors = call(
        combine_kernel, [plane, (3, 8, width)], [layer, layer], name="combine"
    )(gathered, v0, v0_high, v1, v1_high, v2, v2_high, slope_factor)
    slopes = [slope] + [lax.ppermute(slope, "mod", pairs) for pairs in module_routes(mods)]
    (displacement,) = call(displace_kernel, [(3, 2, half, width)], name="displace", work=True)(
        factors, v0, v0_inner, v1, inner, v2, v2_inner
    )
    window = half + 8
    scaled, same, cross, across = call(
        scale_kernel, [plane, (window, width), (window, width), (window, width)], name="scale"
    )(*slopes, chain_factor)
    scaled, displacement = lax.optimization_barrier((scaled, displacement))
    outer = move(cross, "halo_cross")
    far = move(same, "halo_same")
    partner = move(across, "swap")
    (gradient,) = call(
        gradient_kernel, [(2, half, width)], [(4, window, width), (window, width)], name="gradient"
    )(scaled, outer, far, partner)
    return displacement, gradient


def solution(mesh):
    mods, slabs = mesh.shape["mod"], mesh.shape["slab"]
    assert mesh.shape["sub"] == 2
    deck = P(None, ("mod", "slab"), "sub", None)

    def body(design, fixed_mask, load_mask):
        return local(mods, slabs, design, fixed_mask, load_mask)

    return jax.shard_map(
        body,
        mesh=mesh,
        in_specs=(P("slab", "sub", None), deck, deck),
        out_specs=(deck, P("slab", "sub", None)),
        check_vma=False,
    )
```

```python
import math

import jax
import jax.numpy as jnp
import numpy as np
from jax import lax
from jax.experimental import pallas as pl
from jax.experimental.pallas import tpu as pltpu
from jax.sharding import PartitionSpec as P

stiff_floor = 0.01
penalty = 3.0
sharpness = 4.0
threshold = 0.5
filter_reach = 1.8

AXES = ("mod", "slab", "sub")
ROWS = 64
FEW = 16
FACE = filter_reach - 1.0
EDGE = filter_reach - math.sqrt(2.0)
CORNER = filter_reach - math.sqrt(3.0)
LOWER = math.tanh(sharpness * threshold)
UPPER = math.tanh(sharpness * (1.0 - threshold))


def stiffness_modes():
    poisson = 0.3
    lame = poisson / ((1.0 + poisson) * (1.0 - 2.0 * poisson))
    shear = 1.0 / (2.0 * (1.0 + poisson))
    elastic = np.zeros((6, 6))
    elastic[:3, :3] = lame
    for axis in range(3):
        elastic[axis, axis] += 2.0 * shear
        elastic[axis + 3, axis + 3] = shear
    offset = 0.5 / math.sqrt(3.0)
    points = [0.5 - offset, 0.5 + offset]
    stiffness = np.zeros((24, 24))
    for point in ((a, b, c) for a in points for b in points for c in points):
        strain = np.zeros((6, 24))
        for corner in range(8):
            bits = (corner >> 2 & 1, corner >> 1 & 1, corner & 1)
            along = [point[a] if bits[a] else 1.0 - point[a] for a in range(3)]
            sign = [1.0 if bits[a] else -1.0 for a in range(3)]
            gx = sign[0] * along[1] * along[2]
            gy = along[0] * sign[1] * along[2]
            gz = along[0] * along[1] * sign[2]
            col = 3 * corner
            strain[0, col] = gx
            strain[1, col + 1] = gy
            strain[2, col + 2] = gz
            strain[3, col], strain[3, col + 1] = gy, gx
            strain[4, col + 1], strain[4, col + 2] = gz, gy
            strain[5, col], strain[5, col + 2] = gz, gx
        stiffness += strain.T @ elastic @ strain / 8.0
    basis = np.zeros((24, 24))
    for mode in range(8):
        for corner in range(8):
            value = 1.0
            for bit in range(3):
                if mode >> bit & 1 and not corner >> bit & 1:
                    value = -value
            for k in range(3):
                basis[3 * mode + k, 3 * corner + k] = value
    table = basis @ stiffness @ basis.T / 64.0
    table[np.abs(table) < 1e-9] = 0.0
    return table


TABLE = stiffness_modes()


def lanes(shape):
    return lax.broadcasted_iota(jnp.int32, shape, 1)


def rows(shape):
    return lax.broadcasted_iota(jnp.int32, shape, 0)


def z_up(x):
    return jnp.where(lanes(x.shape) < x.shape[1] - 1, pltpu.roll(x, x.shape[1] - 1, 1), 0.0)


def z_down(x):
    return jnp.where(lanes(x.shape) > 0, pltpu.roll(x, 1, 1), 0.0)


def y_up(x):
    return jnp.where(rows(x.shape) < x.shape[0] - 1, pltpu.roll(x, x.shape[0] - 1, 0), 0.0)


def y_down(x):
    return jnp.where(rows(x.shape) > 0, pltpu.roll(x, 1, 0), 0.0)


def two_rows(read, y0, count, size):
    here = read(y0)
    above = y_up(here) if y0 + size == count else read(y0 + 1)
    return here, above


def face_modes(here, above):
    out = []
    for part in (here + above, above - here):
        shifted = z_up(part)
        out += [part + shifted, shifted - part]
    return out


def element_modes(own, other, side):
    sums = [[other[k][m] + own[k][m] for m in range(4)] for k in range(3)]
    diffs = [[(other[k][m] - own[k][m]) * side for m in range(4)] for k in range(3)]
    return [sums[k] + diffs[k] for k in range(3)]


def mode_forces(q):
    made = {}

    def scaled(j, value):
        key = (j, round(value, 12))
        if key not in made:
            made[key] = q[j % 3][j // 3] * np.float32(value)
        return made[key]

    out = [[None] * 8 for _ in range(3)]
    for i in range(24):
        total = None
        for j in np.nonzero(TABLE[i])[0]:
            term = scaled(int(j), float(TABLE[i, j]))
            total = term if total is None else total + term
        out[i % 3][i // 3] = total
    return out


def element_energy(q):
    r = mode_forces(q)
    total = None
    for k in range(3):
        for m in range(1, 8):
            term = q[k][m] * r[k][m]
            total = term if total is None else total + term
    return total


def own_fields(own, other, side):
    r = mode_forces(element_modes(own, other, side))
    fields = []
    for k in range(3):
        for m in range(4):
            d = r[k][m + 4] * side
            fields.append(-d if r[k][m] is None else r[k][m] - d)
    return fields


def layer_modes(read, y0, count, size=ROWS):
    heres, modes = [], []
    for k in range(3):
        here, above = two_rows(lambda y, k=k: read(k, y), y0, count, size)
        heres.append(here)
        modes.append(face_modes(here, above))
    return heres, modes


def fields_loop(count, read_own, read_other, side, fields):
    for y0 in range(0, count, ROWS):
        _, own = layer_modes(read_own, y0, count)
        _, other = layer_modes(read_other, y0, count)
        for n, value in enumerate(own_fields(own, other, side)):
            fields[n, pl.ds(y0, ROWS), :] = value


def operator_loop(count, read_own, read_other, side, fields, mod_inner, mod_outer, free, out_ref):
    shape = (ROWS, out_ref.shape[2])
    square = jnp.zeros(shape, jnp.float32)
    cross = jnp.zeros(shape, jnp.float32)
    norm = jnp.zeros(shape, jnp.float32)
    carry = [jnp.zeros(shape, jnp.float32)] * 3
    first = rows(shape) == 0
    for y0 in range(0, count, ROWS):
        part = pl.ds(y0, ROWS)
        owns, own = layer_modes(read_own, y0, count)
        _, other = layer_modes(read_other, y0, count)
        inner, outer = mod_inner[part, :], mod_outer[part, :]
        total = [
            outer * value + inner * fields[n, part, :]
            for n, value in enumerate(own_fields(own, other, side))
        ]
        for k in range(3):
            faces = []
            for py in range(2):
                s, d = total[4 * k + 2 * py], total[4 * k + 2 * py + 1]
                faces.append((s - d) + z_down(s + d))
            rolled = pltpu.roll(faces[0] + faces[1], 1, 0)
            force = (faces[0] - faces[1]) + jnp.where(first, carry[k], rolled)
            carry[k] = rolled
            image = free[k, part, :] * force
            out_ref[k, part, :] = image
            square += image * image
            cross += owns[k] * image
            norm += owns[k] * owns[k]
    return norm, cross, square


def energy_loop(count, read_own, read_high, use):
    for y0 in range(0, count, FEW):
        _, own = layer_modes(read_own, y0, count, FEW)
        _, high = layer_modes(read_high, y0, count, FEW)
        use(y0, element_energy(element_modes(own, high, 1.0)))


def rows_of(ref, size=ROWS):
    return lambda k, y: ref[k, pl.ds(y, size), :]


def inner_side(sub):
    return jnp.where(sub == 0, 1.0, -1.0).astype(jnp.float32)


def line(tile):
    return jnp.sum(tile, axis=0, keepdims=True)


def prepare_kernel(free, load, design, swap, first, second, third, fourth, own):
    sub = lax.axis_index("sub")
    for k in range(3):
        frees = [free[k, layer] for layer in range(2)]
        values = [frees[layer] * load[k, layer].astype(jnp.float32) for layer in range(2)]
        for layer in range(2):
            swap[2 * k + layer] = values[layer]
            own[2 * k + layer] = values[layer]
        low = sub == 0
        swap[6 + k] = jnp.where(low, frees[1], frees[0])
        own[6 + k] = jnp.where(low, frees[0], frees[1])
        first[k] = jnp.where(low, values[1], values[0])
        second[k] = jnp.where(low, values[0], values[1])
    low = sub == 0
    for layer in range(2):
        swap[9 + layer] = design[layer]
        own[9 + layer] = design[layer]
    later = jnp.where(low, design[1], design[0])
    sooner = jnp.where(low, design[0], design[1])
    first[3] = later
    third[...] = later
    second[3] = sooner
    fourth[...] = sooner


def around(p):
    across = y_up(p) + y_down(p)
    return across + z_up(p) + z_down(p), z_up(across) + z_down(across)


def filter_mid(p):
    face, diag = around(p)
    return filter_reach * p + FACE * face + EDGE * diag


def filter_side(p):
    face, diag = around(p)
    return FACE * p + EDGE * face + CORNER * diag


def filter_planes(low, mid, high):
    return filter_side(low + high) + filter_mid(mid)


def weight_plane(shape, row_offset, count):
    row = rows(shape) + row_offset
    lane = lanes(shape)

    def neighbours(index, size):
        return jnp.where(index > 0, 1.0, 0.0) + jnp.where(index < size - 1, 1.0, 0.0)

    ry = neighbours(row, count)
    rz = neighbours(lane, shape[1])
    face, diag = ry + rz, ry * rz
    return (
        filter_reach
        + FACE * (2.0 + face)
        + EDGE * (2.0 * face + diag)
        + (2.0 * CORNER) * diag
    )


def start_inner_kernel(own, swap, v0, v0_inner, free, fields, parts, layers):
    sub = lax.axis_index("sub")
    half = own.shape[1]
    count = 2 * half
    mine = pl.ds(pl.multiple_of(sub * half, half), half)
    other = pl.ds(pl.multiple_of((1 - sub) * half, half), half)
    for layer in range(2):
        layers[layer, mine, :] = own[9 + layer]
        layers[layer, other, :] = swap[9 + layer]

    @pl.when(sub == 0)
    def _():
        parts[0] = filter_side(layers[0])
        parts[1] = filter_mid(layers[0]) + filter_side(layers[1])

    @pl.when(sub == 1)
    def _():
        parts[0] = filter_mid(layers[0]) + filter_side(layers[1])
        parts[1] = filter_side(layers[0]) + filter_mid(layers[1])

    parts[2] = 1.0 / weight_plane((count, own.shape[2]), 0, count)
    for k in range(3):
        free[k, mine, :] = own[6 + k]
        free[k, other, :] = swap[6 + k]
        v0[k, mine, :] = own[2 * k + sub]
        v0[k, other, :] = swap[2 * k + sub]
        v0_inner[k, mine, :] = own[2 * k + 1 - sub]
        v0_inner[k, other, :] = swap[2 * k + 1 - sub]
    fields_loop(count, rows_of(v0), rows_of(v0_inner), inner_side(sub), fields)


def start_outer_kernel(
    mods, slabs,
    first, second, third, fourth, v0, v0_inner, free, fields, parts,
    v1, v0_high, mod_inner, mod_outer, mod_own, slope_factor, chain_factor, moments,
    v0_outer, near, deep,
):
    mod, slab, sub = (lax.axis_index(a) for a in AXES)
    half = third.shape[0]
    count = 2 * half
    even = sub == 0
    mine = pl.ds(pl.multiple_of(sub * half, half), half)
    other = pl.ds(pl.multiple_of((1 - sub) * half, half), half)
    near[mine, :] = first[3]
    near[other, :] = second[3]
    deep[mine, :] = fourth[...]
    deep[other, :] = third[...]
    starts = (mod == 0) & (slab == 0) & even
    ends = (mod == mods - 1) & (slab == slabs - 1) & (sub == 1)
    inside = jnp.where(ends, 0.0, 1.0)
    for k in range(3):
        v0_outer[k, mine, :] = first[k] * inside
        v0_outer[k, other, :] = second[k] * inside
        v0_high[k] = jnp.where(even, v0_inner[k], v0_outer[k])

    side = filter_side(near[...])
    mid = filter_mid(near[...])
    inverse = parts[2]
    filtered = (parts[0] + filter_side(deep[...]) + jnp.where(even, mid, 0.0)) * inverse
    hyper = jnp.tanh(sharpness * (filtered - threshold))
    projected = (LOWER + hyper) * (1.0 / (LOWER + UPPER))
    below = stiff_floor + (1.0 - stiff_floor) * projected * projected * projected
    below = below * jnp.where(starts, 0.0, 1.0)
    filtered = (parts[1] + side) * inverse
    hyper = jnp.tanh(sharpness * (filtered - threshold))
    projected = (LOWER + hyper) * (1.0 / (LOWER + UPPER))
    squared = projected * projected
    stiff = stiff_floor + (1.0 - stiff_floor) * squared * projected
    mod_own[...] = stiff
    mod_inner[...] = jnp.where(even, stiff, below)
    mod_outer[...] = jnp.where(even, below, stiff)
    slope_factor[...] = (-penalty * (1.0 - stiff_floor)) * squared
    chain_factor[...] = (sharpness / (LOWER + UPPER)) * (1.0 - hyper * hyper) * inverse

    norm, cross, square = operator_loop(
        count, rows_of(v0), rows_of(v0_outer), -inner_side(sub), fields, mod_inner, mod_outer, free, v1
    )
    moments[...] = jnp.concatenate(
        [line(norm), line(cross), line(square), jnp.zeros((5, norm.shape[1]), jnp.float32)], axis=0
    )


def second_inner_kernel(v1, inner, fields):
    fields_loop(v1.shape[1], rows_of(v1), rows_of(inner), inner_side(lax.axis_index("sub")), fields)


def second_outer_kernel(
    v1, outer, inner, fields, free, mod_inner, mod_outer, before, v2, v1_high, moments
):
    sub = lax.axis_index("sub")
    count = v1.shape[1]
    for k in range(3):
        v1_high[k] = jnp.where(sub == 0, inner[k], outer[k])
    _, cross, square = operator_loop(
        count, rows_of(v1), rows_of(outer), -inner_side(sub), fields, mod_inner, mod_outer, free, v2
    )
    zero = jnp.zeros((3, cross.shape[1]), jnp.float32)
    moments[...] = before[...] + jnp.concatenate(
        [zero, line(cross), line(square), zero], axis=0
    )


def third_kernel(v2_outer, v2_inner, v2, mod_own, before, moments, v2_high):
    even = lax.axis_index("sub") == 0
    for k in range(3):
        v2_high[k] = jnp.where(even, v2_inner[k], v2_outer[k])
    count = v2.shape[1]
    total = [jnp.zeros((FEW, v2.shape[2]), jnp.float32)]

    def use(y0, energy):
        total[0] += energy * mod_own[pl.ds(y0, FEW), :]

    energy_loop(
        count,
        lambda k, y: v2[k, pl.ds(y, FEW), :],
        lambda k, y: v2_high[k, pl.ds(y, FEW), :],
        use,
    )
    width = v2.shape[2]
    moments[...] = before[...] + jnp.concatenate(
        [
            jnp.zeros((5, width), jnp.float32),
            line(total[0]),
            jnp.zeros((2, width), jnp.float32),
        ],
        axis=0,
    )


def coefficients(m):
    step = m[0] / m[1]
    x0 = step
    r1 = -step
    norm = m[0] + 2.0 * r1 * m[1] + r1 * r1 * m[2]
    ratio = norm / m[0]
    p0, p1 = 1.0 + ratio, r1
    step = norm / (p0 * p0 * m[1] + 2.0 * p0 * p1 * m[2] + p1 * p1 * m[3])
    x0, x1 = x0 + step * p0, step * p1
    r1, r2 = r1 - step * p0, -step * p1
    after = (
        m[0]
        + 2.0 * r1 * m[1]
        + (r1 * r1 + 2.0 * r2) * m[2]
        + 2.0 * r1 * r2 * m[3]
        + r2 * r2 * m[4]
    )
    ratio = after / norm
    p0, p1, p2 = 1.0 + ratio * p0, r1 + ratio * p1, r2
    step = after / (
        p0 * p0 * m[1]
        + 2.0 * p0 * p1 * m[2]
        + (p1 * p1 + 2.0 * p0 * p2) * m[3]
        + 2.0 * p1 * p2 * m[4]
        + p2 * p2 * m[5]
    )
    return x0 + step * p0, x1 + step * p1, step * p2


def combine_kernel(
    gathered, v0, v0_high, v1, v1_high, v2, v2_high, slope_factor, slope, factors, own, high
):
    count = v0.shape[1]
    sums = jnp.sum(jnp.sum(gathered[...], axis=0), axis=1, keepdims=True)
    c0, c1, c2 = coefficients([sums[k : k + 1] for k in range(6)])
    for n, c in enumerate((c0, c1, c2)):
        factors[n] = jnp.broadcast_to(c, factors.shape[1:])
    for k in range(3):
        own[k] = c0 * v0[k] + c1 * v1[k] + c2 * v2[k]
        high[k] = c0 * v0_high[k] + c1 * v1_high[k] + c2 * v2_high[k]

    def use(y0, energy):
        slope[pl.ds(y0, FEW), :] = slope_factor[pl.ds(y0, FEW), :] * energy

    energy_loop(count, rows_of(own, FEW), rows_of(high, FEW), use)


def displace_kernel(factors, v0, v0_inner, v1, v1_inner, v2, v2_inner, displacement):
    sub = lax.axis_index("sub")
    half = displacement.shape[2]
    mine = pl.ds(pl.multiple_of(sub * half, half), half)
    c0, c1, c2 = (factors[n][:1, :1] for n in range(3))
    for k in range(3):
        displacement[k, sub] = c0 * v0[k, mine, :] + c1 * v1[k, mine, :] + c2 * v2[k, mine, :]
        displacement[k, 1 - sub] = (
            c0 * v0_inner[k, mine, :] + c1 * v1_inner[k, mine, :] + c2 * v2_inner[k, mine, :]
        )


def scale_kernel(*refs):
    slopes, (chain_factor, scaled, same, cross, across) = refs[:-5], refs[-5:]
    sub = lax.axis_index("sub")
    total = slopes[0][...]
    for other in slopes[1:]:
        total = total + other[...]
    scaled[...] = total * chain_factor[...]
    window = same.shape[0]
    shift = scaled.shape[0] - window
    same[...] = scaled[pl.ds(pl.multiple_of(sub * shift, 8), window), :]
    cross[...] = scaled[pl.ds(pl.multiple_of((1 - sub) * shift, 8), window), :]
    across[...] = cross[...]


def gradient_kernel(scaled, outer, far, partner, gradient, planes, sums):
    sub = lax.axis_index("sub")
    window = partner.shape[0]
    shift = scaled.shape[0] - window
    mine = scaled[pl.ds(pl.multiple_of(sub * shift, 8), window), :]

    @pl.when(sub == 0)
    def _():
        planes[0] = outer[...]
        planes[1] = mine
        planes[2] = partner[...]
        planes[3] = far[...]

    @pl.when(sub == 1)
    def _():
        planes[0] = far[...]
        planes[1] = partner[...]
        planes[2] = mine
        planes[3] = outer[...]

    half = gradient.shape[1]
    part = pl.ds(pl.multiple_of(sub * (window - half), 8), half)
    for layer in range(2):
        sums[...] = filter_planes(planes[layer], planes[layer + 1], planes[layer + 2])
        gradient[layer] = sums[part, :]


def call(body, outs, scratch=(), name=None, work=False):
    cost = pl.CostEstimate(flops=10**7, bytes_accessed=4 * 10**6, transcendentals=0)
    return pl.pallas_call(
        body,
        out_shape=[jax.ShapeDtypeStruct(shape, jnp.float32) for shape in outs],
        scratch_shapes=[pltpu.VMEM(shape, jnp.float32) for shape in scratch],
        compiler_params=pltpu.CompilerParams(vmem_limit_bytes=16 * 2**20),
        cost_estimate=cost if work else None,
        name=name,
    )


def routes(mods, slabs):
    chips = mods * slabs

    def at(chip, sub):
        return 2 * chip + sub

    def beside(chip, steps, cyclic):
        target = chip + steps
        if cyclic:
            return target % chips
        return target if 0 <= target < chips else None

    def built(moves, cyclic):
        pairs = []
        for chip in range(chips):
            for sub, steps, to in moves:
                target = beside(chip, steps, cyclic)
                if target is not None:
                    pairs.append((at(chip, sub), at(target, to)))
        return pairs

    def in_module(moves):
        pairs = []
        for chip in range(chips):
            mod, slab = divmod(chip, slabs)
            for sub, steps, to in moves:
                pairs.append((at(chip, sub), at(mod * slabs + (slab + steps) % slabs, to)))
        return pairs

    return dict(
        swap=built([(0, 0, 1), (1, 0, 0)], True),
        first=built([(0, 1, 0), (1, -1, 1)], True),
        second=built([(1, 1, 0), (0, -1, 1)], True),
        third=in_module([(0, 1, 1), (1, 1, 0)]),
        fourth=in_module([(0, 1, 0), (1, 1, 1)]),
        outer=built([(1, 1, 0), (0, -1, 1)], False),
        down=built([(0, -1, 1)], False),
        halo_cross=in_module([(1, 1, 0), (0, -1, 1)]),
        halo_same=in_module([(0, -1, 0), (1, 1, 1)]),
    )


def module_routes(mods):
    if mods & (mods - 1) == 0:
        return [[(m, m ^ s) for m in range(mods)] for s in range(1, mods)]
    return [[(m, (m + s) % mods) for m in range(mods)] for s in range(1, mods)]


def local(mods, slabs, design, fixed, load):
    half, width = design.shape[1:]
    count = 2 * half
    path = routes(mods, slabs)

    def move(value, name):
        return lax.ppermute(value, AXES, path[name])

    plane = (count, width)
    layer = (3, count, width)
    block = (half, width)
    free = (1 - fixed).astype(jnp.float32)
    swap, first, second, third, fourth, own = call(
        prepare_kernel,
        [(11,) + block, (4,) + block, (4,) + block, block, block, (11,) + block],
        name="prepare",
    )(free, load, design)
    first = move(first, "first")
    second = move(second, "second")
    third = move(third, "third")
    fourth = move(fourth, "fourth")
    swap = move(swap, "swap")

    def start_body(*refs):
        start_outer_kernel(mods, slabs, *refs)

    v0, v0_inner, free, fields, parts = call(
        start_inner_kernel,
        [layer, layer, layer, (12,) + plane, (3,) + plane],
        [(2,) + plane],
        name="start_inner",
        work=True,
    )(own, swap)
    v1, v0_high, mod_inner, mod_outer, mod_own, slope_factor, chain_factor, moments = call(
        start_body,
        [layer, layer, plane, plane, plane, plane, plane, (8, width)],
        [layer, plane, plane],
        name="start_outer",
    )(first, second, third, fourth, v0, v0_inner, free, fields, parts)
    outer = move(v1, "outer")
    inner = move(v1, "swap")
    (fields,) = call(second_inner_kernel, [(12,) + plane], name="second_inner", work=True)(v1, inner)
    v2, v1_high, moments = call(
        second_outer_kernel, [layer, layer, (8, width)], name="second_outer"
    )(v1, outer, inner, fields, free, mod_inner, mod_outer, moments)
    v2_outer = move(v2, "down")
    v2_inner = move(v2, "swap")
    moments, v2_high = call(third_kernel, [(8, width), layer], name="third")(
        v2_outer, v2_inner, v2, mod_own, moments
    )
    devices = 2 * mods * slabs
    gathered = lax.all_to_all(
        jnp.broadcast_to(moments, (devices, 8, width)), AXES, 0, 0, tiled=True
    )
    slope, factors = call(
        combine_kernel, [plane, (3, 8, width)], [layer, layer], name="combine"
    )(gathered, v0, v0_high, v1, v1_high, v2, v2_high, slope_factor)
    slopes = [slope] + [lax.ppermute(slope, "mod", pairs) for pairs in module_routes(mods)]
    (displacement,) = call(displace_kernel, [(3, 2, half, width)], name="displace", work=True)(
        factors, v0, v0_inner, v1, inner, v2, v2_inner
    )
    window = half + 8
    scaled, same, cross, across = call(
        scale_kernel, [plane, (window, width), (window, width), (window, width)], name="scale"
    )(*slopes, chain_factor)
    scaled, displacement = lax.optimization_barrier((scaled, displacement))
    outer = move(cross, "halo_cross")
    far = move(same, "halo_same")
    partner = move(across, "swap")
    (gradient,) = call(
        gradient_kernel, [(2, half, width)], [(4, window, width), (window, width)], name="gradient"
    )(scaled, outer, far, partner)
    return displacement, gradient


def solution(mesh):
    mods, slabs = mesh.shape["mod"], mesh.shape["slab"]
    assert mesh.shape["sub"] == 2
    deck = P(None, ("mod", "slab"), "sub", None)

    def body(design, fixed_mask, load_mask):
        return local(mods, slabs, design, fixed_mask, load_mask)

    return jax.shard_map(
        body,
        mesh=mesh,
        in_specs=(P("slab", "sub", None), deck, deck),
        out_specs=(deck, P("slab", "sub", None)),
        check_vma=False,
    )
```

```python
import math

import jax
import jax.numpy as jnp
import numpy as np
from jax import lax
from jax.experimental import pallas as pl
from jax.experimental.pallas import tpu as pltpu
from jax.sharding import PartitionSpec as P

stiff_floor = 0.01
penalty = 3.0
sharpness = 4.0
threshold = 0.5
filter_reach = 1.8

AXES = ("mod", "slab", "sub")
ROWS = 64
FACE = filter_reach - 1.0
EDGE = filter_reach - math.sqrt(2.0)
CORNER = filter_reach - math.sqrt(3.0)
LOWER = math.tanh(sharpness * threshold)
UPPER = math.tanh(sharpness * (1.0 - threshold))


def stiffness_modes():
    poisson = 0.3
    lame = poisson / ((1.0 + poisson) * (1.0 - 2.0 * poisson))
    shear = 1.0 / (2.0 * (1.0 + poisson))
    elastic = np.zeros((6, 6))
    elastic[:3, :3] = lame
    for axis in range(3):
        elastic[axis, axis] += 2.0 * shear
        elastic[axis + 3, axis + 3] = shear
    offset = 0.5 / math.sqrt(3.0)
    points = [0.5 - offset, 0.5 + offset]
    stiffness = np.zeros((24, 24))
    for point in ((a, b, c) for a in points for b in points for c in points):
        strain = np.zeros((6, 24))
        for corner in range(8):
            bits = (corner >> 2 & 1, corner >> 1 & 1, corner & 1)
            along = [point[a] if bits[a] else 1.0 - point[a] for a in range(3)]
            sign = [1.0 if bits[a] else -1.0 for a in range(3)]
            gx = sign[0] * along[1] * along[2]
            gy = along[0] * sign[1] * along[2]
            gz = along[0] * along[1] * sign[2]
            col = 3 * corner
            strain[0, col] = gx
            strain[1, col + 1] = gy
            strain[2, col + 2] = gz
            strain[3, col], strain[3, col + 1] = gy, gx
            strain[4, col + 1], strain[4, col + 2] = gz, gy
            strain[5, col], strain[5, col + 2] = gz, gx
        stiffness += strain.T @ elastic @ strain / 8.0
    basis = np.zeros((24, 24))
    for mode in range(8):
        for corner in range(8):
            value = 1.0
            for bit in range(3):
                if mode >> bit & 1 and not corner >> bit & 1:
                    value = -value
            for k in range(3):
                basis[3 * mode + k, 3 * corner + k] = value
    table = basis @ stiffness @ basis.T / 64.0
    table[np.abs(table) < 1e-9] = 0.0
    return table


TABLE = stiffness_modes()


def lanes(shape):
    return lax.broadcasted_iota(jnp.int32, shape, 1)


def rows(shape):
    return lax.broadcasted_iota(jnp.int32, shape, 0)


def z_up(x):
    return jnp.where(lanes(x.shape) < x.shape[1] - 1, pltpu.roll(x, x.shape[1] - 1, 1), 0.0)


def z_down(x):
    return jnp.where(lanes(x.shape) > 0, pltpu.roll(x, 1, 1), 0.0)


def y_up(x):
    return jnp.where(rows(x.shape) < x.shape[0] - 1, pltpu.roll(x, x.shape[0] - 1, 0), 0.0)


def y_down(x):
    return jnp.where(rows(x.shape) > 0, pltpu.roll(x, 1, 0), 0.0)


def two_rows(read, y0, count):
    here = read(y0)
    above = y_up(here) if y0 + ROWS == count else read(y0 + 1)
    return here, above


def face_modes(here, above):
    out = []
    for part in (here + above, above - here):
        shifted = z_up(part)
        out += [part + shifted, shifted - part]
    return out


def element_modes(own, other, side):
    sums = [[other[k][m] + own[k][m] for m in range(4)] for k in range(3)]
    diffs = [[(other[k][m] - own[k][m]) * side for m in range(4)] for k in range(3)]
    return [sums[k] + diffs[k] for k in range(3)]


def mode_forces(q):
    made = {}

    def scaled(j, value):
        key = (j, round(value, 12))
        if key not in made:
            made[key] = q[j % 3][j // 3] * np.float32(value)
        return made[key]

    out = [[None] * 8 for _ in range(3)]
    for i in range(24):
        total = None
        for j in np.nonzero(TABLE[i])[0]:
            term = scaled(int(j), float(TABLE[i, j]))
            total = term if total is None else total + term
        out[i % 3][i // 3] = total
    return out


def element_energy(q):
    r = mode_forces(q)
    total = None
    for k in range(3):
        for m in range(1, 8):
            term = q[k][m] * r[k][m]
            total = term if total is None else total + term
    return total


def own_fields(own, other, side):
    r = mode_forces(element_modes(own, other, side))
    fields = []
    for k in range(3):
        for m in range(4):
            d = r[k][m + 4] * side
            fields.append(-d if r[k][m] is None else r[k][m] - d)
    return fields


def layer_modes(read, y0, count):
    heres, modes = [], []
    for k in range(3):
        here, above = two_rows(lambda y, k=k: read(k, y), y0, count)
        heres.append(here)
        modes.append(face_modes(here, above))
    return heres, modes


def fields_loop(count, read_own, read_other, side, fields):
    for y0 in range(0, count, ROWS):
        _, own = layer_modes(read_own, y0, count)
        _, other = layer_modes(read_other, y0, count)
        for n, value in enumerate(own_fields(own, other, side)):
            fields[n, pl.ds(y0, ROWS), :] = value


def operator_loop(count, read_own, read_other, side, fields, mod_inner, mod_outer, free, out_ref):
    shape = (ROWS, out_ref.shape[2])
    square = jnp.zeros(shape, jnp.float32)
    cross = jnp.zeros(shape, jnp.float32)
    norm = jnp.zeros(shape, jnp.float32)
    carry = [jnp.zeros(shape, jnp.float32)] * 3
    first = rows(shape) == 0
    for y0 in range(0, count, ROWS):
        part = pl.ds(y0, ROWS)
        owns, own = layer_modes(read_own, y0, count)
        _, other = layer_modes(read_other, y0, count)
        inner, outer = mod_inner[part, :], mod_outer[part, :]
        total = [
            outer * value + inner * fields[n, part, :]
            for n, value in enumerate(own_fields(own, other, side))
        ]
        for k in range(3):
            faces = []
            for py in range(2):
                s, d = total[4 * k + 2 * py], total[4 * k + 2 * py + 1]
                faces.append((s - d) + z_down(s + d))
            rolled = pltpu.roll(faces[0] + faces[1], 1, 0)
            force = (faces[0] - faces[1]) + jnp.where(first, carry[k], rolled)
            carry[k] = rolled
            image = free[k, part, :] * force
            out_ref[k, part, :] = image
            square += image * image
            cross += owns[k] * image
            norm += owns[k] * owns[k]
    return norm, cross, square


def energy_loop(count, read_own, read_high, use):
    for y0 in range(0, count, ROWS):
        _, own = layer_modes(read_own, y0, count)
        _, high = layer_modes(read_high, y0, count)
        use(y0, element_energy(element_modes(own, high, 1.0)))


def rows_of(ref):
    return lambda k, y: ref[k, pl.ds(y, ROWS), :]


def inner_side(sub):
    return jnp.where(sub == 0, 1.0, -1.0).astype(jnp.float32)


def line(tile):
    return jnp.sum(tile, axis=0, keepdims=True)


def prepare_kernel(free, load, design, swap, first, second, third, fourth, own):
    sub = lax.axis_index("sub")
    for k in range(3):
        frees = [free[k, layer] for layer in range(2)]
        values = [frees[layer] * load[k, layer].astype(jnp.float32) for layer in range(2)]
        for layer in range(2):
            swap[2 * k + layer] = values[layer]
            own[2 * k + layer] = values[layer]
        low = sub == 0
        swap[6 + k] = jnp.where(low, frees[1], frees[0])
        own[6 + k] = jnp.where(low, frees[0], frees[1])
        first[k] = jnp.where(low, values[1], values[0])
        second[k] = jnp.where(low, values[0], values[1])
    low = sub == 0
    for layer in range(2):
        swap[9 + layer] = design[layer]
        own[9 + layer] = design[layer]
    later = jnp.where(low, design[1], design[0])
    sooner = jnp.where(low, design[0], design[1])
    first[3] = later
    third[...] = later
    second[3] = sooner
    fourth[...] = sooner


def around(p):
    across = y_up(p) + y_down(p)
    return across + z_up(p) + z_down(p), z_up(across) + z_down(across)


def filter_mid(p):
    face, diag = around(p)
    return filter_reach * p + FACE * face + EDGE * diag


def filter_side(p):
    face, diag = around(p)
    return FACE * p + EDGE * face + CORNER * diag


def filter_planes(low, mid, high):
    return filter_side(low + high) + filter_mid(mid)


def weight_plane(shape, row_offset, count):
    row = rows(shape) + row_offset
    lane = lanes(shape)

    def neighbours(index, size):
        return jnp.where(index > 0, 1.0, 0.0) + jnp.where(index < size - 1, 1.0, 0.0)

    ry = neighbours(row, count)
    rz = neighbours(lane, shape[1])
    face, diag = ry + rz, ry * rz
    return (
        filter_reach
        + FACE * (2.0 + face)
        + EDGE * (2.0 * face + diag)
        + (2.0 * CORNER) * diag
    )


def start_inner_kernel(own, swap, v0, v0_inner, free, fields, parts, layers):
    sub = lax.axis_index("sub")
    half = own.shape[1]
    count = 2 * half
    mine = pl.ds(pl.multiple_of(sub * half, half), half)
    other = pl.ds(pl.multiple_of((1 - sub) * half, half), half)
    for layer in range(2):
        layers[layer, mine, :] = own[9 + layer]
        layers[layer, other, :] = swap[9 + layer]

    @pl.when(sub == 0)
    def _():
        parts[0] = filter_side(layers[0])
        parts[1] = filter_mid(layers[0]) + filter_side(layers[1])

    @pl.when(sub == 1)
    def _():
        parts[0] = filter_mid(layers[0]) + filter_side(layers[1])
        parts[1] = filter_side(layers[0]) + filter_mid(layers[1])

    parts[2] = 1.0 / weight_plane((count, own.shape[2]), 0, count)
    for k in range(3):
        free[k, mine, :] = own[6 + k]
        free[k, other, :] = swap[6 + k]
        v0[k, mine, :] = own[2 * k + sub]
        v0[k, other, :] = swap[2 * k + sub]
        v0_inner[k, mine, :] = own[2 * k + 1 - sub]
        v0_inner[k, other, :] = swap[2 * k + 1 - sub]
    fields_loop(count, rows_of(v0), rows_of(v0_inner), inner_side(sub), fields)


def start_outer_kernel(
    mods, slabs,
    first, second, third, fourth, v0, v0_inner, free, fields, parts,
    v1, v0_high, mod_inner, mod_outer, mod_own, slope_factor, chain_factor, moments,
    v0_outer, near, deep,
):
    mod, slab, sub = (lax.axis_index(a) for a in AXES)
    half = third.shape[0]
    count = 2 * half
    even = sub == 0
    mine = pl.ds(pl.multiple_of(sub * half, half), half)
    other = pl.ds(pl.multiple_of((1 - sub) * half, half), half)
    near[mine, :] = first[3]
    near[other, :] = second[3]
    deep[mine, :] = fourth[...]
    deep[other, :] = third[...]
    starts = (mod == 0) & (slab == 0) & even
    ends = (mod == mods - 1) & (slab == slabs - 1) & (sub == 1)
    inside = jnp.where(ends, 0.0, 1.0)
    for k in range(3):
        v0_outer[k, mine, :] = first[k] * inside
        v0_outer[k, other, :] = second[k] * inside
        v0_high[k] = jnp.where(even, v0_inner[k], v0_outer[k])

    side = filter_side(near[...])
    mid = filter_mid(near[...])
    inverse = parts[2]
    filtered = (parts[0] + filter_side(deep[...]) + jnp.where(even, mid, 0.0)) * inverse
    hyper = jnp.tanh(sharpness * (filtered - threshold))
    projected = (LOWER + hyper) * (1.0 / (LOWER + UPPER))
    below = stiff_floor + (1.0 - stiff_floor) * projected * projected * projected
    below = below * jnp.where(starts, 0.0, 1.0)
    filtered = (parts[1] + side) * inverse
    hyper = jnp.tanh(sharpness * (filtered - threshold))
    projected = (LOWER + hyper) * (1.0 / (LOWER + UPPER))
    squared = projected * projected
    stiff = stiff_floor + (1.0 - stiff_floor) * squared * projected
    mod_own[...] = stiff
    mod_inner[...] = jnp.where(even, stiff, below)
    mod_outer[...] = jnp.where(even, below, stiff)
    slope_factor[...] = (-penalty * (1.0 - stiff_floor)) * squared
    chain_factor[...] = (sharpness / (LOWER + UPPER)) * (1.0 - hyper * hyper) * inverse

    norm, cross, square = operator_loop(
        count, rows_of(v0), rows_of(v0_outer), -inner_side(sub), fields, mod_inner, mod_outer, free, v1
    )
    moments[...] = jnp.concatenate(
        [line(norm), line(cross), line(square), jnp.zeros((5, norm.shape[1]), jnp.float32)], axis=0
    )


def second_outer_kernel(
    v1, outer, inner, free, mod_inner, mod_outer, before, v2, v1_high, moments, fields
):
    sub = lax.axis_index("sub")
    count = v1.shape[1]
    fields_loop(count, rows_of(v1), rows_of(inner), inner_side(sub), fields)
    for k in range(3):
        v1_high[k] = jnp.where(sub == 0, inner[k], outer[k])
    _, cross, square = operator_loop(
        count, rows_of(v1), rows_of(outer), -inner_side(sub), fields, mod_inner, mod_outer, free, v2
    )
    zero = jnp.zeros((3, cross.shape[1]), jnp.float32)
    moments[...] = before[...] + jnp.concatenate(
        [zero, line(cross), line(square), zero], axis=0
    )


def third_kernel(v2_outer, v2_inner, v2, mod_own, before, moments, v2_high):
    even = lax.axis_index("sub") == 0
    for k in range(3):
        v2_high[k] = jnp.where(even, v2_inner[k], v2_outer[k])
    count = v2.shape[1]
    total = [jnp.zeros((ROWS, v2.shape[2]), jnp.float32)]

    def use(y0, energy):
        total[0] += energy * mod_own[pl.ds(y0, ROWS), :]

    energy_loop(
        count,
        lambda k, y: v2[k, pl.ds(y, ROWS), :],
        lambda k, y: v2_high[k, pl.ds(y, ROWS), :],
        use,
    )
    width = v2.shape[2]
    moments[...] = before[...] + jnp.concatenate(
        [
            jnp.zeros((5, width), jnp.float32),
            line(total[0]),
            jnp.zeros((2, width), jnp.float32),
        ],
        axis=0,
    )


def coefficients(m):
    step = m[0] / m[1]
    x0 = step
    r1 = -step
    norm = m[0] + 2.0 * r1 * m[1] + r1 * r1 * m[2]
    ratio = norm / m[0]
    p0, p1 = 1.0 + ratio, r1
    step = norm / (p0 * p0 * m[1] + 2.0 * p0 * p1 * m[2] + p1 * p1 * m[3])
    x0, x1 = x0 + step * p0, step * p1
    r1, r2 = r1 - step * p0, -step * p1
    after = (
        m[0]
        + 2.0 * r1 * m[1]
        + (r1 * r1 + 2.0 * r2) * m[2]
        + 2.0 * r1 * r2 * m[3]
        + r2 * r2 * m[4]
    )
    ratio = after / norm
    p0, p1, p2 = 1.0 + ratio * p0, r1 + ratio * p1, r2
    step = after / (
        p0 * p0 * m[1]
        + 2.0 * p0 * p1 * m[2]
        + (p1 * p1 + 2.0 * p0 * p2) * m[3]
        + 2.0 * p1 * p2 * m[4]
        + p2 * p2 * m[5]
    )
    return x0 + step * p0, x1 + step * p1, step * p2


def combine_kernel(
    gathered, v0, v0_high, v1, v1_high, v2, v2_high, slope_factor, slope, factors, own, high
):
    count = v0.shape[1]
    sums = jnp.sum(jnp.sum(gathered[...], axis=0), axis=1, keepdims=True)
    c0, c1, c2 = coefficients([sums[k : k + 1] for k in range(6)])
    for n, c in enumerate((c0, c1, c2)):
        factors[n] = jnp.broadcast_to(c, factors.shape[1:])
    for k in range(3):
        own[k] = c0 * v0[k] + c1 * v1[k] + c2 * v2[k]
        high[k] = c0 * v0_high[k] + c1 * v1_high[k] + c2 * v2_high[k]

    def use(y0, energy):
        slope[pl.ds(y0, ROWS), :] = slope_factor[pl.ds(y0, ROWS), :] * energy

    energy_loop(count, rows_of(own), rows_of(high), use)


def displace_kernel(factors, v0, v0_inner, v1, v1_inner, v2, v2_inner, displacement):
    sub = lax.axis_index("sub")
    half = displacement.shape[2]
    mine = pl.ds(pl.multiple_of(sub * half, half), half)
    c0, c1, c2 = (factors[n][:1, :1] for n in range(3))
    for k in range(3):
        displacement[k, sub] = c0 * v0[k, mine, :] + c1 * v1[k, mine, :] + c2 * v2[k, mine, :]
        displacement[k, 1 - sub] = (
            c0 * v0_inner[k, mine, :] + c1 * v1_inner[k, mine, :] + c2 * v2_inner[k, mine, :]
        )


def scale_kernel(*refs):
    slopes, (chain_factor, scaled, same, cross, across) = refs[:-5], refs[-5:]
    sub = lax.axis_index("sub")
    total = slopes[0][...]
    for other in slopes[1:]:
        total = total + other[...]
    scaled[...] = total * chain_factor[...]
    window = same.shape[0]
    shift = scaled.shape[0] - window
    same[...] = scaled[pl.ds(pl.multiple_of(sub * shift, 8), window), :]
    cross[...] = scaled[pl.ds(pl.multiple_of((1 - sub) * shift, 8), window), :]
    across[...] = cross[...]


def gradient_kernel(scaled, outer, far, partner, gradient, planes, sums):
    sub = lax.axis_index("sub")
    window = partner.shape[0]
    shift = scaled.shape[0] - window
    mine = scaled[pl.ds(pl.multiple_of(sub * shift, 8), window), :]

    @pl.when(sub == 0)
    def _():
        planes[0] = outer[...]
        planes[1] = mine
        planes[2] = partner[...]
        planes[3] = far[...]

    @pl.when(sub == 1)
    def _():
        planes[0] = far[...]
        planes[1] = partner[...]
        planes[2] = mine
        planes[3] = outer[...]

    half = gradient.shape[1]
    part = pl.ds(pl.multiple_of(sub * (window - half), 8), half)
    for layer in range(2):
        sums[...] = filter_planes(planes[layer], planes[layer + 1], planes[layer + 2])
        gradient[layer] = sums[part, :]


def call(body, outs, scratch=(), name=None, work=False):
    cost = pl.CostEstimate(flops=10**7, bytes_accessed=4 * 10**6, transcendentals=0)
    return pl.pallas_call(
        body,
        out_shape=[jax.ShapeDtypeStruct(shape, jnp.float32) for shape in outs],
        scratch_shapes=[pltpu.VMEM(shape, jnp.float32) for shape in scratch],
        compiler_params=pltpu.CompilerParams(vmem_limit_bytes=16 * 2**20),
        cost_estimate=cost if work else None,
        name=name,
    )


def routes(mods, slabs):
    chips = mods * slabs

    def at(chip, sub):
        return 2 * chip + sub

    def beside(chip, steps, cyclic):
        target = chip + steps
        if cyclic:
            return target % chips
        return target if 0 <= target < chips else None

    def built(moves, cyclic):
        pairs = []
        for chip in range(chips):
            for sub, steps, to in moves:
                target = beside(chip, steps, cyclic)
                if target is not None:
                    pairs.append((at(chip, sub), at(target, to)))
        return pairs

    def in_module(moves):
        pairs = []
        for chip in range(chips):
            mod, slab = divmod(chip, slabs)
            for sub, steps, to in moves:
                pairs.append((at(chip, sub), at(mod * slabs + (slab + steps) % slabs, to)))
        return pairs

    return dict(
        swap=built([(0, 0, 1), (1, 0, 0)], True),
        first=built([(0, 1, 0), (1, -1, 1)], True),
        second=built([(1, 1, 0), (0, -1, 1)], True),
        third=in_module([(0, 1, 1), (1, 1, 0)]),
        fourth=in_module([(0, 1, 0), (1, 1, 1)]),
        outer=built([(1, 1, 0), (0, -1, 1)], False),
        down=built([(0, -1, 1)], False),
        halo_cross=in_module([(1, 1, 0), (0, -1, 1)]),
        halo_same=in_module([(0, -1, 0), (1, 1, 1)]),
    )


def module_routes(mods):
    if mods & (mods - 1) == 0:
        return [[(m, m ^ s) for m in range(mods)] for s in range(1, mods)]
    return [[(m, (m + s) % mods) for m in range(mods)] for s in range(1, mods)]


def local(mods, slabs, design, fixed, load):
    half, width = design.shape[1:]
    count = 2 * half
    path = routes(mods, slabs)

    def move(value, name):
        return lax.ppermute(value, AXES, path[name])

    plane = (count, width)
    layer = (3, count, width)
    block = (half, width)
    free = (1 - fixed).astype(jnp.float32)
    swap, first, second, third, fourth, own = call(
        prepare_kernel,
        [(11,) + block, (4,) + block, (4,) + block, block, block, (11,) + block],
        name="prepare",
    )(free, load, design)
    first = move(first, "first")
    second = move(second, "second")
    third = move(third, "third")
    fourth = move(fourth, "fourth")
    swap = move(swap, "swap")

    def start_body(*refs):
        start_outer_kernel(mods, slabs, *refs)

    v0, v0_inner, free, fields, parts = call(
        start_inner_kernel,
        [layer, layer, layer, (12,) + plane, (3,) + plane],
        [(2,) + plane],
        name="start_inner",
        work=True,
    )(own, swap)
    v1, v0_high, mod_inner, mod_outer, mod_own, slope_factor, chain_factor, moments = call(
        start_body,
        [layer, layer, plane, plane, plane, plane, plane, (8, width)],
        [layer, plane, plane],
        name="start_outer",
    )(first, second, third, fourth, v0, v0_inner, free, fields, parts)
    outer = move(v1, "outer")
    inner = move(v1, "swap")
    v2, v1_high, moments = call(
        second_outer_kernel, [layer, layer, (8, width)], [(12,) + plane], name="second"
    )(v1, outer, inner, free, mod_inner, mod_outer, moments)
    v2_outer = move(v2, "down")
    v2_inner = move(v2, "swap")
    moments, v2_high = call(third_kernel, [(8, width), layer], name="third")(
        v2_outer, v2_inner, v2, mod_own, moments
    )
    devices = 2 * mods * slabs
    gathered = lax.all_to_all(
        jnp.broadcast_to(moments, (devices, 8, width)), AXES, 0, 0, tiled=True
    )
    slope, factors = call(
        combine_kernel, [plane, (3, 8, width)], [layer, layer], name="combine"
    )(gathered, v0, v0_high, v1, v1_high, v2, v2_high, slope_factor)
    slopes = [slope] + [lax.ppermute(slope, "mod", pairs) for pairs in module_routes(mods)]
    (displacement,) = call(displace_kernel, [(3, 2, half, width)], name="displace", work=True)(
        factors, v0, v0_inner, v1, inner, v2, v2_inner
    )
    window = half + 8
    scaled, same, cross, across = call(
        scale_kernel, [plane, (window, width), (window, width), (window, width)], name="scale"
    )(*slopes, chain_factor)
    scaled, displacement = lax.optimization_barrier((scaled, displacement))
    outer = move(cross, "halo_cross")
    far = move(same, "halo_same")
    partner = move(across, "swap")
    (gradient,) = call(
        gradient_kernel, [(2, half, width)], [(4, window, width), (window, width)], name="gradient"
    )(scaled, outer, far, partner)
    return displacement, gradient


def solution(mesh):
    mods, slabs = mesh.shape["mod"], mesh.shape["slab"]
    assert mesh.shape["sub"] == 2
    deck = P(None, ("mod", "slab"), "sub", None)

    def body(design, fixed_mask, load_mask):
        return local(mods, slabs, design, fixed_mask, load_mask)

    return jax.shard_map(
        body,
        mesh=mesh,
        in_specs=(P("slab", "sub", None), deck, deck),
        out_specs=(deck, P("slab", "sub", None)),
        check_vma=False,
    )
```
